32 devices in a mesh: narrow: 4 (over y, core), wide: 8 (over z, x).
Axes of the slice: x: 2, y: 2, z: 4, core: 2. Of those that a mesh axis runs over, the one named last changes fastest.
Arguments:
- queries: bfloat16 [32768, 128], P(('wide', 'narrow')), may hold values from -0.5 to 0.5
- keys: bfloat16 [32768, 128], P(('wide', 'narrow')), may hold values from -6 to 6
- values: bfloat16 [32768, 1024], P(('wide', 'narrow')), may hold values from -6 to 6
- log_decay: float32 [8, 32768], P(None, ('wide', 'narrow')), may hold values from -1 to 0
- level_weight: float32 [8, 8, 32768], P(None, None, ('wide', 'narrow')), may hold values from 0 to 2
- norm_gain: float32 [1024], replicated, may hold values from 0.5 to 1.5
Outputs:
- layer_output: bfloat16 [32768, 1024], P(('wide', 'narrow'))
The draws below stay inside these ranges and needn't reach their ends.
All inputs are finite; a program needn't handle non-finite values.
Results may differ from the reference program's by a relative error of at most 0.005.
Values sent between devices are 32-bit elements; how exact they have to be, the bound alone decides.
No kernel may reach another device: no remote copies, remote signals or barrier semaphores. Data moves between devices by JAX's collectives and lax.ppermute only.
A program may use at most 128 MiB of HBM per device.

```python
import math
import jax
import jax.numpy as jnp
from jax import lax

HEADS = 8
KEY = 128
HEAD = 128
SPAN = 256
TOK_DEV = 1024
TOKEN_COUNT = 32768
LEVELS = 8


def draw_log_decay(key, part):
    sequence_lanes = jax.random.split(key, 7)
    quick = jax.random.randint(sequence_lanes[0], (HEADS,), 0, 2) == 1
    slow_total = jax.random.uniform(sequence_lanes[1], (HEADS,), jnp.float32, 0.03, 0.3)
    quick_rate = jnp.exp(jax.random.uniform(sequence_lanes[2], (HEADS,), jnp.float32, math.log(1.0 / 50.0), math.log(1.0 / 30.0)))
    token_factor_scale = jnp.exp(jax.random.uniform(sequence_lanes[3], (HEADS, TOKEN_COUNT), jnp.float32, -math.log(2.0), math.log(2.0)))
    block_factor_scale = jnp.exp(jax.random.uniform(sequence_lanes[4], (HEADS, TOKEN_COUNT // TOK_DEV), jnp.float32, -math.log(2.0), math.log(2.0)))
    block_factor_scale = jnp.repeat(block_factor_scale, TOK_DEV, axis=1)
    baseline_rate = jnp.where(quick[:, None], quick_rate[:, None], (slow_total / TOKEN_COUNT)[:, None])
    surge_positions = jax.random.randint(sequence_lanes[5], (3,), 0, TOKEN_COUNT)
    surge_lengths = jax.random.uniform(sequence_lanes[6], (3,), jnp.float32, 0.22, 0.5)
    slot_positions = jnp.arange(TOKEN_COUNT)
    surge_groups = jnp.sum(jnp.where(slot_positions[None, :] == surge_positions[:, None], surge_lengths[:, None], 0.0), axis=0)
    return -(baseline_rate * token_factor_scale * block_factor_scale + surge_groups[None, :])


def draw_level_weight(key, part):
    level_index = jnp.arange(LEVELS, dtype=jnp.float32)[:, None, None]
    base_weight = jnp.exp(jax.random.uniform(key, (LEVELS, HEADS, TOKEN_COUNT), jnp.float32, -math.log(2.0), math.log(2.0)))
    return base_weight * jnp.exp2(-0.5 * level_index)


def shard_levels(stream_key, extent, pieces, low, largest):
    factor_of, own = 1.0, jax.random.fold_in(stream_key, 6)
    for dim, shards_of in pieces:
        draws = jnp.exp(jax.random.uniform(jax.random.fold_in(own, dim), (shards_of,), jnp.float32, low / len(pieces), largest / len(pieces)))
        factor_of = factor_of * jnp.repeat(draws, extent[dim] // shards_of).reshape([-1 if axis == dim else 1 for axis in range(len(extent))])
    return factor_of


def gaussian(rng, dims, scale, bound, cuts=(), kind=jnp.bfloat16):
    values = jax.random.normal(rng, dims, jnp.float32) * scale
    if len(cuts) > 0:
        values = shard_levels(rng, dims, cuts, -0.22, 0.18) * values
    return jnp.clip(values, min=-bound, max=bound).astype(kind)


def setup_inputs(seed: int = 0) -> dict:
    splits = jax.random.split(jax.random.key(seed), 7)
    queries = gaussian(splits[0], (TOKEN_COUNT, KEY), KEY ** -0.5, 0.5, ((0, 32),))
    keys = gaussian(splits[1], (TOKEN_COUNT, KEY), 1.0, 6.0, ((0, 32),))
    values = gaussian(splits[2], (TOKEN_COUNT, HEADS * HEAD), 1.0, 6.0, ((0, 32),))
    log_decay = draw_log_decay(jax.random.fold_in(splits[6], 71), 0)
    level_weight = draw_level_weight(jax.random.fold_in(splits[6], 71), 0)
    norm_gain = jnp.clip(1.0 + 0.1 * jax.random.normal(splits[5], (HEADS * HEAD,), jnp.float32), 0.5, 1.5)
    return {"queries": queries, "keys": keys, "values": values, "log_decay": log_decay, "level_weight": level_weight, "norm_gain": norm_gain}


def reference(queries, keys, values, log_decay, level_weight, norm_gain):
    block_count = TOKEN_COUNT // SPAN
    upper_levels = LEVELS - 1
    query_blocks = queries.reshape(block_count, SPAN, KEY)
    key_blocks = keys.reshape(block_count, SPAN, KEY)
    value_blocks = values.reshape(block_count, SPAN, HEADS, HEAD)
    decay_blocks = log_decay.reshape(HEADS, block_count, SPAN).transpose(1, 0, 2)
    weight_blocks = level_weight.reshape(LEVELS, HEADS, block_count, SPAN).transpose(2, 0, 1, 3)
    positions = jnp.arange(SPAN, dtype=jnp.int32)
    causal = positions[:, None] >= positions[None, :]
    level_ids = jnp.arange(upper_levels, dtype=jnp.int32)
    periods = jnp.left_shift(jnp.ones_like(level_ids), level_ids)
    gain_rows = norm_gain.reshape(HEADS, HEAD)

    def advance(carried, inputs):
        running, finished = carried
        query_rows, key_rows, value_rows, decay_rows, weight_rows, block_id = inputs
        within = jnp.cumsum(decay_rows, axis=1)
        scores = jnp.dot(query_rows, key_rows.T, preferred_element_type=jnp.float32)
        spread = jnp.where(causal[None], within[:, :, None] - within[:, None, :], -1e+30)
        mixing = (scores[None] * jnp.exp(spread) * weight_rows[0][:, :, None]).astype(jnp.bfloat16)
        value_float = value_rows.astype(jnp.float32)
        intra = jnp.einsum('hij,jhp->hip', mixing.astype(jnp.float32), value_float)
        present = jnp.bitwise_and(jnp.right_shift(block_id, level_ids), 1).astype(jnp.float32)
        level_states = (finished * present[:, None, None, None]).astype(jnp.bfloat16)
        projected = jnp.einsum('in,lhnp->lhip', query_rows.astype(jnp.float32), level_states.astype(jnp.float32))
        inter = lax.optimization_barrier(jnp.sum(weight_rows[1:][:, :, :, None] * projected, axis=0))
        mixed = intra + jnp.exp(within)[:, :, None] * inter
        block_total = within[:, -1]
        decayed_keys = (jnp.exp(block_total[:, None] - within)[:, :, None] * key_rows.astype(jnp.float32)[None]).astype(jnp.bfloat16)
        state = jnp.einsum('hjn,jhp->hnp', decayed_keys.astype(jnp.float32), value_float)
        fading = jnp.exp(block_total)[None, :, None, None]
        running = running * fading + state[None]
        finished = finished * fading
        closing = (jnp.remainder(block_id + 1, periods) == 0)[:, None, None, None]
        finished = jnp.where(closing, running, finished)
        running = jnp.where(closing, jnp.zeros_like(running), running)
        square = lax.optimization_barrier(jnp.mean(mixed * mixed, axis=-1, keepdims=True))
        normed = mixed * lax.rsqrt(square + 1e-05) * gain_rows[:, None, :]
        output_rows = normed.transpose(1, 0, 2).reshape(SPAN, HEADS * HEAD).astype(jnp.bfloat16)
        return ((running, finished), output_rows)
    empty_state = jnp.zeros((upper_levels, HEADS, KEY, HEAD), jnp.float32)
    block_ids = jnp.arange(block_count, dtype=jnp.int32)
    final_carry, outputs = lax.scan(advance, (empty_state, empty_state), (query_blocks, key_blocks, value_blocks, decay_blocks, weight_blocks, block_ids))
    return outputs.reshape(TOKEN_COUNT, HEADS * HEAD)
```

```python
import functools

import jax
import jax.numpy as jnp
from jax import lax
from jax.experimental import pallas as pl
from jax.experimental.pallas import tpu as pltpu
from jax.sharding import PartitionSpec as P

SPAN = 256
EPS = 1e-05
AXES = ("narrow", "wide")
NT = (((1,), (1,)), ((), ()))
VMEM = 56 * 1024 * 1024


def place():
    return lax.axis_index("wide") * lax.axis_size("narrow") + lax.axis_index("narrow")


def bit_of(value, bit):
    return jnp.bitwise_and(jnp.right_shift(value, bit), 1)


def spread_lanes(column, width):
    return jnp.broadcast_to(column, (column.shape[0], width))


def running_sum(values):
    width = values.shape[1]
    lanes = lax.broadcasted_iota(jnp.int32, values.shape, 1)
    shift = 1
    while shift < width:
        values = values + jnp.where(lanes >= shift, pltpu.roll(values, shift, 1), 0.0)
        shift *= 2
    return values


def state_kernel(k_ref, v_ref, decay_ref, message_ref, local_ref, sums_ref, totals_ref, held, run):
    span = pl.program_id(0)
    heads = decay_ref.shape[0]
    key_width = k_ref.shape[1]
    head_width = v_ref.shape[1] // heads
    local_bits = held.shape[0]

    @pl.when(span == 0)
    def _():
        held[...] = jnp.zeros_like(held)
        run[...] = jnp.zeros_like(run)

    within = running_sum(decay_ref[...])
    total = spread_lanes(within[:, SPAN - 1 :], 128)
    start = run[...]
    sums_ref[0] = within
    sums_ref[1] = within + spread_lanes(start[:, :1], SPAN)
    totals_ref[0] = total
    run[...] = start + total
    fade = jnp.exp(spread_lanes(within[:, SPAN - 1 :], SPAN) - within)
    whole = jnp.exp(total)
    keys_across = k_ref[...].astype(jnp.float32).T
    for head in range(heads):
        columns = slice(head * head_width, (head + 1) * head_width)
        faded = (keys_across * fade[head : head + 1]).astype(jnp.bfloat16)
        state = jnp.dot(faded, v_ref[:, columns], preferred_element_type=jnp.float32)
        offset = 0
        for bit in range(local_bits):
            groups = pl.num_programs(0) >> (bit + 1)
            if bit > 0:
                kept = jnp.where(
                    jnp.bitwise_and(span, 2**bit - 1) == 0, 0.0, held[bit - 1, head]
                )
                merged = kept * whole[head : head + 1] + state
                held[bit - 1, head] = merged
            else:
                merged = state

            @pl.when(
                jnp.logical_and(
                    bit_of(span, bit) == 0,
                    jnp.bitwise_and(span + 1, 2**bit - 1) == 0,
                )
            )
            def _():
                local_ref[offset + jnp.right_shift(span, bit + 1), :, columns] = merged.astype(
                    jnp.bfloat16
                )

            offset = offset + groups
        held[local_bits - 1, head] = held[local_bits - 1, head] * whole[head : head + 1] + state

    @pl.when(span == pl.num_programs(0) - 1)
    def _():
        for head in range(heads):
            message_ref[head * head_width : (head + 1) * head_width] = held[local_bits - 1, head].T
        message_ref[heads * head_width :] = run[...]


def make_states(keys, values, log_decay):
    tokens, key_width = keys.shape
    heads = log_decay.shape[0]
    width = values.shape[1]
    head_width = width // heads
    spans = tokens // SPAN
    local_bits = spans.bit_length() - 1
    return pl.pallas_call(
        state_kernel,
        grid=(spans,),
        in_specs=[
            pl.BlockSpec((SPAN, key_width), lambda c: (c, 0)),
            pl.BlockSpec((SPAN, width), lambda c: (c, 0)),
            pl.BlockSpec((heads, SPAN), lambda c: (0, c)),
        ],
        out_specs=[
            pl.BlockSpec((width + heads, key_width), lambda c: (0, 0)),
            pl.BlockSpec((spans - 1, key_width, width), lambda c: (0, 0, 0)),
            pl.BlockSpec((2, heads, SPAN), lambda c: (0, 0, c)),
            pl.BlockSpec((1, heads, 128), lambda c: (c, 0, 0)),
        ],
        out_shape=[
            jax.ShapeDtypeStruct((width + heads, key_width), jnp.float32),
            jax.ShapeDtypeStruct((spans - 1, key_width, width), jnp.bfloat16),
            jax.ShapeDtypeStruct((2, heads, tokens), jnp.float32),
            jax.ShapeDtypeStruct((spans, heads, 128), jnp.float32),
        ],
        scratch_shapes=[
            pltpu.VMEM((local_bits, heads, key_width, head_width), jnp.float32),
            pltpu.VMEM((heads, 128), jnp.float32),
        ],
        compiler_params=pltpu.CompilerParams(vmem_limit_bytes=VMEM),
        name="states",
    )(keys, values, log_decay)


def local_kernel(
    q_ref, k_ref, v_ref, sums_ref, totals_ref, weight_ref, local_ref, mixed_ref
):
    span = pl.program_id(0)
    heads = weight_ref.shape[1]
    head_width = v_ref.shape[1] // heads
    local_bits = weight_ref.shape[0] - 1
    half = SPAN // 2
    queries = q_ref[...]
    scores = lax.dot_general(k_ref[...], queries, NT, preferred_element_type=jnp.float32)
    within = sums_ref[0]
    within_down = within.T
    values_across = v_ref[...].T
    source = lax.broadcasted_iota(jnp.int32, (half, half), 0)
    target = lax.broadcasted_iota(jnp.int32, (half, half), 1)
    causal = source <= target
    empty = jnp.zeros((half, half), jnp.bfloat16)

    def mix(head, low, high, masked):
        rows = slice(low * half, (low + 1) * half)
        columns = slice(high * half, (high + 1) * half)
        gap = within[head : head + 1, columns] - within_down[rows, head : head + 1]
        if masked:
            gap = jnp.where(causal, gap, -1e30)
        mixing = scores[rows, columns] * jnp.exp(gap) * weight_ref[0, head : head + 1, columns]
        return mixing.astype(jnp.bfloat16)

    for head in range(heads):
        rows = slice(head * head_width, (head + 1) * head_width)
        mixing = jnp.concatenate(
            [
                jnp.concatenate([mix(head, 0, 0, True), mix(head, 0, 1, False)], axis=1),
                jnp.concatenate([empty, mix(head, 1, 1, True)], axis=1),
            ],
            axis=0,
        )
        mixed_ref[rows] = jnp.dot(
            values_across[rows], mixing, preferred_element_type=jnp.float32
        )
    offset = 0
    for bit in range(local_bits):
        since = jnp.zeros((heads, 128), jnp.float32)
        for back in range(1, 2**bit):
            inside = jnp.bitwise_and(span, 2**bit - 1) >= back
            since = since + jnp.where(inside, totals_ref[jnp.maximum(span - back, 0)], 0.0)

        @pl.when(bit_of(span, bit) == 1)
        def _():
            level = local_ref[offset + jnp.right_shift(span, bit + 1)].T
            found = lax.dot_general(level, queries, NT, preferred_element_type=jnp.float32)
            scale = jnp.exp(within + spread_lanes(since[:, :1], SPAN)) * weight_ref[1 + bit]
            for head in range(heads):
                rows = slice(head * head_width, (head + 1) * head_width)
                mixed_ref[rows] += found[rows] * scale[head : head + 1]

        offset = offset + (pl.num_programs(0) >> (bit + 1))


def mix_local(queries, keys, values, sums, totals, level_weight, local):
    tokens, key_width = keys.shape
    heads = level_weight.shape[1]
    width = values.shape[1]
    spans = tokens // SPAN
    local_bits = spans.bit_length() - 1
    return pl.pallas_call(
        local_kernel,
        grid=(spans,),
        in_specs=[
            pl.BlockSpec((SPAN, key_width), lambda c: (c, 0)),
            pl.BlockSpec((SPAN, key_width), lambda c: (c, 0)),
            pl.BlockSpec((SPAN, width), lambda c: (c, 0)),
            pl.BlockSpec((2, heads, SPAN), lambda c: (0, 0, c)),
            pl.BlockSpec((spans, heads, 128), lambda c: (0, 0, 0)),
            pl.BlockSpec((1 + local_bits, heads, SPAN), lambda c: (0, 0, c)),
            pl.BlockSpec((spans - 1, key_width, width), lambda c: (0, 0, 0)),
        ],
        out_specs=pl.BlockSpec((width, SPAN), lambda c: (0, c)),
        out_shape=jax.ShapeDtypeStruct((width, tokens), jnp.float32),
        compiler_params=pltpu.CompilerParams(vmem_limit_bytes=VMEM),
        name="local",
    )(queries, keys, values, sums, totals, level_weight, local)


def merge_kernel(bit, mine_ref, other_ref, prefix_ref, merged_ref, next_ref):
    here = place()
    upper = bit_of(here, bit) == 1
    core = bit_of(here, 0)
    heads = prefix_ref.shape[0]
    held = heads // 2
    rows = merged_ref.shape[0] - heads
    per = rows // held
    width = mine_ref.shape[0] - heads
    first = core * held if width > rows else 0
    mine_total = mine_ref[width:]
    other_total = other_ref[width:]
    fade = jnp.exp(jnp.where(upper, mine_total, other_total))
    for slot in range(held):
        own = jnp.where(
            core == 1, fade[held + slot : held + slot + 1], fade[slot : slot + 1]
        )
        source = pl.ds((first + slot) * per, per)
        mine = mine_ref[source]
        other = other_ref[source]
        merged_ref[slot * per : (slot + 1) * per] = jnp.where(
            upper, other * own + mine, mine * own + other
        )
    merged_ref[rows:] = mine_total + other_total
    next_ref[...] = prefix_ref[...] + jnp.where(upper, other_total, 0.0)


def merge(bit, mine, other, prefix, rows):
    heads = prefix.shape[0]
    return pl.pallas_call(
        functools.partial(merge_kernel, bit),
        out_shape=[
            jax.ShapeDtypeStruct((rows + heads, mine.shape[1]), jnp.float32),
            jax.ShapeDtypeStruct(prefix.shape, jnp.float32),
        ],
        compiler_params=pltpu.CompilerParams(vmem_limit_bytes=VMEM),
        name=f"merge{bit}",
    )(mine, other, prefix)


def finish_kernel(level_count, parts_of, *refs):
    mixed_ref, q_ref, sums_ref, weight_ref, gain_ref = refs[:5]
    prefix_refs = refs[5 : 5 + level_count]
    part_refs = refs[5 + level_count : -2]
    out_ref, levels = refs[-2:]
    heads = weight_ref.shape[1]
    head_width = mixed_ref.shape[0] // heads
    first_level = weight_ref.shape[0] - level_count
    here = place()

    @pl.when(pl.program_id(0) == 0)
    def _():
        at = 0
        for level in range(level_count):
            rows = parts_of[level][0]
            if len(parts_of[level]) == 1:
                levels[level] = part_refs[at][:rows].astype(jnp.bfloat16)
            else:
                mine = bit_of(here, 0) * rows
                levels[level, pl.ds(mine, rows)] = part_refs[at][:rows].astype(jnp.bfloat16)
                levels[level, pl.ds(rows - mine, rows)] = part_refs[at + 1][:rows].astype(
                    jnp.bfloat16
                )
            at += len(parts_of[level])

    queries = q_ref[...]
    since = sums_ref[1]
    gain_down = gain_ref[...].T
    scales = []
    for level in range(level_count):
        active = jnp.where(bit_of(here, level) == 1, 1.0, 0.0)
        reach = jnp.exp(since + spread_lanes(prefix_refs[level][:, :1], SPAN))
        scales.append(reach * weight_ref[first_level + level] * active)
    for head in range(heads):
        rows = slice(head * head_width, (head + 1) * head_width)
        mixed = mixed_ref[rows]
        for level in range(level_count):
            found = lax.dot_general(
                levels[level, rows], queries, NT, preferred_element_type=jnp.float32
            )
            mixed = mixed + found * scales[level][head : head + 1]
        square = jnp.mean(mixed * mixed, axis=0, keepdims=True)
        normed = mixed * lax.rsqrt(square + EPS) * gain_down[:, head : head + 1]
        out_ref[:, rows] = normed.astype(jnp.bfloat16).T


def finish(mixed, queries, sums, level_weight, gain, prefixes, parts):
    width, tokens = mixed.shape
    key_width = queries.shape[1]
    levels, heads, _ = level_weight.shape
    spans = tokens // SPAN
    level_count = len(parts)
    parts_of = []
    for level in parts:
        parts_of.append([width // len(level)] * len(level))
    flat = [part for level in parts for part in level]

    def whole(array):
        return pl.BlockSpec(array.shape, lambda c: (0,) * array.ndim)

    return pl.pallas_call(
        functools.partial(finish_kernel, level_count, parts_of),
        grid=(spans,),
        in_specs=[
            pl.BlockSpec((width, SPAN), lambda c: (0, c)),
            pl.BlockSpec((SPAN, key_width), lambda c: (c, 0)),
            pl.BlockSpec((2, heads, SPAN), lambda c: (0, 0, c)),
            pl.BlockSpec((levels, heads, SPAN), lambda c: (0, 0, c)),
            whole(gain),
            *[whole(array) for array in prefixes],
            *[whole(array) for array in flat],
        ],
        out_specs=pl.BlockSpec((SPAN, width), lambda c: (c, 0)),
        out_shape=jax.ShapeDtypeStruct((tokens, width), jnp.bfloat16),
        scratch_shapes=[pltpu.VMEM((level_count, width, key_width), jnp.bfloat16)],
        compiler_params=pltpu.CompilerParams(vmem_limit_bytes=VMEM),
        name="finish",
    )(mixed, queries, sums, level_weight, gain, *prefixes, *flat)


def trade(value, mask, senders=lambda source: True):
    wide, narrow = lax.axis_size("wide"), lax.axis_size("narrow")

    def ranked(index):
        return index % narrow * wide + index // narrow

    pairs = [
        (ranked(source), ranked(source ^ mask))
        for source in range(wide * narrow)
        if senders(source)
    ]
    return lax.ppermute(value, AXES, pairs)


def swap(value, bit):
    return trade(value, 2**bit)


def per_device(queries, keys, values, log_decay, level_weight, norm_gain):
    heads = log_decay.shape[0]
    width = values.shape[1]
    count = lax.axis_size("wide") * lax.axis_size("narrow")
    message, local, sums, totals = make_states(keys, values, log_decay)
    prefix = jnp.zeros((heads, 128), jnp.float32)
    prefixes, parts = [], []
    rows = width // 2
    for bit in range(count.bit_length() - 1):
        other = swap(message, bit)
        prefixes.append(prefix)
        if bit == 0:
            parts.append([other])
        else:
            parts.append([other, swap(other, 0)])
        if bit < count.bit_length() - 2:
            message, prefix = merge(bit, message, other, prefix, rows)
        elif bit > 0:
            pass
    mixed = mix_local(queries, keys, values, sums, totals, level_weight, local)
    gain = norm_gain.reshape(heads, width // heads)
    return finish(mixed, queries, sums, level_weight, gain, prefixes, parts)


def solution(mesh):
    placed = (
        P(("wide", "narrow"), None),
        P(("wide", "narrow"), None),
        P(("wide", "narrow"), None),
        P(None, ("wide", "narrow")),
        P(None, None, ("wide", "narrow")),
        P(),
    )
    return jax.shard_map(
        per_device,
        mesh=mesh,
        in_specs=placed,
        out_specs=P(("wide", "narrow"), None),
        check_vma=False,
    )
```

```python
import functools

import jax
import jax.numpy as jnp
from jax import lax
from jax.experimental import pallas as pl
from jax.experimental.pallas import tpu as pltpu
from jax.sharding import PartitionSpec as P

SPAN = 256
EPS = 1e-05
AXES = ("narrow", "wide")
NT = (((1,), (1,)), ((), ()))
VMEM = 56 * 1024 * 1024
PARAMS = pltpu.CompilerParams(vmem_limit_bytes=VMEM)


def place():
    return lax.axis_index("wide") * lax.axis_size("narrow") + lax.axis_index("narrow")


def bit_of(value, bit):
    return jnp.bitwise_and(jnp.right_shift(value, bit), 1)


def spread_lanes(column, width):
    return jnp.broadcast_to(column, (column.shape[0], width))


def whole(array):
    return pl.BlockSpec(array.shape, lambda *_: (0,) * len(array.shape))


ANYWHERE = pl.BlockSpec(memory_space=pl.ANY)


def running_sums(rows):
    high = rows.astype(jnp.bfloat16)
    rest = rows - high.astype(jnp.float32)
    middle = rest.astype(jnp.bfloat16)
    low = (rest - middle.astype(jnp.float32)).astype(jnp.bfloat16)
    width = rows.shape[1]
    source = lax.broadcasted_iota(jnp.int32, (width, width), 0)
    target = lax.broadcasted_iota(jnp.int32, (width, width), 1)
    upto = jnp.where(source <= target, 1.0, 0.0).astype(jnp.bfloat16)
    sums = jnp.dot(
        jnp.concatenate([high, middle, low], axis=0), upto, preferred_element_type=jnp.float32
    )
    count = rows.shape[0]
    return sums[:count] + (sums[count : 2 * count] + sums[2 * count :])


def state_kernel(
    k_ref, decay_ref, v_hbm, keep_ref, send_ref, local_ref, sums_ref, totals_ref, v_ref, held, arrived
):
    heads, tokens = decay_ref.shape
    head_width = v_ref.shape[1] // heads
    spans = tokens // SPAN
    rows_of = [slice(span * SPAN, (span + 1) * SPAN) for span in range(spans)]
    copies = [
        pltpu.make_async_copy(v_hbm.at[rows], v_ref.at[rows], arrived.at[span])
        for span, rows in enumerate(rows_of)
    ]
    for copy in copies:
        copy.start()
    within = running_sums(jnp.concatenate([decay_ref[:, rows] for rows in rows_of], axis=0))
    run = jnp.zeros((heads, 128), jnp.float32)
    fades, wholes = [], []
    for span, rows in enumerate(rows_of):
        here = within[span * heads : (span + 1) * heads]
        last = here[:, SPAN - 1 :]
        total = spread_lanes(last, 128)
        sums_ref[0, :, rows] = here
        sums_ref[1, :, rows] = here + spread_lanes(run[:, :1], SPAN)
        totals_ref[span] = total
        run = run + total
        fades.append(jnp.exp(spread_lanes(last, SPAN) - here))
        wholes.append(jnp.exp(total))
    across = [k_ref[rows].astype(jnp.float32).T for rows in rows_of]
    for copy in copies:
        copy.wait()
    for head in range(heads):
        columns = slice(head * head_width, (head + 1) * head_width)
        states = []
        for span, rows in enumerate(rows_of):
            faded = (across[span] * fades[span][head : head + 1]).astype(jnp.bfloat16)
            states.append(
                jnp.dot(faded, v_ref[rows, columns], preferred_element_type=jnp.float32)
            )
        at = 0
        size = 1
        while size < spans:
            for first in range(0, spans, 2 * size):
                group = states[first]
                for span in range(first + 1, first + size):
                    group = group * wholes[span][head : head + 1] + states[span]
                local_ref[at, :, columns] = group.astype(jnp.bfloat16)
                at += 1
            size *= 2
        group = states[0]
        for span in range(1, spans):
            group = group * wholes[span][head : head + 1] + states[span]
        held[columns] = group.T
    half = held.shape[0] // 2
    core = bit_of(place(), 0)
    keep_ref[:half] = held[pl.ds(core * half, half)]
    send_ref[:half] = held[pl.ds((1 - core) * half, half)]
    keep_ref[half:] = run
    send_ref[half:] = run


def make_states(keys, values, log_decay):
    tokens, key_width = keys.shape
    heads = log_decay.shape[0]
    width = values.shape[1]
    spans = tokens // SPAN
    message = jax.ShapeDtypeStruct((width // 2 + heads, key_width), jnp.float32)
    return pl.pallas_call(
        state_kernel,
        in_specs=[whole(keys), whole(log_decay), ANYWHERE],
        out_shape=[
            message,
            message,
            jax.ShapeDtypeStruct((spans - 1, key_width, width), jnp.bfloat16),
            jax.ShapeDtypeStruct((2, heads, tokens), jnp.float32),
            jax.ShapeDtypeStruct((spans, heads, 128), jnp.float32),
        ],
        scratch_shapes=[
            pltpu.VMEM((tokens, width), jnp.bfloat16),
            pltpu.VMEM((width, key_width), jnp.float32),
            pltpu.SemaphoreType.DMA((spans,)),
        ],
        compiler_params=PARAMS,
        name="states",
    )(keys, log_decay, values)


def local_kernel(
    first_span, spans, q_ref, k_ref, v_ref, sums_ref, totals_ref, weight_ref, local_ref, *refs
):
    mixed_ref, done_ref = refs[-2:]
    span = pl.program_id(0) + first_span
    heads = weight_ref.shape[1]
    head_width = v_ref.shape[1] // heads
    local_bits = weight_ref.shape[0] - 1
    half = SPAN // 2
    done_ref[...] = jnp.zeros_like(done_ref)
    queries = q_ref[...]
    scores = lax.dot_general(k_ref[...], queries, NT, preferred_element_type=jnp.float32)
    within = sums_ref[0]
    within_down = within.T
    values_across = v_ref[...].T
    source = lax.broadcasted_iota(jnp.int32, (half, half), 0)
    target = lax.broadcasted_iota(jnp.int32, (half, half), 1)
    causal = source <= target
    empty = jnp.zeros((half, half), jnp.bfloat16)

    def mix(head, low, high, masked):
        rows = slice(low * half, (low + 1) * half)
        columns = slice(high * half, (high + 1) * half)
        gap = within[head : head + 1, columns] - within_down[rows, head : head + 1]
        if masked:
            gap = jnp.where(causal, gap, -1e30)
        mixing = scores[rows, columns] * jnp.exp(gap) * weight_ref[0, head : head + 1, columns]
        return mixing.astype(jnp.bfloat16)

    for head in range(heads):
        rows = slice(head * head_width, (head + 1) * head_width)
        mixing = jnp.concatenate(
            [
                jnp.concatenate([mix(head, 0, 0, True), mix(head, 0, 1, False)], axis=1),
                jnp.concatenate([empty, mix(head, 1, 1, True)], axis=1),
            ],
            axis=0,
        )
        mixed_ref[rows] = jnp.dot(
            values_across[rows], mixing, preferred_element_type=jnp.float32
        )
    offset = 0
    for bit in range(local_bits):
        since = jnp.zeros((heads, 128), jnp.float32)
        for back in range(1, 2**bit):
            inside = jnp.bitwise_and(span, 2**bit - 1) >= back
            since = since + jnp.where(inside, totals_ref[jnp.maximum(span - back, 0)], 0.0)

        @pl.when(bit_of(span, bit) == 1)
        def _():
            level = local_ref[offset + jnp.right_shift(span, bit + 1)].T
            found = lax.dot_general(level, queries, NT, preferred_element_type=jnp.float32)
            scale = jnp.exp(within + spread_lanes(since[:, :1], SPAN)) * weight_ref[1 + bit]
            for head in range(heads):
                rows = slice(head * head_width, (head + 1) * head_width)
                mixed_ref[rows] += found[rows] * scale[head : head + 1]

        offset = offset + (spans >> (bit + 1))


def mix_local(first, count, queries, keys, values, sums, totals, level_weight, local, mixed):
    tokens, key_width = keys.shape
    heads = level_weight.shape[1]
    width = values.shape[1]
    spans = tokens // SPAN
    local_bits = spans.bit_length() - 1
    rest = [] if mixed is None else [mixed]
    return pl.pallas_call(
        functools.partial(local_kernel, first, spans),
        grid=(count,),
        in_specs=[
            pl.BlockSpec((SPAN, key_width), lambda c: (c + first, 0)),
            pl.BlockSpec((SPAN, key_width), lambda c: (c + first, 0)),
            pl.BlockSpec((SPAN, width), lambda c: (c + first, 0)),
            pl.BlockSpec((2, heads, SPAN), lambda c: (0, 0, c + first)),
            whole(totals),
            pl.BlockSpec((1 + local_bits, heads, SPAN), lambda c: (0, 0, c + first)),
            whole(local),
            *[ANYWHERE for _ in rest],
        ],
        out_specs=[
            pl.BlockSpec((width, SPAN), lambda c: (0, c + first)),
            pl.BlockSpec((8, 128), lambda c: (0, 0)),
        ],
        out_shape=[
            jax.ShapeDtypeStruct((width, tokens), jnp.float32),
            jax.ShapeDtypeStruct((8, 128), jnp.float32),
        ],
        input_output_aliases={7: 0} if rest else {},
        compiler_params=PARAMS,
        name=f"local{first}",
    )(queries, keys, values, sums, totals, level_weight, local, *rest)


def join(upper, mine, mine_total, other, other_total):
    fade = jnp.exp(jnp.where(upper, mine_total, other_total))
    return jnp.where(upper, other * fade + mine, mine * fade + other)


def chip_kernel(mine_ref, other_ref, *refs):
    chip_ref, prefix_ref, *message_refs = refs
    heads = prefix_ref.shape[0]
    half = chip_ref.shape[0]
    held = heads // 2
    per = half // held
    here = place()
    core = bit_of(here, 0)
    chip = jnp.bitwise_and(jnp.right_shift(here, 1), held - 1)
    upper = core == 1
    mine_total = mine_ref[half:]
    other_total = other_ref[half:]
    total = mine_total + other_total
    prefix_ref[...] = jnp.where(upper, other_total, 0.0)
    for slot in range(held):
        rows = slice(slot * per, (slot + 1) * per)
        mine_row = jnp.where(upper, mine_total[held + slot][None], mine_total[slot][None])
        other_row = jnp.where(upper, other_total[held + slot][None], other_total[slot][None])
        chip_ref[rows] = join(upper, mine_ref[rows], mine_row, other_ref[rows], other_row)
    for mask, message_ref in enumerate(message_refs):
        slot = jnp.bitwise_xor(chip, mask)
        message_ref[:per] = chip_ref[pl.ds(slot * per, per)]
        message_ref[per:] = total


def make_chip(mine, other, heads):
    half = mine.shape[0] - heads
    held = heads // 2
    message = jax.ShapeDtypeStruct((half // held + heads, mine.shape[1]), jnp.float32)
    return pl.pallas_call(
        chip_kernel,
        out_shape=[
            jax.ShapeDtypeStruct((half, mine.shape[1]), jnp.float32),
            jax.ShapeDtypeStruct((heads, mine.shape[1]), jnp.float32),
            *[message] * held,
        ],
        compiler_params=PARAMS,
        name="chip",
    )(mine, other)


def own_row(ref, per, heads):
    here = place()
    held = heads // 2
    chip = jnp.bitwise_and(jnp.right_shift(here, 1), held - 1)
    return ref[pl.ds(per + bit_of(here, 0) * held + chip, 1)]


def group_kernel(bits, *refs):
    part_refs = refs[: 2**bits]
    prefix_ref = refs[2**bits]
    group_ref = refs[-2 - (bits - 1)]
    lower_refs = refs[-1 - (bits - 1) : -1]
    prefixes_ref = refs[-1]
    heads = prefix_ref.shape[0]
    per = group_ref.shape[0] - heads
    here = place()
    states = [ref[:per] for ref in part_refs]
    totals = [ref[per:] for ref in part_refs]
    rows = [own_row(ref, per, heads) for ref in part_refs]
    prefix = prefix_ref[...]
    for bit in range(bits):
        upper = bit_of(here, bit + 1) == 1
        half = len(states) // 2
        if bit > 0:
            lower_refs[bit - 1][...] = jnp.where(upper, states[1], states[0])
        prefix = prefix + jnp.where(upper, totals[1], 0.0)
        prefixes_ref[bit] = prefix
        states = [
            join(upper, states[2 * at], rows[2 * at], states[2 * at + 1], rows[2 * at + 1])
            for at in range(half)
        ]
        totals = [totals[2 * at] + totals[2 * at + 1] for at in range(half)]
        rows = [rows[2 * at] + rows[2 * at + 1] for at in range(half)]
    group_ref[:per] = states[0]
    group_ref[per:] = totals[0]


def make_group(parts, prefix, token):
    heads, lanes = prefix.shape
    bits = len(parts).bit_length() - 1
    per = parts[0].shape[0] - heads
    state = jax.ShapeDtypeStruct((per, lanes), jnp.float32)
    return pl.pallas_call(
        functools.partial(group_kernel, bits),
        in_specs=[*[whole(part) for part in parts], whole(prefix), ANYWHERE],
        out_shape=[
            jax.ShapeDtypeStruct(parts[0].shape, jnp.float32),
            *[state] * (bits - 1),
            jax.ShapeDtypeStruct((bits, heads, lanes), jnp.float32),
        ],
        compiler_params=PARAMS,
        name="group",
    )(*parts, prefix, token)


def merge_kernel(bit, mine_ref, other_ref, prefix_ref, token_ref, merged_ref, next_ref):
    upper = bit_of(place(), bit) == 1
    heads = next_ref.shape[1]
    per = merged_ref.shape[0] - heads
    mine_row = own_row(mine_ref, per, heads)
    other_row = own_row(other_ref, per, heads)
    merged_ref[:per] = join(upper, mine_ref[:per], mine_row, other_ref[:per], other_row)
    other_total = other_ref[per:]
    merged_ref[per:] = mine_ref[per:] + other_total
    last = prefix_ref.shape[0] - 1
    next_ref[0] = prefix_ref[last] + jnp.where(upper, other_total, 0.0)


def merge(bit, mine, other, prefixes, token):
    _, heads, lanes = prefixes.shape
    return pl.pallas_call(
        functools.partial(merge_kernel, bit),
        in_specs=[whole(mine), whole(other), whole(prefixes), ANYWHERE],
        out_shape=[
            jax.ShapeDtypeStruct(mine.shape, jnp.float32),
            jax.ShapeDtypeStruct((1, heads, lanes), jnp.float32),
        ],
        compiler_params=PARAMS,
        name=f"merge{bit}",
    )(mine, other, prefixes, token)


def reach_kernel(plan, last, first_level, *refs):
    mixed_ref, q_ref, sums_ref, weight_ref, gain_ref = refs[:5]
    prefix_refs = refs[5 : 5 + len(plan)]
    part_refs = refs[5 + len(plan) : -2]
    out_ref, levels = refs[-2:]
    heads = weight_ref.shape[1]
    head_width = mixed_ref.shape[0] // heads
    held = heads // 2
    here = place()
    core = bit_of(here, 0)
    chip = jnp.bitwise_and(jnp.right_shift(here, 1), held - 1)

    @pl.when(pl.program_id(0) == 0)
    def _():
        at = 0
        for slot, (_, _, count) in enumerate(plan):
            for part in range(count):
                ref = part_refs[at]
                at += 1
                if count == 2:
                    side = core if part == 0 else 1 - core
                    first = side * held * head_width
                    rows = held * head_width
                else:
                    side = core if part < held else 1 - core
                    mask = part % held
                    first = (side * held + jnp.bitwise_xor(chip, mask)) * head_width
                    rows = head_width
                levels[slot, pl.ds(pl.multiple_of(first, 128), rows)] = ref[:rows].astype(
                    jnp.bfloat16
                )

    queries = q_ref[...]
    since = sums_ref[1]
    scales = []
    for slot, (bit, at, _) in enumerate(plan):
        active = jnp.where(bit_of(here, bit) == 1, 1.0, 0.0)
        reach = jnp.exp(since + spread_lanes(prefix_refs[slot][at][:, :1], SPAN))
        scales.append(reach * weight_ref[first_level + bit] * active)
    if last:
        gain_down = gain_ref[...].T
    for head in range(heads):
        rows = slice(head * head_width, (head + 1) * head_width)
        mixed = mixed_ref[rows]
        for slot in range(len(plan)):
            found = lax.dot_general(
                levels[slot, rows], queries, NT, preferred_element_type=jnp.float32
            )
            mixed = mixed + found * scales[slot][head : head + 1]
        if last:
            square = jnp.mean(mixed * mixed, axis=0, keepdims=True)
            normed = mixed * lax.rsqrt(square + EPS) * gain_down[:, head : head + 1]
            out_ref[:, rows] = normed.astype(jnp.bfloat16).T
        else:
            out_ref[rows] = mixed


def add_levels(mixed, queries, sums, level_weight, gain, levels, first_level, last):
    width, tokens = mixed.shape
    key_width = queries.shape[1]
    level_count, heads, _ = level_weight.shape
    spans = tokens // SPAN
    plan = [(bit, at, len(parts)) for bit, _, at, parts in levels]
    prefixes = [prefix for _, prefix, _, _ in levels]
    flat = [part for level in levels for part in level[3]]
    across = pl.BlockSpec((width, SPAN), lambda c: (0, c))
    return pl.pallas_call(
        functools.partial(reach_kernel, plan, last, first_level),
        grid=(spans,),
        in_specs=[
            across,
            pl.BlockSpec((SPAN, key_width), lambda c: (c, 0)),
            pl.BlockSpec((2, heads, SPAN), lambda c: (0, 0, c)),
            pl.BlockSpec((level_count, heads, SPAN), lambda c: (0, 0, c)),
            whole(gain),
            *[whole(array) for array in prefixes],
            *[whole(array) for array in flat],
        ],
        out_specs=pl.BlockSpec((SPAN, width), lambda c: (c, 0)) if last else across,
        out_shape=(
            jax.ShapeDtypeStruct((tokens, width), jnp.bfloat16)
            if last
            else jax.ShapeDtypeStruct(mixed.shape, jnp.float32)
        ),
        input_output_aliases={} if last else {0: 0},
        scratch_shapes=[pltpu.VMEM((len(plan), width, key_width), jnp.bfloat16)],
        compiler_params=PARAMS,
        name="finish" if last else "reach",
    )(mixed, queries, sums, level_weight, gain, *prefixes, *flat)


def trade(value, mask, senders=lambda source: True):
    wide, narrow = lax.axis_size("wide"), lax.axis_size("narrow")

    def ranked(index):
        return index % narrow * wide + index // narrow

    pairs = [
        (ranked(source), ranked(source ^ mask))
        for source in range(wide * narrow)
        if senders(source)
    ]
    return lax.ppermute(value, AXES, pairs)


def gather(own, bit, heads):
    parts = [own]
    for mask in range(1, heads // 2):
        parts.append(trade(own, 2 * mask, lambda source: ((source ^ 2 * mask) >> bit) & 1 == 1))
    needed = lambda source: (source >> bit) & 1 == 1
    return parts + [trade(part, 1, needed) for part in parts]


def per_device(queries, keys, values, log_decay, level_weight, norm_gain):
    heads = log_decay.shape[0]
    tokens, width = values.shape
    spans = tokens // SPAN
    bits = (lax.axis_size("wide") * lax.axis_size("narrow")).bit_length() - 1
    group_bits = heads.bit_length() - 1
    first_level = level_weight.shape[0] - bits
    keep, send, local, sums, totals = make_states(keys, values, log_decay)
    shared = (queries, keys, values, sums, totals, level_weight, local)
    other = trade(send, 1)
    chip, prefix, *messages = make_chip(keep, other, heads)
    levels = []
    zero = jnp.zeros((1, heads, 128), jnp.float32)
    levels.append((0, zero, 0, [other, trade(keep, 1, lambda source: source & 1 == 0)]))
    parts = [messages[0]]
    for mask in range(1, heads // 2):
        parts.append(trade(messages[mask], 2 * mask))
    mixed, token = mix_local(0, spans // 2, *shared, None)
    group, lower, prefixes = make_group(parts, prefix, token)
    near = trade(chip, 2, lambda source: (source >> 1) & 1 == 0)
    upper = lambda source: (source >> 1) & 1 == 1
    levels.append((1, prefix[None], 0, [near, trade(near, 1, upper)]))
    levels.append((2, prefixes, 0, gather(lower, 2, heads)))
    at = spans // 2
    for bit in range(group_bits, bits):
        other = trade(group, 2**bit)
        levels.append((bit, prefixes, prefixes.shape[0] - 1, gather(other, bit, heads)))
        if at < spans:
            mixed, token = mix_local(at, 1, *shared, mixed)
            at += 1
        if bit + 1 < bits:
            group, prefixes = merge(bit, group, other, prefixes, token)
    if at < spans:
        mixed, token = mix_local(at, spans - at, *shared, mixed)
    gain = norm_gain.reshape(heads, width // heads)
    rest = (queries, sums, level_weight, gain)
    mixed = add_levels(mixed, *rest, levels[:-1], first_level, False)
    return add_levels(mixed, *rest, levels[-1:], first_level, True)


def solution(mesh):
    placed = (
        P(("wide", "narrow"), None),
        P(("wide", "narrow"), None),
        P(("wide", "narrow"), None),
        P(None, ("wide", "narrow")),
        P(None, None, ("wide", "narrow")),
        P(),
    )
    return jax.shard_map(
        per_device,
        mesh=mesh,
        in_specs=placed,
        out_specs=P(("wide", "narrow"), None),
        check_vma=False,
    )
```

```python
import functools

import jax
import jax.numpy as jnp
from jax import lax
from jax.experimental import pallas as pl
from jax.experimental.pallas import tpu as pltpu
from jax.sharding import PartitionSpec as P

SPAN = 256
EPS = 1e-05
NT = (((1,), (1,)), ((), ()))
VMEM = 56 * 1024 * 1024
PARAMS = pltpu.CompilerParams(vmem_limit_bytes=VMEM)


def place():
    inner = lax.axis_index("low") * lax.axis_size("narrow") + lax.axis_index("narrow")
    return lax.axis_index("high") * lax.axis_size("low") * lax.axis_size("narrow") + inner


def bit_of(value, bit):
    return jnp.bitwise_and(jnp.right_shift(value, bit), 1)


def spread_lanes(column, width):
    return jnp.broadcast_to(column, (column.shape[0], width))


def whole(array):
    return pl.BlockSpec(array.shape, lambda *_: (0,) * len(array.shape))


ANYWHERE = pl.BlockSpec(memory_space=pl.ANY)


def running_sums(rows):
    high = rows.astype(jnp.bfloat16)
    rest = rows - high.astype(jnp.float32)
    middle = rest.astype(jnp.bfloat16)
    low = (rest - middle.astype(jnp.float32)).astype(jnp.bfloat16)
    width = rows.shape[1]
    source = lax.broadcasted_iota(jnp.int32, (width, width), 0)
    target = lax.broadcasted_iota(jnp.int32, (width, width), 1)
    upto = jnp.where(source <= target, 1.0, 0.0).astype(jnp.bfloat16)
    sums = jnp.dot(
        jnp.concatenate([high, middle, low], axis=0), upto, preferred_element_type=jnp.float32
    )
    count = rows.shape[0]
    return sums[:count] + (sums[count : 2 * count] + sums[2 * count :])


def state_kernel(
    k_ref, decay_ref, v_hbm, message_ref, local_ref, sums_ref, totals_ref, v_ref, arrived
):
    heads, tokens = decay_ref.shape
    head_width = v_ref.shape[1] // heads
    spans = tokens // SPAN
    rows_of = [slice(span * SPAN, (span + 1) * SPAN) for span in range(spans)]
    copies = [
        pltpu.make_async_copy(v_hbm.at[rows], v_ref.at[rows], arrived.at[span])
        for span, rows in enumerate(rows_of)
    ]
    for copy in copies:
        copy.start()
    within = running_sums(jnp.concatenate([decay_ref[:, rows] for rows in rows_of], axis=0))
    run = jnp.zeros((heads, 128), jnp.float32)
    fades, wholes = [], []
    for span, rows in enumerate(rows_of):
        here = within[span * heads : (span + 1) * heads]
        last = here[:, SPAN - 1 :]
        total = spread_lanes(last, 128)
        sums_ref[0, :, rows] = here
        sums_ref[1, :, rows] = here + spread_lanes(run[:, :1], SPAN)
        totals_ref[span] = total
        run = run + total
        fades.append(jnp.exp(spread_lanes(last, SPAN) - here))
        wholes.append(jnp.exp(total))
    across = [k_ref[rows].astype(jnp.float32).T for rows in rows_of]
    for copy in copies:
        copy.wait()
    for head in range(heads):
        columns = slice(head * head_width, (head + 1) * head_width)
        states = []
        for span, rows in enumerate(rows_of):
            faded = (across[span] * fades[span][head : head + 1]).astype(jnp.bfloat16)
            states.append(
                jnp.dot(faded, v_ref[rows, columns], preferred_element_type=jnp.float32)
            )
        at = 0
        size = 1
        while size < spans:
            for first in range(0, spans, 2 * size):
                group = states[first]
                for span in range(first + 1, first + size):
                    group = group * wholes[span][head : head + 1] + states[span]
                local_ref[at, :, columns] = group.astype(jnp.bfloat16)
                at += 1
            size *= 2
        group = states[0]
        for span in range(1, spans):
            group = group * wholes[span][head : head + 1] + states[span]
        message_ref[head, :head_width] = group.T
        message_ref[head, head_width:] = run


def make_states(keys, values, log_decay):
    tokens, key_width = keys.shape
    heads = log_decay.shape[0]
    width = values.shape[1]
    spans = tokens // SPAN
    return pl.pallas_call(
        state_kernel,
        in_specs=[whole(keys), whole(log_decay), ANYWHERE],
        out_shape=[
            jax.ShapeDtypeStruct((heads, width // heads + heads, key_width), jnp.float32),
            jax.ShapeDtypeStruct((spans - 1, key_width, width), jnp.bfloat16),
            jax.ShapeDtypeStruct((2, heads, tokens), jnp.float32),
            jax.ShapeDtypeStruct((spans, heads, 128), jnp.float32),
        ],
        scratch_shapes=[
            pltpu.VMEM((tokens, width), jnp.bfloat16),
            pltpu.SemaphoreType.DMA((spans,)),
        ],
        compiler_params=PARAMS,
        name="states",
    )(keys, log_decay, values)


def local_kernel(
    first_span, spans, q_ref, k_ref, v_ref, sums_ref, totals_ref, weight_ref, local_ref, *refs
):
    mixed_ref, done_ref = refs[-2:]
    span = pl.program_id(0) + first_span
    heads = weight_ref.shape[1]
    head_width = v_ref.shape[1] // heads
    local_bits = weight_ref.shape[0] - 1
    half = SPAN // 2
    done_ref[...] = jnp.zeros_like(done_ref)
    queries = q_ref[...]
    scores = lax.dot_general(k_ref[...], queries, NT, preferred_element_type=jnp.float32)
    within = sums_ref[0]
    within_down = within.T
    values_across = v_ref[...].T
    source = lax.broadcasted_iota(jnp.int32, (half, half), 0)
    target = lax.broadcasted_iota(jnp.int32, (half, half), 1)
    causal = source <= target
    empty = jnp.zeros((half, half), jnp.bfloat16)

    def mix(head, low, high, masked):
        rows = slice(low * half, (low + 1) * half)
        columns = slice(high * half, (high + 1) * half)
        gap = within[head : head + 1, columns] - within_down[rows, head : head + 1]
        if masked:
            gap = jnp.where(causal, gap, -1e30)
        mixing = scores[rows, columns] * jnp.exp(gap) * weight_ref[0, head : head + 1, columns]
        return mixing.astype(jnp.bfloat16)

    for head in range(heads):
        rows = slice(head * head_width, (head + 1) * head_width)
        mixing = jnp.concatenate(
            [
                jnp.concatenate([mix(head, 0, 0, True), mix(head, 0, 1, False)], axis=1),
                jnp.concatenate([empty, mix(head, 1, 1, True)], axis=1),
            ],
            axis=0,
        )
        mixed_ref[rows] = jnp.dot(
            values_across[rows], mixing, preferred_element_type=jnp.float32
        )
    offset = 0
    for bit in range(local_bits):
        since = jnp.zeros((heads, 128), jnp.float32)
        for back in range(1, 2**bit):
            inside = jnp.bitwise_and(span, 2**bit - 1) >= back
            since = since + jnp.where(inside, totals_ref[jnp.maximum(span - back, 0)], 0.0)

        @pl.when(bit_of(span, bit) == 1)
        def _():
            level = local_ref[offset + jnp.right_shift(span, bit + 1)].T
            found = lax.dot_general(level, queries, NT, preferred_element_type=jnp.float32)
            scale = jnp.exp(within + spread_lanes(since[:, :1], SPAN)) * weight_ref[1 + bit]
            for head in range(heads):
                rows = slice(head * head_width, (head + 1) * head_width)
                mixed_ref[rows] += found[rows] * scale[head : head + 1]

        offset = offset + (spans >> (bit + 1))


def mix_local(first, count, queries, keys, values, sums, totals, level_weight, local, mixed):
    tokens, key_width = keys.shape
    heads = level_weight.shape[1]
    width = values.shape[1]
    spans = tokens // SPAN
    local_bits = spans.bit_length() - 1
    rest = [] if mixed is None else [mixed]
    return pl.pallas_call(
        functools.partial(local_kernel, first, spans),
        grid=(count,),
        in_specs=[
            pl.BlockSpec((SPAN, key_width), lambda c: (c + first, 0)),
            pl.BlockSpec((SPAN, key_width), lambda c: (c + first, 0)),
            pl.BlockSpec((SPAN, width), lambda c: (c + first, 0)),
            pl.BlockSpec((2, heads, SPAN), lambda c: (0, 0, c + first)),
            whole(totals),
            pl.BlockSpec((1 + local_bits, heads, SPAN), lambda c: (0, 0, c + first)),
            whole(local),
            *[ANYWHERE for _ in rest],
        ],
        out_specs=[
            pl.BlockSpec((width, SPAN), lambda c: (0, c + first)),
            pl.BlockSpec((8, 128), lambda c: (0, 0)),
        ],
        out_shape=[
            jax.ShapeDtypeStruct((width, tokens), jnp.float32),
            jax.ShapeDtypeStruct((8, 128), jnp.float32),
        ],
        input_output_aliases={7: 0} if rest else {},
        compiler_params=PARAMS,
        name=f"local{first}",
    )(queries, keys, values, sums, totals, level_weight, local, *rest)


def tree(states, totals, rows):
    sizes = [(states, totals)]
    while len(states) > 1:
        states = [
            states[at] * jnp.exp(rows[at + 1]) + states[at + 1] for at in range(0, len(states), 2)
        ]
        totals = [totals[at] + totals[at + 1] for at in range(0, len(totals), 2)]
        rows = [rows[at] + rows[at + 1] for at in range(0, len(rows), 2)]
        sizes.append((states, totals))
    return sizes


def prefixes_of(sizes, here, prefix, bits):
    found = [prefix]
    for bit in range(bits):
        for at in range(0, len(sizes[bit][1]), 2):
            inside = jnp.right_shift(here, bit) == at + 1
            prefix = prefix + jnp.where(inside, sizes[bit][1][at], 0.0)
        found.append(prefix)
    return found


def pick(sizes, here, bit):
    chosen = sizes[bit][0][0]
    for at in range(2, len(sizes[bit][0]), 2):
        chosen = jnp.where(jnp.right_shift(here, bit) == at + 1, sizes[bit][0][at], chosen)
    return chosen


def group_kernel(parts_ref, token_ref, group_ref, lower_ref, prefixes_ref):
    members = parts_ref.shape[0]
    per = lower_ref.shape[1]
    bits = members.bit_length() - 1
    mine = jnp.bitwise_and(place(), members - 1)
    states = [parts_ref[member, :per] for member in range(members)]
    totals = [parts_ref[member, per:] for member in range(members)]
    rows = [parts_ref[member, pl.ds(per + mine, 1)] for member in range(members)]
    sizes = tree(states, totals, rows)
    at = 0
    for bit in range(1, bits):
        for first in range(0, members >> bit, 2):
            lower_ref[at] = sizes[bit][0][first]
            at += 1
    for bit, prefix in enumerate(prefixes_of(sizes, mine, jnp.zeros_like(totals[0]), bits)):
        prefixes_ref[bit] = prefix
    group_ref[:per] = sizes[bits][0][0]
    group_ref[per:] = sizes[bits][1][0]


def make_group(parts, token):
    members, rows, lanes = parts.shape
    bits = members.bit_length() - 1
    per = rows - members
    kinds = sum(members >> (bit + 1) for bit in range(1, bits))
    return pl.pallas_call(
        group_kernel,
        in_specs=[whole(parts), ANYWHERE],
        out_shape=[
            jax.ShapeDtypeStruct((rows, lanes), jnp.float32),
            jax.ShapeDtypeStruct((kinds, per, lanes), jnp.float32),
            jax.ShapeDtypeStruct((bits + 1, members, lanes), jnp.float32),
        ],
        compiler_params=PARAMS,
        name="group",
    )(parts, token)


def upper_kernel(parts_ref, prefix_ref, token_ref, lower_ref, prefixes_ref):
    groups = parts_ref.shape[0]
    per = lower_ref.shape[1]
    heads = prefix_ref.shape[1]
    bits = groups.bit_length() - 1
    here = place()
    mine = jnp.bitwise_and(here, heads - 1)
    high = jnp.right_shift(here, heads.bit_length() - 1)
    states = [parts_ref[group, :per] for group in range(groups)]
    totals = [parts_ref[group, per:] for group in range(groups)]
    rows = [parts_ref[group, pl.ds(per + mine, 1)] for group in range(groups)]
    sizes = tree(states, totals, rows)
    last = prefix_ref.shape[0] - 1
    found = prefixes_of(sizes, high, prefix_ref[last], bits)
    for bit in range(bits):
        lower_ref[bit] = pick(sizes, high, bit)
        prefixes_ref[bit] = found[bit]


def make_upper(parts, prefixes, token):
    groups, rows, lanes = parts.shape
    bits = groups.bit_length() - 1
    heads = prefixes.shape[1]
    return pl.pallas_call(
        upper_kernel,
        in_specs=[whole(parts), whole(prefixes), ANYWHERE],
        out_shape=[
            jax.ShapeDtypeStruct((bits, rows - heads, lanes), jnp.float32),
            jax.ShapeDtypeStruct((bits, heads, lanes), jnp.float32),
        ],
        compiler_params=PARAMS,
        name="upper",
    )(parts, prefixes, token)


def reach_kernel(plan, last, first_level, *refs):
    mixed_ref, q_ref, sums_ref, weight_ref, gain_ref = refs[:5]
    prefix_refs = refs[5 : 5 + len(plan)]
    part_refs = refs[5 + len(plan) : -2]
    out_ref, levels = refs[-2:]
    heads = weight_ref.shape[1]
    head_width = mixed_ref.shape[0] // heads
    here = place()
    mine = jnp.bitwise_and(here, heads - 1)

    @pl.when(pl.program_id(0) == 0)
    def _():
        for slot, (bit, _, kinds) in enumerate(plan):
            ref = part_refs[slot]
            kind = kinds(jnp.right_shift(mine, bit))
            for head in range(heads):
                rows = slice(head * head_width, (head + 1) * head_width)
                if kind is None:
                    level = ref[head, :head_width]
                else:
                    level = ref[head, kind]
                levels[slot, rows] = level.astype(jnp.bfloat16)

    queries = q_ref[...]
    since = sums_ref[1]
    scales = []
    for slot, (bit, at, _) in enumerate(plan):
        active = jnp.where(bit_of(here, bit) == 1, 1.0, 0.0)
        reach = jnp.exp(since + spread_lanes(prefix_refs[slot][at][:, :1], SPAN))
        scales.append(reach * weight_ref[first_level + bit] * active)
    if last:
        gain_down = gain_ref[...].T
    for head in range(heads):
        rows = slice(head * head_width, (head + 1) * head_width)
        mixed = mixed_ref[rows]
        for slot in range(len(plan)):
            found = lax.dot_general(
                levels[slot, rows], queries, NT, preferred_element_type=jnp.float32
            )
            mixed = mixed + found * scales[slot][head : head + 1]
        if last:
            square = jnp.mean(mixed * mixed, axis=0, keepdims=True)
            normed = mixed * lax.rsqrt(square + EPS) * gain_down[:, head : head + 1]
            out_ref[:, rows] = normed.astype(jnp.bfloat16).T
        else:
            out_ref[rows] = mixed


def add_levels(mixed, queries, sums, level_weight, gain, levels, first_level, last):
    width, tokens = mixed.shape
    key_width = queries.shape[1]
    level_count, heads, _ = level_weight.shape
    spans = tokens // SPAN
    plan = [(bit, at, kinds) for bit, _, at, _, kinds in levels]
    prefixes = [level[1] for level in levels]
    flat = [level[3] for level in levels]
    across = pl.BlockSpec((width, SPAN), lambda c: (0, c))
    return pl.pallas_call(
        functools.partial(reach_kernel, plan, last, first_level),
        grid=(spans,),
        in_specs=[
            across,
            pl.BlockSpec((SPAN, key_width), lambda c: (c, 0)),
            pl.BlockSpec((2, heads, SPAN), lambda c: (0, 0, c)),
            pl.BlockSpec((level_count, heads, SPAN), lambda c: (0, 0, c)),
            whole(gain),
            *[whole(array) for array in prefixes],
            *[whole(array) for array in flat],
        ],
        out_specs=pl.BlockSpec((SPAN, width), lambda c: (c, 0)) if last else across,
        out_shape=(
            jax.ShapeDtypeStruct((tokens, width), jnp.bfloat16)
            if last
            else jax.ShapeDtypeStruct(mixed.shape, jnp.float32)
        ),
        input_output_aliases={} if last else {0: 0},
        scratch_shapes=[pltpu.VMEM((len(plan), width, key_width), jnp.bfloat16)],
        compiler_params=PARAMS,
        name="finish" if last else "reach",
    )(mixed, queries, sums, level_weight, gain, *prefixes, *flat)


def per_device(queries, keys, values, log_decay, level_weight, norm_gain):
    heads = log_decay.shape[0]
    tokens, width = values.shape
    spans = tokens // SPAN
    group_bits = heads.bit_length() - 1
    high_bits = lax.axis_size("high").bit_length() - 1
    first_level = level_weight.shape[0] - group_bits - high_bits
    message, local, sums, totals = make_states(keys, values, log_decay)
    shared = (queries, keys, values, sums, totals, level_weight, local)
    inner = lax.axis_size("narrow")
    parts = lax.all_to_all(message, ("low", "narrow"), 0, 0)
    partner = lax.ppermute(message, "narrow", [(at, at + 1) for at in range(0, inner, 2)])
    mixed, token = mix_local(0, spans // 2, *shared, None)
    group, lower, prefixes = make_group(parts, token)
    groups = lax.all_gather(group, "high")
    near = lax.all_gather(lower, ("low", "narrow"))
    mixed, token = mix_local(spans // 2, spans - spans // 2, *shared, mixed)
    upper, upper_prefixes = make_upper(groups, prefixes, token)
    far = lax.all_gather(upper, ("low", "narrow"))
    levels = [(0, prefixes, 0, partner, lambda group: None)]
    at = 0
    for bit in range(1, group_bits):
        levels.append(
            (bit, prefixes, bit, near, lambda group, at=at: at + jnp.right_shift(group, 1))
        )
        at += heads >> (bit + 1)
    gain = norm_gain.reshape(heads, width // heads)
    rest = (queries, sums, level_weight, gain)
    mixed = add_levels(mixed, *rest, levels, first_level, False)
    levels = [
        (group_bits + bit, upper_prefixes, bit, far, lambda group, bit=bit: bit)
        for bit in range(high_bits)
    ]
    return add_levels(mixed, *rest, levels, first_level, True)


def solution(mesh):
    narrow, wide = mesh.shape["narrow"], mesh.shape["wide"]
    along = ("high", "low", "narrow")
    placed = (P(along), P(along), P(along), P(None, along), P(None, None, along), P())

    def run(*inputs):
        low = inputs[3].shape[0] // narrow
        split = jax.sharding.Mesh(
            mesh.devices.reshape(narrow, wide // low, low), ("narrow", "high", "low")
        )
        return jax.shard_map(
            per_device, mesh=split, in_specs=placed, out_specs=P(along), check_vma=False
        )(*inputs)

    return run
```

```python
import functools

import jax
import jax.numpy as jnp
from jax import lax
from jax.experimental import pallas as pl
from jax.experimental.pallas import tpu as pltpu
from jax.sharding import PartitionSpec as P

SPAN = 256
EPS = 1e-05
AXES = ("narrow", "wide")
NT = (((1,), (1,)), ((), ()))
PARAMS = pltpu.CompilerParams(vmem_limit_bytes=32 * 1024 * 1024)
HELD = pl.BlockSpec(memory_space=pltpu.VMEM)


def place():
    return lax.axis_index("wide") * lax.axis_size("narrow") + lax.axis_index("narrow")


def bit_of(value, bit):
    return jnp.bitwise_and(jnp.right_shift(value, bit), 1)


def spread_lanes(column, width):
    return jnp.broadcast_to(column, (column.shape[0], width))


ANYWHERE = pl.BlockSpec(memory_space=pl.ANY)


def hold(array):
    return pltpu.with_memory_space_constraint(array, pltpu.VMEM)


def call(kernel, name, inputs, outputs, scratch=(), in_specs=None, aliases=None):
    specs = in_specs or [HELD] * len(inputs)
    inputs = [hold(array) if spec is HELD else array for array, spec in zip(inputs, specs)]
    return pl.pallas_call(
        kernel,
        in_specs=specs,
        out_specs=[HELD] * len(outputs),
        out_shape=[pltpu.VMEM(shape, dtype) for shape, dtype in outputs],
        scratch_shapes=list(scratch),
        input_output_aliases=aliases or {},
        compiler_params=PARAMS,
        name=name,
    )(*inputs)


def running_sums(rows):
    high = rows.astype(jnp.bfloat16)
    rest = rows - high.astype(jnp.float32)
    middle = rest.astype(jnp.bfloat16)
    low = (rest - middle.astype(jnp.float32)).astype(jnp.bfloat16)
    width = rows.shape[1]
    source = lax.broadcasted_iota(jnp.int32, (width, width), 0)
    target = lax.broadcasted_iota(jnp.int32, (width, width), 1)
    upto = jnp.where(source <= target, 1.0, 0.0).astype(jnp.bfloat16)
    sums = jnp.dot(
        jnp.concatenate([high, middle, low], axis=0), upto, preferred_element_type=jnp.float32
    )
    count = rows.shape[0]
    return sums[:count] + (sums[count : 2 * count] + sums[2 * count :])


def state_kernel(
    k_ref, decay_ref, v_hbm, keep_ref, send_ref, local_ref, sums_ref, totals_ref, v_ref, held, arrived
):
    heads, tokens = decay_ref.shape
    head_width = v_ref.shape[1] // heads
    spans = tokens // SPAN
    rows_of = [slice(span * SPAN, (span + 1) * SPAN) for span in range(spans)]
    copies = [
        pltpu.make_async_copy(v_hbm.at[rows], v_ref.at[rows], arrived.at[span])
        for span, rows in enumerate(rows_of)
    ]
    for copy in copies:
        copy.start()
    within = running_sums(jnp.concatenate([decay_ref[:, rows] for rows in rows_of], axis=0))
    run = jnp.zeros((heads, 128), jnp.float32)
    fades, wholes = [], []
    for span, rows in enumerate(rows_of):
        here = within[span * heads : (span + 1) * heads]
        last = here[:, SPAN - 1 :]
        total = spread_lanes(last, 128)
        sums_ref[0, :, rows] = here
        sums_ref[1, :, rows] = here + spread_lanes(run[:, :1], SPAN)
        totals_ref[span] = total
        run = run + total
        fades.append(jnp.exp(spread_lanes(last, SPAN) - here))
        wholes.append(jnp.exp(total))
    across = [k_ref[rows].astype(jnp.float32).T for rows in rows_of]
    for copy in copies:
        copy.wait()
    for head in range(heads):
        columns = slice(head * head_width, (head + 1) * head_width)
        states = []
        for span, rows in enumerate(rows_of):
            faded = (across[span] * fades[span][head : head + 1]).astype(jnp.bfloat16)
            states.append(
                jnp.dot(faded, v_ref[rows, columns], preferred_element_type=jnp.float32)
            )
        at = 0
        size = 1
        while size < spans:
            for first in range(0, spans, 2 * size):
                group = states[first]
                for span in range(first + 1, first + size):
                    group = group * wholes[span][head : head + 1] + states[span]
                local_ref[at, :, columns] = group.astype(jnp.bfloat16)
                at += 1
            size *= 2
        group = states[0]
        for span in range(1, spans):
            group = group * wholes[span][head : head + 1] + states[span]
        held[columns] = group.T
    half = held.shape[0] // 2
    core = bit_of(place(), 0)
    keep_ref[:half] = held[pl.ds(core * half, half)]
    send_ref[:half] = held[pl.ds((1 - core) * half, half)]
    keep_ref[half:] = run
    send_ref[half:] = run


def make_states(keys, values, log_decay):
    tokens, key_width = keys.shape
    heads = log_decay.shape[0]
    width = values.shape[1]
    spans = tokens // SPAN
    message = ((width // 2 + heads, key_width), jnp.float32)
    plain = pl.BlockSpec()
    return call(
        state_kernel,
        "states",
        [keys, log_decay, values],
        [
            message,
            message,
            ((spans - 1, key_width, width), jnp.bfloat16),
            ((2, heads, tokens), jnp.float32),
            ((spans, heads, 128), jnp.float32),
            ((tokens, width), jnp.bfloat16),
        ],
        [pltpu.VMEM((width, key_width), jnp.float32), pltpu.SemaphoreType.DMA((spans,))],
        [plain, plain, ANYWHERE],
    )


def local_kernel(first, last, *refs):
    q_ref, k_ref, v_ref, sums_ref, totals_ref, weight_ref, local_ref = refs[:7]
    mixed_ref, done_ref = refs[-2:]
    heads = weight_ref.shape[1]
    head_width = v_ref.shape[1] // heads
    spans = totals_ref.shape[0]
    local_bits = spans.bit_length() - 1
    half = SPAN // 2
    done_ref[...] = jnp.zeros_like(done_ref)
    source = lax.broadcasted_iota(jnp.int32, (half, half), 0)
    target = lax.broadcasted_iota(jnp.int32, (half, half), 1)
    causal = source <= target
    empty = jnp.zeros((half, half), jnp.bfloat16)

    for span in range(first, last):
        tokens = slice(span * SPAN, (span + 1) * SPAN)
        queries = q_ref[tokens]
        scores = lax.dot_general(
            k_ref[tokens], queries, NT, preferred_element_type=jnp.float32
        )
        within = sums_ref[0, :, tokens]
        within_down = within.T
        weight = weight_ref[0, :, tokens]
        values_across = v_ref[tokens].T

        def mix(head, low, high):
            rows = slice(low * half, (low + 1) * half)
            columns = slice(high * half, (high + 1) * half)
            gap = within[head : head + 1, columns] - within_down[rows, head : head + 1]
            if low == high:
                gap = jnp.where(causal, gap, -1e30)
            mixing = scores[rows, columns] * jnp.exp(gap) * weight[head : head + 1, columns]
            return mixing.astype(jnp.bfloat16)

        levels = []
        offset = 0
        for bit in range(local_bits):
            if span >> bit & 1:
                since = within
                for back in range(1, span % 2**bit + 1):
                    since = since + spread_lanes(totals_ref[span - back][:, :1], SPAN)
                scale = jnp.exp(since) * weight_ref[1 + bit, :, tokens]
                levels.append((local_ref[offset + (span >> (bit + 1))].T, scale))
            offset += spans >> (bit + 1)
        for head in range(heads):
            rows = slice(head * head_width, (head + 1) * head_width)
            mixing = jnp.concatenate(
                [
                    jnp.concatenate([mix(head, 0, 0), mix(head, 0, 1)], axis=1),
                    jnp.concatenate([empty, mix(head, 1, 1)], axis=1),
                ],
                axis=0,
            )
            mixed = jnp.dot(values_across[rows], mixing, preferred_element_type=jnp.float32)
            for level, scale in levels:
                found = lax.dot_general(
                    level[rows], queries, NT, preferred_element_type=jnp.float32
                )
                mixed = mixed + found * scale[head : head + 1]
            mixed_ref[rows, tokens] = mixed


def mix_local(first, last, shared, mixed):
    queries, keys, values, sums, totals, level_weight, local = shared
    rest = [] if mixed is None else [mixed]
    return call(
        functools.partial(local_kernel, first, last),
        f"local{first}",
        [*shared, *rest],
        [(values.shape[::-1], jnp.float32), ((8, 128), jnp.float32)],
        aliases={7: 0} if rest else None,
    )


def join(upper, mine, mine_total, other, other_total):
    fade = jnp.exp(jnp.where(upper, mine_total, other_total))
    return jnp.where(upper, other * fade + mine, mine * fade + other)


def fade_row(ref, state_rows, head):
    return ref[pl.ds(state_rows + head, 1)]


def chip_kernel(mine_ref, other_ref, stay_ref, give_ref, prefix_ref, chip_ref):
    heads = prefix_ref.shape[0]
    half = chip_ref.shape[0]
    held = heads // 2
    per = half // held
    here = place()
    core = bit_of(here, 0)
    upper = core == 1
    for slot in range(held):
        rows = slice(slot * per, (slot + 1) * per)
        head = core * held + slot
        chip_ref[rows] = join(
            upper,
            mine_ref[rows],
            fade_row(mine_ref, half, head),
            other_ref[rows],
            fade_row(other_ref, half, head),
        )
    other_total = other_ref[half:]
    total = mine_ref[half:] + other_total
    prefix_ref[...] = jnp.where(upper, other_total, 0.0)
    quarter = half // 2
    side = bit_of(here, 1)
    stay_ref[:quarter] = chip_ref[pl.ds(side * quarter, quarter)]
    give_ref[:quarter] = chip_ref[pl.ds((1 - side) * quarter, quarter)]
    stay_ref[quarter:] = total
    give_ref[quarter:] = total


def make_chip(mine, other, heads):
    rows, lanes = mine.shape
    half = rows - heads
    message = ((half // 2 + heads, lanes), jnp.float32)
    return call(
        chip_kernel,
        "chip",
        [mine, other],
        [message, message, ((heads, lanes), jnp.float32)],
        [pltpu.VMEM((half, lanes), jnp.float32)],
    )


def merge_kernel(bit, mine_ref, other_ref, prefix_ref, token_ref, merged_ref, next_ref):
    here = place()
    upper = bit_of(here, bit) == 1
    heads = next_ref.shape[0]
    count = heads // 4
    quarter = merged_ref.shape[0] - heads
    per = quarter // count
    for slot in range(count):
        rows = slice(slot * per, (slot + 1) * per)
        head = bit_of(here, 0) * (heads // 2) + bit_of(here, 1) * count + slot
        merged_ref[rows] = join(
            upper,
            mine_ref[rows],
            fade_row(mine_ref, quarter, head),
            other_ref[rows],
            fade_row(other_ref, quarter, head),
        )
    other_total = other_ref[quarter:]
    merged_ref[quarter:] = mine_ref[quarter:] + other_total
    next_ref[...] = prefix_ref[...] + jnp.where(upper, other_total, 0.0)


def merge(bit, mine, other, prefix, token):
    return call(
        functools.partial(merge_kernel, bit),
        f"merge{bit}",
        [mine, other, prefix, token],
        [(mine.shape, jnp.float32), (prefix.shape, jnp.float32)],
    )


def level_scale(bit, first_level, prefix_ref, sums_ref, weight_ref, tokens):
    active = jnp.where(bit_of(place(), bit) == 1, 1.0, 0.0)
    reach = jnp.exp(sums_ref[1, :, tokens] + spread_lanes(prefix_ref[:, :1], SPAN))
    return reach * weight_ref[first_level + bit, :, tokens] * active


def take_levels(plan, part_refs, levels, heads):
    here = place()
    per = levels.shape[1] // heads
    for slot, pieces in enumerate(plan):
        for index, row, far_core, far_side, count in pieces:
            core = jnp.bitwise_xor(bit_of(here, 0), far_core)
            side = jnp.bitwise_xor(bit_of(here, 1), far_side)
            head = core * (heads // 2)
            if count < heads // 2:
                head = head + side * count
            rows = count * per
            start = pl.multiple_of(head * per, 128)
            levels[slot, pl.ds(start, rows)] = part_refs[index][row : row + rows].astype(
                jnp.bfloat16
            )


def reach_kernel(plan, bits, first_level, *refs):
    mixed_ref, q_ref, sums_ref, weight_ref = refs[:4]
    prefix_refs = refs[4 : 4 + len(bits)]
    part_refs = refs[4 + len(bits) : -2]
    out_ref, levels = refs[-2:]
    heads = weight_ref.shape[1]
    head_width = mixed_ref.shape[0] // heads
    take_levels(plan, part_refs, levels, heads)
    for span in range(q_ref.shape[0] // SPAN):
        tokens = slice(span * SPAN, (span + 1) * SPAN)
        queries = q_ref[tokens]
        scales = [
            level_scale(bit, first_level, prefix_ref, sums_ref, weight_ref, tokens)
            for bit, prefix_ref in zip(bits, prefix_refs)
        ]
        for head in range(heads):
            rows = slice(head * head_width, (head + 1) * head_width)
            mixed = mixed_ref[rows, tokens]
            for slot, scale in enumerate(scales):
                found = lax.dot_general(
                    levels[slot, rows], queries, NT, preferred_element_type=jnp.float32
                )
                mixed = mixed + found * scale[head : head + 1]
            out_ref[rows, tokens] = mixed


def add_levels(mixed, queries, sums, level_weight, levels, parts, first_level):
    width = mixed.shape[0]
    bits = [bit for bit, _, _ in levels]
    plan = [pieces for _, _, pieces in levels]
    return call(
        functools.partial(reach_kernel, plan, bits, first_level),
        "reach",
        [mixed, queries, sums, level_weight, *[prefix for _, prefix, _ in levels], *parts],
        [(mixed.shape, jnp.float32)],
        [pltpu.VMEM((len(bits), width, queries.shape[1]), jnp.bfloat16)],
        aliases={0: 0},
    )[0]


def finish_kernel(pieces, bit, first_level, *refs):
    mixed_ref, q_ref, sums_ref, weight_ref, gain_ref, prefix_ref = refs[:6]
    part_refs = refs[6:-4]
    out_hbm, levels, out_ref, sent = refs[-4:]
    heads = weight_ref.shape[1]
    head_width = mixed_ref.shape[0] // heads
    take_levels([pieces], part_refs, levels, heads)
    gain_down = gain_ref[...].T
    copies = []
    for span in range(q_ref.shape[0] // SPAN):
        tokens = slice(span * SPAN, (span + 1) * SPAN)
        queries = q_ref[tokens]
        scale = level_scale(bit, first_level, prefix_ref, sums_ref, weight_ref, tokens)
        for head in range(heads):
            rows = slice(head * head_width, (head + 1) * head_width)
            found = lax.dot_general(
                levels[0, rows], queries, NT, preferred_element_type=jnp.float32
            )
            mixed = mixed_ref[rows, tokens] + found * scale[head : head + 1]
            square = jnp.mean(mixed * mixed, axis=0, keepdims=True)
            normed = mixed * lax.rsqrt(square + EPS) * gain_down[:, head : head + 1]
            out_ref[tokens, rows] = normed.astype(jnp.bfloat16).T
        copy = pltpu.make_async_copy(out_ref.at[tokens], out_hbm.at[tokens], sent.at[span])
        copy.start()
        copies.append(copy)
    for copy in copies:
        copy.wait()


def finish(mixed, queries, sums, level_weight, gain, prefix, pieces, bit, parts, first_level):
    width, tokens = mixed.shape
    inputs = [mixed, queries, sums, level_weight, gain, prefix, *parts]
    return pl.pallas_call(
        functools.partial(finish_kernel, pieces, bit, first_level),
        in_specs=[HELD] * len(inputs),
        out_specs=ANYWHERE,
        out_shape=jax.ShapeDtypeStruct((tokens, width), jnp.bfloat16),
        scratch_shapes=[
            pltpu.VMEM((1, width, queries.shape[1]), jnp.bfloat16),
            pltpu.VMEM((tokens, width), jnp.bfloat16),
            pltpu.SemaphoreType.DMA((tokens // SPAN,)),
        ],
        compiler_params=PARAMS,
        name="finish",
    )(*[hold(array) for array in inputs])


def trade(value, mask, senders=lambda source: True):
    wide, narrow = lax.axis_size("wide"), lax.axis_size("narrow")

    def ranked(index):
        return index % narrow * wide + index // narrow

    pairs = [
        (ranked(source), ranked(source ^ mask))
        for source in range(wide * narrow)
        if senders(source)
    ]
    return lax.ppermute(value, AXES, pairs)


def per_device(queries, keys, values, log_decay, level_weight, norm_gain):
    heads = log_decay.shape[0]
    tokens, width = values.shape
    spans = tokens // SPAN
    half, quarter = width // 2, width // 4
    bits = (lax.axis_size("wide") * lax.axis_size("narrow")).bit_length() - 1
    first_level = level_weight.shape[0] - bits
    keep, send, local, sums, totals, held_values = make_states(keys, values, log_decay)
    shared = (queries, keys, held_values, sums, totals, level_weight, local)
    near = trade(send, 1)
    stay, give, prefix = make_chip(keep, near, heads)
    got = trade(give, 2)
    near_rest = trade(keep, 1, lambda source: source & 1 == 0)
    got_rest = trade(stay, 2, lambda source: source & 2 == 0)
    prefixes = [jnp.zeros((heads, 128), jnp.float32), prefix]
    mixed, at = None, 0
    found = [got]
    for bit in range(1, bits):
        if bit > 1:
            found.append(trade(group, 2**bit))
        mine = group if bit > 1 else stay
        if at < spans and bit < bits - 1:
            mixed, token = mix_local(at, at + 1, shared, mixed)
            at += 1
        if bit < bits - 1:
            group, prefix = merge(bit, mine, found[-1], prefixes[-1], token)
            prefixes.append(prefix)
    if at < spans:
        mixed, token = mix_local(at, spans, shared, mixed)
    middle = jnp.concatenate([state[:quarter] for state in found[1:-1]], axis=0)
    middle_far = trade(middle, 2)
    packed = jnp.concatenate([got[:quarter], got_rest[:quarter], middle, middle_far], axis=0)
    packed_far = trade(packed, 1)
    last = found[-1]
    last_side = trade(last, 2)
    last_parts = [last, last_side, trade(last, 1), trade(last_side, 1)]
    two = heads // 4
    levels = [(0, prefixes[0], [(0, 0, 0, 0, 2 * two), (1, 0, 1, 0, 2 * two)])]
    levels.append(
        (1, prefixes[1], [(2 + far, side * quarter, far, side, two) for far in (0, 1) for side in (0, 1)])
    )
    for bit in range(2, bits - 1):
        row = half + (bit - 2) * quarter
        step = (bits - 3) * quarter
        levels.append(
            (
                bit,
                prefixes[bit],
                [(2 + far, row + side * step, far, side, two) for far in (0, 1) for side in (0, 1)],
            )
        )
    parts = [near, near_rest, packed, packed_far]
    mixed = add_levels(mixed, queries, sums, level_weight, levels, parts, first_level)
    gain = norm_gain.reshape(heads, width // heads)
    pieces = [(0, 0, 0, 0, two), (1, 0, 0, 1, two), (2, 0, 1, 0, two), (3, 0, 1, 1, two)]
    return finish(
        mixed, queries, sums, level_weight, gain, prefixes[bits - 1], pieces, bits - 1, last_parts, first_level
    )


def solution(mesh):
    placed = (
        P(("wide", "narrow"), None),
        P(("wide", "narrow"), None),
        P(("wide", "narrow"), None),
        P(None, ("wide", "narrow")),
        P(None, None, ("wide", "narrow")),
        P(),
    )
    return jax.shard_map(
        per_device,
        mesh=mesh,
        in_specs=placed,
        out_specs=P(("wide", "narrow"), None),
        check_vma=False,
    )
```

```python
import functools

import jax
import jax.numpy as jnp
from jax import lax
from jax.experimental import pallas as pl
from jax.experimental.pallas import tpu as pltpu
from jax.sharding import PartitionSpec as P

SPAN = 256
EPS = 1e-05
AXES = ("narrow", "wide")
NT = (((1,), (1,)), ((), ()))
PARAMS = pltpu.CompilerParams(vmem_limit_bytes=32 * 1024 * 1024)
HELD = pl.BlockSpec(memory_space=pltpu.VMEM)


def place():
    return lax.axis_index("wide") * lax.axis_size("narrow") + lax.axis_index("narrow")


def bit_of(value, bit):
    return jnp.bitwise_and(jnp.right_shift(value, bit), 1)


def spread_lanes(column, width):
    return jnp.broadcast_to(column, (column.shape[0], width))


ANYWHERE = pl.BlockSpec(memory_space=pl.ANY)


def hold(array):
    return pltpu.with_memory_space_constraint(array, pltpu.VMEM)


def call(kernel, name, inputs, outputs, scratch=(), in_specs=None, aliases=None):
    specs = in_specs or [HELD] * len(inputs)
    inputs = [hold(array) if spec is HELD else array for array, spec in zip(inputs, specs)]
    return pl.pallas_call(
        kernel,
        in_specs=specs,
        out_specs=[HELD] * len(outputs),
        out_shape=[pltpu.VMEM(shape, dtype) for shape, dtype in outputs],
        scratch_shapes=list(scratch),
        input_output_aliases=aliases or {},
        compiler_params=PARAMS,
        name=name,
    )(*inputs)


def running_sums(rows):
    high = rows.astype(jnp.bfloat16)
    rest = rows - high.astype(jnp.float32)
    middle = rest.astype(jnp.bfloat16)
    low = (rest - middle.astype(jnp.float32)).astype(jnp.bfloat16)
    width = rows.shape[1]
    source = lax.broadcasted_iota(jnp.int32, (width, width), 0)
    target = lax.broadcasted_iota(jnp.int32, (width, width), 1)
    upto = jnp.where(source <= target, 1.0, 0.0).astype(jnp.bfloat16)
    sums = jnp.dot(
        jnp.concatenate([high, middle, low], axis=0), upto, preferred_element_type=jnp.float32
    )
    count = rows.shape[0]
    return sums[:count] + (sums[count : 2 * count] + sums[2 * count :])


def state_kernel(*refs):
    q_hbm, k_hbm, v_hbm, decay_hbm, weight_hbm, gain_hbm = refs[:6]
    keep_ref, send_ref, local_ref, sums_ref, totals_ref = refs[6:11]
    q_ref, k_ref, v_ref, weight_ref, gain_ref, decay_ref, held, arrived = refs[11:]
    heads, tokens = decay_ref.shape
    head_width = v_ref.shape[1] // heads
    spans = tokens // SPAN
    rows_of = [slice(span * SPAN, (span + 1) * SPAN) for span in range(spans)]
    loads = [(decay_hbm, decay_ref), (k_hbm, k_ref)]
    loads += [(v_hbm.at[rows], v_ref.at[rows]) for rows in rows_of]
    loads += [(q_hbm, q_ref), (weight_hbm, weight_ref), (gain_hbm, gain_ref)]
    copies = [
        pltpu.make_async_copy(source, target, arrived.at[at])
        for at, (source, target) in enumerate(loads)
    ]
    for copy in copies:
        copy.start()
    copies[0].wait()
    within = running_sums(jnp.concatenate([decay_ref[:, rows] for rows in rows_of], axis=0))
    run = jnp.zeros((heads, 128), jnp.float32)
    fades, wholes = [], []
    for span, rows in enumerate(rows_of):
        here = within[span * heads : (span + 1) * heads]
        last = here[:, SPAN - 1 :]
        total = spread_lanes(last, 128)
        sums_ref[0, :, rows] = here
        sums_ref[1, :, rows] = here + spread_lanes(run[:, :1], SPAN)
        totals_ref[span] = total
        run = run + total
        fades.append(jnp.exp(spread_lanes(last, SPAN) - here))
        wholes.append(jnp.exp(total))
    copies[1].wait()
    across = [k_ref[rows].astype(jnp.float32).T for rows in rows_of]
    for copy in copies[2 : 2 + spans]:
        copy.wait()
    for head in range(heads):
        columns = slice(head * head_width, (head + 1) * head_width)
        states = []
        for span, rows in enumerate(rows_of):
            faded = (across[span] * fades[span][head : head + 1]).astype(jnp.bfloat16)
            states.append(
                jnp.dot(faded, v_ref[rows, columns], preferred_element_type=jnp.float32)
            )
        at = 0
        size = 1
        while size < spans:
            for first in range(0, spans, 2 * size):
                group = states[first]
                for span in range(first + 1, first + size):
                    group = group * wholes[span][head : head + 1] + states[span]
                local_ref[at, :, columns] = group.astype(jnp.bfloat16)
                at += 1
            size *= 2
        group = states[0]
        for span in range(1, spans):
            group = group * wholes[span][head : head + 1] + states[span]
        held[columns] = group.T
    half = held.shape[0] // 2
    core = bit_of(place(), 0)
    keep_ref[:half] = held[pl.ds(core * half, half)]
    send_ref[:half] = held[pl.ds((1 - core) * half, half)]
    keep_ref[half:] = run
    send_ref[half:] = run
    for copy in copies[2 + spans :]:
        copy.wait()


def make_states(queries, keys, values, log_decay, level_weight, gain):
    tokens, key_width = keys.shape
    heads = log_decay.shape[0]
    width = values.shape[1]
    spans = tokens // SPAN
    message = ((width // 2 + heads, key_width), jnp.float32)
    inputs = [queries, keys, values, log_decay, level_weight, gain]
    kept = [queries, keys, values, level_weight, gain]
    return call(
        state_kernel,
        "states",
        [pltpu.with_memory_space_constraint(array, pltpu.HBM) for array in inputs],
        [
            message,
            message,
            ((spans - 1, key_width, width), jnp.bfloat16),
            ((2, heads, tokens), jnp.float32),
            ((spans, heads, 128), jnp.float32),
            *[(array.shape, array.dtype) for array in kept],
        ],
        [
            pltpu.VMEM(log_decay.shape, jnp.float32),
            pltpu.VMEM((width, key_width), jnp.float32),
            pltpu.SemaphoreType.DMA((spans + 5,)),
        ],
        [pl.BlockSpec(memory_space=pltpu.HBM)] * len(inputs),
    )


def local_kernel(first, last, *refs):
    q_ref, k_ref, v_ref, sums_ref, totals_ref, weight_ref, local_ref = refs[:7]
    mixed_ref, done_ref = refs[-2:]
    heads = weight_ref.shape[1]
    head_width = v_ref.shape[1] // heads
    spans = totals_ref.shape[0]
    local_bits = spans.bit_length() - 1
    half = SPAN // 2
    done_ref[...] = jnp.zeros_like(done_ref)
    source = lax.broadcasted_iota(jnp.int32, (half, half), 0)
    target = lax.broadcasted_iota(jnp.int32, (half, half), 1)
    causal = source <= target
    empty = jnp.zeros((half, half), jnp.bfloat16)

    for span in range(first, last):
        tokens = slice(span * SPAN, (span + 1) * SPAN)
        queries = q_ref[tokens]
        scores = lax.dot_general(
            k_ref[tokens], queries, NT, preferred_element_type=jnp.float32
        )
        within = sums_ref[0, :, tokens]
        within_down = within.T
        weight = weight_ref[0, :, tokens]
        values_across = v_ref[tokens].T

        def mix(head, low, high):
            rows = slice(low * half, (low + 1) * half)
            columns = slice(high * half, (high + 1) * half)
            gap = within[head : head + 1, columns] - within_down[rows, head : head + 1]
            if low == high:
                gap = jnp.where(causal, gap, -1e30)
            mixing = scores[rows, columns] * jnp.exp(gap) * weight[head : head + 1, columns]
            return mixing.astype(jnp.bfloat16)

        levels = []
        offset = 0
        for bit in range(local_bits):
            if span >> bit & 1:
                since = within
                for back in range(1, span % 2**bit + 1):
                    since = since + spread_lanes(totals_ref[span - back][:, :1], SPAN)
                scale = jnp.exp(since) * weight_ref[1 + bit, :, tokens]
                levels.append((local_ref[offset + (span >> (bit + 1))].T, scale))
            offset += spans >> (bit + 1)
        for head in range(heads):
            rows = slice(head * head_width, (head + 1) * head_width)
            mixing = jnp.concatenate(
                [
                    jnp.concatenate([mix(head, 0, 0), mix(head, 0, 1)], axis=1),
                    jnp.concatenate([empty, mix(head, 1, 1)], axis=1),
                ],
                axis=0,
            )
            mixed = jnp.dot(values_across[rows], mixing, preferred_element_type=jnp.float32)
            for level, scale in levels:
                found = lax.dot_general(
                    level[rows], queries, NT, preferred_element_type=jnp.float32
                )
                mixed = mixed + found * scale[head : head + 1]
            mixed_ref[rows, tokens] = mixed


def mix_local(first, last, shared, mixed):
    queries, keys, values, sums, totals, level_weight, local = shared
    rest = [] if mixed is None else [mixed]
    return call(
        functools.partial(local_kernel, first, last),
        f"local{first}",
        [*shared, *rest],
        [(values.shape[::-1], jnp.float32), ((8, 128), jnp.float32)],
        aliases={7: 0} if rest else None,
    )


def join(upper, mine, mine_total, other, other_total):
    fade = jnp.exp(jnp.where(upper, mine_total, other_total))
    return jnp.where(upper, other * fade + mine, mine * fade + other)


def first_head(far, heads):
    here = place()
    first = 0
    for bit, flip in enumerate(far):
        first = first + jnp.bitwise_xor(bit_of(here, bit), flip) * (heads >> (bit + 1))
    return first


def merge_kernel(bit, near, split, *refs):
    mine_ref, other_ref, prefix_ref = refs[:3]
    whole_ref = refs[-1]
    next_ref = refs[-2]
    heads = prefix_ref.shape[0]
    rows = mine_ref.shape[0] - heads
    count = heads >> near
    per = rows // count
    upper = bit_of(place(), bit) == 1
    first = first_head((0,) * near, heads)
    for slot in range(count):
        part = slice(slot * per, (slot + 1) * per)
        total = pl.ds(rows + first + slot, 1)
        whole_ref[part] = join(
            upper, mine_ref[part], mine_ref[total], other_ref[part], other_ref[total]
        )
    other_total = other_ref[rows:]
    total = mine_ref[rows:] + other_total
    next_ref[...] = prefix_ref[...] + jnp.where(upper, other_total, 0.0)
    if split:
        stay_ref, give_ref = refs[-4:-2]
        half = rows // 2
        side = bit_of(place(), bit + 1)
        stay_ref[:half] = whole_ref[pl.ds(side * half, half)]
        give_ref[:half] = whole_ref[pl.ds((1 - side) * half, half)]
        stay_ref[half:] = total
        give_ref[half:] = total
    else:
        merged_ref = refs[-3]
        merged_ref[:rows] = whole_ref[...]
        merged_ref[rows:] = total


def merge(bit, mine, other, prefix, tokens=()):
    heads, lanes = prefix.shape
    group_bits = heads.bit_length() - 1
    near = min(bit + 1, group_bits)
    split = bit + 1 < group_bits
    rows = mine.shape[0] - heads
    if split:
        messages = [((rows // 2 + heads, lanes), jnp.float32)] * 2
    else:
        messages = [(mine.shape, jnp.float32)]
    return call(
        functools.partial(merge_kernel, bit, near, split),
        f"merge{bit}",
        [mine, other, prefix, *tokens],
        [*messages, (prefix.shape, jnp.float32)],
        [pltpu.VMEM((rows, lanes), jnp.float32)],
    )


def pack_kernel(takes, *refs):
    out_ref = refs[-1]
    at = 0
    for ref, rows in zip(refs, takes):
        out_ref[at : at + rows] = ref[:rows]
        at += rows


def pack(name, pieces, tokens=()):
    takes = [rows for _, rows in pieces]
    lanes = pieces[0][0].shape[1]
    return call(
        functools.partial(pack_kernel, takes),
        name,
        [*[array for array, _ in pieces], *tokens],
        [((sum(takes), lanes), jnp.float32)],
    )[0]


def level_scale(bit, first_level, prefix_ref, sums_ref, weight_ref, tokens):
    active = jnp.where(bit_of(place(), bit) == 1, 1.0, 0.0)
    reach = jnp.exp(sums_ref[1, :, tokens] + spread_lanes(prefix_ref[:, :1], SPAN))
    return reach * weight_ref[first_level + bit, :, tokens] * active


def take_levels(plan, part_refs, levels, heads):
    per = levels.shape[1] // heads
    for slot, pieces in enumerate(plan):
        for index, row, far in pieces:
            rows = (heads >> len(far)) * per
            start = pl.multiple_of(first_head(far, heads) * per, 128)
            levels[slot, pl.ds(start, rows)] = part_refs[index][row : row + rows].astype(
                jnp.bfloat16
            )


def reach_kernel(plan, bits, first_level, *refs):
    mixed_ref, q_ref, sums_ref, weight_ref = refs[:4]
    prefix_refs = refs[4 : 4 + len(bits)]
    part_refs = refs[4 + len(bits) : -2]
    out_ref, levels = refs[-2:]
    heads = weight_ref.shape[1]
    head_width = mixed_ref.shape[0] // heads
    take_levels(plan, part_refs, levels, heads)
    for span in range(q_ref.shape[0] // SPAN):
        tokens = slice(span * SPAN, (span + 1) * SPAN)
        queries = q_ref[tokens]
        scales = [
            level_scale(bit, first_level, prefix_ref, sums_ref, weight_ref, tokens)
            for bit, prefix_ref in zip(bits, prefix_refs)
        ]
        for head in range(heads):
            rows = slice(head * head_width, (head + 1) * head_width)
            mixed = mixed_ref[rows, tokens]
            for slot, scale in enumerate(scales):
                found = lax.dot_general(
                    levels[slot, rows], queries, NT, preferred_element_type=jnp.float32
                )
                mixed = mixed + found * scale[head : head + 1]
            out_ref[rows, tokens] = mixed


def add_levels(mixed, queries, sums, level_weight, levels, parts, first_level):
    width = mixed.shape[0]
    bits = [bit for bit, _, _ in levels]
    plan = [pieces for _, _, pieces in levels]
    return call(
        functools.partial(reach_kernel, plan, bits, first_level),
        "reach",
        [mixed, queries, sums, level_weight, *[prefix for _, prefix, _ in levels], *parts],
        [(mixed.shape, jnp.float32)],
        [pltpu.VMEM((len(bits), width, queries.shape[1]), jnp.bfloat16)],
        aliases={0: 0},
    )[0]


def finish_kernel(far, bit, first_level, *refs):
    mixed_ref, q_ref, sums_ref, weight_ref, gain_ref, prefix_ref, state_ref = refs[:7]
    out_hbm, out_ref, level, scale_ref, sent = refs[-5:]
    heads = weight_ref.shape[1]
    head_width = mixed_ref.shape[0] // heads
    half = heads // 2
    first = first_head((far,), heads)
    flips = half.bit_length() - 1
    for slot in range(half):
        beyond = tuple(slot >> (flips - 1 - bit) & 1 for bit in range(flips))
        start = pl.multiple_of((first_head((far, *beyond), heads) - first) * head_width, 128)
        rows = slice(slot * head_width, (slot + 1) * head_width)
        level[pl.ds(start, head_width)] = state_ref[rows].astype(jnp.bfloat16)
    gains = []
    for slot in range(half):
        row = jnp.broadcast_to(gain_ref[pl.ds(first + slot, 1)], (8, head_width))
        gains.append(row.T[:, :1])
    columns = pl.ds(pl.multiple_of(first * head_width, 128), half * head_width)
    copies = []
    for span in range(q_ref.shape[0] // SPAN):
        tokens = slice(span * SPAN, (span + 1) * SPAN)
        queries = q_ref[tokens]
        scale_ref[...] = level_scale(bit, first_level, prefix_ref, sums_ref, weight_ref, tokens)
        for slot in range(half):
            rows = slice(slot * head_width, (slot + 1) * head_width)
            found = lax.dot_general(level[rows], queries, NT, preferred_element_type=jnp.float32)
            start = pl.multiple_of((first + slot) * head_width, 128)
            mixed = mixed_ref[pl.ds(start, head_width), tokens]
            mixed = mixed + found * scale_ref[pl.ds(first + slot, 1)]
            square = jnp.mean(mixed * mixed, axis=0, keepdims=True)
            normed = mixed * lax.rsqrt(square + EPS) * gains[slot]
            out_ref[tokens, rows] = normed.astype(jnp.bfloat16).T
        copy = pltpu.make_async_copy(
            out_ref.at[tokens], out_hbm.at[tokens, columns], sent.at[span]
        )
        copy.start()
        copies.append(copy)
    for copy in copies:
        copy.wait()


def finish(far, bit, first_level, mixed, queries, sums, level_weight, gain, prefix, state, begun):
    width, tokens = mixed.shape
    heads = level_weight.shape[1]
    inputs = [mixed, queries, sums, level_weight, gain, prefix, state]
    specs = [HELD] * len(inputs)
    inputs = [hold(array) for array in inputs]
    out = pl.BlockSpec(memory_space=pltpu.HBM)
    if begun is not None:
        specs.append(out)
        inputs.append(begun)
    return pl.pallas_call(
        functools.partial(finish_kernel, far, bit, first_level),
        in_specs=specs,
        out_specs=out,
        out_shape=jax.ShapeDtypeStruct((tokens, width), jnp.bfloat16),
        scratch_shapes=[
            pltpu.VMEM((tokens, width // 2), jnp.bfloat16),
            pltpu.VMEM(state.shape, jnp.bfloat16),
            pltpu.VMEM((heads, SPAN), jnp.float32),
            pltpu.SemaphoreType.DMA((tokens // SPAN,)),
        ],
        input_output_aliases={} if begun is None else {7: 0},
        compiler_params=PARAMS,
        name=f"finish{far}",
    )(*inputs)


def trade(value, mask, senders=lambda source: True):
    wide, narrow = lax.axis_size("wide"), lax.axis_size("narrow")

    def ranked(index):
        return index % narrow * wide + index // narrow

    pairs = [
        (ranked(source), ranked(source ^ mask))
        for source in range(wide * narrow)
        if senders(source)
    ]
    return lax.ppermute(value, AXES, pairs)


def per_device(queries, keys, values, log_decay, level_weight, norm_gain):
    heads = log_decay.shape[0]
    tokens, width = values.shape
    per = width // heads
    spans = tokens // SPAN
    group_bits = heads.bit_length() - 1
    bits = (lax.axis_size("wide") * lax.axis_size("narrow")).bit_length() - 1
    first_level = level_weight.shape[0] - bits
    gain = norm_gain.reshape(heads, per)
    mine, give, local, sums, totals, queries, keys, values, level_weight, gain = make_states(
        queries, keys, values, log_decay, level_weight, gain
    )
    shared = (queries, keys, values, sums, totals, level_weight, local)

    prefix = jnp.zeros((heads, 128), jnp.float32)
    prefixes, found, rests = [], [], []
    mixed, at, tokens_done = None, 0, ()
    for bit in range(bits):
        lower = lambda source, bit=bit: (source >> bit) & 1 == 0
        sent = give if bit < group_bits else mine
        both = bit < bits - 1
        found.append(trade(sent, 2**bit) if both else trade(sent, 2**bit, lower))
        prefixes.append(prefix)
        if bit < group_bits:
            rests.append(trade(mine, 2**bit, lower))
        if 0 < bit and at < spans:
            stop = spans if bit == bits - 2 else at + 1
            mixed, token = mix_local(at, stop, shared, mixed)
            at, tokens_done = stop, (token,)
        if both:
            *messages, prefix = merge(bit, mine, found[bit], prefix, tokens_done)
            mine, give = messages if len(messages) == 2 else (messages[0], None)
    after = (mine,)

    early = range(group_bits, bits - 1)
    ahead = pack("ahead", [(found[bit], per) for bit in early], after)
    beside = trade(ahead, 4)
    pieces = [(found[2], per), (rests[2], per)]
    for slot, bit in enumerate(early):
        pieces += [(ahead[slot * per : (slot + 1) * per], per), (beside[slot * per : (slot + 1) * per], per)]
    quarter = pack("quarter", pieces)
    across = trade(quarter, 2)
    step = quarter.shape[0]
    near = pack(
        "near", [(found[1], 2 * per), (rests[1], 2 * per), (quarter, step), (across, step)]
    )
    far = trade(near, 1)
    levels = [(0, prefixes[0], [(0, 0, (0,)), (1, 0, (1,))])]
    levels.append(
        (1, prefixes[1], [(2 + core, side * 2 * per, (core, side)) for core in (0, 1) for side in (0, 1)])
    )
    for slot, bit in enumerate(range(2, bits - 1)):
        row = 4 * per + slot * 2 * per
        taken = [
            (2 + core, row + side * step + last * per, (core, side, last))
            for core in (0, 1)
            for side in (0, 1)
            for last in (0, 1)
        ]
        levels.append((bit, prefixes[bit], taken))
    parts = [found[0], rests[0], near, far]
    mixed = add_levels(mixed, queries, sums, level_weight, levels, parts, first_level)

    last = bits - 1
    needed = lambda source: (source >> last) & 1 == 1
    state = pack("last1", [(found[last], per), (trade(found[last], 4, needed), per)])
    state = pack("last2", [(state, 2 * per), (trade(state, 2, needed), 2 * per)])
    other = trade(state, 1, needed)
    rest = (mixed, queries, sums, level_weight, gain, prefixes[last])
    begun = finish(0, last, first_level, *rest, state, None)
    return finish(1, last, first_level, *rest, other, begun)


def solution(mesh):
    placed = (
        P(("wide", "narrow"), None),
        P(("wide", "narrow"), None),
        P(("wide", "narrow"), None),
        P(None, ("wide", "narrow")),
        P(None, None, ("wide", "narrow")),
        P(),
    )
    return jax.shard_map(
        per_device,
        mesh=mesh,
        in_specs=placed,
        out_specs=P(("wide", "narrow"), None),
        check_vma=False,
    )
```

```python
import functools

import jax
import jax.numpy as jnp
from jax import lax
from jax.experimental import pallas as pl
from jax.experimental.pallas import tpu as pltpu
from jax.sharding import PartitionSpec as P

SPAN = 256
SPLIT_BITS = 2
EPS = 1e-05
AXES = ("narrow", "wide")
NT = (((1,), (1,)), ((), ()))
PARAMS = pltpu.CompilerParams(vmem_limit_bytes=32 * 1024 * 1024)
HELD = pl.BlockSpec(memory_space=pltpu.VMEM)


def place():
    return lax.axis_index("wide") * lax.axis_size("narrow") + lax.axis_index("narrow")


def bit_of(value, bit):
    return jnp.bitwise_and(jnp.right_shift(value, bit), 1)


def spread_lanes(column, width):
    return jnp.broadcast_to(column, (column.shape[0], width))


ANYWHERE = pl.BlockSpec(memory_space=pl.ANY)


def hold(array):
    return pltpu.with_memory_space_constraint(array, pltpu.VMEM)


def call(kernel, name, inputs, outputs, scratch=(), in_specs=None, aliases=None):
    specs = in_specs or [HELD] * len(inputs)
    inputs = [hold(array) if spec is HELD else array for array, spec in zip(inputs, specs)]
    return pl.pallas_call(
        kernel,
        in_specs=specs,
        out_specs=[HELD] * len(outputs),
        out_shape=[pltpu.VMEM(shape, dtype) for shape, dtype in outputs],
        scratch_shapes=list(scratch),
        input_output_aliases=aliases or {},
        compiler_params=PARAMS,
        name=name,
    )(*inputs)


def running_sums(rows):
    high = rows.astype(jnp.bfloat16)
    rest = rows - high.astype(jnp.float32)
    middle = rest.astype(jnp.bfloat16)
    low = (rest - middle.astype(jnp.float32)).astype(jnp.bfloat16)
    width = rows.shape[1]
    source = lax.broadcasted_iota(jnp.int32, (width, width), 0)
    target = lax.broadcasted_iota(jnp.int32, (width, width), 1)
    upto = jnp.where(source <= target, 1.0, 0.0).astype(jnp.bfloat16)
    sums = jnp.dot(
        jnp.concatenate([high, middle, low], axis=0), upto, preferred_element_type=jnp.float32
    )
    count = rows.shape[0]
    return sums[:count] + (sums[count : 2 * count] + sums[2 * count :])


def state_kernel(*refs):
    q_hbm, k_hbm, v_hbm, decay_hbm, weight_hbm, gain_hbm = refs[:6]
    keep_ref, send_ref, local_ref, sums_ref, totals_ref = refs[6:11]
    q_ref, k_ref, v_ref, weight_ref, gain_ref, decay_ref, held, arrived = refs[11:]
    heads, tokens = decay_ref.shape
    head_width = v_ref.shape[1] // heads
    spans = tokens // SPAN
    rows_of = [slice(span * SPAN, (span + 1) * SPAN) for span in range(spans)]
    loads = [(decay_hbm, decay_ref), (k_hbm, k_ref)]
    loads += [(v_hbm.at[rows], v_ref.at[rows]) for rows in rows_of]
    loads += [(q_hbm, q_ref), (weight_hbm, weight_ref), (gain_hbm, gain_ref)]
    copies = [
        pltpu.make_async_copy(source, target, arrived.at[at])
        for at, (source, target) in enumerate(loads)
    ]
    for copy in copies:
        copy.start()
    copies[0].wait()
    within = running_sums(jnp.concatenate([decay_ref[:, rows] for rows in rows_of], axis=0))
    run = jnp.zeros((heads, 128), jnp.float32)
    fades, wholes = [], []
    for span, rows in enumerate(rows_of):
        here = within[span * heads : (span + 1) * heads]
        last = here[:, SPAN - 1 :]
        total = spread_lanes(last, 128)
        sums_ref[0, :, rows] = here
        sums_ref[1, :, rows] = here + spread_lanes(run[:, :1], SPAN)
        totals_ref[span] = total
        run = run + total
        fades.append(jnp.exp(spread_lanes(last, SPAN) - here))
        wholes.append(jnp.exp(total))
    copies[1].wait()
    across = [k_ref[rows].astype(jnp.float32).T for rows in rows_of]
    for copy in copies[2 : 2 + spans]:
        copy.wait()
    for head in range(heads):
        columns = slice(head * head_width, (head + 1) * head_width)
        states = []
        for span, rows in enumerate(rows_of):
            faded = (across[span] * fades[span][head : head + 1]).astype(jnp.bfloat16)
            states.append(
                jnp.dot(faded, v_ref[rows, columns], preferred_element_type=jnp.float32)
            )
        at = 0
        size = 1
        while size < spans:
            for first in range(0, spans, 2 * size):
                group = states[first]
                for span in range(first + 1, first + size):
                    group = group * wholes[span][head : head + 1] + states[span]
                local_ref[at, :, columns] = group.astype(jnp.bfloat16)
                at += 1
            size *= 2
        group = states[0]
        for span in range(1, spans):
            group = group * wholes[span][head : head + 1] + states[span]
        held[columns] = group.T
    half = held.shape[0] // 2
    core = bit_of(place(), 0)
    keep_ref[:half] = held[pl.ds(core * half, half)]
    send_ref[:half] = held[pl.ds((1 - core) * half, half)]
    keep_ref[half:] = run
    send_ref[half:] = run
    for copy in copies[2 + spans :]:
        copy.wait()


def make_states(queries, keys, values, log_decay, level_weight, gain):
    tokens, key_width = keys.shape
    heads = log_decay.shape[0]
    width = values.shape[1]
    spans = tokens // SPAN
    message = ((width // 2 + heads, key_width), jnp.float32)
    inputs = [queries, keys, values, log_decay, level_weight, gain]
    kept = [queries, keys, values, level_weight, gain]
    return call(
        state_kernel,
        "states",
        [pltpu.with_memory_space_constraint(array, pltpu.HBM) for array in inputs],
        [
            message,
            message,
            ((spans - 1, key_width, width), jnp.bfloat16),
            ((2, heads, tokens), jnp.float32),
            ((spans, heads, 128), jnp.float32),
            *[(array.shape, array.dtype) for array in kept],
        ],
        [
            pltpu.VMEM(log_decay.shape, jnp.float32),
            pltpu.VMEM((width, key_width), jnp.float32),
            pltpu.SemaphoreType.DMA((spans + 5,)),
        ],
        [pl.BlockSpec(memory_space=pltpu.HBM)] * len(inputs),
    )


def local_kernel(first, last, *refs):
    q_ref, k_ref, v_ref, sums_ref, totals_ref, weight_ref, local_ref = refs[:7]
    mixed_ref, done_ref = refs[-2:]
    heads = weight_ref.shape[1]
    head_width = v_ref.shape[1] // heads
    spans = totals_ref.shape[0]
    local_bits = spans.bit_length() - 1
    half = SPAN // 2
    done_ref[...] = jnp.zeros_like(done_ref)
    source = lax.broadcasted_iota(jnp.int32, (half, half), 0)
    target = lax.broadcasted_iota(jnp.int32, (half, half), 1)
    causal = source <= target
    empty = jnp.zeros((half, half), jnp.bfloat16)

    for span in range(first, last):
        tokens = slice(span * SPAN, (span + 1) * SPAN)
        queries = q_ref[tokens]
        scores = lax.dot_general(
            k_ref[tokens], queries, NT, preferred_element_type=jnp.float32
        )
        within = sums_ref[0, :, tokens]
        within_down = within.T
        weight = weight_ref[0, :, tokens]
        values_across = v_ref[tokens].T

        def mix(head, low, high):
            rows = slice(low * half, (low + 1) * half)
            columns = slice(high * half, (high + 1) * half)
            gap = within[head : head + 1, columns] - within_down[rows, head : head + 1]
            if low == high:
                gap = jnp.where(causal, gap, -1e30)
            mixing = scores[rows, columns] * jnp.exp(gap) * weight[head : head + 1, columns]
            return mixing.astype(jnp.bfloat16)

        levels = []
        offset = 0
        for bit in range(local_bits):
            if span >> bit & 1:
                since = within
                for back in range(1, span % 2**bit + 1):
                    since = since + spread_lanes(totals_ref[span - back][:, :1], SPAN)
                scale = jnp.exp(since) * weight_ref[1 + bit, :, tokens]
                levels.append((local_ref[offset + (span >> (bit + 1))].T, scale))
            offset += spans >> (bit + 1)
        for head in range(heads):
            rows = slice(head * head_width, (head + 1) * head_width)
            mixing = jnp.concatenate(
                [
                    jnp.concatenate([mix(head, 0, 0), mix(head, 0, 1)], axis=1),
                    jnp.concatenate([empty, mix(head, 1, 1)], axis=1),
                ],
                axis=0,
            )
            mixed = jnp.dot(values_across[rows], mixing, preferred_element_type=jnp.float32)
            for level, scale in levels:
                found = lax.dot_general(
                    level[rows], queries, NT, preferred_element_type=jnp.float32
                )
                mixed = mixed + found * scale[head : head + 1]
            mixed_ref[rows, tokens] = mixed


def mix_local(first, last, shared, mixed, tokens=()):
    queries, keys, values, sums, totals, level_weight, local = shared
    rest = [] if mixed is None else [mixed]
    return call(
        functools.partial(local_kernel, first, last),
        f"local{first}",
        [*shared, *rest, *tokens],
        [(values.shape[::-1], jnp.float32), ((8, 128), jnp.float32)],
        aliases={7: 0} if rest else None,
    )


def join(upper, mine, mine_total, other, other_total):
    fade = jnp.exp(jnp.where(upper, mine_total, other_total))
    return jnp.where(upper, other * fade + mine, mine * fade + other)


def first_head(far, heads):
    here = place()
    first = 0
    for bit, flip in enumerate(far):
        first = first + jnp.bitwise_xor(bit_of(here, bit), flip) * (heads >> (bit + 1))
    return first


def merge_kernel(bit, near, split, *refs):
    mine_ref, other_ref, prefix_ref = refs[:3]
    whole_ref = refs[-1]
    next_ref = refs[-2]
    heads = prefix_ref.shape[0]
    rows = mine_ref.shape[0] - heads
    count = heads >> near
    per = rows // count
    upper = bit_of(place(), bit) == 1
    first = first_head((0,) * near, heads)
    for slot in range(count):
        part = slice(slot * per, (slot + 1) * per)
        total = pl.ds(rows + first + slot, 1)
        whole_ref[part] = join(
            upper, mine_ref[part], mine_ref[total], other_ref[part], other_ref[total]
        )
    other_total = other_ref[rows:]
    total = mine_ref[rows:] + other_total
    next_ref[...] = prefix_ref[...] + jnp.where(upper, other_total, 0.0)
    if split:
        stay_ref, give_ref = refs[-4:-2]
        half = rows // 2
        side = bit_of(place(), bit + 1)
        stay_ref[:half] = whole_ref[pl.ds(side * half, half)]
        give_ref[:half] = whole_ref[pl.ds((1 - side) * half, half)]
        stay_ref[half:] = total
        give_ref[half:] = total
    else:
        merged_ref = refs[-3]
        merged_ref[:rows] = whole_ref[...]
        merged_ref[rows:] = total


def merge(bit, mine, other, prefix, tokens=()):
    heads, lanes = prefix.shape
    near = min(bit + 1, SPLIT_BITS)
    split = bit + 1 < SPLIT_BITS
    rows = mine.shape[0] - heads
    if split:
        messages = [((rows // 2 + heads, lanes), jnp.float32)] * 2
    else:
        messages = [(mine.shape, jnp.float32)]
    return call(
        functools.partial(merge_kernel, bit, near, split),
        f"merge{bit}",
        [mine, other, prefix, *tokens],
        [*messages, (prefix.shape, jnp.float32)],
        [pltpu.VMEM((rows, lanes), jnp.float32)],
    )


def pack_kernel(takes, *refs):
    out_ref = refs[-1]
    at = 0
    for ref, rows in zip(refs, takes):
        out_ref[at : at + rows] = ref[:rows]
        at += rows


def pack(name, pieces, tokens=()):
    takes = [rows for _, rows in pieces]
    lanes = pieces[0][0].shape[1]
    return call(
        functools.partial(pack_kernel, takes),
        name,
        [*[array for array, _ in pieces], *tokens],
        [((sum(takes), lanes), jnp.float32)],
    )[0]


def level_scale(bit, first_level, prefix_ref, sums_ref, weight_ref, tokens):
    active = jnp.where(bit_of(place(), bit) == 1, 1.0, 0.0)
    reach = jnp.exp(sums_ref[1, :, tokens] + spread_lanes(prefix_ref[:, :1], SPAN))
    return reach * weight_ref[first_level + bit, :, tokens] * active


def take_levels(plan, part_refs, levels, heads):
    per = levels.shape[1] // heads
    for slot, pieces in enumerate(plan):
        for index, row, far in pieces:
            rows = (heads >> len(far)) * per
            start = pl.multiple_of(first_head(far, heads) * per, 128)
            levels[slot, pl.ds(start, rows)] = part_refs[index][row : row + rows].astype(
                jnp.bfloat16
            )


def reach_kernel(plan, bits, first_level, *refs):
    mixed_ref, q_ref, sums_ref, weight_ref = refs[:4]
    prefix_refs = refs[4 : 4 + len(bits)]
    part_refs = refs[4 + len(bits) : -3]
    out_ref, done_ref, levels = refs[-3:]
    done_ref[...] = jnp.zeros_like(done_ref)
    heads = weight_ref.shape[1]
    head_width = mixed_ref.shape[0] // heads
    take_levels(plan, part_refs, levels, heads)
    for span in range(q_ref.shape[0] // SPAN):
        tokens = slice(span * SPAN, (span + 1) * SPAN)
        queries = q_ref[tokens]
        scales = [
            level_scale(bit, first_level, prefix_ref, sums_ref, weight_ref, tokens)
            for bit, prefix_ref in zip(bits, prefix_refs)
        ]
        for head in range(heads):
            rows = slice(head * head_width, (head + 1) * head_width)
            mixed = mixed_ref[rows, tokens]
            for slot, scale in enumerate(scales):
                found = lax.dot_general(
                    levels[slot, rows], queries, NT, preferred_element_type=jnp.float32
                )
                mixed = mixed + found * scale[head : head + 1]
            out_ref[rows, tokens] = mixed


def add_levels(mixed, queries, sums, level_weight, levels, parts, first_level, tokens=()):
    width = mixed.shape[0]
    bits = [bit for bit, _, _ in levels]
    plan = [pieces for _, _, pieces in levels]
    prefixes = [prefix for _, prefix, _ in levels]
    return call(
        functools.partial(reach_kernel, plan, bits, first_level),
        f"reach{bits[0]}",
        [mixed, queries, sums, level_weight, *prefixes, *parts, *tokens],
        [(mixed.shape, jnp.float32), ((8, 128), jnp.float32)],
        [pltpu.VMEM((len(bits), width, queries.shape[1]), jnp.bfloat16)],
        aliases={0: 0},
    )


def finish_kernel(far, bit, first_level, *refs):
    mixed_ref, q_ref, sums_ref, weight_ref, gain_ref, prefix_ref, state_ref = refs[:7]
    out_hbm, out_ref, level, scale_ref, sent = refs[-5:]
    heads = weight_ref.shape[1]
    head_width = mixed_ref.shape[0] // heads
    half = heads // 2
    first = first_head((far,), heads)
    size = half * head_width // 2
    for side in range(2):
        start = pl.multiple_of((first_head((far, side), heads) - first) * head_width, 128)
        rows = slice(side * size, (side + 1) * size)
        level[pl.ds(start, size)] = state_ref[rows].astype(jnp.bfloat16)
    gains = []
    for slot in range(half):
        row = jnp.broadcast_to(gain_ref[pl.ds(first + slot, 1)], (8, head_width))
        gains.append(row.T[:, :1])
    columns = pl.ds(pl.multiple_of(first * head_width, 128), half * head_width)
    copies = []
    for span in range(q_ref.shape[0] // SPAN):
        tokens = slice(span * SPAN, (span + 1) * SPAN)
        queries = q_ref[tokens]
        scale_ref[...] = level_scale(bit, first_level, prefix_ref, sums_ref, weight_ref, tokens)
        for slot in range(half):
            rows = slice(slot * head_width, (slot + 1) * head_width)
            found = lax.dot_general(level[rows], queries, NT, preferred_element_type=jnp.float32)
            start = pl.multiple_of((first + slot) * head_width, 128)
            mixed = mixed_ref[pl.ds(start, head_width), tokens]
            mixed = mixed + found * scale_ref[pl.ds(first + slot, 1)]
            square = jnp.mean(mixed * mixed, axis=0, keepdims=True)
            normed = mixed * lax.rsqrt(square + EPS) * gains[slot]
            out_ref[tokens, rows] = normed.astype(jnp.bfloat16).T
        copy = pltpu.make_async_copy(
            out_ref.at[tokens], out_hbm.at[tokens, columns], sent.at[span]
        )
        copy.start()
        copies.append(copy)
    for copy in copies:
        copy.wait()


def finish(far, bit, first_level, mixed, queries, sums, level_weight, gain, prefix, state, begun):
    width, tokens = mixed.shape
    heads = level_weight.shape[1]
    inputs = [mixed, queries, sums, level_weight, gain, prefix, state]
    specs = [HELD] * len(inputs)
    inputs = [hold(array) for array in inputs]
    out = pl.BlockSpec(memory_space=pltpu.HBM)
    if begun is not None:
        specs.append(out)
        inputs.append(begun)
    return pl.pallas_call(
        functools.partial(finish_kernel, far, bit, first_level),
        in_specs=specs,
        out_specs=out,
        out_shape=jax.ShapeDtypeStruct((tokens, width), jnp.bfloat16),
        scratch_shapes=[
            pltpu.VMEM((tokens, width // 2), jnp.bfloat16),
            pltpu.VMEM(state.shape, jnp.bfloat16),
            pltpu.VMEM((heads, SPAN), jnp.float32),
            pltpu.SemaphoreType.DMA((tokens // SPAN,)),
        ],
        input_output_aliases={} if begun is None else {7: 0},
        compiler_params=PARAMS,
        name=f"finish{far}",
    )(*inputs)


def trade(value, mask, senders=lambda source: True):
    wide, narrow = lax.axis_size("wide"), lax.axis_size("narrow")

    def ranked(index):
        return index % narrow * wide + index // narrow

    pairs = [
        (ranked(source), ranked(source ^ mask))
        for source in range(wide * narrow)
        if senders(source)
    ]
    return lax.ppermute(value, AXES, pairs)


def per_device(queries, keys, values, log_decay, level_weight, norm_gain):
    heads = log_decay.shape[0]
    tokens, width = values.shape
    per = width // heads
    spans = tokens // SPAN
    group_bits = heads.bit_length() - 1
    bits = (lax.axis_size("wide") * lax.axis_size("narrow")).bit_length() - 1
    first_level = level_weight.shape[0] - bits
    gain = norm_gain.reshape(heads, per)
    mine, give, local, sums, totals, queries, keys, values, level_weight, gain = make_states(
        queries, keys, values, log_decay, level_weight, gain
    )
    shared = (queries, keys, values, sums, totals, level_weight, local)

    last = bits - 1
    prefix = jnp.zeros((heads, 128), jnp.float32)
    prefixes, found, rests = [], [], []
    mixed, at, waits = None, 0, ()
    for bit in range(bits):
        lower = lambda source, bit=bit: (source >> bit) & 1 == 0
        prefixes.append(prefix)
        if bit < last:
            found.append(trade(give if bit < SPLIT_BITS else mine, 2**bit))
        else:
            found.append(trade(mine, 2**bit, lower))
        if bit < SPLIT_BITS:
            rests.append(trade(mine, 2**bit, lower))
        if 0 < bit and at < spans:
            stop = spans if bit == last else at + 1
            mixed, token = mix_local(at, stop, shared, mixed, (mine,))
            at, waits = stop, (token,)
        if 1 < bit < 2 + SPLIT_BITS:
            waits = (*waits, rests[bit - 2])
        if bit < last:
            *messages, prefix = merge(bit, mine, found[bit], prefix, waits)
            mine, give = messages if len(messages) == 2 else (messages[0], None)

    rest = (queries, sums, level_weight)
    two = 2 * per
    middle = pack("middle", [(found[bit], two) for bit in range(2, last)], (mine,))
    across = trade(middle, 2)
    step = middle.shape[0]

    needed = lambda source: (source >> last) & 1 == 1
    state = found[last]
    beside = trade(state, 2, needed)
    levels = [(0, prefixes[0], [(0, 0, (0,)), (1, 0, (1,))])]
    parts = [found[0], rests[0]]
    mixed, token = add_levels(mixed, *rest, levels, parts, first_level)

    near = pack(
        "near", [(found[1], two), (rests[1], two), (middle, step), (across, step)], (state,)
    )
    far = trade(near, 1)
    sides = [(core, side) for core in (0, 1) for side in (0, 1)]
    levels = [(1, prefixes[1], [(core, side * two, (core, side)) for core, side in sides])]
    for slot, bit in enumerate(range(2, last)):
        row = 2 * two + slot * two
        levels.append(
            (bit, prefixes[bit], [(core, row + side * step, (core, side)) for core, side in sides])
        )
    mixed, token = add_levels(mixed, *rest, levels, [near, far], first_level)

    state = pack("last", [(state, two), (beside, two)], (token,))
    other = trade(state, 1, needed)
    rest = (mixed, *rest, gain, prefixes[last])
    begun = finish(0, last, first_level, *rest, state, None)
    return finish(1, last, first_level, *rest, other, begun)


def solution(mesh):
    placed = (
        P(("wide", "narrow"), None),
        P(("wide", "narrow"), None),
        P(("wide", "narrow"), None),
        P(None, ("wide", "narrow")),
        P(None, None, ("wide", "narrow")),
        P(),
    )
    return jax.shard_map(
        per_device,
        mesh=mesh,
        in_specs=placed,
        out_specs=P(("wide", "narrow"), None),
        check_vma=False,
    )
```

```python
import functools

import jax
import jax.numpy as jnp
from jax import lax
from jax.experimental import pallas as pl
from jax.experimental.pallas import tpu as pltpu
from jax.sharding import PartitionSpec as P

SPAN = 256
SPLIT_BITS = 2
EPS = 1e-05
AXES = ("narrow", "wide")
NT = (((1,), (1,)), ((), ()))
PARAMS = pltpu.CompilerParams(vmem_limit_bytes=32 * 1024 * 1024)
HELD = pl.BlockSpec(memory_space=pltpu.VMEM)


def place():
    return lax.axis_index("wide") * lax.axis_size("narrow") + lax.axis_index("narrow")


def bit_of(value, bit):
    return jnp.bitwise_and(jnp.right_shift(value, bit), 1)


def spread_lanes(column, width):
    return jnp.broadcast_to(column, (column.shape[0], width))


ANYWHERE = pl.BlockSpec(memory_space=pl.ANY)


def hold(array):
    return pltpu.with_memory_space_constraint(array, pltpu.VMEM)


def call(kernel, name, inputs, outputs, scratch=(), in_specs=None, aliases=None):
    specs = in_specs or [HELD] * len(inputs)
    inputs = [hold(array) if spec is HELD else array for array, spec in zip(inputs, specs)]
    return pl.pallas_call(
        kernel,
        in_specs=specs,
        out_specs=[HELD] * len(outputs),
        out_shape=[pltpu.VMEM(shape, dtype) for shape, dtype in outputs],
        scratch_shapes=list(scratch),
        input_output_aliases=aliases or {},
        compiler_params=PARAMS,
        name=name,
    )(*inputs)


def running_sums(rows):
    high = rows.astype(jnp.bfloat16)
    rest = rows - high.astype(jnp.float32)
    middle = rest.astype(jnp.bfloat16)
    low = (rest - middle.astype(jnp.float32)).astype(jnp.bfloat16)
    width = rows.shape[1]
    source = lax.broadcasted_iota(jnp.int32, (width, width), 0)
    target = lax.broadcasted_iota(jnp.int32, (width, width), 1)
    upto = jnp.where(source <= target, 1.0, 0.0).astype(jnp.bfloat16)
    sums = jnp.dot(
        jnp.concatenate([high, middle, low], axis=0), upto, preferred_element_type=jnp.float32
    )
    count = rows.shape[0]
    return sums[:count] + (sums[count : 2 * count] + sums[2 * count :])


def state_kernel(*refs):
    q_hbm, k_hbm, v_hbm, decay_hbm, weight_hbm, gain_hbm = refs[:6]
    keep_ref, send_ref, local_ref, sums_ref, totals_ref = refs[6:11]
    q_ref, k_ref, v_ref, weight_ref, gain_ref, decay_ref, held, arrived = refs[11:]
    heads, tokens = decay_ref.shape
    head_width = v_ref.shape[1] // heads
    spans = tokens // SPAN
    rows_of = [slice(span * SPAN, (span + 1) * SPAN) for span in range(spans)]
    loads = [(decay_hbm, decay_ref), (k_hbm, k_ref)]
    loads += [(v_hbm.at[rows], v_ref.at[rows]) for rows in rows_of]
    loads += [(q_hbm, q_ref), (weight_hbm, weight_ref), (gain_hbm, gain_ref)]
    copies = [
        pltpu.make_async_copy(source, target, arrived.at[at])
        for at, (source, target) in enumerate(loads)
    ]
    for copy in copies:
        copy.start()
    copies[0].wait()
    within = running_sums(jnp.concatenate([decay_ref[:, rows] for rows in rows_of], axis=0))
    run = jnp.zeros((heads, 128), jnp.float32)
    fades, wholes = [], []
    for span, rows in enumerate(rows_of):
        here = within[span * heads : (span + 1) * heads]
        last = here[:, SPAN - 1 :]
        total = spread_lanes(last, 128)
        sums_ref[0, :, rows] = here
        sums_ref[1, :, rows] = here + spread_lanes(run[:, :1], SPAN)
        totals_ref[span] = total
        run = run + total
        fades.append(jnp.exp(spread_lanes(last, SPAN) - here))
        wholes.append(jnp.exp(total))
    copies[1].wait()
    across = [k_ref[rows].astype(jnp.float32).T for rows in rows_of]
    for copy in copies[2 : 2 + spans]:
        copy.wait()
    for head in range(heads):
        columns = slice(head * head_width, (head + 1) * head_width)
        states = []
        for span, rows in enumerate(rows_of):
            faded = (across[span] * fades[span][head : head + 1]).astype(jnp.bfloat16)
            states.append(
                jnp.dot(faded, v_ref[rows, columns], preferred_element_type=jnp.float32)
            )
        at = 0
        size = 1
        while size < spans:
            for first in range(0, spans, 2 * size):
                group = states[first]
                for span in range(first + 1, first + size):
                    group = group * wholes[span][head : head + 1] + states[span]
                local_ref[at, :, columns] = group.astype(jnp.bfloat16)
                at += 1
            size *= 2
        group = states[0]
        for span in range(1, spans):
            group = group * wholes[span][head : head + 1] + states[span]
        held[columns] = group.T
    half = held.shape[0] // 2
    core = bit_of(place(), 0)
    keep_ref[:half] = held[pl.ds(core * half, half)]
    send_ref[:half] = held[pl.ds((1 - core) * half, half)]
    keep_ref[half:] = run
    send_ref[half:] = run
    for copy in copies[2 + spans :]:
        copy.wait()


def make_states(queries, keys, values, log_decay, level_weight, gain):
    tokens, key_width = keys.shape
    heads = log_decay.shape[0]
    width = values.shape[1]
    spans = tokens // SPAN
    message = ((width // 2 + heads, key_width), jnp.float32)
    inputs = [queries, keys, values, log_decay, level_weight, gain]
    kept = [queries, keys, values, level_weight, gain]
    return call(
        state_kernel,
        "states",
        [pltpu.with_memory_space_constraint(array, pltpu.HBM) for array in inputs],
        [
            message,
            message,
            ((spans - 1, key_width, width), jnp.bfloat16),
            ((2, heads, tokens), jnp.float32),
            ((spans, heads, 128), jnp.float32),
            *[(array.shape, array.dtype) for array in kept],
        ],
        [
            pltpu.VMEM(log_decay.shape, jnp.float32),
            pltpu.VMEM((width, key_width), jnp.float32),
            pltpu.SemaphoreType.DMA((spans + 5,)),
        ],
        [pl.BlockSpec(memory_space=pltpu.HBM)] * len(inputs),
    )


def local_kernel(first, last, *refs):
    q_ref, k_ref, v_ref, sums_ref, totals_ref, weight_ref, local_ref = refs[:7]
    mixed_ref, done_ref = refs[-2:]
    heads = weight_ref.shape[1]
    head_width = v_ref.shape[1] // heads
    spans = totals_ref.shape[0]
    local_bits = spans.bit_length() - 1
    half = SPAN // 2
    done_ref[...] = jnp.zeros_like(done_ref)
    source = lax.broadcasted_iota(jnp.int32, (half, half), 0)
    target = lax.broadcasted_iota(jnp.int32, (half, half), 1)
    causal = source <= target
    empty = jnp.zeros((half, half), jnp.bfloat16)

    for span in range(first, last):
        tokens = slice(span * SPAN, (span + 1) * SPAN)
        queries = q_ref[tokens]
        scores = lax.dot_general(
            k_ref[tokens], queries, NT, preferred_element_type=jnp.float32
        )
        within = sums_ref[0, :, tokens]
        within_down = within.T
        weight = weight_ref[0, :, tokens]
        values_across = v_ref[tokens].T

        def mix(head, low, high):
            rows = slice(low * half, (low + 1) * half)
            columns = slice(high * half, (high + 1) * half)
            gap = within[head : head + 1, columns] - within_down[rows, head : head + 1]
            if low == high:
                gap = jnp.where(causal, gap, -1e30)
            mixing = scores[rows, columns] * jnp.exp(gap) * weight[head : head + 1, columns]
            return mixing.astype(jnp.bfloat16)

        levels = []
        offset = 0
        for bit in range(local_bits):
            if span >> bit & 1:
                since = within
                for back in range(1, span % 2**bit + 1):
                    since = since + spread_lanes(totals_ref[span - back][:, :1], SPAN)
                scale = jnp.exp(since) * weight_ref[1 + bit, :, tokens]
                levels.append((local_ref[offset + (span >> (bit + 1))].T, scale))
            offset += spans >> (bit + 1)
        for head in range(heads):
            rows = slice(head * head_width, (head + 1) * head_width)
            mixing = jnp.concatenate(
                [
                    jnp.concatenate([mix(head, 0, 0), mix(head, 0, 1)], axis=1),
                    jnp.concatenate([empty, mix(head, 1, 1)], axis=1),
                ],
                axis=0,
            )
            mixed = jnp.dot(values_across[rows], mixing, preferred_element_type=jnp.float32)
            for level, scale in levels:
                found = lax.dot_general(
                    level[rows], queries, NT, preferred_element_type=jnp.float32
                )
                mixed = mixed + found * scale[head : head + 1]
            mixed_ref[rows, tokens] = mixed


def mix_local(first, last, shared, mixed, tokens=()):
    queries, keys, values, sums, totals, level_weight, local = shared
    rest = [] if mixed is None else [mixed]
    return call(
        functools.partial(local_kernel, first, last),
        f"local{first}",
        [*shared, *rest, *tokens],
        [(values.shape[::-1], jnp.float32), ((8, 128), jnp.float32)],
        aliases={7: 0} if rest else None,
    )


def join(upper, mine, mine_total, other, other_total):
    fade = jnp.exp(jnp.where(upper, mine_total, other_total))
    return jnp.where(upper, other * fade + mine, mine * fade + other)


def first_head(far, heads):
    here = place()
    first = 0
    for bit, flip in enumerate(far):
        first = first + jnp.bitwise_xor(bit_of(here, bit), flip) * (heads >> (bit + 1))
    return first


def merge_kernel(bit, near, split, *refs):
    mine_ref, other_ref, prefix_ref = refs[:3]
    whole_ref = refs[-1]
    next_ref = refs[-2]
    heads = prefix_ref.shape[0]
    rows = mine_ref.shape[0] - heads
    count = heads >> near
    per = rows // count
    upper = bit_of(place(), bit) == 1
    first = first_head((0,) * near, heads)
    for slot in range(count):
        part = slice(slot * per, (slot + 1) * per)
        total = pl.ds(rows + first + slot, 1)
        whole_ref[part] = join(
            upper, mine_ref[part], mine_ref[total], other_ref[part], other_ref[total]
        )
    other_total = other_ref[rows:]
    total = mine_ref[rows:] + other_total
    next_ref[...] = prefix_ref[...] + jnp.where(upper, other_total, 0.0)
    if split:
        stay_ref, give_ref = refs[-4:-2]
        half = rows // 2
        side = bit_of(place(), bit + 1)
        stay_ref[:half] = whole_ref[pl.ds(side * half, half)]
        give_ref[:half] = whole_ref[pl.ds((1 - side) * half, half)]
        stay_ref[half:] = total
        give_ref[half:] = total
    else:
        merged_ref = refs[-3]
        merged_ref[:rows] = whole_ref[...]
        merged_ref[rows:] = total


def merge(bit, mine, other, prefix, tokens=()):
    heads, lanes = prefix.shape
    near = min(bit + 1, SPLIT_BITS)
    split = bit + 1 < SPLIT_BITS
    rows = mine.shape[0] - heads
    if split:
        messages = [((rows // 2 + heads, lanes), jnp.float32)] * 2
    else:
        messages = [(mine.shape, jnp.float32)]
    return call(
        functools.partial(merge_kernel, bit, near, split),
        f"merge{bit}",
        [mine, other, prefix, *tokens],
        [*messages, (prefix.shape, jnp.float32)],
        [pltpu.VMEM((rows, lanes), jnp.float32)],
    )


def pack_kernel(takes, *refs):
    out_ref = refs[-1]
    at = 0
    for ref, rows in zip(refs, takes):
        out_ref[at : at + rows] = ref[:rows]
        at += rows


def pack(name, pieces, tokens=()):
    takes = [rows for _, rows in pieces]
    lanes = pieces[0][0].shape[1]
    return call(
        functools.partial(pack_kernel, takes),
        name,
        [*[array for array, _ in pieces], *tokens],
        [((sum(takes), lanes), jnp.float32)],
    )[0]


def level_scale(bit, first_level, prefix_ref, sums_ref, weight_ref, tokens):
    active = jnp.where(bit_of(place(), bit) == 1, 1.0, 0.0)
    reach = jnp.exp(sums_ref[1, :, tokens] + spread_lanes(prefix_ref[:, :1], SPAN))
    return reach * weight_ref[first_level + bit, :, tokens] * active


def take_levels(plan, part_refs, levels, heads):
    per = levels.shape[1] // heads
    for slot, pieces in enumerate(plan):
        for index, row, far in pieces:
            rows = (heads >> len(far)) * per
            start = pl.multiple_of(first_head(far, heads) * per, 128)
            levels[slot, pl.ds(start, rows)] = part_refs[index][row : row + rows].astype(
                jnp.bfloat16
            )


def reach_kernel(plan, bits, first_level, *refs):
    mixed_ref, q_ref, sums_ref, weight_ref = refs[:4]
    prefix_refs = refs[4 : 4 + len(bits)]
    part_refs = refs[4 + len(bits) : -3]
    out_ref, done_ref, levels = refs[-3:]
    done_ref[...] = jnp.zeros_like(done_ref)
    heads = weight_ref.shape[1]
    head_width = mixed_ref.shape[0] // heads
    take_levels(plan, part_refs, levels, heads)
    for span in range(q_ref.shape[0] // SPAN):
        tokens = slice(span * SPAN, (span + 1) * SPAN)
        queries = q_ref[tokens]
        scales = [
            level_scale(bit, first_level, prefix_ref, sums_ref, weight_ref, tokens)
            for bit, prefix_ref in zip(bits, prefix_refs)
        ]
        for head in range(heads):
            rows = slice(head * head_width, (head + 1) * head_width)
            mixed = mixed_ref[rows, tokens]
            for slot, scale in enumerate(scales):
                found = lax.dot_general(
                    levels[slot, rows], queries, NT, preferred_element_type=jnp.float32
                )
                mixed = mixed + found * scale[head : head + 1]
            out_ref[rows, tokens] = mixed


def add_levels(mixed, queries, sums, level_weight, levels, parts, first_level, tokens=()):
    width = mixed.shape[0]
    bits = [bit for bit, _, _ in levels]
    plan = [pieces for _, _, pieces in levels]
    prefixes = [prefix for _, prefix, _ in levels]
    return call(
        functools.partial(reach_kernel, plan, bits, first_level),
        f"reach{bits[0]}",
        [mixed, queries, sums, level_weight, *prefixes, *parts, *tokens],
        [(mixed.shape, jnp.float32), ((8, 128), jnp.float32)],
        [pltpu.VMEM((len(bits), width, queries.shape[1]), jnp.bfloat16)],
        aliases={0: 0},
    )


def finish_kernel(far, bit, first_level, *refs):
    mixed_ref, q_ref, sums_ref, weight_ref, gain_ref, prefix_ref, state_ref = refs[:7]
    out_hbm, out_ref, level, scale_ref, sent = refs[-5:]
    heads = weight_ref.shape[1]
    head_width = mixed_ref.shape[0] // heads
    count = heads >> len(far)
    first = first_head(far, heads)
    level[...] = state_ref[: level.shape[0]].astype(jnp.bfloat16)
    gains = []
    for slot in range(count):
        row = jnp.broadcast_to(gain_ref[pl.ds(first + slot, 1)], (8, head_width))
        gains.append(row.T[:, :1])
    columns = pl.ds(pl.multiple_of(first * head_width, 128), count * head_width)
    copies = []
    for span in range(q_ref.shape[0] // SPAN):
        tokens = slice(span * SPAN, (span + 1) * SPAN)
        queries = q_ref[tokens]
        scale_ref[...] = level_scale(bit, first_level, prefix_ref, sums_ref, weight_ref, tokens)
        for slot in range(count):
            rows = slice(slot * head_width, (slot + 1) * head_width)
            found = lax.dot_general(level[rows], queries, NT, preferred_element_type=jnp.float32)
            start = pl.multiple_of((first + slot) * head_width, 128)
            mixed = mixed_ref[pl.ds(start, head_width), tokens]
            mixed = mixed + found * scale_ref[pl.ds(first + slot, 1)]
            square = jnp.mean(mixed * mixed, axis=0, keepdims=True)
            normed = mixed * lax.rsqrt(square + EPS) * gains[slot]
            out_ref[tokens, rows] = normed.astype(jnp.bfloat16).T
        copy = pltpu.make_async_copy(
            out_ref.at[tokens], out_hbm.at[tokens, columns], sent.at[span]
        )
        copy.start()
        copies.append(copy)
    for copy in copies:
        copy.wait()


def finish(far, bit, first_level, mixed, queries, sums, level_weight, gain, prefix, state, begun):
    width, tokens = mixed.shape
    heads = level_weight.shape[1]
    inputs = [mixed, queries, sums, level_weight, gain, prefix, state]
    specs = [HELD] * len(inputs)
    inputs = [hold(array) for array in inputs]
    out = pl.BlockSpec(memory_space=pltpu.HBM)
    if begun is not None:
        specs.append(out)
        inputs.append(begun)
    return pl.pallas_call(
        functools.partial(finish_kernel, far, bit, first_level),
        in_specs=specs,
        out_specs=out,
        out_shape=jax.ShapeDtypeStruct((tokens, width), jnp.bfloat16),
        scratch_shapes=[
            pltpu.VMEM((tokens, width >> len(far)), jnp.bfloat16),
            pltpu.VMEM((width >> len(far), queries.shape[1]), jnp.bfloat16),
            pltpu.VMEM((heads, SPAN), jnp.float32),
            pltpu.SemaphoreType.DMA((tokens // SPAN,)),
        ],
        input_output_aliases={} if begun is None else {7: 0},
        compiler_params=PARAMS,
        name=f"finish{far[0]}{far[1]}",
    )(*inputs)


def trade(value, mask):
    wide, narrow = lax.axis_size("wide"), lax.axis_size("narrow")

    def ranked(index):
        return index % narrow * wide + index // narrow

    pairs = [(ranked(source), ranked(source ^ mask)) for source in range(wide * narrow)]
    return lax.ppermute(value, AXES, pairs)


def per_device(queries, keys, values, log_decay, level_weight, norm_gain):
    heads = log_decay.shape[0]
    tokens, width = values.shape
    per = width // heads
    spans = tokens // SPAN
    group_bits = heads.bit_length() - 1
    bits = (lax.axis_size("wide") * lax.axis_size("narrow")).bit_length() - 1
    first_level = level_weight.shape[0] - bits
    gain = norm_gain.reshape(heads, per)
    mine, give, local, sums, totals, queries, keys, values, level_weight, gain = make_states(
        queries, keys, values, log_decay, level_weight, gain
    )
    shared = (queries, keys, values, sums, totals, level_weight, local)

    last = bits - 1
    two = 2 * per
    sides = [(core, side) for core in (0, 1) for side in (0, 1)]
    prefix = jnp.zeros((heads, 128), jnp.float32)
    prefixes, found, rests, across = [], [], [], {}
    mixed, at, waits = None, 0, ()
    for bit in range(bits):
        prefixes.append(prefix)
        found.append(trade(give if bit < SPLIT_BITS else mine, 2**bit))
        if bit < SPLIT_BITS:
            rests.append(trade(mine, 2**bit))
        if 0 < bit and at < spans:
            stop = spans if bit == last else at + 1
            mixed, token = mix_local(at, stop, shared, mixed, (mine,))
            at, waits = stop, (token,)
        if 1 < bit < 2 + SPLIT_BITS:
            waits = (*waits, rests[bit - 2])
        if bit < last:
            *messages, prefix = merge(bit, mine, found[bit], prefix, waits)
            mine, give = messages if len(messages) == 2 else (messages[0], None)
        if 1 < bit < last:
            found[bit] = pack(f"found{bit}", [(found[bit], two)], (mine,))
            across[bit] = trade(found[bit], 2)

    rest = (queries, sums, level_weight)
    near = pack("near1", [(found[1], two), (rests[1], two)])
    far = trade(near, 1)
    levels = [(0, prefixes[0], [(0, 0, (0,)), (1, 0, (1,))])]
    levels.append((1, prefixes[1], [(2 + core, side * two, (core, side)) for core, side in sides]))
    parts = [found[0], rests[0], near, far]
    mixed, token = add_levels(mixed, *rest, levels, parts, first_level)
    state = pack("state", [(found[last], two)], (token,))

    pieces = []
    for bit in range(2, last - 1):
        pieces += [(found[bit], two), (across[bit], two)]
    near = pack("near2", [*pieces, (found[last - 1], two)], (mine,))
    far = trade(near, 1)
    near_side, far_side = across[last - 1], trade(across[last - 1], 1)
    levels = []
    for slot, bit in enumerate(range(2, last)):
        taken = [
            (core if bit < last - 1 or side == 0 else 2 + core, (2 * slot + side) * two, (core, side))
            for core, side in sides
        ]
        if bit == last - 1:
            taken = [(at, row if at < 2 else 0, far_bits) for at, row, far_bits in taken]
        levels.append((bit, prefixes[bit], taken))
    parts = [near, far, near_side, far_side]
    mixed, token = add_levels(mixed, *rest, levels, parts, first_level, (state,))

    rest = (last, first_level, mixed, *rest, gain, prefixes[last])
    beside = pack("beside", [(trade(state, 2), two)], (token,))
    out = finish((0, 0), *rest, state, None)
    out = finish((1, 0), *rest, trade(state, 1), out)
    out = finish((0, 1), *rest, beside, out)
    return finish((1, 1), *rest, trade(beside, 1), out)


def solution(mesh):
    placed = (
        P(("wide", "narrow"), None),
        P(("wide", "narrow"), None),
        P(("wide", "narrow"), None),
        P(None, ("wide", "narrow")),
        P(None, None, ("wide", "narrow")),
        P(),
    )
    return jax.shard_map(
        per_device,
        mesh=mesh,
        in_specs=placed,
        out_specs=P(("wide", "narrow"), None),
        check_vma=False,
    )
```

```python
import functools

import jax
import jax.numpy as jnp
from jax import lax
from jax.experimental import pallas as pl
from jax.experimental.pallas import tpu as pltpu
from jax.sharding import PartitionSpec as P

SPAN = 256
SPLIT_BITS = 2
EPS = 1e-05
AXES = ("narrow", "wide")
NT = (((1,), (1,)), ((), ()))
PARAMS = pltpu.CompilerParams(vmem_limit_bytes=32 * 1024 * 1024)
HELD = pl.BlockSpec(memory_space=pltpu.VMEM)


def place():
    return lax.axis_index("wide") * lax.axis_size("narrow") + lax.axis_index("narrow")


def bit_of(value, bit):
    return jnp.bitwise_and(jnp.right_shift(value, bit), 1)


def spread_lanes(column, width):
    return jnp.broadcast_to(column, (column.shape[0], width))


ANYWHERE = pl.BlockSpec(memory_space=pl.ANY)


def hold(array):
    return pltpu.with_memory_space_constraint(array, pltpu.VMEM)


def call(kernel, name, inputs, outputs, scratch=(), in_specs=None, aliases=None):
    specs = in_specs or [HELD] * len(inputs)
    inputs = [hold(array) if spec is HELD else array for array, spec in zip(inputs, specs)]
    return pl.pallas_call(
        kernel,
        in_specs=specs,
        out_specs=[HELD] * len(outputs),
        out_shape=[pltpu.VMEM(shape, dtype) for shape, dtype in outputs],
        scratch_shapes=list(scratch),
        input_output_aliases=aliases or {},
        compiler_params=PARAMS,
        name=name,
    )(*inputs)


def running_sums(rows):
    high = rows.astype(jnp.bfloat16)
    rest = rows - high.astype(jnp.float32)
    middle = rest.astype(jnp.bfloat16)
    low = (rest - middle.astype(jnp.float32)).astype(jnp.bfloat16)
    width = rows.shape[1]
    source = lax.broadcasted_iota(jnp.int32, (width, width), 0)
    target = lax.broadcasted_iota(jnp.int32, (width, width), 1)
    upto = jnp.where(source <= target, 1.0, 0.0).astype(jnp.bfloat16)
    sums = jnp.dot(
        jnp.concatenate([high, middle, low], axis=0), upto, preferred_element_type=jnp.float32
    )
    count = rows.shape[0]
    return sums[:count] + (sums[count : 2 * count] + sums[2 * count :])


def state_kernel(*refs):
    q_hbm, k_hbm, v_hbm, decay_hbm, weight_hbm, gain_hbm = refs[:6]
    keep_ref, send_ref, local_ref, sums_ref, totals_ref = refs[6:11]
    q_ref, k_ref, v_ref, weight_ref, gain_ref, decay_ref, held, arrived = refs[11:]
    heads, tokens = decay_ref.shape
    head_width = v_ref.shape[1] // heads
    spans = tokens // SPAN
    rows_of = [slice(span * SPAN, (span + 1) * SPAN) for span in range(spans)]
    loads = [(decay_hbm, decay_ref), (k_hbm, k_ref)]
    loads += [(v_hbm.at[rows], v_ref.at[rows]) for rows in rows_of]
    loads += [(q_hbm, q_ref), (weight_hbm, weight_ref), (gain_hbm, gain_ref)]
    copies = [
        pltpu.make_async_copy(source, target, arrived.at[at])
        for at, (source, target) in enumerate(loads)
    ]
    for copy in copies:
        copy.start()
    copies[0].wait()
    within = running_sums(jnp.concatenate([decay_ref[:, rows] for rows in rows_of], axis=0))
    run = jnp.zeros((heads, 128), jnp.float32)
    fades, wholes = [], []
    for span, rows in enumerate(rows_of):
        here = within[span * heads : (span + 1) * heads]
        last = here[:, SPAN - 1 :]
        total = spread_lanes(last, 128)
        sums_ref[0, :, rows] = here
        sums_ref[1, :, rows] = here + spread_lanes(run[:, :1], SPAN)
        totals_ref[span] = total
        run = run + total
        fades.append(jnp.exp(spread_lanes(last, SPAN) - here))
        wholes.append(jnp.exp(total))
    copies[1].wait()
    across = [k_ref[rows].astype(jnp.float32).T for rows in rows_of]
    for copy in copies[2 : 2 + spans]:
        copy.wait()
    for head in range(heads):
        columns = slice(head * head_width, (head + 1) * head_width)
        states = []
        for span, rows in enumerate(rows_of):
            faded = (across[span] * fades[span][head : head + 1]).astype(jnp.bfloat16)
            states.append(
                jnp.dot(faded, v_ref[rows, columns], preferred_element_type=jnp.float32)
            )
        at = 0
        size = 1
        while size < spans:
            for first in range(0, spans, 2 * size):
                group = states[first]
                for span in range(first + 1, first + size):
                    group = group * wholes[span][head : head + 1] + states[span]
                local_ref[at, :, columns] = group.astype(jnp.bfloat16)
                at += 1
            size *= 2
        group = states[0]
        for span in range(1, spans):
            group = group * wholes[span][head : head + 1] + states[span]
        held[columns] = group.T
    half = held.shape[0] // 2
    core = bit_of(place(), 0)
    keep_ref[:half] = held[pl.ds(core * half, half)]
    send_ref[:half] = held[pl.ds((1 - core) * half, half)]
    keep_ref[half:] = run
    send_ref[half:] = run
    for copy in copies[2 + spans :]:
        copy.wait()


def make_states(queries, keys, values, log_decay, level_weight, gain):
    tokens, key_width = keys.shape
    heads = log_decay.shape[0]
    width = values.shape[1]
    spans = tokens // SPAN
    message = ((width // 2 + heads, key_width), jnp.float32)
    inputs = [queries, keys, values, log_decay, level_weight, gain]
    kept = [queries, keys, values, level_weight, gain]
    return call(
        state_kernel,
        "states",
        [pltpu.with_memory_space_constraint(array, pltpu.HBM) for array in inputs],
        [
            message,
            message,
            ((spans - 1, key_width, width), jnp.bfloat16),
            ((2, heads, tokens), jnp.float32),
            ((spans, heads, 128), jnp.float32),
            *[(array.shape, array.dtype) for array in kept],
        ],
        [
            pltpu.VMEM(log_decay.shape, jnp.float32),
            pltpu.VMEM((width, key_width), jnp.float32),
            pltpu.SemaphoreType.DMA((spans + 5,)),
        ],
        [pl.BlockSpec(memory_space=pltpu.HBM)] * len(inputs),
    )


def local_kernel(first, last, *refs):
    q_ref, k_ref, v_ref, sums_ref, totals_ref, weight_ref, local_ref = refs[:7]
    mixed_ref, done_ref = refs[-2:]
    heads = weight_ref.shape[1]
    head_width = v_ref.shape[1] // heads
    spans = totals_ref.shape[0]
    local_bits = spans.bit_length() - 1
    half = SPAN // 2
    done_ref[...] = jnp.zeros_like(done_ref)
    source = lax.broadcasted_iota(jnp.int32, (half, half), 0)
    target = lax.broadcasted_iota(jnp.int32, (half, half), 1)
    causal = source <= target
    empty = jnp.zeros((half, half), jnp.bfloat16)

    for span in range(first, last):
        tokens = slice(span * SPAN, (span + 1) * SPAN)
        queries = q_ref[tokens]
        scores = lax.dot_general(
            k_ref[tokens], queries, NT, preferred_element_type=jnp.float32
        )
        within = sums_ref[0, :, tokens]
        within_down = within.T
        weight = weight_ref[0, :, tokens]
        values_across = v_ref[tokens].T

        def mix(head, low, high):
            rows = slice(low * half, (low + 1) * half)
            columns = slice(high * half, (high + 1) * half)
            gap = within[head : head + 1, columns] - within_down[rows, head : head + 1]
            if low == high:
                gap = jnp.where(causal, gap, -1e30)
            mixing = scores[rows, columns] * jnp.exp(gap) * weight[head : head + 1, columns]
            return mixing.astype(jnp.bfloat16)

        levels = []
        offset = 0
        for bit in range(local_bits):
            if span >> bit & 1:
                since = within
                for back in range(1, span % 2**bit + 1):
                    since = since + spread_lanes(totals_ref[span - back][:, :1], SPAN)
                scale = jnp.exp(since) * weight_ref[1 + bit, :, tokens]
                levels.append((local_ref[offset + (span >> (bit + 1))].T, scale))
            offset += spans >> (bit + 1)
        for head in range(heads):
            rows = slice(head * head_width, (head + 1) * head_width)
            mixing = jnp.concatenate(
                [
                    jnp.concatenate([mix(head, 0, 0), mix(head, 0, 1)], axis=1),
                    jnp.concatenate([empty, mix(head, 1, 1)], axis=1),
                ],
                axis=0,
            )
            mixed = jnp.dot(values_across[rows], mixing, preferred_element_type=jnp.float32)
            for level, scale in levels:
                found = lax.dot_general(
                    level[rows], queries, NT, preferred_element_type=jnp.float32
                )
                mixed = mixed + found * scale[head : head + 1]
            mixed_ref[rows, tokens] = mixed


def mix_local(first, last, shared, mixed, tokens=()):
    queries, keys, values, sums, totals, level_weight, local = shared
    rest = [] if mixed is None else [mixed]
    return call(
        functools.partial(local_kernel, first, last),
        f"local{first}",
        [*shared, *rest, *tokens],
        [(values.shape[::-1], jnp.float32), ((8, 128), jnp.float32)],
        aliases={7: 0} if rest else None,
    )


def join(upper, mine, mine_total, other, other_total):
    fade = jnp.exp(jnp.where(upper, mine_total, other_total))
    return jnp.where(upper, other * fade + mine, mine * fade + other)


def first_head(far, heads):
    here = place()
    first = 0
    for bit, flip in enumerate(far):
        first = first + jnp.bitwise_xor(bit_of(here, bit), flip) * (heads >> (bit + 1))
    return first


def merge_kernel(bit, offset, mode, *refs):
    mine_ref, other_ref, prefix_ref = refs[:3]
    whole_ref = refs[-1]
    next_ref = refs[-2]
    heads = prefix_ref.shape[0]
    near = min(bit + 1, SPLIT_BITS)
    rows = mine_ref.shape[0] - heads
    per = mine_ref.shape[1]
    upper = bit_of(place(), bit) == 1
    first = first_head((0,) * near, heads) + offset
    for slot in range(rows // per):
        part = slice(slot * per, (slot + 1) * per)
        total = pl.ds(rows + first + slot, 1)
        whole_ref[part] = join(
            upper, mine_ref[part], mine_ref[total], other_ref[part], other_ref[total]
        )
    other_total = other_ref[rows:]
    total = mine_ref[rows:] + other_total
    next_ref[...] = prefix_ref[...] + jnp.where(upper, other_total, 0.0)
    if mode == "whole":
        merged_ref = refs[-3]
        merged_ref[:rows] = whole_ref[...]
        merged_ref[rows:] = total
    else:
        first_ref, second_ref = refs[-4:-2]
        half = rows // 2
        side = bit_of(place(), bit + 1) if mode == "side" else 0
        first_ref[:half] = whole_ref[pl.ds(side * half, half)]
        second_ref[:half] = whole_ref[pl.ds((1 - side) * half, half)]
        first_ref[half:] = total
        second_ref[half:] = total


def merge(bit, mine, other, prefix, mode, offset, tokens=()):
    heads, lanes = prefix.shape
    rows = mine.shape[0] - heads
    if mode == "whole":
        messages = [(mine.shape, jnp.float32)]
    else:
        messages = [((rows // 2 + heads, lanes), jnp.float32)] * 2
    *messages, prefix = call(
        functools.partial(merge_kernel, bit, offset, mode),
        f"merge{bit}{offset}",
        [mine, other, prefix, *tokens],
        [*messages, (prefix.shape, jnp.float32)],
        [pltpu.VMEM((rows, lanes), jnp.float32)],
    )
    return messages, prefix


def pack_kernel(takes, *refs):
    out_ref = refs[-1]
    at = 0
    for ref, rows in zip(refs, takes):
        out_ref[at : at + rows] = ref[:rows]
        at += rows


def pack(name, pieces, tokens=()):
    takes = [rows for _, rows in pieces]
    lanes = pieces[0][0].shape[1]
    return call(
        functools.partial(pack_kernel, takes),
        name,
        [*[array for array, _ in pieces], *tokens],
        [((sum(takes), lanes), jnp.float32)],
    )[0]


def level_scale(bit, first_level, prefix_ref, sums_ref, weight_ref, tokens):
    active = jnp.where(bit_of(place(), bit) == 1, 1.0, 0.0)
    reach = jnp.exp(sums_ref[1, :, tokens] + spread_lanes(prefix_ref[:, :1], SPAN))
    return reach * weight_ref[first_level + bit, :, tokens] * active


def take_levels(plan, part_refs, levels, heads):
    per = levels.shape[1] // heads
    for slot, pieces in enumerate(plan):
        for index, row, far in pieces:
            rows = (heads >> len(far)) * per
            start = pl.multiple_of(first_head(far, heads) * per, 128)
            levels[slot, pl.ds(start, rows)] = part_refs[index][row : row + rows].astype(
                jnp.bfloat16
            )


def reach_kernel(plan, bits, first_level, *refs):
    mixed_ref, q_ref, sums_ref, weight_ref = refs[:4]
    prefix_refs = refs[4 : 4 + len(bits)]
    part_refs = refs[4 + len(bits) : -3]
    out_ref, done_ref, levels = refs[-3:]
    done_ref[...] = jnp.zeros_like(done_ref)
    heads = weight_ref.shape[1]
    head_width = mixed_ref.shape[0] // heads
    take_levels(plan, part_refs, levels, heads)
    parts = [slice(head * head_width, (head + 1) * head_width) for head in range(heads)]
    states = [[levels[slot, rows] for slot in range(len(bits))] for rows in parts]
    for span in range(q_ref.shape[0] // SPAN):
        tokens = slice(span * SPAN, (span + 1) * SPAN)
        queries = q_ref[tokens]
        scales = [
            level_scale(bit, first_level, prefix_ref, sums_ref, weight_ref, tokens)
            for bit, prefix_ref in zip(bits, prefix_refs)
        ]
        mixed = [mixed_ref[rows, tokens] for rows in parts]
        for head in range(heads):
            for state, scale in zip(states[head], scales):
                found = lax.dot_general(state, queries, NT, preferred_element_type=jnp.float32)
                mixed[head] = mixed[head] + found * scale[head : head + 1]
        for head, rows in enumerate(parts):
            out_ref[rows, tokens] = mixed[head]


def add_levels(mixed, queries, sums, level_weight, levels, parts, first_level, tokens=()):
    width = mixed.shape[0]
    bits = [bit for bit, _, _ in levels]
    plan = [pieces for _, _, pieces in levels]
    prefixes = [prefix for _, prefix, _ in levels]
    return call(
        functools.partial(reach_kernel, plan, bits, first_level),
        f"reach{bits[0]}",
        [mixed, queries, sums, level_weight, *prefixes, *parts, *tokens],
        [(mixed.shape, jnp.float32), ((8, 128), jnp.float32)],
        [pltpu.VMEM((len(bits), width, queries.shape[1]), jnp.bfloat16)],
        aliases={0: 0},
    )


def finish_kernel(far, bit, first_level, *refs):
    mixed_ref, q_ref, sums_ref, weight_ref, gain_ref, prefix_ref, state_ref = refs[:7]
    out_hbm, done_ref, out_ref, level, sent = refs[-5:]
    done_ref[...] = jnp.zeros_like(done_ref)
    heads = weight_ref.shape[1]
    head_width = mixed_ref.shape[0] // heads
    count = heads >> len(far)
    first = first_head(far, heads)
    level[...] = state_ref[: level.shape[0]].astype(jnp.bfloat16)
    gains = []
    for slot in range(count):
        row = jnp.broadcast_to(gain_ref[pl.ds(first + slot, 1)], (8, head_width))
        gains.append(row.T[:, :1])
    columns = pl.ds(pl.multiple_of(first * head_width, 128), count * head_width)
    spans = q_ref.shape[0] // SPAN
    states = [level[slot * head_width : (slot + 1) * head_width] for slot in range(count)]
    copies = []
    for begin in range(0, spans, 2):
        batch = [slice(span * SPAN, (span + 1) * SPAN) for span in range(begin, min(begin + 2, spans))]
        results = []
        for tokens in batch:
            queries = q_ref[tokens]
            active = jnp.where(bit_of(place(), bit) == 1, 1.0, 0.0)
            for slot in range(count):
                row = pl.ds(first + slot, 1)
                reach = jnp.exp(sums_ref[1, row, tokens] + prefix_ref[row][:, :1])
                scale = reach * weight_ref[first_level + bit, row, tokens] * active
                found = lax.dot_general(
                    states[slot], queries, NT, preferred_element_type=jnp.float32
                )
                start = pl.multiple_of((first + slot) * head_width, 128)
                mixed = mixed_ref[pl.ds(start, head_width), tokens] + found * scale
                square = jnp.mean(mixed * mixed, axis=0, keepdims=True)
                normed = mixed * lax.rsqrt(square + EPS) * gains[slot]
                rows = slice(slot * head_width, (slot + 1) * head_width)
                results.append((tokens, rows, normed.astype(jnp.bfloat16).T))
        for tokens, rows, result in results:
            out_ref[tokens, rows] = result
        for tokens in batch:
            copy = pltpu.make_async_copy(
                out_ref.at[tokens], out_hbm.at[tokens, columns], sent.at[len(copies)]
            )
            copy.start()
            copies.append(copy)
    for copy in copies:
        copy.wait()


def finish(far, bit, first_level, mixed, queries, sums, level_weight, gain, prefix, state, begun):
    width, tokens = mixed.shape
    inputs = [mixed, queries, sums, level_weight, gain, prefix, state]
    specs = [HELD] * len(inputs)
    inputs = [hold(array) for array in inputs]
    out = pl.BlockSpec(memory_space=pltpu.HBM)
    if begun is not None:
        specs.append(out)
        inputs.append(begun)
    return pl.pallas_call(
        functools.partial(finish_kernel, far, bit, first_level),
        in_specs=specs,
        out_specs=[out, HELD],
        out_shape=[
            jax.ShapeDtypeStruct((tokens, width), jnp.bfloat16),
            pltpu.VMEM((8, 128), jnp.float32),
        ],
        scratch_shapes=[
            pltpu.VMEM((tokens, width >> len(far)), jnp.bfloat16),
            pltpu.VMEM((width >> len(far), queries.shape[1]), jnp.bfloat16),
            pltpu.SemaphoreType.DMA((tokens // SPAN,)),
        ],
        input_output_aliases={} if begun is None else {7: 0},
        compiler_params=PARAMS,
        name=f"finish{far[0]}{far[1]}",
    )(*inputs)


def trade(value, mask):
    wide, narrow = lax.axis_size("wide"), lax.axis_size("narrow")

    def ranked(index):
        return index % narrow * wide + index // narrow

    pairs = [(ranked(source), ranked(source ^ mask)) for source in range(wide * narrow)]
    return lax.ppermute(value, AXES, pairs)


def per_device(queries, keys, values, log_decay, level_weight, norm_gain):
    heads = log_decay.shape[0]
    tokens, width = values.shape
    per = width // heads
    spans = tokens // SPAN
    group_bits = heads.bit_length() - 1
    bits = (lax.axis_size("wide") * lax.axis_size("narrow")).bit_length() - 1
    first_level = level_weight.shape[0] - bits
    gain = norm_gain.reshape(heads, per)
    mine, give, local, sums, totals, queries, keys, values, level_weight, gain = make_states(
        queries, keys, values, log_decay, level_weight, gain
    )
    shared = (queries, keys, values, sums, totals, level_weight, local)

    last = bits - 1
    two = 2 * per
    sides = [(core, side) for core in (0, 1) for side in (0, 1)]
    prefix = jnp.zeros((heads, 128), jnp.float32)
    prefixes, found, rests, across = [], [], [], {}
    mixed, at, waits = None, 0, ()
    chunks = [mine]
    for bit in range(bits):
        prefixes.append(prefix)
        sent = [give] if bit < SPLIT_BITS else chunks
        found.append([trade(chunk, 2**bit) for chunk in sent])
        if bit < SPLIT_BITS:
            rests.append(trade(chunks[0], 2**bit))
        if 0 < bit and at < spans:
            stop = spans if bit == last else at + 1
            mixed, token = mix_local(at, stop, shared, mixed, (chunks[0],))
            at, waits = stop, (token,)
        if 1 < bit < 2 + SPLIT_BITS:
            waits = (*waits, rests[bit - 2])
        if bit < last:
            mode = "side" if bit + 1 < SPLIT_BITS else "whole"
            merged = [
                merge(bit, chunk, other, prefix, mode, offset, waits)
                for offset, (chunk, other) in enumerate(zip(chunks, found[bit]))
            ]
            prefix = merged[0][1]
            chunks = [message for messages, _ in merged for message in messages]
            if mode == "side":
                chunks, give = chunks[:1], chunks[1]
        if 1 < bit < last:
            pieces = [(state, two // len(found[bit])) for state in found[bit]]
            found[bit] = [pack(f"found{bit}", pieces, (chunks[0],))]
            across[bit] = trade(found[bit][0], 2)
    ends = found[last]
    found = [states[0] for states in found]

    rest = (queries, sums, level_weight)
    near = pack("near1", [(found[1], two), (rests[1], two)])
    far = trade(near, 1)
    levels = [(0, prefixes[0], [(0, 0, (0,)), (1, 0, (1,))])]
    levels.append((1, prefixes[1], [(2 + core, side * two, (core, side)) for core, side in sides]))
    parts = [found[0], rests[0], near, far]
    mixed, token = add_levels(mixed, *rest, levels, parts, first_level)
    state = pack("state", [(ends[0], two)], (token,))

    pieces = []
    for bit in range(2, last - 1):
        pieces += [(found[bit], two), (across[bit], two)]
    near = pack("near2", [*pieces, (found[last - 1], two)], (chunks[0],))
    far = trade(near, 1)
    near_side, far_side = across[last - 1], trade(across[last - 1], 1)
    levels = []
    for slot, bit in enumerate(range(2, last)):
        taken = [
            (core if bit < last - 1 or side == 0 else 2 + core, (2 * slot + side) * two, (core, side))
            for core, side in sides
        ]
        if bit == last - 1:
            taken = [(at, row if at < 2 else 0, far_bits) for at, row, far_bits in taken]
        levels.append((bit, prefixes[bit], taken))
    parts = [near, far, near_side, far_side]
    mixed, token = add_levels(mixed, *rest, levels, parts, first_level, (state,))

    rest = (last, first_level, mixed, *rest, gain, prefixes[last])
    beside = [(trade(state, 2), two)]
    out, _ = finish((0, 0), *rest, state, None)
    out, token = finish((1, 0), *rest, trade(state, 1), out)
    beside = pack("beside", beside, (token,))
    out, _ = finish((0, 1), *rest, beside, out)
    return finish((1, 1), *rest, trade(beside, 1), out)[0]


def solution(mesh):
    placed = (
        P(("wide", "narrow"), None),
        P(("wide", "narrow"), None),
        P(("wide", "narrow"), None),
        P(None, ("wide", "narrow")),
        P(None, None, ("wide", "narrow")),
        P(),
    )
    return jax.shard_map(
        per_device,
        mesh=mesh,
        in_specs=placed,
        out_specs=P(("wide", "narrow"), None),
        check_vma=False,
    )
```

```python
import functools

import jax
import jax.numpy as jnp
from jax import lax
from jax.experimental import pallas as pl
from jax.experimental.pallas import tpu as pltpu
from jax.sharding import PartitionSpec as P

SPAN = 256
SPLIT_BITS = 2
EPS = 1e-05
AXES = ("narrow", "wide")
NT = (((1,), (1,)), ((), ()))
PARAMS = pltpu.CompilerParams(vmem_limit_bytes=32 * 1024 * 1024)
HELD = pl.BlockSpec(memory_space=pltpu.VMEM)


def place():
    return lax.axis_index("wide") * lax.axis_size("narrow") + lax.axis_index("narrow")


def bit_of(value, bit):
    return jnp.bitwise_and(jnp.right_shift(value, bit), 1)


def spread_lanes(column, width):
    return jnp.broadcast_to(column, (column.shape[0], width))


ANYWHERE = pl.BlockSpec(memory_space=pl.ANY)


def hold(array):
    return pltpu.with_memory_space_constraint(array, pltpu.VMEM)


def call(kernel, name, inputs, outputs, scratch=(), in_specs=None, aliases=None):
    specs = in_specs or [HELD] * len(inputs)
    inputs = [hold(array) if spec is HELD else array for array, spec in zip(inputs, specs)]
    return pl.pallas_call(
        kernel,
        in_specs=specs,
        out_specs=[HELD] * len(outputs),
        out_shape=[pltpu.VMEM(shape, dtype) for shape, dtype in outputs],
        scratch_shapes=list(scratch),
        input_output_aliases=aliases or {},
        compiler_params=PARAMS,
        name=name,
    )(*inputs)


def running_sums(rows):
    high = rows.astype(jnp.bfloat16)
    rest = rows - high.astype(jnp.float32)
    middle = rest.astype(jnp.bfloat16)
    low = (rest - middle.astype(jnp.float32)).astype(jnp.bfloat16)
    width = rows.shape[1]
    source = lax.broadcasted_iota(jnp.int32, (width, width), 0)
    target = lax.broadcasted_iota(jnp.int32, (width, width), 1)
    upto = jnp.where(source <= target, 1.0, 0.0).astype(jnp.bfloat16)
    sums = jnp.dot(
        jnp.concatenate([high, middle, low], axis=0), upto, preferred_element_type=jnp.float32
    )
    count = rows.shape[0]
    return sums[:count] + (sums[count : 2 * count] + sums[2 * count :])


def state_kernel(*refs):
    q_hbm, k_hbm, v_hbm, decay_hbm, weight_hbm, gain_hbm = refs[:6]
    keep_ref, send_ref, local_ref, sums_ref, totals_ref = refs[6:11]
    q_ref, k_ref, v_ref, weight_ref, gain_ref, decay_ref, held, arrived = refs[11:]
    heads, tokens = decay_ref.shape
    head_width = v_ref.shape[1] // heads
    spans = tokens // SPAN
    rows_of = [slice(span * SPAN, (span + 1) * SPAN) for span in range(spans)]
    loads = [(decay_hbm, decay_ref), (k_hbm, k_ref)]
    loads += [(v_hbm.at[rows], v_ref.at[rows]) for rows in rows_of]
    loads += [(q_hbm, q_ref), (weight_hbm, weight_ref), (gain_hbm, gain_ref)]
    copies = [
        pltpu.make_async_copy(source, target, arrived.at[at])
        for at, (source, target) in enumerate(loads)
    ]
    for copy in copies:
        copy.start()
    copies[0].wait()
    within = running_sums(jnp.concatenate([decay_ref[:, rows] for rows in rows_of], axis=0))
    run = jnp.zeros((heads, 128), jnp.float32)
    fades, wholes = [], []
    for span, rows in enumerate(rows_of):
        here = within[span * heads : (span + 1) * heads]
        last = here[:, SPAN - 1 :]
        total = spread_lanes(last, 128)
        sums_ref[0, :, rows] = here
        sums_ref[1, :, rows] = here + spread_lanes(run[:, :1], SPAN)
        totals_ref[span] = total
        run = run + total
        fades.append(jnp.exp(spread_lanes(last, SPAN) - here))
        wholes.append(jnp.exp(total))
    copies[1].wait()
    across = [k_ref[rows].astype(jnp.float32).T for rows in rows_of]
    for copy in copies[2 : 2 + spans]:
        copy.wait()
    for head in range(heads):
        columns = slice(head * head_width, (head + 1) * head_width)
        states = []
        for span, rows in enumerate(rows_of):
            faded = (across[span] * fades[span][head : head + 1]).astype(jnp.bfloat16)
            states.append(
                jnp.dot(faded, v_ref[rows, columns], preferred_element_type=jnp.float32)
            )
        at = 0
        size = 1
        while size < spans:
            for first in range(0, spans, 2 * size):
                group = states[first]
                for span in range(first + 1, first + size):
                    group = group * wholes[span][head : head + 1] + states[span]
                local_ref[at, :, columns] = group.astype(jnp.bfloat16)
                at += 1
            size *= 2
        group = states[0]
        for span in range(1, spans):
            group = group * wholes[span][head : head + 1] + states[span]
        held[columns] = group.T
    half = held.shape[0] // 2
    core = bit_of(place(), 0)
    keep_ref[:half] = held[pl.ds(core * half, half)]
    send_ref[:half] = held[pl.ds((1 - core) * half, half)]
    keep_ref[half:] = run
    send_ref[half:] = run
    for copy in copies[2 + spans :]:
        copy.wait()


def make_states(queries, keys, values, log_decay, level_weight, gain):
    tokens, key_width = keys.shape
    heads = log_decay.shape[0]
    width = values.shape[1]
    spans = tokens // SPAN
    message = ((width // 2 + heads, key_width), jnp.float32)
    inputs = [queries, keys, values, log_decay, level_weight, gain]
    kept = [queries, keys, values, level_weight, gain]
    return call(
        state_kernel,
        "states",
        [pltpu.with_memory_space_constraint(array, pltpu.HBM) for array in inputs],
        [
            message,
            message,
            ((spans - 1, key_width, width), jnp.bfloat16),
            ((2, heads, tokens), jnp.float32),
            ((spans, heads, 128), jnp.float32),
            *[(array.shape, array.dtype) for array in kept],
        ],
        [
            pltpu.VMEM(log_decay.shape, jnp.float32),
            pltpu.VMEM((width, key_width), jnp.float32),
            pltpu.SemaphoreType.DMA((spans + 5,)),
        ],
        [pl.BlockSpec(memory_space=pltpu.HBM)] * len(inputs),
    )


def local_kernel(first, last, *refs):
    q_ref, k_ref, v_ref, sums_ref, totals_ref, weight_ref, local_ref = refs[:7]
    mixed_ref, done_ref = refs[-2:]
    heads = weight_ref.shape[1]
    head_width = v_ref.shape[1] // heads
    spans = totals_ref.shape[0]
    local_bits = spans.bit_length() - 1
    half = SPAN // 2
    done_ref[...] = jnp.zeros_like(done_ref)
    source = lax.broadcasted_iota(jnp.int32, (half, half), 0)
    target = lax.broadcasted_iota(jnp.int32, (half, half), 1)
    causal = source <= target
    empty = jnp.zeros((half, half), jnp.bfloat16)

    for span in range(first, last):
        tokens = slice(span * SPAN, (span + 1) * SPAN)
        queries = q_ref[tokens]
        scores = lax.dot_general(
            k_ref[tokens], queries, NT, preferred_element_type=jnp.float32
        )
        within = sums_ref[0, :, tokens]
        within_down = within.T
        weight = weight_ref[0, :, tokens]
        values_across = v_ref[tokens].T

        def mix(head, low, high):
            rows = slice(low * half, (low + 1) * half)
            columns = slice(high * half, (high + 1) * half)
            gap = within[head : head + 1, columns] - within_down[rows, head : head + 1]
            if low == high:
                gap = jnp.where(causal, gap, -1e30)
            mixing = scores[rows, columns] * jnp.exp(gap) * weight[head : head + 1, columns]
            return mixing.astype(jnp.bfloat16)

        levels = []
        offset = 0
        for bit in range(local_bits):
            if span >> bit & 1:
                since = within
                for back in range(1, span % 2**bit + 1):
                    since = since + spread_lanes(totals_ref[span - back][:, :1], SPAN)
                scale = jnp.exp(since) * weight_ref[1 + bit, :, tokens]
                levels.append((local_ref[offset + (span >> (bit + 1))].T, scale))
            offset += spans >> (bit + 1)
        for head in range(heads):
            rows = slice(head * head_width, (head + 1) * head_width)
            mixing = jnp.concatenate(
                [
                    jnp.concatenate([mix(head, 0, 0), mix(head, 0, 1)], axis=1),
                    jnp.concatenate([empty, mix(head, 1, 1)], axis=1),
                ],
                axis=0,
            )
            mixed = jnp.dot(values_across[rows], mixing, preferred_element_type=jnp.float32)
            for level, scale in levels:
                found = lax.dot_general(
                    level[rows], queries, NT, preferred_element_type=jnp.float32
                )
                mixed = mixed + found * scale[head : head + 1]
            mixed_ref[rows, tokens] = mixed


def mix_local(first, last, shared, mixed, tokens=()):
    queries, keys, values, sums, totals, level_weight, local = shared
    rest = [] if mixed is None else [mixed]
    return call(
        functools.partial(local_kernel, first, last),
        f"local{first}",
        [*shared, *rest, *tokens],
        [(values.shape[::-1], jnp.float32), ((8, 128), jnp.float32)],
        aliases={7: 0} if rest else None,
    )


def join(upper, mine, mine_total, other, other_total):
    fade = jnp.exp(jnp.where(upper, mine_total, other_total))
    return jnp.where(upper, other * fade + mine, mine * fade + other)


def first_head(far, heads):
    here = place()
    first = 0
    for bit, flip in enumerate(far):
        first = first + jnp.bitwise_xor(bit_of(here, bit), flip) * (heads >> (bit + 1))
    return first


def merge_kernel(bit, offset, mode, *refs):
    mine_ref, other_ref, prefix_ref = refs[:3]
    whole_ref = refs[-1]
    next_ref = refs[-2]
    heads = prefix_ref.shape[0]
    near = min(bit + 1, SPLIT_BITS)
    rows = mine_ref.shape[0] - heads
    per = mine_ref.shape[1]
    upper = bit_of(place(), bit) == 1
    first = first_head((0,) * near, heads) + offset
    for slot in range(rows // per):
        part = slice(slot * per, (slot + 1) * per)
        total = pl.ds(rows + first + slot, 1)
        whole_ref[part] = join(
            upper, mine_ref[part], mine_ref[total], other_ref[part], other_ref[total]
        )
    other_total = other_ref[rows:]
    total = mine_ref[rows:] + other_total
    next_ref[...] = prefix_ref[...] + jnp.where(upper, other_total, 0.0)
    if mode == "whole":
        merged_ref = refs[-3]
        merged_ref[:rows] = whole_ref[...]
        merged_ref[rows:] = total
    else:
        first_ref, second_ref = refs[-4:-2]
        half = rows // 2
        side = bit_of(place(), bit + 1) if mode == "side" else 0
        first_ref[:half] = whole_ref[pl.ds(side * half, half)]
        second_ref[:half] = whole_ref[pl.ds((1 - side) * half, half)]
        first_ref[half:] = total
        second_ref[half:] = total


def merge(bit, mine, other, prefix, mode, offset, tokens=()):
    heads, lanes = prefix.shape
    rows = mine.shape[0] - heads
    if mode == "whole":
        messages = [(mine.shape, jnp.float32)]
    else:
        messages = [((rows // 2 + heads, lanes), jnp.float32)] * 2
    *messages, prefix = call(
        functools.partial(merge_kernel, bit, offset, mode),
        f"merge{bit}{offset}",
        [mine, other, prefix, *tokens],
        [*messages, (prefix.shape, jnp.float32)],
        [pltpu.VMEM((rows, lanes), jnp.float32)],
    )
    return messages, prefix


def pack_kernel(takes, *refs):
    out_ref = refs[-1]
    at = 0
    for ref, rows in zip(refs, takes):
        out_ref[at : at + rows] = ref[:rows]
        at += rows


def pack(name, pieces, tokens=()):
    takes = [rows for _, rows in pieces]
    lanes = pieces[0][0].shape[1]
    return call(
        functools.partial(pack_kernel, takes),
        name,
        [*[array for array, _ in pieces], *tokens],
        [((sum(takes), lanes), jnp.float32)],
    )[0]


def level_scale(bit, first_level, prefix_ref, sums_ref, weight_ref, tokens):
    active = jnp.where(bit_of(place(), bit) == 1, 1.0, 0.0)
    reach = jnp.exp(sums_ref[1, :, tokens] + spread_lanes(prefix_ref[:, :1], SPAN))
    return reach * weight_ref[first_level + bit, :, tokens] * active


def take_levels(plan, part_refs, levels, heads):
    per = levels.shape[1] // heads
    for slot, pieces in enumerate(plan):
        for index, row, far in pieces:
            rows = (heads >> len(far)) * per
            start = pl.multiple_of(first_head(far, heads) * per, 128)
            levels[slot, pl.ds(start, rows)] = part_refs[index][row : row + rows].astype(
                jnp.bfloat16
            )


def reach_kernel(plan, bits, first_level, *refs):
    mixed_ref, q_ref, sums_ref, weight_ref = refs[:4]
    prefix_refs = refs[4 : 4 + len(bits)]
    part_refs = refs[4 + len(bits) : -3]
    out_ref, done_ref, levels = refs[-3:]
    done_ref[...] = jnp.zeros_like(done_ref)
    heads = weight_ref.shape[1]
    head_width = mixed_ref.shape[0] // heads
    take_levels(plan, part_refs, levels, heads)
    for span in range(q_ref.shape[0] // SPAN):
        tokens = slice(span * SPAN, (span + 1) * SPAN)
        queries = q_ref[tokens]
        scales = [
            level_scale(bit, first_level, prefix_ref, sums_ref, weight_ref, tokens)
            for bit, prefix_ref in zip(bits, prefix_refs)
        ]
        for head in range(heads):
            rows = slice(head * head_width, (head + 1) * head_width)
            mixed = mixed_ref[rows, tokens]
            for slot, scale in enumerate(scales):
                found = lax.dot_general(
                    levels[slot, rows], queries, NT, preferred_element_type=jnp.float32
                )
                mixed = mixed + found * scale[head : head + 1]
            out_ref[rows, tokens] = mixed


def add_levels(mixed, queries, sums, level_weight, levels, parts, first_level, tokens=()):
    width = mixed.shape[0]
    bits = [bit for bit, _, _ in levels]
    plan = [pieces for _, _, pieces in levels]
    prefixes = [prefix for _, prefix, _ in levels]
    return call(
        functools.partial(reach_kernel, plan, bits, first_level),
        f"reach{bits[0]}",
        [mixed, queries, sums, level_weight, *prefixes, *parts, *tokens],
        [(mixed.shape, jnp.float32), ((8, 128), jnp.float32)],
        [pltpu.VMEM((len(bits), width, queries.shape[1]), jnp.bfloat16)],
        aliases={0: 0},
    )


def finish_kernel(far, bit, first_level, *refs):
    mixed_ref, q_ref, sums_ref, weight_ref, gain_ref, prefix_ref, state_ref = refs[:7]
    out_hbm, done_ref, out_ref, level, scale_ref, sent = refs[-6:]
    done_ref[...] = jnp.zeros_like(done_ref)
    heads = weight_ref.shape[1]
    head_width = mixed_ref.shape[0] // heads
    count = heads >> len(far)
    first = first_head(far, heads)
    level[...] = state_ref[: level.shape[0]].astype(jnp.bfloat16)
    gains = []
    for slot in range(count):
        row = jnp.broadcast_to(gain_ref[pl.ds(first + slot, 1)], (8, head_width))
        gains.append(row.T[:, :1])
    columns = pl.ds(pl.multiple_of(first * head_width, 128), count * head_width)
    copies = []
    for span in range(q_ref.shape[0] // SPAN):
        tokens = slice(span * SPAN, (span + 1) * SPAN)
        queries = q_ref[tokens]
        scale_ref[...] = level_scale(bit, first_level, prefix_ref, sums_ref, weight_ref, tokens)
        for slot in range(count):
            rows = slice(slot * head_width, (slot + 1) * head_width)
            found = lax.dot_general(level[rows], queries, NT, preferred_element_type=jnp.float32)
            start = pl.multiple_of((first + slot) * head_width, 128)
            mixed = mixed_ref[pl.ds(start, head_width), tokens]
            mixed = mixed + found * scale_ref[pl.ds(first + slot, 1)]
            square = jnp.mean(mixed * mixed, axis=0, keepdims=True)
            normed = mixed * lax.rsqrt(square + EPS) * gains[slot]
            out_ref[tokens, rows] = normed.astype(jnp.bfloat16).T
        copy = pltpu.make_async_copy(
            out_ref.at[tokens], out_hbm.at[tokens, columns], sent.at[span]
        )
        copy.start()
        copies.append(copy)
    for copy in copies:
        copy.wait()


def finish(far, bit, first_level, mixed, queries, sums, level_weight, gain, prefix, state, begun):
    width, tokens = mixed.shape
    inputs = [mixed, queries, sums, level_weight, gain, prefix, state]
    specs = [HELD] * len(inputs)
    inputs = [hold(array) for array in inputs]
    out = pl.BlockSpec(memory_space=pltpu.HBM)
    if begun is not None:
        specs.append(out)
        inputs.append(begun)
    return pl.pallas_call(
        functools.partial(finish_kernel, far, bit, first_level),
        in_specs=specs,
        out_specs=[out, HELD],
        out_shape=[
            jax.ShapeDtypeStruct((tokens, width), jnp.bfloat16),
            pltpu.VMEM((8, 128), jnp.float32),
        ],
        scratch_shapes=[
            pltpu.VMEM((tokens, width >> len(far)), jnp.bfloat16),
            pltpu.VMEM((width >> len(far), queries.shape[1]), jnp.bfloat16),
            pltpu.VMEM((level_weight.shape[1], SPAN), jnp.float32),
            pltpu.SemaphoreType.DMA((tokens // SPAN,)),
        ],
        input_output_aliases={} if begun is None else {7: 0},
        compiler_params=PARAMS,
        name=f"finish{far[0]}{far[1]}",
    )(*inputs)


def trade(value, mask):
    wide, narrow = lax.axis_size("wide"), lax.axis_size("narrow")

    def ranked(index):
        return index % narrow * wide + index // narrow

    pairs = [(ranked(source), ranked(source ^ mask)) for source in range(wide * narrow)]
    return lax.ppermute(value, AXES, pairs)


def per_device(queries, keys, values, log_decay, level_weight, norm_gain):
    heads = log_decay.shape[0]
    tokens, width = values.shape
    per = width // heads
    spans = tokens // SPAN
    group_bits = heads.bit_length() - 1
    bits = (lax.axis_size("wide") * lax.axis_size("narrow")).bit_length() - 1
    first_level = level_weight.shape[0] - bits
    gain = norm_gain.reshape(heads, per)
    mine, give, local, sums, totals, queries, keys, values, level_weight, gain = make_states(
        queries, keys, values, log_decay, level_weight, gain
    )
    shared = (queries, keys, values, sums, totals, level_weight, local)

    last = bits - 1
    two = 2 * per
    sides = [(core, side) for core in (0, 1) for side in (0, 1)]
    prefix = jnp.zeros((heads, 128), jnp.float32)
    prefixes, found, rests, across = [], [], [], {}
    mixed, at, waits = None, 0, ()
    chunks = [mine]
    for bit in range(bits):
        prefixes.append(prefix)
        sent = [give] if bit < SPLIT_BITS else chunks
        found.append([trade(chunk, 2**bit) for chunk in sent])
        if bit < SPLIT_BITS:
            rests.append(trade(chunks[0], 2**bit))
        if 0 < bit and at < spans:
            stop = spans if bit == last else at + 1
            mixed, token = mix_local(at, stop, shared, mixed, (chunks[0],))
            at, waits = stop, (token,)
        if 1 < bit < 2 + SPLIT_BITS:
            waits = (*waits, rests[bit - 2])
        if bit < last:
            mode = "side" if bit + 1 < SPLIT_BITS else "whole"
            merged = [
                merge(bit, chunk, other, prefix, mode, offset, waits)
                for offset, (chunk, other) in enumerate(zip(chunks, found[bit]))
            ]
            prefix = merged[0][1]
            chunks = [message for messages, _ in merged for message in messages]
            if mode == "side":
                chunks, give = chunks[:1], chunks[1]
        if 1 < bit < last:
            pieces = [(state, two // len(found[bit])) for state in found[bit]]
            found[bit] = [pack(f"found{bit}", pieces, (chunks[0],))]
            across[bit] = trade(found[bit][0], 2)
    ends = found[last]
    found = [states[0] for states in found]

    rest = (queries, sums, level_weight)
    near = pack("near1", [(found[1], two), (rests[1], two)])
    far = trade(near, 1)
    levels = [(0, prefixes[0], [(0, 0, (0,)), (1, 0, (1,))])]
    levels.append((1, prefixes[1], [(2 + core, side * two, (core, side)) for core, side in sides]))
    parts = [found[0], rests[0], near, far]
    mixed, token = add_levels(mixed, *rest, levels, parts, first_level)
    state = pack("state", [(ends[0], two)], (token,))

    pieces = []
    for bit in range(2, last - 1):
        pieces += [(found[bit], two), (across[bit], two)]
    near = pack("near2", [*pieces, (found[last - 1], two)], (chunks[0],))
    far = trade(near, 1)
    near_side = pack("side", [(across[last - 1], two)], (token,))
    far_side = trade(near_side, 1)
    levels = []
    for slot, bit in enumerate(range(2, last)):
        taken = [
            (core if bit < last - 1 or side == 0 else 2 + core, (2 * slot + side) * two, (core, side))
            for core, side in sides
        ]
        if bit == last - 1:
            taken = [(at, row if at < 2 else 0, far_bits) for at, row, far_bits in taken]
        levels.append((bit, prefixes[bit], taken))
    parts = [near, far, near_side, far_side]
    mixed, token = add_levels(mixed, *rest, levels, parts, first_level, (state,))

    rest = (last, first_level, mixed, *rest, gain, prefixes[last])
    beside = [(trade(state, 2), two)]
    out, _ = finish((0, 0), *rest, state, None)
    out, token = finish((1, 0), *rest, trade(state, 1), out)
    beside = pack("beside", beside, (token,))
    out, _ = finish((0, 1), *rest, beside, out)
    return finish((1, 1), *rest, trade(beside, 1), out)[0]


def solution(mesh):
    placed = (
        P(("wide", "narrow"), None),
        P(("wide", "narrow"), None),
        P(("wide", "narrow"), None),
        P(None, ("wide", "narrow")),
        P(None, None, ("wide", "narrow")),
        P(),
    )
    return jax.shard_map(
        per_device,
        mesh=mesh,
        in_specs=placed,
        out_specs=P(("wide", "narrow"), None),
        check_vma=False,
    )
```

```python
import functools

import jax
import jax.numpy as jnp
from jax import lax
from jax.experimental import pallas as pl
from jax.experimental.pallas import tpu as pltpu
from jax.sharding import PartitionSpec as P

SPAN = 256
SPLIT_BITS = 2
EPS = 1e-05
AXES = ("narrow", "wide")
NT = (((1,), (1,)), ((), ()))
PARAMS = pltpu.CompilerParams(vmem_limit_bytes=32 * 1024 * 1024)
HELD = pl.BlockSpec(memory_space=pltpu.VMEM)


def place():
    return lax.axis_index("wide") * lax.axis_size("narrow") + lax.axis_index("narrow")


def bit_of(value, bit):
    return jnp.bitwise_and(jnp.right_shift(value, bit), 1)


def spread_lanes(column, width):
    return jnp.broadcast_to(column, (column.shape[0], width))


ANYWHERE = pl.BlockSpec(memory_space=pl.ANY)


def hold(array):
    return pltpu.with_memory_space_constraint(array, pltpu.VMEM)


def call(kernel, name, inputs, outputs, scratch=(), in_specs=None, aliases=None):
    specs = in_specs or [HELD] * len(inputs)
    inputs = [hold(array) if spec is HELD else array for array, spec in zip(inputs, specs)]
    return pl.pallas_call(
        kernel,
        in_specs=specs,
        out_specs=[HELD] * len(outputs),
        out_shape=[pltpu.VMEM(shape, dtype) for shape, dtype in outputs],
        scratch_shapes=list(scratch),
        input_output_aliases=aliases or {},
        compiler_params=PARAMS,
        name=name,
    )(*inputs)


def running_sums(rows):
    high = rows.astype(jnp.bfloat16)
    rest = rows - high.astype(jnp.float32)
    middle = rest.astype(jnp.bfloat16)
    low = (rest - middle.astype(jnp.float32)).astype(jnp.bfloat16)
    width = rows.shape[1]
    source = lax.broadcasted_iota(jnp.int32, (width, width), 0)
    target = lax.broadcasted_iota(jnp.int32, (width, width), 1)
    upto = jnp.where(source <= target, 1.0, 0.0).astype(jnp.bfloat16)
    sums = jnp.dot(
        jnp.concatenate([high, middle, low], axis=0), upto, preferred_element_type=jnp.float32
    )
    count = rows.shape[0]
    return sums[:count] + (sums[count : 2 * count] + sums[2 * count :])


def state_kernel(*refs):
    q_hbm, k_hbm, v_hbm, decay_hbm, weight_hbm, gain_hbm = refs[:6]
    keep_ref, send_ref, local_ref, sums_ref, totals_ref = refs[6:11]
    q_ref, k_ref, v_ref, weight_ref, gain_ref, decay_ref, held, arrived = refs[11:]
    heads, tokens = decay_ref.shape
    head_width = v_ref.shape[1] // heads
    spans = tokens // SPAN
    rows_of = [slice(span * SPAN, (span + 1) * SPAN) for span in range(spans)]
    loads = [(decay_hbm, decay_ref), (k_hbm, k_ref)]
    loads += [(v_hbm.at[rows], v_ref.at[rows]) for rows in rows_of]
    loads += [(q_hbm, q_ref), (weight_hbm, weight_ref), (gain_hbm, gain_ref)]
    copies = [
        pltpu.make_async_copy(source, target, arrived.at[at])
        for at, (source, target) in enumerate(loads)
    ]
    for copy in copies:
        copy.start()
    copies[0].wait()
    within = running_sums(jnp.concatenate([decay_ref[:, rows] for rows in rows_of], axis=0))
    run = jnp.zeros((heads, 128), jnp.float32)
    fades, wholes = [], []
    for span, rows in enumerate(rows_of):
        here = within[span * heads : (span + 1) * heads]
        last = here[:, SPAN - 1 :]
        total = spread_lanes(last, 128)
        sums_ref[0, :, rows] = here
        sums_ref[1, :, rows] = here + spread_lanes(run[:, :1], SPAN)
        totals_ref[span] = total
        run = run + total
        fades.append(jnp.exp(spread_lanes(last, SPAN) - here))
        wholes.append(jnp.exp(total))
    copies[1].wait()
    across = [k_ref[rows].astype(jnp.float32).T for rows in rows_of]
    for copy in copies[2 : 2 + spans]:
        copy.wait()
    for head in range(heads):
        columns = slice(head * head_width, (head + 1) * head_width)
        states = []
        for span, rows in enumerate(rows_of):
            faded = (across[span] * fades[span][head : head + 1]).astype(jnp.bfloat16)
            states.append(
                jnp.dot(faded, v_ref[rows, columns], preferred_element_type=jnp.float32)
            )
        at = 0
        size = 1
        while size < spans:
            for first in range(0, spans, 2 * size):
                group = states[first]
                for span in range(first + 1, first + size):
                    group = group * wholes[span][head : head + 1] + states[span]
                local_ref[at, :, columns] = group.astype(jnp.bfloat16)
                at += 1
            size *= 2
        group = states[0]
        for span in range(1, spans):
            group = group * wholes[span][head : head + 1] + states[span]
        held[columns] = group.T
    half = held.shape[0] // 2
    core = bit_of(place(), 0)
    keep_ref[:half] = held[pl.ds(core * half, half)]
    send_ref[:half] = held[pl.ds((1 - core) * half, half)]
    keep_ref[half:] = run
    send_ref[half:] = run
    for copy in copies[2 + spans :]:
        copy.wait()


def make_states(queries, keys, values, log_decay, level_weight, gain):
    tokens, key_width = keys.shape
    heads = log_decay.shape[0]
    width = values.shape[1]
    spans = tokens // SPAN
    message = ((width // 2 + heads, key_width), jnp.float32)
    inputs = [queries, keys, values, log_decay, level_weight, gain]
    kept = [queries, keys, values, level_weight, gain]
    return call(
        state_kernel,
        "states",
        [pltpu.with_memory_space_constraint(array, pltpu.HBM) for array in inputs],
        [
            message,
            message,
            ((spans - 1, key_width, width), jnp.bfloat16),
            ((2, heads, tokens), jnp.float32),
            ((spans, heads, 128), jnp.float32),
            *[(array.shape, array.dtype) for array in kept],
        ],
        [
            pltpu.VMEM(log_decay.shape, jnp.float32),
            pltpu.VMEM((width, key_width), jnp.float32),
            pltpu.SemaphoreType.DMA((spans + 5,)),
        ],
        [pl.BlockSpec(memory_space=pltpu.HBM)] * len(inputs),
    )


def local_kernel(first, last, has_token, *refs):
    q_ref, k_ref, v_ref, sums_ref, totals_ref, weight_ref, local_ref = refs[:7]
    if has_token:
        mixed_ref, done_ref = refs[-2:]
        done_ref[...] = jnp.zeros_like(done_ref)
    else:
        mixed_ref = refs[-1]
    heads = weight_ref.shape[1]
    head_width = v_ref.shape[1] // heads
    spans = totals_ref.shape[0]
    local_bits = spans.bit_length() - 1
    half = SPAN // 2
    source = lax.broadcasted_iota(jnp.int32, (half, half), 0)
    target = lax.broadcasted_iota(jnp.int32, (half, half), 1)
    causal = source <= target
    empty = jnp.zeros((half, half), jnp.bfloat16)

    for span in range(first, last):
        tokens = slice(span * SPAN, (span + 1) * SPAN)
        queries = q_ref[tokens]
        scores = lax.dot_general(
            k_ref[tokens], queries, NT, preferred_element_type=jnp.float32
        )
        within = sums_ref[0, :, tokens]
        within_down = within.T
        weight = weight_ref[0, :, tokens]
        values_across = v_ref[tokens].T

        def mix(head, low, high):
            rows = slice(low * half, (low + 1) * half)
            columns = slice(high * half, (high + 1) * half)
            gap = within[head : head + 1, columns] - within_down[rows, head : head + 1]
            if low == high:
                gap = jnp.where(causal, gap, -1e30)
            mixing = scores[rows, columns] * jnp.exp(gap) * weight[head : head + 1, columns]
            return mixing.astype(jnp.bfloat16)

        levels = []
        offset = 0
        for bit in range(local_bits):
            if span >> bit & 1:
                since = within
                for back in range(1, span % 2**bit + 1):
                    since = since + spread_lanes(totals_ref[span - back][:, :1], SPAN)
                scale = jnp.exp(since) * weight_ref[1 + bit, :, tokens]
                levels.append((local_ref[offset + (span >> (bit + 1))].T, scale))
            offset += spans >> (bit + 1)
        for head in range(heads):
            rows = slice(head * head_width, (head + 1) * head_width)
            mixing = jnp.concatenate(
                [
                    jnp.concatenate([mix(head, 0, 0), mix(head, 0, 1)], axis=1),
                    jnp.concatenate([empty, mix(head, 1, 1)], axis=1),
                ],
                axis=0,
            )
            mixed = jnp.dot(values_across[rows], mixing, preferred_element_type=jnp.float32)
            for level, scale in levels:
                found = lax.dot_general(
                    level[rows], queries, NT, preferred_element_type=jnp.float32
                )
                mixed = mixed + found * scale[head : head + 1]
            mixed_ref[rows, tokens] = mixed


def mix_local(first, last, shared, mixed, tokens, has_token):
    queries, keys, values, sums, totals, level_weight, local = shared
    rest = [] if mixed is None else [mixed]
    return call(
        functools.partial(local_kernel, first, last, has_token),
        f"local{first}",
        [*shared, *rest, *tokens],
        [(values.shape[::-1], jnp.float32), ((8, 128), jnp.float32)][: 1 + has_token],
        aliases={7: 0} if rest else None,
    )


def join(upper, mine, mine_total, other, other_total):
    fade = jnp.exp(jnp.where(upper, mine_total, other_total))
    return jnp.where(upper, other * fade + mine, mine * fade + other)


def first_head(far, heads):
    here = place()
    first = 0
    for bit, flip in enumerate(far):
        first = first + jnp.bitwise_xor(bit_of(here, bit), flip) * (heads >> (bit + 1))
    return first


def merge_kernel(bit, offset, mode, *refs):
    mine_ref, other_ref, prefix_ref = refs[:3]
    whole_ref = refs[-1]
    next_ref = refs[-2]
    heads = prefix_ref.shape[0]
    near = min(bit + 1, SPLIT_BITS)
    rows = mine_ref.shape[0] - heads
    per = mine_ref.shape[1]
    upper = bit_of(place(), bit) == 1
    first = first_head((0,) * near, heads) + offset
    for slot in range(rows // per):
        part = slice(slot * per, (slot + 1) * per)
        total = pl.ds(rows + first + slot, 1)
        whole_ref[part] = join(
            upper, mine_ref[part], mine_ref[total], other_ref[part], other_ref[total]
        )
    other_total = other_ref[rows:]
    total = mine_ref[rows:] + other_total
    next_ref[...] = prefix_ref[...] + jnp.where(upper, other_total, 0.0)
    if mode == "whole":
        merged_ref = refs[-3]
        merged_ref[:rows] = whole_ref[...]
        merged_ref[rows:] = total
    else:
        first_ref, second_ref = refs[-4:-2]
        half = rows // 2
        side = bit_of(place(), bit + 1) if mode == "side" else 0
        first_ref[:half] = whole_ref[pl.ds(side * half, half)]
        second_ref[:half] = whole_ref[pl.ds((1 - side) * half, half)]
        first_ref[half:] = total
        second_ref[half:] = total


def merge(bit, mine, other, prefix, mode, offset, tokens=()):
    heads, lanes = prefix.shape
    rows = mine.shape[0] - heads
    if mode == "whole":
        messages = [(mine.shape, jnp.float32)]
    else:
        messages = [((rows // 2 + heads, lanes), jnp.float32)] * 2
    *messages, prefix = call(
        functools.partial(merge_kernel, bit, offset, mode),
        f"merge{bit}{offset}",
        [mine, other, prefix, *tokens],
        [*messages, (prefix.shape, jnp.float32)],
        [pltpu.VMEM((rows, lanes), jnp.float32)],
    )
    return messages, prefix


def pack_kernel(takes, *refs):
    out_ref = refs[-1]
    at = 0
    for ref, rows in zip(refs, takes):
        out_ref[at : at + rows] = ref[:rows]
        at += rows


def pack(name, pieces, tokens=()):
    takes = [rows for _, rows in pieces]
    lanes = pieces[0][0].shape[1]
    return call(
        functools.partial(pack_kernel, takes),
        name,
        [*[array for array, _ in pieces], *tokens],
        [((sum(takes), lanes), jnp.float32)],
    )[0]


def level_scale(bit, first_level, prefix_ref, sums_ref, weight_ref, tokens):
    active = jnp.where(bit_of(place(), bit) == 1, 1.0, 0.0)
    reach = jnp.exp(sums_ref[1, :, tokens] + spread_lanes(prefix_ref[:, :1], SPAN))
    return reach * weight_ref[first_level + bit, :, tokens] * active


def take_levels(plan, part_refs, levels, heads):
    per = levels.shape[1] // heads
    for slot, pieces in enumerate(plan):
        for index, row, far in pieces:
            rows = (heads >> len(far)) * per
            start = pl.multiple_of(first_head(far, heads) * per, 128)
            levels[slot, pl.ds(start, rows)] = part_refs[index][row : row + rows].astype(
                jnp.bfloat16
            )


def reach_kernel(plan, bits, first_level, *refs):
    mixed_ref, q_ref, sums_ref, weight_ref = refs[:4]
    prefix_refs = refs[4 : 4 + len(bits)]
    part_refs = refs[4 + len(bits) : -3]
    out_ref, done_ref, levels = refs[-3:]
    done_ref[...] = jnp.zeros_like(done_ref)
    heads = weight_ref.shape[1]
    head_width = mixed_ref.shape[0] // heads
    take_levels(plan, part_refs, levels, heads)
    for span in range(q_ref.shape[0] // SPAN):
        tokens = slice(span * SPAN, (span + 1) * SPAN)
        queries = q_ref[tokens]
        scales = [
            level_scale(bit, first_level, prefix_ref, sums_ref, weight_ref, tokens)
            for bit, prefix_ref in zip(bits, prefix_refs)
        ]
        for head in range(heads):
            rows = slice(head * head_width, (head + 1) * head_width)
            mixed = mixed_ref[rows, tokens]
            for slot, scale in enumerate(scales):
                found = lax.dot_general(
                    levels[slot, rows], queries, NT, preferred_element_type=jnp.float32
                )
                mixed = mixed + found * scale[head : head + 1]
            out_ref[rows, tokens] = mixed


def add_levels(mixed, queries, sums, level_weight, levels, parts, first_level, tokens=()):
    width = mixed.shape[0]
    bits = [bit for bit, _, _ in levels]
    plan = [pieces for _, _, pieces in levels]
    prefixes = [prefix for _, prefix, _ in levels]
    return call(
        functools.partial(reach_kernel, plan, bits, first_level),
        f"reach{bits[0]}",
        [mixed, queries, sums, level_weight, *prefixes, *parts, *tokens],
        [(mixed.shape, jnp.float32), ((8, 128), jnp.float32)],
        [pltpu.VMEM((len(bits), width, queries.shape[1]), jnp.bfloat16)],
        aliases={0: 0},
    )


def finish_kernel(quarters, first_level, bits, has_token, *refs):
    mixed_ref, q_ref, sums_ref, weight_ref, gain_ref = refs[:5]
    prefix_refs = refs[5 : 5 + len(bits)]
    part_refs = refs[5 + len(bits) :]
    out_ref, scale_ref, sent = refs[-3:]
    out_hbm = refs[-5] if has_token else refs[-4]
    if has_token:
        refs[-4][...] = jnp.zeros_like(refs[-4])
    heads = weight_ref.shape[1]
    head_width = mixed_ref.shape[0] // heads
    count = heads // 4
    work = []
    for at, (far, pieces) in enumerate(quarters):
        first = first_head(far, heads)
        for slot in range(count):
            row = jnp.broadcast_to(gain_ref[pl.ds(first + slot, 1)], (8, head_width))
            states = []
            for index, start in pieces:
                rows = slice(start + slot * head_width, start + (slot + 1) * head_width)
                states.append(part_refs[index][rows].astype(jnp.bfloat16))
            work.append((first + slot, at * count + slot, row.T[:, :1], states))
    copies = []
    for span in range(q_ref.shape[0] // SPAN):
        tokens = slice(span * SPAN, (span + 1) * SPAN)
        queries = q_ref[tokens]
        for level, (bit, prefix_ref) in enumerate(zip(bits, prefix_refs)):
            scale_ref[level] = level_scale(
                bit, first_level, prefix_ref, sums_ref, weight_ref, tokens
            )
        for head, place_out, gain_column, states in work:
            start = pl.multiple_of(head * head_width, 128)
            mixed = mixed_ref[pl.ds(start, head_width), tokens]
            for level, state in enumerate(states):
                found = lax.dot_general(state, queries, NT, preferred_element_type=jnp.float32)
                mixed = mixed + found * scale_ref[level, pl.ds(head, 1)]
            square = jnp.mean(mixed * mixed, axis=0, keepdims=True)
            normed = mixed * lax.rsqrt(square + EPS) * gain_column
            columns = slice(place_out * head_width, (place_out + 1) * head_width)
            out_ref[tokens, columns] = normed.astype(jnp.bfloat16).T
        for at, (far, _) in enumerate(quarters):
            size = count * head_width
            columns = pl.ds(pl.multiple_of(first_head(far, heads) * head_width, 128), size)
            copy = pltpu.make_async_copy(
                out_ref.at[tokens, at * size : (at + 1) * size],
                out_hbm.at[tokens, columns],
                sent.at[len(copies)],
            )
            copy.start()
            copies.append(copy)
    for copy in copies:
        copy.wait()


def finish(quarters, first_level, bits, shared, prefixes, parts, begun, has_token):
    mixed, queries, sums, level_weight, gain = shared
    width, tokens = mixed.shape
    heads = level_weight.shape[1]
    inputs = [*shared, *prefixes, *parts]
    specs = [HELD] * len(inputs)
    inputs = [hold(array) for array in inputs]
    out = pl.BlockSpec(memory_space=pltpu.HBM)
    aliases = {}
    if begun is not None:
        aliases = {len(inputs): 0}
        specs.append(out)
        inputs.append(begun)
    shapes = [jax.ShapeDtypeStruct((tokens, width), jnp.bfloat16)]
    if has_token:
        shapes.append(pltpu.VMEM((8, 128), jnp.float32))
    return pl.pallas_call(
        functools.partial(finish_kernel, quarters, first_level, bits, has_token),
        in_specs=specs,
        out_specs=[out, HELD][: len(shapes)],
        out_shape=shapes,
        scratch_shapes=[
            pltpu.VMEM((tokens, len(quarters) * width // 4), jnp.bfloat16),
            pltpu.VMEM((len(bits), heads, SPAN), jnp.float32),
            pltpu.SemaphoreType.DMA((len(quarters) * (tokens // SPAN),)),
        ],
        input_output_aliases=aliases,
        compiler_params=PARAMS,
        name="finish" + "".join(f"{core}{side}" for (core, side), _ in quarters),
    )(*inputs)


def trade(value, mask):
    wide, narrow = lax.axis_size("wide"), lax.axis_size("narrow")

    def ranked(index):
        return index % narrow * wide + index // narrow

    pairs = [(ranked(source), ranked(source ^ mask)) for source in range(wide * narrow)]
    return lax.ppermute(value, AXES, pairs)


def per_device(queries, keys, values, log_decay, level_weight, norm_gain):
    heads = log_decay.shape[0]
    tokens, width = values.shape
    per = width // heads
    spans = tokens // SPAN
    group_bits = heads.bit_length() - 1
    bits = (lax.axis_size("wide") * lax.axis_size("narrow")).bit_length() - 1
    first_level = level_weight.shape[0] - bits
    gain = norm_gain.reshape(heads, per)
    mine, give, local, sums, totals, queries, keys, values, level_weight, gain = make_states(
        queries, keys, values, log_decay, level_weight, gain
    )
    shared = (queries, keys, values, sums, totals, level_weight, local)

    last = bits - 1
    two = 2 * per
    sides = [(core, side) for core in (0, 1) for side in (0, 1)]
    prefix = jnp.zeros((heads, 128), jnp.float32)
    prefixes, found, rests, across = [], [], [], {}
    mixed, at, waits = None, 0, ()
    chunks = [mine]
    for bit in range(bits):
        prefixes.append(prefix)
        sent = [give] if bit < SPLIT_BITS else chunks
        found.append([trade(chunk, 2**bit) for chunk in sent])
        if bit < SPLIT_BITS:
            rests.append(trade(chunks[0], 2**bit))
        if 0 < bit and at < spans:
            stop = spans if bit == last else at + 1
            mixed, *waits = mix_local(at, stop, shared, mixed, (chunks[0],), bit < last)
            at = stop
        if 1 < bit < 2 + SPLIT_BITS:
            waits = (*waits, rests[bit - 2])
        if bit < last:
            mode = "side" if bit + 1 < SPLIT_BITS else "whole"
            merged = [
                merge(bit, chunk, other, prefix, mode, offset, waits)
                for offset, (chunk, other) in enumerate(zip(chunks, found[bit]))
            ]
            prefix = merged[0][1]
            chunks = [message for messages, _ in merged for message in messages]
            if mode == "side":
                chunks, give = chunks[:1], chunks[1]
        if 1 < bit < last:
            pieces = [(state, two // len(found[bit])) for state in found[bit]]
            found[bit] = [pack(f"found{bit}", pieces, (chunks[0],))]
            across[bit] = trade(found[bit][0], 2)
    ends = found[last]
    found = [states[0] for states in found]

    rest = (queries, sums, level_weight)
    near = pack("near1", [(found[1], two), (rests[1], two)])
    far = trade(near, 1)
    levels = [(0, prefixes[0], [(0, 0, (0,)), (1, 0, (1,))])]
    levels.append((1, prefixes[1], [(2 + core, side * two, (core, side)) for core, side in sides]))
    parts = [found[0], rests[0], near, far]
    mixed, token = add_levels(mixed, *rest, levels, parts, first_level)
    state = pack("state", [(ends[0], two)], (token,))

    pieces = []
    for bit in range(2, last - 1):
        pieces += [(found[bit], two), (across[bit], two)]
    near = pack("near2", [*pieces, (found[last - 1], two)], (chunks[0],))
    far = trade(near, 1)
    near_side = pack("side", [(across[last - 1], two)], (token,))
    far_side = trade(near_side, 1)
    late = list(range(2, bits))
    where = {}
    for core, side in sides:
        where[core, side] = [(core, (2 * slot + side) * two) for slot in range(len(late) - 2)]
        top = (core, 2 * (len(late) - 2) * two) if side == 0 else (2 + core, 0)
        where[core, side].append(top)
    parts = [near, far, near_side, far_side]
    shared = (mixed, queries, sums, level_weight, gain)
    rest = (first_level, late, shared, [prefixes[bit] for bit in late])
    beside = [(trade(state, 2), two)]
    quarters = [((core, 0), [*where[core, 0], (4 + core, 0)]) for core in (0, 1)]
    out, token = finish(quarters, *rest, [*parts, state, trade(state, 1)], None, True)
    beside = pack("beside", beside, (token,))
    quarters = [((0, 1), [*where[0, 1], (4, 0)])]
    (out,) = finish(quarters, *rest, [*parts, beside], out, False)
    quarters = [((1, 1), [*where[1, 1], (4, 0)])]
    return finish(quarters, *rest, [*parts, trade(beside, 1)], out, False)[0]


def solution(mesh):
    placed = (
        P(("wide", "narrow"), None),
        P(("wide", "narrow"), None),
        P(("wide", "narrow"), None),
        P(None, ("wide", "narrow")),
        P(None, None, ("wide", "narrow")),
        P(),
    )
    return jax.shard_map(
        per_device,
        mesh=mesh,
        in_specs=placed,
        out_specs=P(("wide", "narrow"), None),
        check_vma=False,
    )
```

```python
import functools

import jax
import jax.numpy as jnp
from jax import lax
from jax.experimental import pallas as pl
from jax.experimental.pallas import tpu as pltpu
from jax.sharding import PartitionSpec as P

SPAN = 256
SPLIT_BITS = 2
CUTS = 2
EPS = 1e-05
AXES = ("narrow", "wide")
NT = (((1,), (1,)), ((), ()))
PARAMS = pltpu.CompilerParams(vmem_limit_bytes=32 * 1024 * 1024)
HELD = pl.BlockSpec(memory_space=pltpu.VMEM)


def place():
    return lax.axis_index("wide") * lax.axis_size("narrow") + lax.axis_index("narrow")


def bit_of(value, bit):
    return jnp.bitwise_and(jnp.right_shift(value, bit), 1)


def spread_lanes(column, width):
    return jnp.broadcast_to(column, (column.shape[0], width))


ANYWHERE = pl.BlockSpec(memory_space=pl.ANY)


def hold(array):
    return pltpu.with_memory_space_constraint(array, pltpu.VMEM)


def call(kernel, name, inputs, outputs, scratch=(), in_specs=None, aliases=None):
    specs = in_specs or [HELD] * len(inputs)
    inputs = [hold(array) if spec is HELD else array for array, spec in zip(inputs, specs)]
    return pl.pallas_call(
        kernel,
        in_specs=specs,
        out_specs=[HELD] * len(outputs),
        out_shape=[pltpu.VMEM(shape, dtype) for shape, dtype in outputs],
        scratch_shapes=list(scratch),
        input_output_aliases=aliases or {},
        compiler_params=PARAMS,
        name=name,
    )(*inputs)


def running_sums(rows):
    high = rows.astype(jnp.bfloat16)
    rest = rows - high.astype(jnp.float32)
    middle = rest.astype(jnp.bfloat16)
    low = (rest - middle.astype(jnp.float32)).astype(jnp.bfloat16)
    width = rows.shape[1]
    source = lax.broadcasted_iota(jnp.int32, (width, width), 0)
    target = lax.broadcasted_iota(jnp.int32, (width, width), 1)
    upto = jnp.where(source <= target, 1.0, 0.0).astype(jnp.bfloat16)
    sums = jnp.dot(
        jnp.concatenate([high, middle, low], axis=0), upto, preferred_element_type=jnp.float32
    )
    count = rows.shape[0]
    return sums[:count] + (sums[count : 2 * count] + sums[2 * count :])


def state_kernel(*refs):
    q_hbm, k_hbm, v_hbm, decay_hbm, weight_hbm, gain_hbm = refs[:6]
    message_ref, local_ref, sums_ref, totals_ref = refs[6:10]
    q_ref, k_ref, v_ref, weight_ref, gain_ref, decay_ref, arrived = refs[10:]
    heads, tokens = decay_ref.shape
    head_width = v_ref.shape[1] // heads
    spans = tokens // SPAN
    rows_of = [slice(span * SPAN, (span + 1) * SPAN) for span in range(spans)]
    loads = [(decay_hbm, decay_ref), (k_hbm, k_ref)]
    loads += [(v_hbm.at[rows], v_ref.at[rows]) for rows in rows_of]
    loads += [(q_hbm, q_ref), (weight_hbm, weight_ref), (gain_hbm, gain_ref)]
    copies = [
        pltpu.make_async_copy(source, target, arrived.at[at])
        for at, (source, target) in enumerate(loads)
    ]
    for copy in copies:
        copy.start()
    copies[0].wait()
    within = running_sums(jnp.concatenate([decay_ref[:, rows] for rows in rows_of], axis=0))
    run = jnp.zeros((heads, 128), jnp.float32)
    fades, wholes = [], []
    for span, rows in enumerate(rows_of):
        here = within[span * heads : (span + 1) * heads]
        last = here[:, SPAN - 1 :]
        total = spread_lanes(last, 128)
        sums_ref[0, :, rows] = here
        sums_ref[1, :, rows] = here + spread_lanes(run[:, :1], SPAN)
        totals_ref[span] = total
        run = run + total
        fades.append(jnp.exp(spread_lanes(last, SPAN) - here))
        wholes.append(jnp.exp(total))
    copies[1].wait()
    across = [k_ref[rows].astype(jnp.float32).T for rows in rows_of]
    for copy in copies[2 : 2 + spans]:
        copy.wait()
    for head in range(heads):
        columns = slice(head * head_width, (head + 1) * head_width)
        states = []
        for span, rows in enumerate(rows_of):
            faded = (across[span] * fades[span][head : head + 1]).astype(jnp.bfloat16)
            states.append(
                jnp.dot(faded, v_ref[rows, columns], preferred_element_type=jnp.float32)
            )
        at = 0
        size = 1
        while size < spans:
            for first in range(0, spans, 2 * size):
                group = states[first]
                for span in range(first + 1, first + size):
                    group = group * wholes[span][head : head + 1] + states[span]
                local_ref[at, :, columns] = group.astype(jnp.bfloat16)
                at += 1
            size *= 2
        group = states[0]
        for span in range(1, spans):
            group = group * wholes[span][head : head + 1] + states[span]
        message_ref[columns] = group.T
    message_ref[heads * head_width :] = run
    for copy in copies[2 + spans :]:
        copy.wait()


def make_states(queries, keys, values, log_decay, level_weight, gain):
    tokens, key_width = keys.shape
    heads = log_decay.shape[0]
    width = values.shape[1]
    spans = tokens // SPAN
    inputs = [queries, keys, values, log_decay, level_weight, gain]
    kept = [queries, keys, values, level_weight, gain]
    return call(
        state_kernel,
        "states",
        [pltpu.with_memory_space_constraint(array, pltpu.HBM) for array in inputs],
        [
            ((width + heads, key_width), jnp.float32),
            ((spans - 1, key_width, width), jnp.bfloat16),
            ((2, heads, tokens), jnp.float32),
            ((spans, heads, 128), jnp.float32),
            *[(array.shape, array.dtype) for array in kept],
        ],
        [
            pltpu.VMEM(log_decay.shape, jnp.float32),
            pltpu.SemaphoreType.DMA((spans + 5,)),
        ],
        [pl.BlockSpec(memory_space=pltpu.HBM)] * len(inputs),
    )


def local_kernel(first, last, has_token, *refs):
    q_ref, k_ref, v_ref, sums_ref, totals_ref, weight_ref, local_ref = refs[:7]
    if has_token:
        mixed_ref, done_ref = refs[-2:]
        done_ref[...] = jnp.zeros_like(done_ref)
    else:
        mixed_ref = refs[-1]
    heads = weight_ref.shape[1]
    head_width = v_ref.shape[1] // heads
    spans = totals_ref.shape[0]
    local_bits = spans.bit_length() - 1
    half = SPAN // 2
    source = lax.broadcasted_iota(jnp.int32, (half, half), 0)
    target = lax.broadcasted_iota(jnp.int32, (half, half), 1)
    causal = source <= target
    empty = jnp.zeros((half, half), jnp.bfloat16)

    for span in range(first, last):
        tokens = slice(span * SPAN, (span + 1) * SPAN)
        queries = q_ref[tokens]
        scores = lax.dot_general(
            k_ref[tokens], queries, NT, preferred_element_type=jnp.float32
        )
        within = sums_ref[0, :, tokens]
        within_down = within.T
        weight = weight_ref[0, :, tokens]
        values_across = v_ref[tokens].T

        def mix(head, low, high):
            rows = slice(low * half, (low + 1) * half)
            columns = slice(high * half, (high + 1) * half)
            gap = within[head : head + 1, columns] - within_down[rows, head : head + 1]
            if low == high:
                gap = jnp.where(causal, gap, -1e30)
            mixing = scores[rows, columns] * jnp.exp(gap) * weight[head : head + 1, columns]
            return mixing.astype(jnp.bfloat16)

        levels = []
        offset = 0
        for bit in range(local_bits):
            if span >> bit & 1:
                since = within
                for back in range(1, span % 2**bit + 1):
                    since = since + spread_lanes(totals_ref[span - back][:, :1], SPAN)
                scale = jnp.exp(since) * weight_ref[1 + bit, :, tokens]
                levels.append((local_ref[offset + (span >> (bit + 1))].T, scale))
            offset += spans >> (bit + 1)
        for head in range(heads):
            rows = slice(head * head_width, (head + 1) * head_width)
            mixing = jnp.concatenate(
                [
                    jnp.concatenate([mix(head, 0, 0), mix(head, 0, 1)], axis=1),
                    jnp.concatenate([empty, mix(head, 1, 1)], axis=1),
                ],
                axis=0,
            )
            mixed = jnp.dot(values_across[rows], mixing, preferred_element_type=jnp.float32)
            for level, scale in levels:
                found = lax.dot_general(
                    level[rows], queries, NT, preferred_element_type=jnp.float32
                )
                mixed = mixed + found * scale[head : head + 1]
            mixed_ref[rows, tokens] = mixed


def mix_local(first, last, shared, mixed, tokens, has_token):
    queries, keys, values, sums, totals, level_weight, local = shared
    rest = [] if mixed is None else [mixed]
    return call(
        functools.partial(local_kernel, first, last, has_token),
        f"local{first}",
        [*shared, *rest, *tokens],
        [(values.shape[::-1], jnp.float32), ((8, 128), jnp.float32)][: 1 + has_token],
        aliases={7: 0} if rest else None,
    )


def join(upper, mine, mine_total, other, other_total):
    fade = jnp.exp(jnp.where(upper, mine_total, other_total))
    return jnp.where(upper, other * fade + mine, mine * fade + other)


def first_head(far, heads):
    here = place()
    first = 0
    for bit, flip in enumerate(far):
        first = first + jnp.bitwise_xor(bit_of(here, bit), flip) * (heads >> (bit + 1))
    return first


def chip_kernel(mine_ref, other_ref, *refs):
    *message_refs, next_ref, whole_ref = refs
    heads = next_ref.shape[0]
    width = mine_ref.shape[0] - heads
    per = width // heads
    held = whole_ref.shape[0] // per
    here = place()
    upper = bit_of(here, 0) == 1
    first = first_head((0,), heads)
    for slot in range(held):
        part = pl.ds(pl.multiple_of((first + slot) * per, 8), per)
        total = pl.ds(width + first + slot, 1)
        whole_ref[slot * per : (slot + 1) * per] = join(
            upper, mine_ref[part], mine_ref[total], other_ref[part], other_ref[total]
        )
    other_total = other_ref[width:]
    total = mine_ref[width:] + other_total
    next_ref[...] = jnp.where(upper, other_total, 0.0)
    half = held * per // 2
    side = bit_of(here, 1)
    cuts = len(message_refs) // 2
    size = half // cuts
    for at, ref in enumerate(message_refs):
        start = (side if at < cuts else 1 - side) * half + at % cuts * size
        ref[:size] = whole_ref[pl.ds(pl.multiple_of(start, 8), size)]
        ref[size:] = total


def make_chip(mine, other, heads, cuts):
    rows, lanes = mine.shape
    half = (rows - heads) // 2
    *messages, prefix = call(
        chip_kernel,
        "chip",
        [mine, other],
        [
            *[((half // 2 // cuts + heads, lanes), jnp.float32)] * (2 * cuts),
            ((heads, lanes), jnp.float32),
        ],
        [pltpu.VMEM((half, lanes), jnp.float32)],
    )
    return messages[:cuts], messages[cuts:], prefix


def merge_kernel(bit, offset, *refs):
    mine_ref, other_ref, prefix_ref = refs[:3]
    merged_ref, next_ref = refs[-2:]
    heads = prefix_ref.shape[0]
    rows = mine_ref.shape[0] - heads
    per = mine_ref.shape[1]
    upper = bit_of(place(), bit) == 1
    first = first_head((0,) * SPLIT_BITS, heads) + offset
    for slot in range(rows // per):
        part = slice(slot * per, (slot + 1) * per)
        total = pl.ds(rows + first + slot, 1)
        merged_ref[part] = join(
            upper, mine_ref[part], mine_ref[total], other_ref[part], other_ref[total]
        )
    other_total = other_ref[rows:]
    merged_ref[rows:] = mine_ref[rows:] + other_total
    next_ref[...] = prefix_ref[...] + jnp.where(upper, other_total, 0.0)


def merge(bit, offset, mine, other, prefix, tokens=()):
    return call(
        functools.partial(merge_kernel, bit, offset),
        f"merge{bit}{offset}",
        [mine, other, prefix, *tokens],
        [(mine.shape, jnp.float32), (prefix.shape, jnp.float32)],
    )


def pack_kernel(takes, *refs):
    out_ref = refs[-1]
    at = 0
    for ref, rows in zip(refs, takes):
        out_ref[at : at + rows] = ref[:rows]
        at += rows


def pack(name, pieces, tokens=()):
    takes = [rows for _, rows in pieces]
    lanes = pieces[0][0].shape[1]
    return call(
        functools.partial(pack_kernel, takes),
        name,
        [*[array for array, _ in pieces], *tokens],
        [((sum(takes), lanes), jnp.float32)],
    )[0]


def level_scale(bit, first_level, prefix_ref, sums_ref, weight_ref, tokens):
    active = jnp.where(bit_of(place(), bit) == 1, 1.0, 0.0)
    reach = jnp.exp(sums_ref[1, :, tokens] + spread_lanes(prefix_ref[:, :1], SPAN))
    return reach * weight_ref[first_level + bit, :, tokens] * active


def gather_work(quarters, part_refs, heads, per):
    work = []
    for far, pieces in quarters:
        first = first_head(far, heads)
        for slot in range(heads // 4):
            states = []
            for level, index, start in pieces:
                if start is None:
                    rows = pl.ds(pl.multiple_of((first + slot) * per, 128), per)
                else:
                    rows = slice(start + slot * per, start + (slot + 1) * per)
                states.append((level, part_refs[index][rows].astype(jnp.bfloat16)))
            work.append((first + slot, states))
    return work


def add_found(mixed, queries, head, states, scale_ref):
    for level, state in states:
        found = lax.dot_general(state, queries, NT, preferred_element_type=jnp.float32)
        mixed = mixed + found * scale_ref[level, pl.ds(head, 1)]
    return mixed


def reach_kernel(quarters, first_level, bits, *refs):
    mixed_ref, q_ref, sums_ref, weight_ref = refs[:4]
    prefix_refs = refs[4 : 4 + len(bits)]
    part_refs = refs[4 + len(bits) :]
    out_ref, done_ref, scale_ref = refs[-3:]
    done_ref[...] = jnp.zeros_like(done_ref)
    heads = weight_ref.shape[1]
    head_width = mixed_ref.shape[0] // heads
    work = gather_work(quarters, part_refs, heads, head_width)
    for span in range(q_ref.shape[0] // SPAN):
        tokens = slice(span * SPAN, (span + 1) * SPAN)
        queries = q_ref[tokens]
        for level, (bit, prefix_ref) in enumerate(zip(bits, prefix_refs)):
            scale_ref[level] = level_scale(
                bit, first_level, prefix_ref, sums_ref, weight_ref, tokens
            )
        for head, states in work:
            rows = pl.ds(pl.multiple_of(head * head_width, 128), head_width)
            out_ref[rows, tokens] = add_found(
                mixed_ref[rows, tokens], queries, head, states, scale_ref
            )


def add_levels(quarters, first_level, bits, shared, prefixes, parts):
    mixed, _, _, level_weight = shared
    return call(
        functools.partial(reach_kernel, quarters, first_level, bits),
        "reach",
        [*shared, *prefixes, *parts],
        [(mixed.shape, jnp.float32), ((8, 128), jnp.float32)],
        [pltpu.VMEM((len(bits), level_weight.shape[1], SPAN), jnp.float32)],
        aliases={0: 0},
    )


def finish_kernel(quarters, first_level, bits, has_token, *refs):
    mixed_ref, q_ref, sums_ref, weight_ref, gain_ref = refs[:5]
    prefix_refs = refs[5 : 5 + len(bits)]
    part_refs = refs[5 + len(bits) :]
    out_ref, scale_ref, sent = refs[-3:]
    out_hbm = refs[-5] if has_token else refs[-4]
    if has_token:
        refs[-4][...] = jnp.zeros_like(refs[-4])
    heads = weight_ref.shape[1]
    head_width = mixed_ref.shape[0] // heads
    count = heads // 4
    size = count * head_width
    work = gather_work(quarters, part_refs, heads, head_width)
    gains = []
    for head, _ in work:
        row = jnp.broadcast_to(gain_ref[pl.ds(head, 1)], (8, head_width))
        gains.append(row.T[:, :1])
    copies = []
    for span in range(q_ref.shape[0] // SPAN):
        tokens = slice(span * SPAN, (span + 1) * SPAN)
        queries = q_ref[tokens]
        for level, (bit, prefix_ref) in enumerate(zip(bits, prefix_refs)):
            scale_ref[level] = level_scale(
                bit, first_level, prefix_ref, sums_ref, weight_ref, tokens
            )
        for at, (head, states) in enumerate(work):
            rows = pl.ds(pl.multiple_of(head * head_width, 128), head_width)
            mixed = add_found(mixed_ref[rows, tokens], queries, head, states, scale_ref)
            square = jnp.mean(mixed * mixed, axis=0, keepdims=True)
            normed = mixed * lax.rsqrt(square + EPS) * gains[at]
            columns = slice(at * head_width, (at + 1) * head_width)
            out_ref[tokens, columns] = normed.astype(jnp.bfloat16).T
        for at, (far, _) in enumerate(quarters):
            columns = pl.ds(pl.multiple_of(first_head(far, heads) * head_width, 128), size)
            copy = pltpu.make_async_copy(
                out_ref.at[tokens, at * size : (at + 1) * size],
                out_hbm.at[tokens, columns],
                sent.at[len(copies)],
            )
            copy.start()
            copies.append(copy)
    for copy in copies:
        copy.wait()


def finish(quarters, first_level, bits, shared, prefixes, parts, begun, has_token):
    mixed, queries, sums, level_weight, gain = shared
    width, tokens = mixed.shape
    heads = level_weight.shape[1]
    inputs = [*shared, *prefixes, *parts]
    specs = [HELD] * len(inputs)
    inputs = [hold(array) for array in inputs]
    out = pl.BlockSpec(memory_space=pltpu.HBM)
    aliases = {}
    if begun is not None:
        aliases = {len(inputs): 0}
        specs.append(out)
        inputs.append(begun)
    shapes = [jax.ShapeDtypeStruct((tokens, width), jnp.bfloat16)]
    if has_token:
        shapes.append(pltpu.VMEM((8, 128), jnp.float32))
    return pl.pallas_call(
        functools.partial(finish_kernel, quarters, first_level, bits, has_token),
        in_specs=specs,
        out_specs=[out, HELD][: len(shapes)],
        out_shape=shapes,
        scratch_shapes=[
            pltpu.VMEM((tokens, len(quarters) * width // 4), jnp.bfloat16),
            pltpu.VMEM((len(bits), heads, SPAN), jnp.float32),
            pltpu.SemaphoreType.DMA((len(quarters) * (tokens // SPAN),)),
        ],
        input_output_aliases=aliases,
        compiler_params=PARAMS,
        name="finish" + "".join(f"{core}{side}" for (core, side), _ in quarters),
    )(*inputs)


def trade(value, mask):
    wide, narrow = lax.axis_size("wide"), lax.axis_size("narrow")

    def ranked(index):
        return index % narrow * wide + index // narrow

    pairs = [(ranked(source), ranked(source ^ mask)) for source in range(wide * narrow)]
    return lax.ppermute(value, AXES, pairs)


def per_device(queries, keys, values, log_decay, level_weight, norm_gain):
    heads = log_decay.shape[0]
    tokens, width = values.shape
    per = width // heads
    spans = tokens // SPAN
    group_bits = heads.bit_length() - 1
    bits = (lax.axis_size("wide") * lax.axis_size("narrow")).bit_length() - 1
    first_level = level_weight.shape[0] - bits
    gain = norm_gain.reshape(heads, per)
    message, local, sums, totals, queries, keys, values, level_weight, gain = make_states(
        queries, keys, values, log_decay, level_weight, gain
    )
    shared = (queries, keys, values, sums, totals, level_weight, local)
    last = bits - 1
    two = 2 * per
    size = two // CUTS
    sides = [(core, side) for core in (0, 1) for side in (0, 1)]
    other = trade(message, 1)
    zero = jnp.zeros((heads, 128), jnp.float32)
    chunks, give, prefix = make_chip(message, other, heads, CUTS)
    prefixes = [zero, prefix]
    found, across = {}, {}
    mixed, at = None, 0

    def both(name, messages, tokens=()):
        return pack(name, [(state, size) for state in messages], tokens)

    for bit in range(1, bits):
        found[bit] = [trade(chunk, 2**bit) for chunk in (give if bit == 1 else chunks)]
        if bit == 1:
            rest = trade(both("rest", chunks), 2)
        waits = ()
        if at < spans:
            stop = spans if bit == last else at + 1
            mixed, *waits = mix_local(at, stop, shared, mixed, chunks[-1:], bit < last)
            at = stop
        if bit < last:
            merged, tokens_of = [], ()
            for offset, (chunk, state) in enumerate(zip(chunks, found[bit])):
                tokens_of = (*tokens_of, *waits) if offset == CUTS - 1 else tokens_of
                chunk, prefix = merge(
                    bit, offset * two // CUTS // per, chunk, state, prefixes[bit], tokens_of
                )
                merged.append(chunk)
                tokens_of = (chunk,)
            chunks = merged
            prefixes.append(prefix)
            found[bit] = both(f"found{bit}", found[bit], chunks[-1:])
            if bit > 1:
                across[bit] = trade(found[bit], 2)

    quarters = [((core, side), [(0, 0, None)]) for core, side in sides]
    shared = (mixed, queries, sums, level_weight)
    mixed, token = add_levels(quarters, first_level, [0], shared, [zero], [other])
    ended = token
    ended = pack("ended0", [(ended, 8)], found[last])
    ended = pack("ended1", [(ended, 8)])
    ended = pack("ended2", [(ended, 8)])
    early = list(range(2, last))
    pieces = [(found[1], two), (rest, two)]
    for bit in early:
        pieces += [(found[bit], two), (across[bit], two)]
    near = pack("near", pieces, (ended,))
    far = trade(near, 1)
    middle = [1, *early]
    ahead = [prefixes[bit] for bit in middle]

    def states_of(side, index, first):
        return [(first + slot, index, (2 * slot + side) * two) for slot in range(len(middle))]

    shared = (mixed, queries, sums, level_weight, gain)
    every = (first_level, [last, *middle], shared, [prefixes[last], *ahead])
    state = both("state", found[last])
    beside = trade(state, 2)
    quarters = {(core, side): [(0, 0, 0), *states_of(side, 1, 1)] for core, side in sides}
    (out,) = finish([((0, 0), quarters[0, 0])], *every, [state, near], None, False)
    out, token = finish([((1, 0), quarters[1, 0])], *every, [trade(state, 1), far], out, True)
    beside = pack("beside", [(beside, two)], (token,))
    (out,) = finish([((0, 1), quarters[0, 1])], *every, [beside, near], out, False)
    return finish([((1, 1), quarters[1, 1])], *every, [trade(beside, 1), far], out, False)[0]


def solution(mesh):
    placed = (
        P(("wide", "narrow"), None),
        P(("wide", "narrow"), None),
        P(("wide", "narrow"), None),
        P(None, ("wide", "narrow")),
        P(None, None, ("wide", "narrow")),
        P(),
    )
    return jax.shard_map(
        per_device,
        mesh=mesh,
        in_specs=placed,
        out_specs=P(("wide", "narrow"), None),
        check_vma=False,
    )
```

```python
import functools

import jax
import jax.numpy as jnp
from jax import lax
from jax.experimental import pallas as pl
from jax.experimental.pallas import tpu as pltpu
from jax.sharding import PartitionSpec as P

SPAN = 256
SPLIT_BITS = 2
CUTS = 2
EPS = 1e-05
AXES = ("narrow", "wide")
NT = (((1,), (1,)), ((), ()))
PARAMS = pltpu.CompilerParams(vmem_limit_bytes=32 * 1024 * 1024)
HELD = pl.BlockSpec(memory_space=pltpu.VMEM)


def place():
    return lax.axis_index("wide") * lax.axis_size("narrow") + lax.axis_index("narrow")


def bit_of(value, bit):
    return jnp.bitwise_and(jnp.right_shift(value, bit), 1)


def spread_lanes(column, width):
    return jnp.broadcast_to(column, (column.shape[0], width))


ANYWHERE = pl.BlockSpec(memory_space=pl.ANY)


def hold(array):
    return pltpu.with_memory_space_constraint(array, pltpu.VMEM)


def call(kernel, name, inputs, outputs, scratch=(), in_specs=None, aliases=None):
    specs = in_specs or [HELD] * len(inputs)
    inputs = [hold(array) if spec is HELD else array for array, spec in zip(inputs, specs)]
    return pl.pallas_call(
        kernel,
        in_specs=specs,
        out_specs=[HELD] * len(outputs),
        out_shape=[pltpu.VMEM(shape, dtype) for shape, dtype in outputs],
        scratch_shapes=list(scratch),
        input_output_aliases=aliases or {},
        compiler_params=PARAMS,
        name=name,
    )(*inputs)


def running_sums(rows):
    high = rows.astype(jnp.bfloat16)
    rest = rows - high.astype(jnp.float32)
    middle = rest.astype(jnp.bfloat16)
    low = (rest - middle.astype(jnp.float32)).astype(jnp.bfloat16)
    width = rows.shape[1]
    source = lax.broadcasted_iota(jnp.int32, (width, width), 0)
    target = lax.broadcasted_iota(jnp.int32, (width, width), 1)
    upto = jnp.where(source <= target, 1.0, 0.0).astype(jnp.bfloat16)
    sums = jnp.dot(
        jnp.concatenate([high, middle, low], axis=0), upto, preferred_element_type=jnp.float32
    )
    count = rows.shape[0]
    return sums[:count] + (sums[count : 2 * count] + sums[2 * count :])


def state_kernel(*refs):
    q_hbm, k_hbm, v_hbm, decay_hbm, weight_hbm, gain_hbm = refs[:6]
    message_ref, local_ref, sums_ref, totals_ref = refs[6:10]
    q_ref, k_ref, v_ref, weight_ref, gain_ref, decay_ref, arrived = refs[10:]
    heads, tokens = decay_ref.shape
    head_width = v_ref.shape[1] // heads
    spans = tokens // SPAN
    rows_of = [slice(span * SPAN, (span + 1) * SPAN) for span in range(spans)]
    loads = [(decay_hbm, decay_ref), (k_hbm, k_ref)]
    loads += [(v_hbm.at[rows], v_ref.at[rows]) for rows in rows_of]
    loads += [(q_hbm, q_ref), (weight_hbm, weight_ref), (gain_hbm, gain_ref)]
    copies = [
        pltpu.make_async_copy(source, target, arrived.at[at])
        for at, (source, target) in enumerate(loads)
    ]
    for copy in copies:
        copy.start()
    copies[0].wait()
    within = running_sums(jnp.concatenate([decay_ref[:, rows] for rows in rows_of], axis=0))
    run = jnp.zeros((heads, 128), jnp.float32)
    fades, wholes = [], []
    for span, rows in enumerate(rows_of):
        here = within[span * heads : (span + 1) * heads]
        last = here[:, SPAN - 1 :]
        total = spread_lanes(last, 128)
        sums_ref[0, :, rows] = here
        sums_ref[1, :, rows] = here + spread_lanes(run[:, :1], SPAN)
        totals_ref[span] = total
        run = run + total
        fades.append(jnp.exp(spread_lanes(last, SPAN) - here))
        wholes.append(jnp.exp(total))
    copies[1].wait()
    across = [k_ref[rows].astype(jnp.float32).T for rows in rows_of]
    for copy in copies[2 : 2 + spans]:
        copy.wait()
    for head in range(heads):
        columns = slice(head * head_width, (head + 1) * head_width)
        states = []
        for span, rows in enumerate(rows_of):
            faded = (across[span] * fades[span][head : head + 1]).astype(jnp.bfloat16)
            states.append(
                jnp.dot(faded, v_ref[rows, columns], preferred_element_type=jnp.float32)
            )
        at = 0
        size = 1
        while size < spans:
            for first in range(0, spans, 2 * size):
                group = states[first]
                for span in range(first + 1, first + size):
                    group = group * wholes[span][head : head + 1] + states[span]
                local_ref[at, :, columns] = group.astype(jnp.bfloat16)
                at += 1
            size *= 2
        group = states[0]
        for span in range(1, spans):
            group = group * wholes[span][head : head + 1] + states[span]
        message_ref[columns] = group.T
    message_ref[heads * head_width :] = run
    for copy in copies[2 + spans :]:
        copy.wait()


def make_states(queries, keys, values, log_decay, level_weight, gain):
    tokens, key_width = keys.shape
    heads = log_decay.shape[0]
    width = values.shape[1]
    spans = tokens // SPAN
    inputs = [queries, keys, values, log_decay, level_weight, gain]
    kept = [queries, keys, values, level_weight, gain]
    return call(
        state_kernel,
        "states",
        [pltpu.with_memory_space_constraint(array, pltpu.HBM) for array in inputs],
        [
            ((width + heads, key_width), jnp.float32),
            ((spans - 1, key_width, width), jnp.bfloat16),
            ((2, heads, tokens), jnp.float32),
            ((spans, heads, 128), jnp.float32),
            *[(array.shape, array.dtype) for array in kept],
        ],
        [
            pltpu.VMEM(log_decay.shape, jnp.float32),
            pltpu.SemaphoreType.DMA((spans + 5,)),
        ],
        [pl.BlockSpec(memory_space=pltpu.HBM)] * len(inputs),
    )


def local_kernel(first, last, has_token, *refs):
    q_ref, k_ref, v_ref, sums_ref, totals_ref, weight_ref, local_ref = refs[:7]
    if has_token:
        mixed_ref, done_ref = refs[-2:]
        done_ref[...] = jnp.zeros_like(done_ref)
    else:
        mixed_ref = refs[-1]
    heads = weight_ref.shape[1]
    head_width = v_ref.shape[1] // heads
    spans = totals_ref.shape[0]
    local_bits = spans.bit_length() - 1
    half = SPAN // 2
    source = lax.broadcasted_iota(jnp.int32, (half, half), 0)
    target = lax.broadcasted_iota(jnp.int32, (half, half), 1)
    causal = source <= target
    empty = jnp.zeros((half, half), jnp.bfloat16)

    for span in range(first, last):
        tokens = slice(span * SPAN, (span + 1) * SPAN)
        queries = q_ref[tokens]
        scores = lax.dot_general(
            k_ref[tokens], queries, NT, preferred_element_type=jnp.float32
        )
        within = sums_ref[0, :, tokens]
        within_down = within.T
        weight = weight_ref[0, :, tokens]
        values_across = v_ref[tokens].T

        def mix(head, low, high):
            rows = slice(low * half, (low + 1) * half)
            columns = slice(high * half, (high + 1) * half)
            gap = within[head : head + 1, columns] - within_down[rows, head : head + 1]
            if low == high:
                gap = jnp.where(causal, gap, -1e30)
            mixing = scores[rows, columns] * jnp.exp(gap) * weight[head : head + 1, columns]
            return mixing.astype(jnp.bfloat16)

        levels = []
        offset = 0
        for bit in range(local_bits):
            if span >> bit & 1:
                since = within
                for back in range(1, span % 2**bit + 1):
                    since = since + spread_lanes(totals_ref[span - back][:, :1], SPAN)
                scale = jnp.exp(since) * weight_ref[1 + bit, :, tokens]
                levels.append((local_ref[offset + (span >> (bit + 1))].T, scale))
            offset += spans >> (bit + 1)
        for head in range(heads):
            rows = slice(head * head_width, (head + 1) * head_width)
            mixing = jnp.concatenate(
                [
                    jnp.concatenate([mix(head, 0, 0), mix(head, 0, 1)], axis=1),
                    jnp.concatenate([empty, mix(head, 1, 1)], axis=1),
                ],
                axis=0,
            )
            mixed = jnp.dot(values_across[rows], mixing, preferred_element_type=jnp.float32)
            for level, scale in levels:
                found = lax.dot_general(
                    level[rows], queries, NT, preferred_element_type=jnp.float32
                )
                mixed = mixed + found * scale[head : head + 1]
            mixed_ref[rows, tokens] = mixed


def mix_local(first, last, shared, mixed, tokens, has_token):
    queries, keys, values, sums, totals, level_weight, local = shared
    rest = [] if mixed is None else [mixed]
    return call(
        functools.partial(local_kernel, first, last, has_token),
        f"local{first}",
        [*shared, *rest, *tokens],
        [(values.shape[::-1], jnp.float32), ((8, 128), jnp.float32)][: 1 + has_token],
        aliases={7: 0} if rest else None,
    )


def join(upper, mine, mine_total, other, other_total):
    fade = jnp.exp(jnp.where(upper, mine_total, other_total))
    return jnp.where(upper, other * fade + mine, mine * fade + other)


def first_head(far, heads):
    here = place()
    first = 0
    for bit, flip in enumerate(far):
        first = first + jnp.bitwise_xor(bit_of(here, bit), flip) * (heads >> (bit + 1))
    return first


def chip_kernel(mine_ref, other_ref, *refs):
    *message_refs, next_ref, whole_ref = refs
    heads = next_ref.shape[0]
    width = mine_ref.shape[0] - heads
    per = width // heads
    held = whole_ref.shape[0] // per
    here = place()
    upper = bit_of(here, 0) == 1
    first = first_head((0,), heads)
    for slot in range(held):
        part = pl.ds(pl.multiple_of((first + slot) * per, 8), per)
        total = pl.ds(width + first + slot, 1)
        whole_ref[slot * per : (slot + 1) * per] = join(
            upper, mine_ref[part], mine_ref[total], other_ref[part], other_ref[total]
        )
    other_total = other_ref[width:]
    total = mine_ref[width:] + other_total
    next_ref[...] = jnp.where(upper, other_total, 0.0)
    half = held * per // 2
    side = bit_of(here, 1)
    cuts = len(message_refs) // 2
    size = half // cuts
    for at, ref in enumerate(message_refs):
        start = (side if at < cuts else 1 - side) * half + at % cuts * size
        ref[:size] = whole_ref[pl.ds(pl.multiple_of(start, 8), size)]
        ref[size:] = total


def make_chip(mine, other, heads, cuts):
    rows, lanes = mine.shape
    half = (rows - heads) // 2
    *messages, prefix = call(
        chip_kernel,
        "chip",
        [mine, other],
        [
            *[((half // 2 // cuts + heads, lanes), jnp.float32)] * (2 * cuts),
            ((heads, lanes), jnp.float32),
        ],
        [pltpu.VMEM((half, lanes), jnp.float32)],
    )
    return messages[:cuts], messages[cuts:], prefix


def merge_kernel(bit, offset, has_prefix, *refs):
    mine_ref, other_ref, prefix_ref = refs[:3]
    merged_ref = refs[-2] if has_prefix else refs[-1]
    heads = prefix_ref.shape[0]
    rows = mine_ref.shape[0] - heads
    per = mine_ref.shape[1]
    upper = bit_of(place(), bit) == 1
    first = first_head((0,) * SPLIT_BITS, heads) + offset
    for slot in range(rows // per):
        part = slice(slot * per, (slot + 1) * per)
        total = pl.ds(rows + first + slot, 1)
        merged_ref[part] = join(
            upper, mine_ref[part], mine_ref[total], other_ref[part], other_ref[total]
        )
    other_total = other_ref[rows:]
    merged_ref[rows:] = mine_ref[rows:] + other_total
    if has_prefix:
        refs[-1][...] = prefix_ref[...] + jnp.where(upper, other_total, 0.0)


def merge(bit, offset, has_prefix, mine, other, prefix, tokens=()):
    return call(
        functools.partial(merge_kernel, bit, offset, has_prefix),
        f"merge{bit}{offset}",
        [mine, other, prefix, *tokens],
        [(mine.shape, jnp.float32), (prefix.shape, jnp.float32)][: 1 + has_prefix],
    )


def pack_kernel(takes, *refs):
    out_ref = refs[-1]
    at = 0
    for ref, rows in zip(refs, takes):
        out_ref[at : at + rows] = ref[:rows]
        at += rows


def pack(name, pieces, tokens=()):
    takes = [rows for _, rows in pieces]
    lanes = pieces[0][0].shape[1]
    return call(
        functools.partial(pack_kernel, takes),
        name,
        [*[array for array, _ in pieces], *tokens],
        [((sum(takes), lanes), jnp.float32)],
    )[0]


def level_scale(bit, first_level, prefix_ref, sums_ref, weight_ref, tokens):
    active = jnp.where(bit_of(place(), bit) == 1, 1.0, 0.0)
    reach = jnp.exp(sums_ref[1, :, tokens] + spread_lanes(prefix_ref[:, :1], SPAN))
    return reach * weight_ref[first_level + bit, :, tokens] * active


def gather_work(quarters, part_refs, heads, per):
    work = []
    for far, pieces in quarters:
        first = first_head(far, heads)
        for slot in range(heads // 4):
            states = []
            for level, index, start in pieces:
                if start is None:
                    rows = pl.ds(pl.multiple_of((first + slot) * per, 128), per)
                else:
                    rows = slice(start + slot * per, start + (slot + 1) * per)
                states.append((level, part_refs[index][rows].astype(jnp.bfloat16)))
            work.append((first + slot, states))
    return work


def add_found(mixed, queries, head, states, scale_ref):
    for level, state in states:
        found = lax.dot_general(state, queries, NT, preferred_element_type=jnp.float32)
        mixed = mixed + found * scale_ref[level, pl.ds(head, 1)]
    return mixed


def reach_kernel(quarters, first_level, bits, *refs):
    mixed_ref, q_ref, sums_ref, weight_ref = refs[:4]
    prefix_refs = refs[4 : 4 + len(bits)]
    part_refs = refs[4 + len(bits) :]
    out_ref, done_ref, scale_ref = refs[-3:]
    done_ref[...] = jnp.zeros_like(done_ref)
    heads = weight_ref.shape[1]
    head_width = mixed_ref.shape[0] // heads
    work = gather_work(quarters, part_refs, heads, head_width)
    for span in range(q_ref.shape[0] // SPAN):
        tokens = slice(span * SPAN, (span + 1) * SPAN)
        queries = q_ref[tokens]
        for level, (bit, prefix_ref) in enumerate(zip(bits, prefix_refs)):
            scale_ref[level] = level_scale(
                bit, first_level, prefix_ref, sums_ref, weight_ref, tokens
            )
        for head, states in work:
            rows = pl.ds(pl.multiple_of(head * head_width, 128), head_width)
            out_ref[rows, tokens] = add_found(
                mixed_ref[rows, tokens], queries, head, states, scale_ref
            )


def add_levels(quarters, first_level, bits, shared, prefixes, parts):
    mixed, _, _, level_weight = shared
    return call(
        functools.partial(reach_kernel, quarters, first_level, bits),
        "reach",
        [*shared, *prefixes, *parts],
        [(mixed.shape, jnp.float32), ((8, 128), jnp.float32)],
        [pltpu.VMEM((len(bits), level_weight.shape[1], SPAN), jnp.float32)],
        aliases={0: 0},
    )


def finish_kernel(quarters, first_level, bits, has_token, *refs):
    mixed_ref, q_ref, sums_ref, weight_ref, gain_ref = refs[:5]
    prefix_refs = refs[5 : 5 + len(bits)]
    part_refs = refs[5 + len(bits) :]
    out_ref, scale_ref, sent = refs[-3:]
    out_hbm = refs[-5] if has_token else refs[-4]
    if has_token:
        refs[-4][...] = jnp.zeros_like(refs[-4])
    heads = weight_ref.shape[1]
    head_width = mixed_ref.shape[0] // heads
    count = heads // 4
    size = count * head_width
    work = gather_work(quarters, part_refs, heads, head_width)
    gains = []
    for head, _ in work:
        row = jnp.broadcast_to(gain_ref[pl.ds(head, 1)], (8, head_width))
        gains.append(row.T[:, :1])
    copies = []
    for span in range(q_ref.shape[0] // SPAN):
        tokens = slice(span * SPAN, (span + 1) * SPAN)
        queries = q_ref[tokens]
        for level, (bit, prefix_ref) in enumerate(zip(bits, prefix_refs)):
            scale_ref[level] = level_scale(
                bit, first_level, prefix_ref, sums_ref, weight_ref, tokens
            )
        for at, (head, states) in enumerate(work):
            rows = pl.ds(pl.multiple_of(head * head_width, 128), head_width)
            mixed = add_found(mixed_ref[rows, tokens], queries, head, states, scale_ref)
            square = jnp.mean(mixed * mixed, axis=0, keepdims=True)
            normed = mixed * lax.rsqrt(square + EPS) * gains[at]
            columns = slice(at * head_width, (at + 1) * head_width)
            out_ref[tokens, columns] = normed.astype(jnp.bfloat16).T
        for at, (far, _) in enumerate(quarters):
            columns = pl.ds(pl.multiple_of(first_head(far, heads) * head_width, 128), size)
            copy = pltpu.make_async_copy(
                out_ref.at[tokens, at * size : (at + 1) * size],
                out_hbm.at[tokens, columns],
                sent.at[len(copies)],
            )
            copy.start()
            copies.append(copy)
    for copy in copies:
        copy.wait()


def finish(quarters, first_level, bits, shared, prefixes, parts, begun, has_token):
    mixed, queries, sums, level_weight, gain = shared
    width, tokens = mixed.shape
    heads = level_weight.shape[1]
    inputs = [*shared, *prefixes, *parts]
    specs = [HELD] * len(inputs)
    inputs = [hold(array) for array in inputs]
    out = pl.BlockSpec(memory_space=pltpu.HBM)
    aliases = {}
    if begun is not None:
        aliases = {len(inputs): 0}
        specs.append(out)
        inputs.append(begun)
    shapes = [jax.ShapeDtypeStruct((tokens, width), jnp.bfloat16)]
    if has_token:
        shapes.append(pltpu.VMEM((8, 128), jnp.float32))
    return pl.pallas_call(
        functools.partial(finish_kernel, quarters, first_level, bits, has_token),
        in_specs=specs,
        out_specs=[out, HELD][: len(shapes)],
        out_shape=shapes,
        scratch_shapes=[
            pltpu.VMEM((tokens, len(quarters) * width // 4), jnp.bfloat16),
            pltpu.VMEM((len(bits), heads, SPAN), jnp.float32),
            pltpu.SemaphoreType.DMA((len(quarters) * (tokens // SPAN),)),
        ],
        input_output_aliases=aliases,
        compiler_params=PARAMS,
        name="finish" + "".join(f"{core}{side}" for (core, side), _ in quarters),
    )(*inputs)


def trade(value, mask):
    wide, narrow = lax.axis_size("wide"), lax.axis_size("narrow")

    def ranked(index):
        return index % narrow * wide + index // narrow

    pairs = [(ranked(source), ranked(source ^ mask)) for source in range(wide * narrow)]
    return lax.ppermute(value, AXES, pairs)


def per_device(queries, keys, values, log_decay, level_weight, norm_gain):
    heads = log_decay.shape[0]
    tokens, width = values.shape
    per = width // heads
    spans = tokens // SPAN
    group_bits = heads.bit_length() - 1
    bits = (lax.axis_size("wide") * lax.axis_size("narrow")).bit_length() - 1
    first_level = level_weight.shape[0] - bits
    gain = norm_gain.reshape(heads, per)
    message, local, sums, totals, queries, keys, values, level_weight, gain = make_states(
        queries, keys, values, log_decay, level_weight, gain
    )
    shared = (queries, keys, values, sums, totals, level_weight, local)
    last = bits - 1
    two = 2 * per
    size = two // CUTS
    sides = [(core, side) for core in (0, 1) for side in (0, 1)]
    other = trade(message, 1)
    zero = jnp.zeros((heads, 128), jnp.float32)
    chunks, give, prefix = make_chip(message, other, heads, CUTS)
    prefixes = [zero, prefix]
    found, across = {}, {}
    mixed, at = None, 0

    def both(name, messages, tokens=()):
        return pack(name, [(state, size) for state in messages], tokens)

    for bit in range(1, bits):
        found[bit] = [trade(chunk, 2**bit) for chunk in (give if bit == 1 else chunks)]
        if bit == 1:
            rest = trade(both("rest", chunks), 2)
        waits = []
        if bit < 3 or bit == last:
            stop = spans if bit == last else at + 1
            mixed, *waits = mix_local(at, stop, shared, mixed, chunks[-1:], bit < last)
            at = stop
        if bit == 3:
            waits.append(rest)
        if bit < last:
            merged = []
            for offset, (chunk, state) in enumerate(zip(chunks, found[bit])):
                ending = offset == CUTS - 1
                tokens_of = [*merged[-1:], *(waits if ending else ())]
                chunk, *after = merge(
                    bit, offset, ending, chunk, state, prefixes[bit], tokens_of
                )
                merged.append(chunk)
            chunks = merged
            prefixes += after
            found[bit] = both(f"found{bit}", found[bit], chunks[-1:])
            if bit > 1:
                across[bit] = trade(found[bit], 2)

    quarters = [((core, side), [(0, 0, None)]) for core, side in sides]
    shared = (mixed, queries, sums, level_weight)
    mixed, token = add_levels(quarters, first_level, [0], shared, [zero], [other])
    ended = token
    ended = pack("ended0", [(ended, 8)], found[last])
    ended = pack("ended1", [(ended, 8)])
    ended = pack("ended2", [(ended, 8)])
    early = list(range(2, last))
    pieces = [(found[1], two), (rest, two)]
    for bit in early:
        pieces += [(found[bit], two), (across[bit], two)]
    near = pack("near", pieces, (ended,))
    far = trade(near, 1)
    middle = [1, *early]
    ahead = [prefixes[bit] for bit in middle]

    def states_of(side, index, first):
        return [(first + slot, index, (2 * slot + side) * two) for slot in range(len(middle))]

    shared = (mixed, queries, sums, level_weight, gain)
    every = (first_level, [last, *middle], shared, [prefixes[last], *ahead])
    state = both("state", found[last])
    beside = trade(state, 2)
    quarters = {(core, side): [(0, 0, 0), *states_of(side, 1, 1)] for core, side in sides}
    (out,) = finish([((0, 0), quarters[0, 0])], *every, [state, near], None, False)
    out, token = finish([((1, 0), quarters[1, 0])], *every, [trade(state, 1), far], out, True)
    beside = pack("beside", [(beside, two)], (token,))
    (out,) = finish([((0, 1), quarters[0, 1])], *every, [beside, near], out, False)
    return finish([((1, 1), quarters[1, 1])], *every, [trade(beside, 1), far], out, False)[0]


def solution(mesh):
    placed = (
        P(("wide", "narrow"), None),
        P(("wide", "narrow"), None),
        P(("wide", "narrow"), None),
        P(None, ("wide", "narrow")),
        P(None, None, ("wide", "narrow")),
        P(),
    )
    return jax.shard_map(
        per_device,
        mesh=mesh,
        in_specs=placed,
        out_specs=P(("wide", "narrow"), None),
        check_vma=False,
    )
```

```python
import functools

import jax
import jax.numpy as jnp
from jax import lax
from jax.experimental import pallas as pl
from jax.experimental.pallas import tpu as pltpu
from jax.sharding import PartitionSpec as P

SPAN = 256
SPLIT_BITS = 2
CUTS = 2
EPS = 1e-05
AXES = ("narrow", "wide")
NT = (((1,), (1,)), ((), ()))
COST = pl.CostEstimate(flops=2_000_000_000, transcendentals=0, bytes_accessed=1_000_000)
PARAMS = pltpu.CompilerParams(vmem_limit_bytes=32 * 1024 * 1024)
HELD = pl.BlockSpec(memory_space=pltpu.VMEM)


def place():
    return lax.axis_index("wide") * lax.axis_size("narrow") + lax.axis_index("narrow")


def bit_of(value, bit):
    return jnp.bitwise_and(jnp.right_shift(value, bit), 1)


def spread_lanes(column, width):
    return jnp.broadcast_to(column, (column.shape[0], width))


ANYWHERE = pl.BlockSpec(memory_space=pl.ANY)


def hold(array):
    return pltpu.with_memory_space_constraint(array, pltpu.VMEM)


def call(kernel, name, inputs, outputs, scratch=(), in_specs=None, aliases=None):
    specs = in_specs or [HELD] * len(inputs)
    inputs = [hold(array) if spec is HELD else array for array, spec in zip(inputs, specs)]
    return pl.pallas_call(
        kernel,
        in_specs=specs,
        out_specs=[HELD] * len(outputs),
        out_shape=[pltpu.VMEM(shape, dtype) for shape, dtype in outputs],
        scratch_shapes=list(scratch),
        input_output_aliases=aliases or {},
        compiler_params=PARAMS,
        cost_estimate=COST,
        name=name,
    )(*inputs)


def running_sums(rows):
    high = rows.astype(jnp.bfloat16)
    rest = rows - high.astype(jnp.float32)
    middle = rest.astype(jnp.bfloat16)
    low = (rest - middle.astype(jnp.float32)).astype(jnp.bfloat16)
    width = rows.shape[1]
    source = lax.broadcasted_iota(jnp.int32, (width, width), 0)
    target = lax.broadcasted_iota(jnp.int32, (width, width), 1)
    upto = jnp.where(source <= target, 1.0, 0.0).astype(jnp.bfloat16)
    sums = jnp.dot(
        jnp.concatenate([high, middle, low], axis=0), upto, preferred_element_type=jnp.float32
    )
    count = rows.shape[0]
    return sums[:count] + (sums[count : 2 * count] + sums[2 * count :])


def state_kernel(*refs):
    q_hbm, k_hbm, v_hbm, decay_hbm, weight_hbm, gain_hbm = refs[:6]
    keep_ref, send_ref, local_ref, sums_ref, totals_ref = refs[6:11]
    q_ref, k_ref, v_ref, weight_ref, gain_ref, decay_ref, held, arrived = refs[11:]
    heads, tokens = decay_ref.shape
    head_width = v_ref.shape[1] // heads
    spans = tokens // SPAN
    rows_of = [slice(span * SPAN, (span + 1) * SPAN) for span in range(spans)]
    loads = [(decay_hbm, decay_ref), (k_hbm, k_ref)]
    loads += [(v_hbm.at[rows], v_ref.at[rows]) for rows in rows_of]
    loads += [(q_hbm, q_ref), (weight_hbm, weight_ref), (gain_hbm, gain_ref)]
    copies = [
        pltpu.make_async_copy(source, target, arrived.at[at])
        for at, (source, target) in enumerate(loads)
    ]
    for copy in copies:
        copy.start()
    copies[0].wait()
    within = running_sums(jnp.concatenate([decay_ref[:, rows] for rows in rows_of], axis=0))
    run = jnp.zeros((heads, 128), jnp.float32)
    fades, wholes = [], []
    for span, rows in enumerate(rows_of):
        here = within[span * heads : (span + 1) * heads]
        last = here[:, SPAN - 1 :]
        total = spread_lanes(last, 128)
        sums_ref[0, :, rows] = here
        sums_ref[1, :, rows] = here + spread_lanes(run[:, :1], SPAN)
        totals_ref[span] = total
        run = run + total
        fades.append(jnp.exp(spread_lanes(last, SPAN) - here))
        wholes.append(jnp.exp(total))
    copies[1].wait()
    across = [k_ref[rows].astype(jnp.float32).T for rows in rows_of]
    for copy in copies[2 : 2 + spans]:
        copy.wait()
    for head in range(heads):
        columns = slice(head * head_width, (head + 1) * head_width)
        states = []
        for span, rows in enumerate(rows_of):
            faded = (across[span] * fades[span][head : head + 1]).astype(jnp.bfloat16)
            states.append(
                jnp.dot(faded, v_ref[rows, columns], preferred_element_type=jnp.float32)
            )
        at = 0
        size = 1
        while size < spans:
            for first in range(0, spans, 2 * size):
                group = states[first]
                for span in range(first + 1, first + size):
                    group = group * wholes[span][head : head + 1] + states[span]
                local_ref[at, :, columns] = group.astype(jnp.bfloat16)
                at += 1
            size *= 2
        group = states[0]
        for span in range(1, spans):
            group = group * wholes[span][head : head + 1] + states[span]
        held[columns] = group.T
    half = held.shape[0] // 2
    core = bit_of(place(), 0)
    keep_ref[:half] = held[pl.ds(pl.multiple_of(core * half, 8), half)]
    send_ref[:half] = held[pl.ds(pl.multiple_of((1 - core) * half, 8), half)]
    keep_ref[half:] = run
    send_ref[half:] = run
    for copy in copies[2 + spans :]:
        copy.wait()


def make_states(queries, keys, values, log_decay, level_weight, gain):
    tokens, key_width = keys.shape
    heads = log_decay.shape[0]
    width = values.shape[1]
    spans = tokens // SPAN
    inputs = [queries, keys, values, log_decay, level_weight, gain]
    kept = [queries, keys, values, level_weight, gain]
    return call(
        state_kernel,
        "states",
        [pltpu.with_memory_space_constraint(array, pltpu.HBM) for array in inputs],
        [
            ((width // 2 + heads, key_width), jnp.float32),
            ((width // 2 + heads, key_width), jnp.float32),
            ((spans - 1, key_width, width), jnp.bfloat16),
            ((2, heads, tokens), jnp.float32),
            ((spans, heads, 128), jnp.float32),
            *[(array.shape, array.dtype) for array in kept],
        ],
        [
            pltpu.VMEM(log_decay.shape, jnp.float32),
            pltpu.VMEM((width, key_width), jnp.float32),
            pltpu.SemaphoreType.DMA((spans + 5,)),
        ],
        [pl.BlockSpec(memory_space=pltpu.HBM)] * len(inputs),
    )


def local_kernel(first, last, has_token, *refs):
    q_ref, k_ref, v_ref, sums_ref, totals_ref, weight_ref, local_ref = refs[:7]
    if has_token:
        mixed_ref, done_ref = refs[-2:]
        done_ref[...] = jnp.zeros_like(done_ref)
    else:
        mixed_ref = refs[-1]
    heads = weight_ref.shape[1]
    head_width = v_ref.shape[1] // heads
    spans = totals_ref.shape[0]
    local_bits = spans.bit_length() - 1
    half = SPAN // 2
    source = lax.broadcasted_iota(jnp.int32, (half, half), 0)
    target = lax.broadcasted_iota(jnp.int32, (half, half), 1)
    causal = source <= target
    empty = jnp.zeros((half, half), jnp.bfloat16)

    for span in range(first, last):
        tokens = slice(span * SPAN, (span + 1) * SPAN)
        queries = q_ref[tokens]
        scores = lax.dot_general(
            k_ref[tokens], queries, NT, preferred_element_type=jnp.float32
        )
        within = sums_ref[0, :, tokens]
        within_down = within.T
        weight = weight_ref[0, :, tokens]
        values_across = v_ref[tokens].T

        def mix(head, low, high):
            rows = slice(low * half, (low + 1) * half)
            columns = slice(high * half, (high + 1) * half)
            gap = within[head : head + 1, columns] - within_down[rows, head : head + 1]
            if low == high:
                gap = jnp.where(causal, gap, -1e30)
            mixing = scores[rows, columns] * jnp.exp(gap) * weight[head : head + 1, columns]
            return mixing.astype(jnp.bfloat16)

        levels = []
        offset = 0
        for bit in range(local_bits):
            if span >> bit & 1:
                since = within
                for back in range(1, span % 2**bit + 1):
                    since = since + spread_lanes(totals_ref[span - back][:, :1], SPAN)
                scale = jnp.exp(since) * weight_ref[1 + bit, :, tokens]
                levels.append((local_ref[offset + (span >> (bit + 1))].T, scale))
            offset += spans >> (bit + 1)
        for head in range(heads):
            rows = slice(head * head_width, (head + 1) * head_width)
            mixing = jnp.concatenate(
                [
                    jnp.concatenate([mix(head, 0, 0), mix(head, 0, 1)], axis=1),
                    jnp.concatenate([empty, mix(head, 1, 1)], axis=1),
                ],
                axis=0,
            )
            mixed = jnp.dot(values_across[rows], mixing, preferred_element_type=jnp.float32)
            for level, scale in levels:
                found = lax.dot_general(
                    level[rows], queries, NT, preferred_element_type=jnp.float32
                )
                mixed = mixed + found * scale[head : head + 1]
            mixed_ref[rows, tokens] = mixed


def mix_local(first, last, shared, mixed, tokens, has_token):
    queries, keys, values, sums, totals, level_weight, local = shared
    rest = [] if mixed is None else [mixed]
    return call(
        functools.partial(local_kernel, first, last, has_token),
        f"local{first}",
        [*shared, *rest, *tokens],
        [(values.shape[::-1], jnp.float32), ((8, 128), jnp.float32)][: 1 + has_token],
        aliases={7: 0} if rest else None,
    )


def join(upper, mine, mine_total, other, other_total):
    fade = jnp.exp(jnp.where(upper, mine_total, other_total))
    return jnp.where(upper, other * fade + mine, mine * fade + other)


def first_head(far, heads):
    here = place()
    first = 0
    for bit, flip in enumerate(far):
        first = first + jnp.bitwise_xor(bit_of(here, bit), flip) * (heads >> (bit + 1))
    return first


def chip_kernel(mine_ref, other_ref, *refs):
    *message_refs, next_ref, whole_ref = refs
    heads = next_ref.shape[0]
    width = whole_ref.shape[0]
    held = heads // 2
    per = width // held
    here = place()
    upper = bit_of(here, 0) == 1
    first = first_head((0,), heads)
    for slot in range(held):
        part = slice(slot * per, (slot + 1) * per)
        total = pl.ds(width + first + slot, 1)
        whole_ref[part] = join(
            upper, mine_ref[part], mine_ref[total], other_ref[part], other_ref[total]
        )
    other_total = other_ref[width:]
    total = mine_ref[width:] + other_total
    next_ref[...] = jnp.where(upper, other_total, 0.0)
    half = width // 2
    side = bit_of(here, 1)
    cuts = len(message_refs) // 2
    size = half // cuts
    for at, ref in enumerate(message_refs):
        start = (side if at < cuts else 1 - side) * half + at % cuts * size
        ref[:size] = whole_ref[pl.ds(pl.multiple_of(start, 8), size)]
        ref[size:] = total


def make_chip(mine, other, heads, cuts):
    rows, lanes = mine.shape
    half = rows - heads
    *messages, prefix = call(
        chip_kernel,
        "chip",
        [mine, other],
        [
            *[((half // 2 // cuts + heads, lanes), jnp.float32)] * (2 * cuts),
            ((heads, lanes), jnp.float32),
        ],
        [pltpu.VMEM((half, lanes), jnp.float32)],
    )
    return messages[:cuts], messages[cuts:], prefix


def merge_kernel(bit, offset, has_prefix, *refs):
    mine_ref, other_ref, prefix_ref = refs[:3]
    merged_ref = refs[-2] if has_prefix else refs[-1]
    heads = prefix_ref.shape[0]
    rows = mine_ref.shape[0] - heads
    per = mine_ref.shape[1]
    upper = bit_of(place(), bit) == 1
    first = first_head((0,) * SPLIT_BITS, heads) + offset
    for slot in range(rows // per):
        part = slice(slot * per, (slot + 1) * per)
        total = pl.ds(rows + first + slot, 1)
        merged_ref[part] = join(
            upper, mine_ref[part], mine_ref[total], other_ref[part], other_ref[total]
        )
    other_total = other_ref[rows:]
    merged_ref[rows:] = mine_ref[rows:] + other_total
    if has_prefix:
        refs[-1][...] = prefix_ref[...] + jnp.where(upper, other_total, 0.0)


def merge(bit, offset, has_prefix, mine, other, prefix, tokens=()):
    return call(
        functools.partial(merge_kernel, bit, offset, has_prefix),
        f"merge{bit}{offset}",
        [mine, other, prefix, *tokens],
        [(mine.shape, jnp.float32), (prefix.shape, jnp.float32)][: 1 + has_prefix],
    )


def pack_kernel(takes, *refs):
    out_ref = refs[-1]
    at = 0
    for ref, rows in zip(refs, takes):
        out_ref[at : at + rows] = ref[:rows]
        at += rows


def pack(name, pieces, tokens=()):
    takes = [rows for _, rows in pieces]
    lanes = pieces[0][0].shape[1]
    return call(
        functools.partial(pack_kernel, takes),
        name,
        [*[array for array, _ in pieces], *tokens],
        [((sum(takes), lanes), jnp.float32)],
    )[0]


def level_scale(bit, first_level, prefix_ref, sums_ref, weight_ref, tokens):
    active = jnp.where(bit_of(place(), bit) == 1, 1.0, 0.0)
    reach = jnp.exp(sums_ref[1, :, tokens] + spread_lanes(prefix_ref[:, :1], SPAN))
    return reach * weight_ref[first_level + bit, :, tokens] * active


def gather_work(quarters, part_refs, heads, per):
    work = []
    for far, pieces in quarters:
        first = first_head(far, heads)
        for slot in range(heads >> len(far)):
            states = []
            for level, index, start in pieces:
                rows = slice(start + slot * per, start + (slot + 1) * per)
                states.append((level, part_refs[index][rows].astype(jnp.bfloat16)))
            work.append((first + slot, states))
    return work


def add_found(mixed, queries, head, states, scale_ref):
    for level, state in states:
        found = lax.dot_general(state, queries, NT, preferred_element_type=jnp.float32)
        mixed = mixed + found * scale_ref[level, pl.ds(head, 1)]
    return mixed


def reach_kernel(quarters, first_level, bits, *refs):
    mixed_ref, q_ref, sums_ref, weight_ref = refs[:4]
    prefix_refs = refs[4 : 4 + len(bits)]
    part_refs = refs[4 + len(bits) :]
    out_ref, done_ref, scale_ref = refs[-3:]
    done_ref[...] = jnp.zeros_like(done_ref)
    heads = weight_ref.shape[1]
    head_width = mixed_ref.shape[0] // heads
    work = gather_work(quarters, part_refs, heads, head_width)
    for span in range(q_ref.shape[0] // SPAN):
        tokens = slice(span * SPAN, (span + 1) * SPAN)
        queries = q_ref[tokens]
        for level, (bit, prefix_ref) in enumerate(zip(bits, prefix_refs)):
            scale_ref[level] = level_scale(
                bit, first_level, prefix_ref, sums_ref, weight_ref, tokens
            )
        for head, states in work:
            rows = pl.ds(pl.multiple_of(head * head_width, 128), head_width)
            out_ref[rows, tokens] = add_found(
                mixed_ref[rows, tokens], queries, head, states, scale_ref
            )


def add_levels(quarters, first_level, bits, shared, prefixes, parts):
    mixed, _, _, level_weight = shared
    return call(
        functools.partial(reach_kernel, quarters, first_level, bits),
        "reach",
        [*shared, *prefixes, *parts],
        [(mixed.shape, jnp.float32), ((8, 128), jnp.float32)],
        [pltpu.VMEM((len(bits), level_weight.shape[1], SPAN), jnp.float32)],
        aliases={0: 0},
    )


def finish_kernel(quarters, first_level, bits, has_token, *refs):
    mixed_ref, q_ref, sums_ref, weight_ref, gain_ref = refs[:5]
    prefix_refs = refs[5 : 5 + len(bits)]
    part_refs = refs[5 + len(bits) :]
    out_ref, scale_ref, sent = refs[-3:]
    out_hbm = refs[-5] if has_token else refs[-4]
    if has_token:
        refs[-4][...] = jnp.zeros_like(refs[-4])
    heads = weight_ref.shape[1]
    head_width = mixed_ref.shape[0] // heads
    count = heads // 4
    size = count * head_width
    work = gather_work(quarters, part_refs, heads, head_width)
    gains = []
    for head, _ in work:
        row = jnp.broadcast_to(gain_ref[pl.ds(head, 1)], (8, head_width))
        gains.append(row.T[:, :1])
    copies = []
    for span in range(q_ref.shape[0] // SPAN):
        tokens = slice(span * SPAN, (span + 1) * SPAN)
        queries = q_ref[tokens]
        for level, (bit, prefix_ref) in enumerate(zip(bits, prefix_refs)):
            scale_ref[level] = level_scale(
                bit, first_level, prefix_ref, sums_ref, weight_ref, tokens
            )
        for at, (head, states) in enumerate(work):
            rows = pl.ds(pl.multiple_of(head * head_width, 128), head_width)
            mixed = add_found(mixed_ref[rows, tokens], queries, head, states, scale_ref)
            square = jnp.mean(mixed * mixed, axis=0, keepdims=True)
            normed = mixed * lax.rsqrt(square + EPS) * gains[at]
            columns = slice(at * head_width, (at + 1) * head_width)
            out_ref[tokens, columns] = normed.astype(jnp.bfloat16).T
        for at, (far, _) in enumerate(quarters):
            columns = pl.ds(pl.multiple_of(first_head(far, heads) * head_width, 128), size)
            copy = pltpu.make_async_copy(
                out_ref.at[tokens, at * size : (at + 1) * size],
                out_hbm.at[tokens, columns],
                sent.at[len(copies)],
            )
            copy.start()
            copies.append(copy)
    for copy in copies:
        copy.wait()


def finish(quarters, first_level, bits, shared, prefixes, parts, begun, has_token):
    mixed, queries, sums, level_weight, gain = shared
    width, tokens = mixed.shape
    heads = level_weight.shape[1]
    inputs = [*shared, *prefixes, *parts]
    specs = [HELD] * len(inputs)
    inputs = [hold(array) for array in inputs]
    out = pl.BlockSpec(memory_space=pltpu.HBM)
    aliases = {}
    if begun is not None:
        aliases = {len(inputs): 0}
        specs.append(out)
        inputs.append(begun)
    shapes = [jax.ShapeDtypeStruct((tokens, width), jnp.bfloat16)]
    if has_token:
        shapes.append(pltpu.VMEM((8, 128), jnp.float32))
    return pl.pallas_call(
        functools.partial(finish_kernel, quarters, first_level, bits, has_token),
        in_specs=specs,
        out_specs=[out, HELD][: len(shapes)],
        out_shape=shapes,
        scratch_shapes=[
            pltpu.VMEM((tokens, len(quarters) * width // 4), jnp.bfloat16),
            pltpu.VMEM((len(bits), heads, SPAN), jnp.float32),
            pltpu.SemaphoreType.DMA((len(quarters) * (tokens // SPAN),)),
        ],
        input_output_aliases=aliases,
        compiler_params=PARAMS,
        cost_estimate=COST,
        name="finish" + "".join(f"{core}{side}" for (core, side), _ in quarters),
    )(*inputs)


def trade(value, mask):
    wide, narrow = lax.axis_size("wide"), lax.axis_size("narrow")

    def ranked(index):
        return index % narrow * wide + index // narrow

    pairs = [(ranked(source), ranked(source ^ mask)) for source in range(wide * narrow)]
    return lax.ppermute(value, AXES, pairs)


def per_device(queries, keys, values, log_decay, level_weight, norm_gain):
    heads = log_decay.shape[0]
    tokens, width = values.shape
    per = width // heads
    spans = tokens // SPAN
    group_bits = heads.bit_length() - 1
    bits = (lax.axis_size("wide") * lax.axis_size("narrow")).bit_length() - 1
    first_level = level_weight.shape[0] - bits
    gain = norm_gain.reshape(heads, per)
    keep, send, local, sums, totals, queries, keys, values, level_weight, gain = make_states(
        queries, keys, values, log_decay, level_weight, gain
    )
    shared = (queries, keys, values, sums, totals, level_weight, local)
    last = bits - 1
    two = 2 * per
    size = two // CUTS
    sides = [(core, side) for core in (0, 1) for side in (0, 1)]
    other = trade(send, 1)
    zero = jnp.zeros((heads, 128), jnp.float32)
    chunks, give, prefix = make_chip(keep, other, heads, CUTS)
    other_rest = trade(pack("kept", [(keep, width // 2)], chunks[:1]), 1)
    prefixes = [zero, prefix]
    found, across = {}, {}
    mixed, at = None, 0

    def both(name, messages, tokens=()):
        return pack(name, [(state, size) for state in messages], tokens)

    for bit in range(1, bits):
        found[bit] = [trade(chunk, 2**bit) for chunk in (give if bit == 1 else chunks)]
        stays = chunks if bit == 1 else stays
        waits = []
        if bit < 3 or bit == last:
            stop = spans if bit == last else at + 1
            begun = [*chunks[-1:], *([other_rest] if bit == 1 else [])]
            mixed, *waits = mix_local(at, stop, shared, mixed, begun, bit < last)
            at = stop
        if bit == 3:
            waits.append(rest)
        if bit < last:
            merged = []
            for offset, (chunk, state) in enumerate(zip(chunks, found[bit])):
                ending = offset == CUTS - 1
                tokens_of = [*merged[-1:], *(waits if ending else ())]
                chunk, *after = merge(
                    bit, offset, ending, chunk, state, prefixes[bit], tokens_of
                )
                merged.append(chunk)
            chunks = merged
            prefixes += after
            found[bit] = both(f"found{bit}", found[bit], chunks[-1:])
            if bit > 1:
                across[bit] = trade(found[bit], 2)
            else:
                rest = trade(both("rest", stays, chunks[-1:]), 2)

    halves = [((core,), [(0, core, 0)]) for core in (0, 1)]
    shared = (mixed, queries, sums, level_weight)
    mixed, token = add_levels(halves, first_level, [0], shared, [zero], [other, other_rest])
    early = list(range(2, last))
    pieces = [(found[1], two), (rest, two)]
    for bit in early:
        pieces += [(found[bit], two), (across[bit], two)]
    near = pack("near", pieces, (token,))
    middle = [1, *early]
    ahead = [prefixes[bit] for bit in middle]

    def states_of(side, index, first):
        return [(first + slot, index, (2 * slot + side) * two) for slot in range(len(middle))]

    shared = (mixed, queries, sums, level_weight, gain)
    every = (first_level, [last, *middle], shared, [prefixes[last], *ahead])
    state = both("state", found[last])
    beside = trade(state, 2)
    quarters = {(core, side): [(0, 0, 0), *states_of(side, 1, 1)] for core, side in sides}
    out, token = finish([((0, 0), quarters[0, 0])], *every, [state, near], None, True)
    far = trade(near, 1)
    beside = pack("beside", [(beside, two)], (token,))
    (out,) = finish([((0, 1), quarters[0, 1])], *every, [beside, near], out, False)
    state_far, beside_far = trade(state, 1), trade(beside, 1)
    pairs = [((1, 0), quarters[1, 0])]
    pairs.append(((1, 1), [(0, 2, 0), *states_of(1, 1, 1)]))
    return finish(pairs, *every, [state_far, far, beside_far], out, False)[0]


def solution(mesh):
    placed = (
        P(("wide", "narrow"), None),
        P(("wide", "narrow"), None),
        P(("wide", "narrow"), None),
        P(None, ("wide", "narrow")),
        P(None, None, ("wide", "narrow")),
        P(),
    )
    return jax.shard_map(
        per_device,
        mesh=mesh,
        in_specs=placed,
        out_specs=P(("wide", "narrow"), None),
        check_vma=False,
    )
```

```python
import functools

import jax
import jax.numpy as jnp
from jax import lax
from jax.experimental import pallas as pl
from jax.experimental.pallas import tpu as pltpu
from jax.sharding import PartitionSpec as P

SPAN = 256
SPLIT_BITS = 2
CUTS = 2
EPS = 1e-05
AXES = ("narrow", "wide")
NT = (((1,), (1,)), ((), ()))


def cost(flops):
    return pl.CostEstimate(flops=flops, transcendentals=0, bytes_accessed=1_000_000)


PARAMS = pltpu.CompilerParams(vmem_limit_bytes=32 * 1024 * 1024)
COSTS = {"finish00": 1000, "finish01": 20000000000}
HELD = pl.BlockSpec(memory_space=pltpu.VMEM)


def place():
    return lax.axis_index("wide") * lax.axis_size("narrow") + lax.axis_index("narrow")


def bit_of(value, bit):
    return jnp.bitwise_and(jnp.right_shift(value, bit), 1)


def spread_lanes(column, width):
    return jnp.broadcast_to(column, (column.shape[0], width))


ANYWHERE = pl.BlockSpec(memory_space=pl.ANY)


def hold(array):
    return pltpu.with_memory_space_constraint(array, pltpu.VMEM)


def call(kernel, name, inputs, outputs, scratch=(), in_specs=None, aliases=None):
    specs = in_specs or [HELD] * len(inputs)
    inputs = [hold(array) if spec is HELD else array for array, spec in zip(inputs, specs)]
    return pl.pallas_call(
        kernel,
        in_specs=specs,
        out_specs=[HELD] * len(outputs),
        out_shape=[pltpu.VMEM(shape, dtype) for shape, dtype in outputs],
        scratch_shapes=list(scratch),
        input_output_aliases=aliases or {},
        compiler_params=PARAMS,
        cost_estimate=cost(COSTS.get(name, 2_000_000_000)),
        name=name,
    )(*inputs)


def running_sums(rows):
    high = rows.astype(jnp.bfloat16)
    rest = rows - high.astype(jnp.float32)
    middle = rest.astype(jnp.bfloat16)
    low = (rest - middle.astype(jnp.float32)).astype(jnp.bfloat16)
    width = rows.shape[1]
    source = lax.broadcasted_iota(jnp.int32, (width, width), 0)
    target = lax.broadcasted_iota(jnp.int32, (width, width), 1)
    upto = jnp.where(source <= target, 1.0, 0.0).astype(jnp.bfloat16)
    sums = jnp.dot(
        jnp.concatenate([high, middle, low], axis=0), upto, preferred_element_type=jnp.float32
    )
    count = rows.shape[0]
    return sums[:count] + (sums[count : 2 * count] + sums[2 * count :])


def state_kernel(*refs):
    q_hbm, k_hbm, v_hbm, decay_hbm, weight_hbm, gain_hbm = refs[:6]
    keep_ref, send_ref, local_ref, sums_ref, totals_ref = refs[6:11]
    q_ref, k_ref, v_ref, weight_ref, gain_ref, decay_ref, held, arrived = refs[11:]
    heads, tokens = decay_ref.shape
    head_width = v_ref.shape[1] // heads
    spans = tokens // SPAN
    rows_of = [slice(span * SPAN, (span + 1) * SPAN) for span in range(spans)]
    loads = [(decay_hbm, decay_ref), (k_hbm, k_ref)]
    loads += [(v_hbm.at[rows], v_ref.at[rows]) for rows in rows_of]
    loads += [(q_hbm, q_ref), (weight_hbm, weight_ref), (gain_hbm, gain_ref)]
    copies = [
        pltpu.make_async_copy(source, target, arrived.at[at])
        for at, (source, target) in enumerate(loads)
    ]
    for copy in copies:
        copy.start()
    copies[0].wait()
    within = running_sums(jnp.concatenate([decay_ref[:, rows] for rows in rows_of], axis=0))
    run = jnp.zeros((heads, 128), jnp.float32)
    fades, wholes = [], []
    for span, rows in enumerate(rows_of):
        here = within[span * heads : (span + 1) * heads]
        last = here[:, SPAN - 1 :]
        total = spread_lanes(last, 128)
        sums_ref[0, :, rows] = here
        sums_ref[1, :, rows] = here + spread_lanes(run[:, :1], SPAN)
        totals_ref[span] = total
        run = run + total
        fades.append(jnp.exp(spread_lanes(last, SPAN) - here))
        wholes.append(jnp.exp(total))
    copies[1].wait()
    across = [k_ref[rows].astype(jnp.float32).T for rows in rows_of]
    for copy in copies[2 : 2 + spans]:
        copy.wait()
    for head in range(heads):
        columns = slice(head * head_width, (head + 1) * head_width)
        states = []
        for span, rows in enumerate(rows_of):
            faded = (across[span] * fades[span][head : head + 1]).astype(jnp.bfloat16)
            states.append(
                jnp.dot(faded, v_ref[rows, columns], preferred_element_type=jnp.float32)
            )
        at = 0
        size = 1
        while size < spans:
            for first in range(0, spans, 2 * size):
                group = states[first]
                for span in range(first + 1, first + size):
                    group = group * wholes[span][head : head + 1] + states[span]
                local_ref[at, :, columns] = group.astype(jnp.bfloat16)
                at += 1
            size *= 2
        group = states[0]
        for span in range(1, spans):
            group = group * wholes[span][head : head + 1] + states[span]
        held[columns] = group.T
    half = held.shape[0] // 2
    core = bit_of(place(), 0)
    keep_ref[:half] = held[pl.ds(pl.multiple_of(core * half, 8), half)]
    send_ref[:half] = held[pl.ds(pl.multiple_of((1 - core) * half, 8), half)]
    keep_ref[half:] = run
    send_ref[half:] = run
    for copy in copies[2 + spans :]:
        copy.wait()


def make_states(queries, keys, values, log_decay, level_weight, gain):
    tokens, key_width = keys.shape
    heads = log_decay.shape[0]
    width = values.shape[1]
    spans = tokens // SPAN
    inputs = [queries, keys, values, log_decay, level_weight, gain]
    kept = [queries, keys, values, level_weight, gain]
    return call(
        state_kernel,
        "states",
        [pltpu.with_memory_space_constraint(array, pltpu.HBM) for array in inputs],
        [
            ((width // 2 + heads, key_width), jnp.float32),
            ((width // 2 + heads, key_width), jnp.float32),
            ((spans - 1, key_width, width), jnp.bfloat16),
            ((2, heads, tokens), jnp.float32),
            ((spans, heads, 128), jnp.float32),
            *[(array.shape, array.dtype) for array in kept],
        ],
        [
            pltpu.VMEM(log_decay.shape, jnp.float32),
            pltpu.VMEM((width, key_width), jnp.float32),
            pltpu.SemaphoreType.DMA((spans + 5,)),
        ],
        [pl.BlockSpec(memory_space=pltpu.HBM)] * len(inputs),
    )


def local_kernel(first, last, has_token, *refs):
    q_ref, k_ref, v_ref, sums_ref, totals_ref, weight_ref, local_ref = refs[:7]
    if has_token:
        mixed_ref, done_ref = refs[-2:]
        done_ref[...] = jnp.zeros_like(done_ref)
    else:
        mixed_ref = refs[-1]
    heads = weight_ref.shape[1]
    head_width = v_ref.shape[1] // heads
    spans = totals_ref.shape[0]
    local_bits = spans.bit_length() - 1
    half = SPAN // 2
    source = lax.broadcasted_iota(jnp.int32, (half, half), 0)
    target = lax.broadcasted_iota(jnp.int32, (half, half), 1)
    causal = source <= target
    empty = jnp.zeros((half, half), jnp.bfloat16)

    for span in range(first, last):
        tokens = slice(span * SPAN, (span + 1) * SPAN)
        queries = q_ref[tokens]
        scores = lax.dot_general(
            k_ref[tokens], queries, NT, preferred_element_type=jnp.float32
        )
        within = sums_ref[0, :, tokens]
        within_down = within.T
        weight = weight_ref[0, :, tokens]
        values_across = v_ref[tokens].T

        def mix(head, low, high):
            rows = slice(low * half, (low + 1) * half)
            columns = slice(high * half, (high + 1) * half)
            gap = within[head : head + 1, columns] - within_down[rows, head : head + 1]
            if low == high:
                gap = jnp.where(causal, gap, -1e30)
            mixing = scores[rows, columns] * jnp.exp(gap) * weight[head : head + 1, columns]
            return mixing.astype(jnp.bfloat16)

        levels = []
        offset = 0
        for bit in range(local_bits):
            if span >> bit & 1:
                since = within
                for back in range(1, span % 2**bit + 1):
                    since = since + spread_lanes(totals_ref[span - back][:, :1], SPAN)
                scale = jnp.exp(since) * weight_ref[1 + bit, :, tokens]
                levels.append((local_ref[offset + (span >> (bit + 1))].T, scale))
            offset += spans >> (bit + 1)
        for head in range(heads):
            rows = slice(head * head_width, (head + 1) * head_width)
            mixing = jnp.concatenate(
                [
                    jnp.concatenate([mix(head, 0, 0), mix(head, 0, 1)], axis=1),
                    jnp.concatenate([empty, mix(head, 1, 1)], axis=1),
                ],
                axis=0,
            )
            mixed = jnp.dot(values_across[rows], mixing, preferred_element_type=jnp.float32)
            for level, scale in levels:
                found = lax.dot_general(
                    level[rows], queries, NT, preferred_element_type=jnp.float32
                )
                mixed = mixed + found * scale[head : head + 1]
            mixed_ref[rows, tokens] = mixed


def mix_local(first, last, shared, mixed, tokens, has_token):
    queries, keys, values, sums, totals, level_weight, local = shared
    rest = [] if mixed is None else [mixed]
    return call(
        functools.partial(local_kernel, first, last, has_token),
        f"local{first}",
        [*shared, *rest, *tokens],
        [(values.shape[::-1], jnp.float32), ((8, 128), jnp.float32)][: 1 + has_token],
        aliases={7: 0} if rest else None,
    )


def join(upper, mine, mine_total, other, other_total):
    fade = jnp.exp(jnp.where(upper, mine_total, other_total))
    return jnp.where(upper, other * fade + mine, mine * fade + other)


def first_head(far, heads):
    here = place()
    first = 0
    for bit, flip in enumerate(far):
        first = first + jnp.bitwise_xor(bit_of(here, bit), flip) * (heads >> (bit + 1))
    return first


def chip_kernel(mine_ref, other_ref, *refs):
    *message_refs, next_ref, whole_ref = refs
    heads = next_ref.shape[0]
    width = whole_ref.shape[0]
    held = heads // 2
    per = width // held
    here = place()
    upper = bit_of(here, 0) == 1
    first = first_head((0,), heads)
    for slot in range(held):
        part = slice(slot * per, (slot + 1) * per)
        total = pl.ds(width + first + slot, 1)
        whole_ref[part] = join(
            upper, mine_ref[part], mine_ref[total], other_ref[part], other_ref[total]
        )
    other_total = other_ref[width:]
    total = mine_ref[width:] + other_total
    next_ref[...] = jnp.where(upper, other_total, 0.0)
    half = width // 2
    side = bit_of(here, 1)
    cuts = len(message_refs) // 2
    size = half // cuts
    for at, ref in enumerate(message_refs):
        start = (side if at < cuts else 1 - side) * half + at % cuts * size
        ref[:size] = whole_ref[pl.ds(pl.multiple_of(start, 8), size)]
        ref[size:] = total


def make_chip(mine, other, heads, cuts):
    rows, lanes = mine.shape
    half = rows - heads
    *messages, prefix = call(
        chip_kernel,
        "chip",
        [mine, other],
        [
            *[((half // 2 // cuts + heads, lanes), jnp.float32)] * (2 * cuts),
            ((heads, lanes), jnp.float32),
        ],
        [pltpu.VMEM((half, lanes), jnp.float32)],
    )
    return messages[:cuts], messages[cuts:], prefix


def merge_kernel(bit, offset, has_prefix, *refs):
    mine_ref, other_ref, prefix_ref = refs[:3]
    merged_ref = refs[-2] if has_prefix else refs[-1]
    heads = prefix_ref.shape[0]
    rows = mine_ref.shape[0] - heads
    per = mine_ref.shape[1]
    upper = bit_of(place(), bit) == 1
    first = first_head((0,) * SPLIT_BITS, heads) + offset
    for slot in range(rows // per):
        part = slice(slot * per, (slot + 1) * per)
        total = pl.ds(rows + first + slot, 1)
        merged_ref[part] = join(
            upper, mine_ref[part], mine_ref[total], other_ref[part], other_ref[total]
        )
    other_total = other_ref[rows:]
    merged_ref[rows:] = mine_ref[rows:] + other_total
    if has_prefix:
        refs[-1][...] = prefix_ref[...] + jnp.where(upper, other_total, 0.0)


def merge(bit, offset, has_prefix, mine, other, prefix, tokens=()):
    return call(
        functools.partial(merge_kernel, bit, offset, has_prefix),
        f"merge{bit}{offset}",
        [mine, other, prefix, *tokens],
        [(mine.shape, jnp.float32), (prefix.shape, jnp.float32)][: 1 + has_prefix],
    )


def pack_kernel(takes, *refs):
    out_ref = refs[-1]
    at = 0
    for ref, rows in zip(refs, takes):
        out_ref[at : at + rows] = ref[:rows]
        at += rows


def pack(name, pieces, tokens=()):
    takes = [rows for _, rows in pieces]
    lanes = pieces[0][0].shape[1]
    return call(
        functools.partial(pack_kernel, takes),
        name,
        [*[array for array, _ in pieces], *tokens],
        [((sum(takes), lanes), jnp.float32)],
    )[0]


def level_scale(bit, first_level, prefix_ref, sums_ref, weight_ref, tokens):
    active = jnp.where(bit_of(place(), bit) == 1, 1.0, 0.0)
    reach = jnp.exp(sums_ref[1, :, tokens] + spread_lanes(prefix_ref[:, :1], SPAN))
    return reach * weight_ref[first_level + bit, :, tokens] * active


def gather_work(quarters, part_refs, heads, per):
    work = []
    for far, pieces in quarters:
        first = first_head(far, heads)
        for slot in range(heads >> len(far)):
            states = []
            for level, index, start in pieces:
                rows = slice(start + slot * per, start + (slot + 1) * per)
                states.append((level, part_refs[index][rows].astype(jnp.bfloat16)))
            work.append((first + slot, states))
    return work


def add_found(mixed, queries, head, states, scale_ref):
    for level, state in states:
        found = lax.dot_general(state, queries, NT, preferred_element_type=jnp.float32)
        mixed = mixed + found * scale_ref[level, pl.ds(head, 1)]
    return mixed


def reach_kernel(quarters, first_level, bits, *refs):
    mixed_ref, q_ref, sums_ref, weight_ref = refs[:4]
    prefix_refs = refs[4 : 4 + len(bits)]
    part_refs = refs[4 + len(bits) :]
    out_ref, done_ref, scale_ref = refs[-3:]
    done_ref[...] = jnp.zeros_like(done_ref)
    heads = weight_ref.shape[1]
    head_width = mixed_ref.shape[0] // heads
    work = gather_work(quarters, part_refs, heads, head_width)
    for span in range(q_ref.shape[0] // SPAN):
        tokens = slice(span * SPAN, (span + 1) * SPAN)
        queries = q_ref[tokens]
        for level, (bit, prefix_ref) in enumerate(zip(bits, prefix_refs)):
            scale_ref[level] = level_scale(
                bit, first_level, prefix_ref, sums_ref, weight_ref, tokens
            )
        for head, states in work:
            rows = pl.ds(pl.multiple_of(head * head_width, 128), head_width)
            out_ref[rows, tokens] = add_found(
                mixed_ref[rows, tokens], queries, head, states, scale_ref
            )


def add_levels(quarters, first_level, bits, shared, prefixes, parts):
    mixed, _, _, level_weight = shared
    return call(
        functools.partial(reach_kernel, quarters, first_level, bits),
        "reach",
        [*shared, *prefixes, *parts],
        [(mixed.shape, jnp.float32), ((8, 128), jnp.float32)],
        [pltpu.VMEM((len(bits), level_weight.shape[1], SPAN), jnp.float32)],
        aliases={0: 0},
    )


def finish_kernel(quarters, first_level, bits, has_token, *refs):
    mixed_ref, q_ref, sums_ref, weight_ref, gain_ref = refs[:5]
    prefix_refs = refs[5 : 5 + len(bits)]
    part_refs = refs[5 + len(bits) :]
    out_ref, scale_ref, sent = refs[-3:]
    out_hbm = refs[-5] if has_token else refs[-4]
    if has_token:
        refs[-4][...] = jnp.zeros_like(refs[-4])
    heads = weight_ref.shape[1]
    head_width = mixed_ref.shape[0] // heads
    count = heads // 4
    size = count * head_width
    work = gather_work(quarters, part_refs, heads, head_width)
    gains = []
    for head, _ in work:
        row = jnp.broadcast_to(gain_ref[pl.ds(head, 1)], (8, head_width))
        gains.append(row.T[:, :1])
    copies = []
    for span in range(q_ref.shape[0] // SPAN):
        tokens = slice(span * SPAN, (span + 1) * SPAN)
        queries = q_ref[tokens]
        for level, (bit, prefix_ref) in enumerate(zip(bits, prefix_refs)):
            scale_ref[level] = level_scale(
                bit, first_level, prefix_ref, sums_ref, weight_ref, tokens
            )
        for at, (head, states) in enumerate(work):
            rows = pl.ds(pl.multiple_of(head * head_width, 128), head_width)
            mixed = add_found(mixed_ref[rows, tokens], queries, head, states, scale_ref)
            square = jnp.mean(mixed * mixed, axis=0, keepdims=True)
            normed = mixed * lax.rsqrt(square + EPS) * gains[at]
            columns = slice(at * head_width, (at + 1) * head_width)
            out_ref[tokens, columns] = normed.astype(jnp.bfloat16).T
        for at, (far, _) in enumerate(quarters):
            columns = pl.ds(pl.multiple_of(first_head(far, heads) * head_width, 128), size)
            copy = pltpu.make_async_copy(
                out_ref.at[tokens, at * size : (at + 1) * size],
                out_hbm.at[tokens, columns],
                sent.at[len(copies)],
            )
            copy.start()
            copies.append(copy)
    for copy in copies:
        copy.wait()


def finish(quarters, first_level, bits, shared, prefixes, parts, begun, has_token):
    mixed, queries, sums, level_weight, gain = shared
    width, tokens = mixed.shape
    heads = level_weight.shape[1]
    inputs = [*shared, *prefixes, *parts]
    specs = [HELD] * len(inputs)
    inputs = [hold(array) for array in inputs]
    out = pl.BlockSpec(memory_space=pltpu.HBM)
    aliases = {}
    if begun is not None:
        aliases = {len(inputs): 0}
        specs.append(out)
        inputs.append(begun)
    name = "finish" + "".join(f"{core}{side}" for (core, side), _ in quarters)
    shapes = [jax.ShapeDtypeStruct((tokens, width), jnp.bfloat16)]
    if has_token:
        shapes.append(pltpu.VMEM((8, 128), jnp.float32))
    return pl.pallas_call(
        functools.partial(finish_kernel, quarters, first_level, bits, has_token),
        in_specs=specs,
        out_specs=[out, HELD][: len(shapes)],
        out_shape=shapes,
        scratch_shapes=[
            pltpu.VMEM((tokens, len(quarters) * width // 4), jnp.bfloat16),
            pltpu.VMEM((len(bits), heads, SPAN), jnp.float32),
            pltpu.SemaphoreType.DMA((len(quarters) * (tokens // SPAN),)),
        ],
        input_output_aliases=aliases,
        compiler_params=PARAMS,
        cost_estimate=cost(COSTS.get(name, 2_000_000_000)),
        name=name,
    )(*inputs)


def trade(value, mask):
    wide, narrow = lax.axis_size("wide"), lax.axis_size("narrow")

    def ranked(index):
        return index % narrow * wide + index // narrow

    pairs = [(ranked(source), ranked(source ^ mask)) for source in range(wide * narrow)]
    return lax.ppermute(value, AXES, pairs)


def per_device(queries, keys, values, log_decay, level_weight, norm_gain):
    heads = log_decay.shape[0]
    tokens, width = values.shape
    per = width // heads
    spans = tokens // SPAN
    group_bits = heads.bit_length() - 1
    bits = (lax.axis_size("wide") * lax.axis_size("narrow")).bit_length() - 1
    first_level = level_weight.shape[0] - bits
    gain = norm_gain.reshape(heads, per)
    keep, send, local, sums, totals, queries, keys, values, level_weight, gain = make_states(
        queries, keys, values, log_decay, level_weight, gain
    )
    shared = (queries, keys, values, sums, totals, level_weight, local)
    last = bits - 1
    two = 2 * per
    size = two // CUTS
    sides = [(core, side) for core in (0, 1) for side in (0, 1)]
    other = trade(send, 1)
    zero = jnp.zeros((heads, 128), jnp.float32)
    chunks, give, prefix = make_chip(keep, other, heads, CUTS)
    other_rest = trade(keep, 1)
    prefixes = [zero, prefix]
    found, across = {}, {}
    mixed, at = None, 0

    def both(name, messages, tokens=()):
        return pack(name, [(state, size) for state in messages], tokens)

    for bit in range(1, bits):
        found[bit] = [trade(chunk, 2**bit) for chunk in (give if bit == 1 else chunks)]
        stays = chunks if bit == 1 else stays
        waits = []
        if bit < 3 or bit == last:
            stop = spans if bit == last else at + 1
            begun = [*chunks[-1:], *([other_rest] if bit == 1 else [])]
            mixed, *waits = mix_local(at, stop, shared, mixed, begun, bit < last)
            at = stop
        if bit == 3:
            waits.append(rest)
        if bit < last:
            merged = []
            for offset, (chunk, state) in enumerate(zip(chunks, found[bit])):
                ending = offset == CUTS - 1
                tokens_of = [*merged[-1:], *(waits if ending else ())]
                chunk, *after = merge(
                    bit, offset, ending, chunk, state, prefixes[bit], tokens_of
                )
                merged.append(chunk)
            chunks = merged
            prefixes += after
            found[bit] = both(f"found{bit}", found[bit], chunks[-1:])
            if bit > 1:
                across[bit] = trade(found[bit], 2)
            else:
                rest = trade(both("rest", stays, chunks[-1:]), 2)

    halves = [((core,), [(0, core, 0)]) for core in (0, 1)]
    shared = (mixed, queries, sums, level_weight)
    mixed, token = add_levels(halves, first_level, [0], shared, [zero], [other, other_rest])
    state = both("state", found[last], (token,))
    beside = trade(state, 2)
    early = list(range(2, last))
    pieces = [(found[1], two), (rest, two)]
    for bit in early:
        pieces += [(found[bit], two), (across[bit], two)]
    near = pack("near", pieces, (state,))
    middle = [1, *early]
    ahead = [prefixes[bit] for bit in middle]

    def states_of(side, index, first):
        return [(first + slot, index, (2 * slot + side) * two) for slot in range(len(middle))]

    shared = (mixed, queries, sums, level_weight, gain)
    every = (first_level, [last, *middle], shared, [prefixes[last], *ahead])
    quarters = {(core, side): [(0, 0, 0), *states_of(side, 1, 1)] for core, side in sides}
    out, token = finish([((0, 0), quarters[0, 0])], *every, [state, near], None, True)
    far = trade(near, 1)
    beside = pack("beside", [(beside, two)], (token,))
    (out,) = finish([((0, 1), quarters[0, 1])], *every, [beside, near], out, False)
    state_far, beside_far = trade(state, 1), trade(beside, 1)
    pairs = [((1, 0), quarters[1, 0])]
    pairs.append(((1, 1), [(0, 2, 0), *states_of(1, 1, 1)]))
    return finish(pairs, *every, [state_far, far, beside_far], out, False)[0]


def solution(mesh):
    placed = (
        P(("wide", "narrow"), None),
        P(("wide", "narrow"), None),
        P(("wide", "narrow"), None),
        P(None, ("wide", "narrow")),
        P(None, None, ("wide", "narrow")),
        P(),
    )
    return jax.shard_map(
        per_device,
        mesh=mesh,
        in_specs=placed,
        out_specs=P(("wide", "narrow"), None),
        check_vma=False,
    )
```

```python
import functools

import jax
import jax.numpy as jnp
from jax import lax
from jax.experimental import pallas as pl
from jax.experimental.pallas import tpu as pltpu
from jax.sharding import PartitionSpec as P

SPAN = 256
SPLIT_BITS = 2
CUTS = 2
EPS = 1e-05
AXES = ("narrow", "wide")
NT = (((1,), (1,)), ((), ()))
COSTS = {"finish00": 20000000000, "finish10": 1000, "finish01": 20000000000, "local2": 1000, "reach": 1000}


def cost(name):
    flops = COSTS.get(name, 2000000000)
    return pl.CostEstimate(flops=flops, transcendentals=0, bytes_accessed=1_000_000)


PARAMS = pltpu.CompilerParams(vmem_limit_bytes=32 * 1024 * 1024)
HELD = pl.BlockSpec(memory_space=pltpu.VMEM)


def place():
    return lax.axis_index("wide") * lax.axis_size("narrow") + lax.axis_index("narrow")


def bit_of(value, bit):
    return jnp.bitwise_and(jnp.right_shift(value, bit), 1)


def spread_lanes(column, width):
    return jnp.broadcast_to(column, (column.shape[0], width))


ANYWHERE = pl.BlockSpec(memory_space=pl.ANY)


def hold(array):
    return pltpu.with_memory_space_constraint(array, pltpu.VMEM)


def call(kernel, name, inputs, outputs, scratch=(), in_specs=None, aliases=None):
    specs = in_specs or [HELD] * len(inputs)
    inputs = [hold(array) if spec is HELD else array for array, spec in zip(inputs, specs)]
    return pl.pallas_call(
        kernel,
        in_specs=specs,
        out_specs=[HELD] * len(outputs),
        out_shape=[pltpu.VMEM(shape, dtype) for shape, dtype in outputs],
        scratch_shapes=list(scratch),
        input_output_aliases=aliases or {},
        compiler_params=PARAMS,
        cost_estimate=cost(name),
        name=name,
    )(*inputs)


def running_sums(rows):
    high = rows.astype(jnp.bfloat16)
    rest = rows - high.astype(jnp.float32)
    middle = rest.astype(jnp.bfloat16)
    low = (rest - middle.astype(jnp.float32)).astype(jnp.bfloat16)
    width = rows.shape[1]
    source = lax.broadcasted_iota(jnp.int32, (width, width), 0)
    target = lax.broadcasted_iota(jnp.int32, (width, width), 1)
    upto = jnp.where(source <= target, 1.0, 0.0).astype(jnp.bfloat16)
    sums = jnp.dot(
        jnp.concatenate([high, middle, low], axis=0), upto, preferred_element_type=jnp.float32
    )
    count = rows.shape[0]
    return sums[:count] + (sums[count : 2 * count] + sums[2 * count :])


def state_kernel(*refs):
    q_hbm, k_hbm, v_hbm, decay_hbm, weight_hbm, gain_hbm = refs[:6]
    message_ref, local_ref, sums_ref, totals_ref = refs[6:10]
    q_ref, k_ref, v_ref, weight_ref, gain_ref, decay_ref, held, arrived = refs[10:]
    heads, tokens = decay_ref.shape
    head_width = v_ref.shape[1] // heads
    spans = tokens // SPAN
    rows_of = [slice(span * SPAN, (span + 1) * SPAN) for span in range(spans)]
    loads = [(decay_hbm, decay_ref), (k_hbm, k_ref)]
    loads += [(v_hbm.at[rows], v_ref.at[rows]) for rows in rows_of]
    loads += [(q_hbm, q_ref), (weight_hbm, weight_ref), (gain_hbm, gain_ref)]
    copies = [
        pltpu.make_async_copy(source, target, arrived.at[at])
        for at, (source, target) in enumerate(loads)
    ]
    for copy in copies:
        copy.start()
    copies[0].wait()
    within = running_sums(jnp.concatenate([decay_ref[:, rows] for rows in rows_of], axis=0))
    run = jnp.zeros((heads, 128), jnp.float32)
    fades, wholes = [], []
    for span, rows in enumerate(rows_of):
        here = within[span * heads : (span + 1) * heads]
        last = here[:, SPAN - 1 :]
        total = spread_lanes(last, 128)
        sums_ref[0, :, rows] = here
        sums_ref[1, :, rows] = here + spread_lanes(run[:, :1], SPAN)
        totals_ref[span] = total
        run = run + total
        fades.append(jnp.exp(spread_lanes(last, SPAN) - here))
        wholes.append(jnp.exp(total))
    copies[1].wait()
    across = [k_ref[rows].astype(jnp.float32).T for rows in rows_of]
    local_bits = spans.bit_length() - 1
    for span, rows in enumerate(rows_of):
        copies[2 + span].wait()
        for head in range(heads):
            columns = slice(head * head_width, (head + 1) * head_width)
            faded = (across[span] * fades[span][head : head + 1]).astype(jnp.bfloat16)
            state = jnp.dot(faded, v_ref[rows, columns], preferred_element_type=jnp.float32)
            at = 0
            for bit in range(local_bits + 1):
                if span >> bit & 1 == 0 or bit == local_bits:
                    group = state
                    if span % 2**bit > 0:
                        group = held[bit - 1, head] * wholes[span][head : head + 1] + state
                    if (span + 1) % 2**bit > 0:
                        held[bit - 1, head] = group
                    elif bit < local_bits:
                        local_ref[at + (span >> (bit + 1)), :, columns] = group.astype(
                            jnp.bfloat16
                        )
                    else:
                        message_ref[columns] = group.T
                at += spans >> (bit + 1)
    message_ref[heads * head_width :] = run
    for copy in copies[2 + spans :]:
        copy.wait()


def make_states(queries, keys, values, log_decay, level_weight, gain):
    tokens, key_width = keys.shape
    heads = log_decay.shape[0]
    width = values.shape[1]
    spans = tokens // SPAN
    inputs = [queries, keys, values, log_decay, level_weight, gain]
    kept = [queries, keys, values, level_weight, gain]
    return call(
        state_kernel,
        "states",
        [pltpu.with_memory_space_constraint(array, pltpu.HBM) for array in inputs],
        [
            ((width + heads, key_width), jnp.float32),
            ((spans - 1, key_width, width), jnp.bfloat16),
            ((2, heads, tokens), jnp.float32),
            ((spans, heads, 128), jnp.float32),
            *[(array.shape, array.dtype) for array in kept],
        ],
        [
            pltpu.VMEM(log_decay.shape, jnp.float32),
            pltpu.VMEM((spans.bit_length() - 1, heads, key_width, width // heads), jnp.float32),
            pltpu.SemaphoreType.DMA((spans + 5,)),
        ],
        [pl.BlockSpec(memory_space=pltpu.HBM)] * len(inputs),
    )


def local_kernel(first, last, has_token, *refs):
    q_ref, k_ref, v_ref, sums_ref, totals_ref, weight_ref, local_ref = refs[:7]
    if has_token:
        mixed_ref, done_ref = refs[-2:]
        done_ref[...] = jnp.zeros_like(done_ref)
    else:
        mixed_ref = refs[-1]
    heads = weight_ref.shape[1]
    head_width = v_ref.shape[1] // heads
    spans = totals_ref.shape[0]
    local_bits = spans.bit_length() - 1
    half = SPAN // 2
    source = lax.broadcasted_iota(jnp.int32, (half, half), 0)
    target = lax.broadcasted_iota(jnp.int32, (half, half), 1)
    causal = source <= target
    empty = jnp.zeros((half, half), jnp.bfloat16)

    for span in range(first, last):
        tokens = slice(span * SPAN, (span + 1) * SPAN)
        queries = q_ref[tokens]
        scores = lax.dot_general(
            k_ref[tokens], queries, NT, preferred_element_type=jnp.float32
        )
        within = sums_ref[0, :, tokens]
        within_down = within.T
        weight = weight_ref[0, :, tokens]
        values_across = v_ref[tokens].T

        def mix(head, low, high):
            rows = slice(low * half, (low + 1) * half)
            columns = slice(high * half, (high + 1) * half)
            gap = within[head : head + 1, columns] - within_down[rows, head : head + 1]
            if low == high:
                gap = jnp.where(causal, gap, -1e30)
            mixing = scores[rows, columns] * jnp.exp(gap) * weight[head : head + 1, columns]
            return mixing.astype(jnp.bfloat16)

        levels = []
        offset = 0
        for bit in range(local_bits):
            if span >> bit & 1:
                since = within
                for back in range(1, span % 2**bit + 1):
                    since = since + spread_lanes(totals_ref[span - back][:, :1], SPAN)
                scale = jnp.exp(since) * weight_ref[1 + bit, :, tokens]
                levels.append((local_ref[offset + (span >> (bit + 1))].T, scale))
            offset += spans >> (bit + 1)
        for head in range(heads):
            rows = slice(head * head_width, (head + 1) * head_width)
            mixing = jnp.concatenate(
                [
                    jnp.concatenate([mix(head, 0, 0), mix(head, 0, 1)], axis=1),
                    jnp.concatenate([empty, mix(head, 1, 1)], axis=1),
                ],
                axis=0,
            )
            mixed = jnp.dot(values_across[rows], mixing, preferred_element_type=jnp.float32)
            for level, scale in levels:
                found = lax.dot_general(
                    level[rows], queries, NT, preferred_element_type=jnp.float32
                )
                mixed = mixed + found * scale[head : head + 1]
            mixed_ref[rows, tokens] = mixed


def mix_local(first, last, shared, mixed, tokens, has_token):
    queries, keys, values, sums, totals, level_weight, local = shared
    rest = [] if mixed is None else [mixed]
    return call(
        functools.partial(local_kernel, first, last, has_token),
        f"local{first}",
        [*shared, *rest, *tokens],
        [(values.shape[::-1], jnp.float32), ((8, 128), jnp.float32)][: 1 + has_token],
        aliases={7: 0} if rest else None,
    )


def join(upper, mine, mine_total, other, other_total):
    fade = jnp.exp(jnp.where(upper, mine_total, other_total))
    return jnp.where(upper, other * fade + mine, mine * fade + other)


def first_head(far, heads):
    here = place()
    first = 0
    for bit, flip in enumerate(far):
        first = first + jnp.bitwise_xor(bit_of(here, bit), flip) * (heads >> (bit + 1))
    return first


def chip_kernel(mine_ref, other_ref, *refs):
    *message_refs, next_ref, whole_ref = refs
    heads = next_ref.shape[0]
    width = mine_ref.shape[0] - heads
    per = width // heads
    held = whole_ref.shape[0] // per
    here = place()
    upper = bit_of(here, 0) == 1
    first = first_head((0,), heads)
    for slot in range(held):
        part = pl.ds(pl.multiple_of((first + slot) * per, 8), per)
        total = pl.ds(width + first + slot, 1)
        whole_ref[slot * per : (slot + 1) * per] = join(
            upper, mine_ref[part], mine_ref[total], other_ref[part], other_ref[total]
        )
    other_total = other_ref[width:]
    total = mine_ref[width:] + other_total
    next_ref[...] = jnp.where(upper, other_total, 0.0)
    half = held * per // 2
    side = bit_of(here, 1)
    cuts = len(message_refs) // 2
    size = half // cuts
    for at, ref in enumerate(message_refs):
        start = (side if at < cuts else 1 - side) * half + at % cuts * size
        ref[:size] = whole_ref[pl.ds(pl.multiple_of(start, 8), size)]
        ref[size:] = total


def make_chip(mine, other, heads, cuts):
    rows, lanes = mine.shape
    half = (rows - heads) // 2
    *messages, prefix = call(
        chip_kernel,
        "chip",
        [mine, other],
        [
            *[((half // 2 // cuts + heads, lanes), jnp.float32)] * (2 * cuts),
            ((heads, lanes), jnp.float32),
        ],
        [pltpu.VMEM((half, lanes), jnp.float32)],
    )
    return messages[:cuts], messages[cuts:], prefix


def merge_kernel(bit, offset, has_prefix, *refs):
    mine_ref, other_ref, prefix_ref = refs[:3]
    merged_ref = refs[-2] if has_prefix else refs[-1]
    heads = prefix_ref.shape[0]
    rows = mine_ref.shape[0] - heads
    per = mine_ref.shape[1]
    upper = bit_of(place(), bit) == 1
    first = first_head((0,) * SPLIT_BITS, heads) + offset
    for slot in range(rows // per):
        part = slice(slot * per, (slot + 1) * per)
        total = pl.ds(rows + first + slot, 1)
        merged_ref[part] = join(
            upper, mine_ref[part], mine_ref[total], other_ref[part], other_ref[total]
        )
    other_total = other_ref[rows:]
    merged_ref[rows:] = mine_ref[rows:] + other_total
    if has_prefix:
        refs[-1][...] = prefix_ref[...] + jnp.where(upper, other_total, 0.0)


def merge(bit, offset, has_prefix, mine, other, prefix, tokens=()):
    return call(
        functools.partial(merge_kernel, bit, offset, has_prefix),
        f"merge{bit}{offset}",
        [mine, other, prefix, *tokens],
        [(mine.shape, jnp.float32), (prefix.shape, jnp.float32)][: 1 + has_prefix],
    )


def pack_kernel(takes, *refs):
    out_ref = refs[-1]
    at = 0
    for ref, rows in zip(refs, takes):
        out_ref[at : at + rows] = ref[:rows]
        at += rows


def pack(name, pieces, tokens=()):
    takes = [rows for _, rows in pieces]
    lanes = pieces[0][0].shape[1]
    return call(
        functools.partial(pack_kernel, takes),
        name,
        [*[array for array, _ in pieces], *tokens],
        [((sum(takes), lanes), jnp.float32)],
    )[0]


def level_scale(bit, first_level, prefix_ref, sums_ref, weight_ref, tokens):
    active = jnp.where(bit_of(place(), bit) == 1, 1.0, 0.0)
    reach = jnp.exp(sums_ref[1, :, tokens] + spread_lanes(prefix_ref[:, :1], SPAN))
    return reach * weight_ref[first_level + bit, :, tokens] * active


def gather_work(quarters, part_refs, heads, per):
    work = []
    for far, pieces in quarters:
        first = first_head(far, heads)
        for slot in range(heads // 4):
            states = []
            for level, index, start in pieces:
                if start is None:
                    rows = pl.ds(pl.multiple_of((first + slot) * per, 128), per)
                else:
                    rows = slice(start + slot * per, start + (slot + 1) * per)
                states.append((level, part_refs[index][rows].astype(jnp.bfloat16)))
            work.append((first + slot, states))
    return work


def add_found(mixed, queries, head, states, scale_ref):
    for level, state in states:
        found = lax.dot_general(state, queries, NT, preferred_element_type=jnp.float32)
        mixed = mixed + found * scale_ref[level, pl.ds(head, 1)]
    return mixed


def reach_kernel(quarters, first_level, bits, *refs):
    mixed_ref, q_ref, sums_ref, weight_ref = refs[:4]
    prefix_refs = refs[4 : 4 + len(bits)]
    part_refs = refs[4 + len(bits) :]
    out_ref, done_ref, scale_ref = refs[-3:]
    done_ref[...] = jnp.zeros_like(done_ref)
    heads = weight_ref.shape[1]
    head_width = mixed_ref.shape[0] // heads
    work = gather_work(quarters, part_refs, heads, head_width)
    for span in range(q_ref.shape[0] // SPAN):
        tokens = slice(span * SPAN, (span + 1) * SPAN)
        queries = q_ref[tokens]
        for level, (bit, prefix_ref) in enumerate(zip(bits, prefix_refs)):
            scale_ref[level] = level_scale(
                bit, first_level, prefix_ref, sums_ref, weight_ref, tokens
            )
        for head, states in work:
            rows = pl.ds(pl.multiple_of(head * head_width, 128), head_width)
            out_ref[rows, tokens] = add_found(
                mixed_ref[rows, tokens], queries, head, states, scale_ref
            )


def add_levels(quarters, first_level, bits, shared, prefixes, parts):
    mixed, _, _, level_weight = shared
    return call(
        functools.partial(reach_kernel, quarters, first_level, bits),
        "reach",
        [*shared, *prefixes, *parts],
        [(mixed.shape, jnp.float32), ((8, 128), jnp.float32)],
        [pltpu.VMEM((len(bits), level_weight.shape[1], SPAN), jnp.float32)],
        aliases={0: 0},
    )


def finish_kernel(quarters, first_level, bits, has_token, *refs):
    mixed_ref, q_ref, sums_ref, weight_ref, gain_ref = refs[:5]
    prefix_refs = refs[5 : 5 + len(bits)]
    part_refs = refs[5 + len(bits) :]
    out_ref, scale_ref, sent = refs[-3:]
    out_hbm = refs[-5] if has_token else refs[-4]
    if has_token:
        refs[-4][...] = jnp.zeros_like(refs[-4])
    heads = weight_ref.shape[1]
    head_width = mixed_ref.shape[0] // heads
    count = heads // 4
    size = count * head_width
    work = gather_work(quarters, part_refs, heads, head_width)
    gains = []
    for head, _ in work:
        row = jnp.broadcast_to(gain_ref[pl.ds(head, 1)], (8, head_width))
        gains.append(row.T[:, :1])
    copies = []
    for span in range(q_ref.shape[0] // SPAN):
        tokens = slice(span * SPAN, (span + 1) * SPAN)
        queries = q_ref[tokens]
        for level, (bit, prefix_ref) in enumerate(zip(bits, prefix_refs)):
            scale_ref[level] = level_scale(
                bit, first_level, prefix_ref, sums_ref, weight_ref, tokens
            )
        for at, (head, states) in enumerate(work):
            rows = pl.ds(pl.multiple_of(head * head_width, 128), head_width)
            mixed = add_found(mixed_ref[rows, tokens], queries, head, states, scale_ref)
            square = jnp.mean(mixed * mixed, axis=0, keepdims=True)
            normed = mixed * lax.rsqrt(square + EPS) * gains[at]
            columns = slice(at * head_width, (at + 1) * head_width)
            out_ref[tokens, columns] = normed.astype(jnp.bfloat16).T
        for at, (far, _) in enumerate(quarters):
            columns = pl.ds(pl.multiple_of(first_head(far, heads) * head_width, 128), size)
            copy = pltpu.make_async_copy(
                out_ref.at[tokens, at * size : (at + 1) * size],
                out_hbm.at[tokens, columns],
                sent.at[len(copies)],
            )
            copy.start()
            copies.append(copy)
    for copy in copies:
        copy.wait()


def finish(quarters, first_level, bits, shared, prefixes, parts, begun, has_token):
    mixed, queries, sums, level_weight, gain = shared
    width, tokens = mixed.shape
    heads = level_weight.shape[1]
    inputs = [*shared, *prefixes, *parts]
    specs = [HELD] * len(inputs)
    inputs = [hold(array) for array in inputs]
    out = pl.BlockSpec(memory_space=pltpu.HBM)
    aliases = {}
    if begun is not None:
        aliases = {len(inputs): 0}
        specs.append(out)
        inputs.append(begun)
    name = "finish" + "".join(f"{core}{side}" for (core, side), _ in quarters)
    shapes = [jax.ShapeDtypeStruct((tokens, width), jnp.bfloat16)]
    if has_token:
        shapes.append(pltpu.VMEM((8, 128), jnp.float32))
    return pl.pallas_call(
        functools.partial(finish_kernel, quarters, first_level, bits, has_token),
        in_specs=specs,
        out_specs=[out, HELD][: len(shapes)],
        out_shape=shapes,
        scratch_shapes=[
            pltpu.VMEM((tokens, len(quarters) * width // 4), jnp.bfloat16),
            pltpu.VMEM((len(bits), heads, SPAN), jnp.float32),
            pltpu.SemaphoreType.DMA((len(quarters) * (tokens // SPAN),)),
        ],
        input_output_aliases=aliases,
        compiler_params=PARAMS,
        cost_estimate=cost(name),
        name=name,
    )(*inputs)


def trade(value, mask):
    wide, narrow = lax.axis_size("wide"), lax.axis_size("narrow")

    def ranked(index):
        return index % narrow * wide + index // narrow

    pairs = [(ranked(source), ranked(source ^ mask)) for source in range(wide * narrow)]
    return lax.ppermute(value, AXES, pairs)


def per_device(queries, keys, values, log_decay, level_weight, norm_gain):
    heads = log_decay.shape[0]
    tokens, width = values.shape
    per = width // heads
    spans = tokens // SPAN
    group_bits = heads.bit_length() - 1
    bits = (lax.axis_size("wide") * lax.axis_size("narrow")).bit_length() - 1
    first_level = level_weight.shape[0] - bits
    gain = norm_gain.reshape(heads, per)
    message, local, sums, totals, queries, keys, values, level_weight, gain = make_states(
        queries, keys, values, log_decay, level_weight, gain
    )
    shared = (queries, keys, values, sums, totals, level_weight, local)
    last = bits - 1
    two = 2 * per
    size = two // CUTS
    sides = [(core, side) for core in (0, 1) for side in (0, 1)]
    other = trade(message, 1)
    zero = jnp.zeros((heads, 128), jnp.float32)
    chunks, give, prefix = make_chip(message, other, heads, CUTS)
    prefixes = [zero, prefix]
    found, across = {}, {}
    mixed, at = None, 0

    def both(name, messages, tokens=()):
        return pack(name, [(state, size) for state in messages], tokens)

    for bit in range(1, bits):
        found[bit] = [trade(chunk, 2**bit) for chunk in (give if bit == 1 else chunks)]
        stays = chunks if bit == 1 else stays
        waits = []
        if bit < 3 or bit == last:
            stop = spans if bit == last else at + 1
            begun = [*chunks[-1:], *([found[bit - 1]] if bit == last else [])]
            mixed, *waits = mix_local(at, stop, shared, mixed, begun, bit < last)
            at = stop
        if bit == 3:
            waits.append(rest)
        if bit < last:
            merged = []
            for offset, (chunk, state) in enumerate(zip(chunks, found[bit])):
                ending = offset == CUTS - 1
                tokens_of = [*merged[-1:], *(waits if ending else ())]
                chunk, *after = merge(
                    bit, offset, ending, chunk, state, prefixes[bit], tokens_of
                )
                merged.append(chunk)
            chunks = merged
            prefixes += after
            found[bit] = both(f"found{bit}", found[bit], chunks[-1:])
            if bit > 1:
                across[bit] = trade(found[bit], 2)
            else:
                rest = trade(both("rest", stays, chunks[-1:]), 2)

    quarters = [((core, side), [(0, 0, None)]) for core, side in sides]
    shared = (mixed, queries, sums, level_weight)
    mixed, token = add_levels(quarters, first_level, [0], shared, [zero], [other])
    state = both("state", found[last], (token,))
    beside = trade(state, 2)
    early = list(range(2, last))
    pieces = [(found[1], two), (rest, two)]
    for bit in early:
        pieces += [(found[bit], two), (across[bit], two)]
    near = pack("near", pieces, (state,))
    far = trade(near, 1)
    middle = [1, *early]
    ahead = [prefixes[bit] for bit in middle]

    def states_of(side, index, first):
        return [(first + slot, index, (2 * slot + side) * two) for slot in range(len(middle))]

    shared = (mixed, queries, sums, level_weight, gain)
    every = (first_level, [last, *middle], shared, [prefixes[last], *ahead])
    quarters = {(core, side): [(0, 0, 0), *states_of(side, 1, 1)] for core, side in sides}
    state_far = trade(pack("shared", [(state, two)], (near,)), 1)
    (out,) = finish([((0, 0), quarters[0, 0])], *every, [state, near], None, False)
    out, token = finish([((1, 0), quarters[1, 0])], *every, [state_far, far], out, True)
    beside = pack("beside", [(beside, two)], (token,))
    (out,) = finish([((0, 1), quarters[0, 1])], *every, [beside, near], out, False)
    return finish([((1, 1), quarters[1, 1])], *every, [trade(beside, 1), far], out, False)[0]


def solution(mesh):
    placed = (
        P(("wide", "narrow"), None),
        P(("wide", "narrow"), None),
        P(("wide", "narrow"), None),
        P(None, ("wide", "narrow")),
        P(None, None, ("wide", "narrow")),
        P(),
    )
    return jax.shard_map(
        per_device,
        mesh=mesh,
        in_specs=placed,
        out_specs=P(("wide", "narrow"), None),
        check_vma=False,
    )
```

```python
import functools

import jax
import jax.numpy as jnp
from jax import lax
from jax.experimental import pallas as pl
from jax.experimental.pallas import tpu as pltpu
from jax.sharding import PartitionSpec as P

SPAN = 256
SPLIT_BITS = 2
CUTS = 2
EPS = 1e-05
AXES = ("narrow", "wide")
NT = (((1,), (1,)), ((), ()))
COSTS = {"finish00": 20000000000, "finish10": 1000, "finish01": 20000000000, "local2": 1000, "reach": 1000}


def cost(name):
    flops = COSTS.get(name, 2000000000)
    return pl.CostEstimate(flops=flops, transcendentals=0, bytes_accessed=1_000_000)


PARAMS = pltpu.CompilerParams(vmem_limit_bytes=32 * 1024 * 1024)
HELD = pl.BlockSpec(memory_space=pltpu.VMEM)


def place():
    return lax.axis_index("wide") * lax.axis_size("narrow") + lax.axis_index("narrow")


def bit_of(value, bit):
    return jnp.bitwise_and(jnp.right_shift(value, bit), 1)


def spread_lanes(column, width):
    return jnp.broadcast_to(column, (column.shape[0], width))


ANYWHERE = pl.BlockSpec(memory_space=pl.ANY)


def hold(array):
    return pltpu.with_memory_space_constraint(array, pltpu.VMEM)


def call(kernel, name, inputs, outputs, scratch=(), in_specs=None, aliases=None):
    specs = in_specs or [HELD] * len(inputs)
    inputs = [hold(array) if spec is HELD else array for array, spec in zip(inputs, specs)]
    return pl.pallas_call(
        kernel,
        in_specs=specs,
        out_specs=[HELD] * len(outputs),
        out_shape=[pltpu.VMEM(shape, dtype) for shape, dtype in outputs],
        scratch_shapes=list(scratch),
        input_output_aliases=aliases or {},
        compiler_params=PARAMS,
        cost_estimate=cost(name),
        name=name,
    )(*inputs)


def running_sums(rows):
    high = rows.astype(jnp.bfloat16)
    rest = rows - high.astype(jnp.float32)
    middle = rest.astype(jnp.bfloat16)
    low = (rest - middle.astype(jnp.float32)).astype(jnp.bfloat16)
    width = rows.shape[1]
    source = lax.broadcasted_iota(jnp.int32, (width, width), 0)
    target = lax.broadcasted_iota(jnp.int32, (width, width), 1)
    upto = jnp.where(source <= target, 1.0, 0.0).astype(jnp.bfloat16)
    sums = jnp.dot(
        jnp.concatenate([high, middle, low], axis=0), upto, preferred_element_type=jnp.float32
    )
    count = rows.shape[0]
    return sums[:count] + (sums[count : 2 * count] + sums[2 * count :])


def state_kernel(*refs):
    q_hbm, k_hbm, v_hbm, decay_hbm, weight_hbm, gain_hbm = refs[:6]
    message_ref, local_ref, sums_ref, totals_ref = refs[6:10]
    q_ref, k_ref, v_ref, weight_ref, gain_ref, decay_ref, held, arrived = refs[10:]
    heads, tokens = decay_ref.shape
    head_width = v_ref.shape[1] // heads
    spans = tokens // SPAN
    rows_of = [slice(span * SPAN, (span + 1) * SPAN) for span in range(spans)]
    loads = [(decay_hbm, decay_ref), (k_hbm, k_ref)]
    loads += [(v_hbm.at[rows], v_ref.at[rows]) for rows in rows_of]
    loads += [(q_hbm, q_ref), (weight_hbm, weight_ref), (gain_hbm, gain_ref)]
    copies = [
        pltpu.make_async_copy(source, target, arrived.at[at])
        for at, (source, target) in enumerate(loads)
    ]
    for copy in copies:
        copy.start()
    copies[0].wait()
    within = running_sums(jnp.concatenate([decay_ref[:, rows] for rows in rows_of], axis=0))
    run = jnp.zeros((heads, 128), jnp.float32)
    fades, wholes = [], []
    for span, rows in enumerate(rows_of):
        here = within[span * heads : (span + 1) * heads]
        last = here[:, SPAN - 1 :]
        total = spread_lanes(last, 128)
        sums_ref[0, :, rows] = here
        sums_ref[1, :, rows] = here + spread_lanes(run[:, :1], SPAN)
        totals_ref[span] = total
        run = run + total
        fades.append(jnp.exp(spread_lanes(last, SPAN) - here))
        wholes.append(jnp.exp(total))
    copies[1].wait()
    across = [k_ref[rows].astype(jnp.float32).T for rows in rows_of]
    local_bits = spans.bit_length() - 1
    for span, rows in enumerate(rows_of):
        copies[2 + span].wait()
        for head in range(heads):
            columns = slice(head * head_width, (head + 1) * head_width)
            faded = (across[span] * fades[span][head : head + 1]).astype(jnp.bfloat16)
            state = jnp.dot(faded, v_ref[rows, columns], preferred_element_type=jnp.float32)
            at = 0
            for bit in range(local_bits + 1):
                if span >> bit & 1 == 0 or bit == local_bits:
                    group = state
                    if span % 2**bit > 0:
                        group = held[bit - 1, head] * wholes[span][head : head + 1] + state
                    if (span + 1) % 2**bit > 0:
                        held[bit - 1, head] = group
                    elif bit < local_bits:
                        local_ref[at + (span >> (bit + 1)), :, columns] = group.astype(
                            jnp.bfloat16
                        )
                    else:
                        message_ref[columns] = group.T
                at += spans >> (bit + 1)
    message_ref[heads * head_width :] = run
    for copy in copies[2 + spans :]:
        copy.wait()


def make_states(queries, keys, values, log_decay, level_weight, gain):
    tokens, key_width = keys.shape
    heads = log_decay.shape[0]
    width = values.shape[1]
    spans = tokens // SPAN
    inputs = [queries, keys, values, log_decay, level_weight, gain]
    kept = [queries, keys, values, level_weight, gain]
    return call(
        state_kernel,
        "states",
        [pltpu.with_memory_space_constraint(array, pltpu.HBM) for array in inputs],
        [
            ((width + heads, key_width), jnp.float32),
            ((spans - 1, key_width, width), jnp.bfloat16),
            ((2, heads, tokens), jnp.float32),
            ((spans, heads, 128), jnp.float32),
            *[(array.shape, array.dtype) for array in kept],
        ],
        [
            pltpu.VMEM(log_decay.shape, jnp.float32),
            pltpu.VMEM((spans.bit_length() - 1, heads, key_width, width // heads), jnp.float32),
            pltpu.SemaphoreType.DMA((spans + 5,)),
        ],
        [pl.BlockSpec(memory_space=pltpu.HBM)] * len(inputs),
    )


def local_kernel(first, last, has_token, *refs):
    q_ref, k_ref, v_ref, sums_ref, totals_ref, weight_ref, local_ref = refs[:7]
    if has_token:
        mixed_ref, done_ref = refs[-2:]
        done_ref[...] = jnp.zeros_like(done_ref)
    else:
        mixed_ref = refs[-1]
    heads = weight_ref.shape[1]
    head_width = v_ref.shape[1] // heads
    spans = totals_ref.shape[0]
    local_bits = spans.bit_length() - 1
    half = SPAN // 2
    source = lax.broadcasted_iota(jnp.int32, (half, half), 0)
    target = lax.broadcasted_iota(jnp.int32, (half, half), 1)
    causal = source <= target
    empty = jnp.zeros((half, half), jnp.bfloat16)

    for span in range(first, last):
        tokens = slice(span * SPAN, (span + 1) * SPAN)
        queries = q_ref[tokens]
        scores = lax.dot_general(
            k_ref[tokens], queries, NT, preferred_element_type=jnp.float32
        )
        within = sums_ref[0, :, tokens]
        within_down = within.T
        weight = weight_ref[0, :, tokens]
        values_across = v_ref[tokens].T

        def mix(head, low, high):
            rows = slice(low * half, (low + 1) * half)
            columns = slice(high * half, (high + 1) * half)
            gap = within[head : head + 1, columns] - within_down[rows, head : head + 1]
            if low == high:
                gap = jnp.where(causal, gap, -1e30)
            mixing = scores[rows, columns] * jnp.exp(gap) * weight[head : head + 1, columns]
            return mixing.astype(jnp.bfloat16)

        levels = []
        offset = 0
        for bit in range(local_bits):
            if span >> bit & 1:
                since = within
                for back in range(1, span % 2**bit + 1):
                    since = since + spread_lanes(totals_ref[span - back][:, :1], SPAN)
                scale = jnp.exp(since) * weight_ref[1 + bit, :, tokens]
                levels.append((local_ref[offset + (span >> (bit + 1))].T, scale))
            offset += spans >> (bit + 1)
        for head in range(heads):
            rows = slice(head * head_width, (head + 1) * head_width)
            mixing = jnp.concatenate(
                [
                    jnp.concatenate([mix(head, 0, 0), mix(head, 0, 1)], axis=1),
                    jnp.concatenate([empty, mix(head, 1, 1)], axis=1),
                ],
                axis=0,
            )
            mixed = jnp.dot(values_across[rows], mixing, preferred_element_type=jnp.float32)
            for level, scale in levels:
                found = lax.dot_general(
                    level[rows], queries, NT, preferred_element_type=jnp.float32
                )
                mixed = mixed + found * scale[head : head + 1]
            mixed_ref[rows, tokens] = mixed


def mix_local(first, last, shared, mixed, tokens, has_token):
    queries, keys, values, sums, totals, level_weight, local = shared
    rest = [] if mixed is None else [mixed]
    return call(
        functools.partial(local_kernel, first, last, has_token),
        f"local{first}",
        [*shared, *rest, *tokens],
        [(values.shape[::-1], jnp.float32), ((8, 128), jnp.float32)][: 1 + has_token],
        aliases={7: 0} if rest else None,
    )


def join(upper, mine, mine_total, other, other_total):
    fade = jnp.exp(jnp.where(upper, mine_total, other_total))
    return jnp.where(upper, other * fade + mine, mine * fade + other)


def first_head(far, heads):
    here = place()
    first = 0
    for bit, flip in enumerate(far):
        first = first + jnp.bitwise_xor(bit_of(here, bit), flip) * (heads >> (bit + 1))
    return first


def chip_kernel(mine_ref, other_ref, *refs):
    *message_refs, next_ref, whole_ref = refs
    heads = next_ref.shape[0]
    width = mine_ref.shape[0] - heads
    per = width // heads
    held = whole_ref.shape[0] // per
    here = place()
    upper = bit_of(here, 0) == 1
    first = first_head((0,), heads)
    for slot in range(held):
        part = pl.ds(pl.multiple_of((first + slot) * per, 8), per)
        total = pl.ds(width + first + slot, 1)
        whole_ref[slot * per : (slot + 1) * per] = join(
            upper, mine_ref[part], mine_ref[total], other_ref[part], other_ref[total]
        )
    other_total = other_ref[width:]
    total = mine_ref[width:] + other_total
    next_ref[...] = jnp.where(upper, other_total, 0.0)
    half = held * per // 2
    side = bit_of(here, 1)
    cuts = len(message_refs) // 2
    size = half // cuts
    for at, ref in enumerate(message_refs):
        start = (side if at < cuts else 1 - side) * half + at % cuts * size
        ref[:size] = whole_ref[pl.ds(pl.multiple_of(start, 8), size)]
        ref[size:] = total


def make_chip(mine, other, heads, cuts):
    rows, lanes = mine.shape
    half = (rows - heads) // 2
    *messages, prefix = call(
        chip_kernel,
        "chip",
        [mine, other],
        [
            *[((half // 2 // cuts + heads, lanes), jnp.float32)] * (2 * cuts),
            ((heads, lanes), jnp.float32),
        ],
        [pltpu.VMEM((half, lanes), jnp.float32)],
    )
    return messages[:cuts], messages[cuts:], prefix


def merge_kernel(bit, offset, has_prefix, *refs):
    mine_ref, other_ref, prefix_ref = refs[:3]
    merged_ref = refs[-2] if has_prefix else refs[-1]
    heads = prefix_ref.shape[0]
    rows = mine_ref.shape[0] - heads
    per = mine_ref.shape[1]
    upper = bit_of(place(), bit) == 1
    first = first_head((0,) * SPLIT_BITS, heads) + offset
    for slot in range(rows // per):
        part = slice(slot * per, (slot + 1) * per)
        total = pl.ds(rows + first + slot, 1)
        merged_ref[part] = join(
            upper, mine_ref[part], mine_ref[total], other_ref[part], other_ref[total]
        )
    other_total = other_ref[rows:]
    merged_ref[rows:] = mine_ref[rows:] + other_total
    if has_prefix:
        refs[-1][...] = prefix_ref[...] + jnp.where(upper, other_total, 0.0)


def merge(bit, offset, has_prefix, mine, other, prefix, tokens=()):
    return call(
        functools.partial(merge_kernel, bit, offset, has_prefix),
        f"merge{bit}{offset}",
        [mine, other, prefix, *tokens],
        [(mine.shape, jnp.float32), (prefix.shape, jnp.float32)][: 1 + has_prefix],
    )


def pack_kernel(takes, *refs):
    out_ref = refs[-1]
    at = 0
    for ref, rows in zip(refs, takes):
        out_ref[at : at + rows] = ref[:rows]
        at += rows


def pack(name, pieces, tokens=()):
    takes = [rows for _, rows in pieces]
    lanes = pieces[0][0].shape[1]
    return call(
        functools.partial(pack_kernel, takes),
        name,
        [*[array for array, _ in pieces], *tokens],
        [((sum(takes), lanes), jnp.float32)],
    )[0]


def level_scale(bit, first_level, prefix_ref, sums_ref, weight_ref, tokens):
    active = jnp.where(bit_of(place(), bit) == 1, 1.0, 0.0)
    reach = jnp.exp(sums_ref[1, :, tokens] + spread_lanes(prefix_ref[:, :1], SPAN))
    return reach * weight_ref[first_level + bit, :, tokens] * active


def gather_work(quarters, part_refs, heads, per):
    work = []
    for far, pieces in quarters:
        first = first_head(far, heads)
        for slot in range(heads // 4):
            states = []
            for level, index, start in pieces:
                if start is None:
                    rows = pl.ds(pl.multiple_of((first + slot) * per, 128), per)
                else:
                    rows = slice(start + slot * per, start + (slot + 1) * per)
                states.append((level, part_refs[index][rows].astype(jnp.bfloat16)))
            work.append((first + slot, states))
    return work


def add_found(mixed, queries, head, states, scale_ref):
    for level, state in states:
        found = lax.dot_general(state, queries, NT, preferred_element_type=jnp.float32)
        mixed = mixed + found * scale_ref[level, pl.ds(head, 1)]
    return mixed


def reach_kernel(quarters, first_level, bits, *refs):
    mixed_ref, q_ref, sums_ref, weight_ref = refs[:4]
    prefix_refs = refs[4 : 4 + len(bits)]
    part_refs = refs[4 + len(bits) :]
    out_ref, done_ref, scale_ref = refs[-3:]
    done_ref[...] = jnp.zeros_like(done_ref)
    heads = weight_ref.shape[1]
    head_width = mixed_ref.shape[0] // heads
    work = gather_work(quarters, part_refs, heads, head_width)
    for span in range(q_ref.shape[0] // SPAN):
        tokens = slice(span * SPAN, (span + 1) * SPAN)
        queries = q_ref[tokens]
        for level, (bit, prefix_ref) in enumerate(zip(bits, prefix_refs)):
            scale_ref[level] = level_scale(
                bit, first_level, prefix_ref, sums_ref, weight_ref, tokens
            )
        for head, states in work:
            rows = pl.ds(pl.multiple_of(head * head_width, 128), head_width)
            out_ref[rows, tokens] = add_found(
                mixed_ref[rows, tokens], queries, head, states, scale_ref
            )


def add_levels(quarters, first_level, bits, shared, prefixes, parts):
    mixed, _, _, level_weight = shared
    return call(
        functools.partial(reach_kernel, quarters, first_level, bits),
        "reach",
        [*shared, *prefixes, *parts],
        [(mixed.shape, jnp.float32), ((8, 128), jnp.float32)],
        [pltpu.VMEM((len(bits), level_weight.shape[1], SPAN), jnp.float32)],
        aliases={0: 0},
    )


def finish_kernel(quarters, first_level, bits, stays, carried, *refs):
    mixed_ref, q_ref, sums_ref, weight_ref, gain_ref = refs[:5]
    prefix_refs = refs[5 : 5 + len(bits)]
    part_refs = refs[5 + len(bits) :]
    out_refs, (own_ref, scale_ref, sent) = refs[-3 - FINISH_OUTS[stays, carried] : -3], refs[-3:]
    if stays:
        own_ref = out_refs[-1]
    heads = weight_ref.shape[1]
    head_width = mixed_ref.shape[0] // heads
    size = heads // 4 * head_width
    copies = []

    def send(block, far, rows):
        columns = pl.ds(pl.multiple_of(first_head(far, heads) * head_width, 128), size)
        copy = pltpu.make_async_copy(
            block.at[rows], out_refs[0].at[rows, columns], sent.at[len(copies)]
        )
        copy.start()
        copies.append(copy)

    if carried is not None:
        index, far = carried
        send(part_refs[index], far, slice(0, q_ref.shape[0]))
    work = gather_work(quarters, part_refs, heads, head_width)
    gains = []
    for head, _ in work:
        row = jnp.broadcast_to(gain_ref[pl.ds(head, 1)], (8, head_width))
        gains.append(row.T[:, :1])
    for span in range(q_ref.shape[0] // SPAN):
        tokens = slice(span * SPAN, (span + 1) * SPAN)
        queries = q_ref[tokens]
        for level, (bit, prefix_ref) in enumerate(zip(bits, prefix_refs)):
            scale_ref[level] = level_scale(
                bit, first_level, prefix_ref, sums_ref, weight_ref, tokens
            )
        for at, (head, states) in enumerate(work):
            rows = pl.ds(pl.multiple_of(head * head_width, 128), head_width)
            mixed = add_found(mixed_ref[rows, tokens], queries, head, states, scale_ref)
            square = jnp.mean(mixed * mixed, axis=0, keepdims=True)
            normed = mixed * lax.rsqrt(square + EPS) * gains[at]
            columns = slice(at * head_width, (at + 1) * head_width)
            own_ref[tokens, columns] = normed.astype(jnp.bfloat16).T
        if not stays:
            send(own_ref, quarters[0][0], tokens)
    for copy in copies:
        copy.wait()


FINISH_OUTS = {}


def finish(quarters, first_level, bits, shared, prefixes, parts, begun, stays, carried):
    mixed, queries, sums, level_weight, gain = shared
    width, tokens = mixed.shape
    heads = level_weight.shape[1]
    inputs = [*shared, *prefixes, *parts]
    specs = [HELD] * len(inputs)
    inputs = [hold(array) for array in inputs]
    hbm = pl.BlockSpec(memory_space=pltpu.HBM)
    aliases = {}
    if begun is not None:
        aliases = {len(inputs): 0}
        specs.append(hbm)
        inputs.append(begun)
    name = "finish" + "".join(f"{core}{side}" for (core, side), _ in quarters)
    block = (tokens, width // 4)
    out_specs, shapes = [], []
    if carried is not None or not stays:
        out_specs.append(hbm)
        shapes.append(jax.ShapeDtypeStruct((tokens, width), jnp.bfloat16))
    if stays:
        out_specs.append(HELD)
        shapes.append(pltpu.VMEM(block, jnp.bfloat16))
    FINISH_OUTS[stays, carried] = len(shapes)
    return pl.pallas_call(
        functools.partial(finish_kernel, quarters, first_level, bits, stays, carried),
        in_specs=specs,
        out_specs=out_specs,
        out_shape=shapes,
        scratch_shapes=[
            pltpu.VMEM((8, 128) if stays else block, jnp.bfloat16),
            pltpu.VMEM((len(bits), heads, SPAN), jnp.float32),
            pltpu.SemaphoreType.DMA((1 + tokens // SPAN,)),
        ],
        input_output_aliases=aliases,
        compiler_params=PARAMS,
        cost_estimate=cost(name),
        name=name,
    )(*inputs)


def trade(value, mask):
    wide, narrow = lax.axis_size("wide"), lax.axis_size("narrow")

    def ranked(index):
        return index % narrow * wide + index // narrow

    pairs = [(ranked(source), ranked(source ^ mask)) for source in range(wide * narrow)]
    return lax.ppermute(value, AXES, pairs)


def per_device(queries, keys, values, log_decay, level_weight, norm_gain):
    heads = log_decay.shape[0]
    tokens, width = values.shape
    per = width // heads
    spans = tokens // SPAN
    group_bits = heads.bit_length() - 1
    bits = (lax.axis_size("wide") * lax.axis_size("narrow")).bit_length() - 1
    first_level = level_weight.shape[0] - bits
    gain = norm_gain.reshape(heads, per)
    message, local, sums, totals, queries, keys, values, level_weight, gain = make_states(
        queries, keys, values, log_decay, level_weight, gain
    )
    shared = (queries, keys, values, sums, totals, level_weight, local)
    last = bits - 1
    two = 2 * per
    size = two // CUTS
    sides = [(core, side) for core in (0, 1) for side in (0, 1)]
    other = trade(message, 1)
    zero = jnp.zeros((heads, 128), jnp.float32)
    chunks, give, prefix = make_chip(message, other, heads, CUTS)
    prefixes = [zero, prefix]
    found, across = {}, {}
    mixed, at = None, 0

    def both(name, messages, tokens=()):
        return pack(name, [(state, size) for state in messages], tokens)

    for bit in range(1, bits):
        found[bit] = [trade(chunk, 2**bit) for chunk in (give if bit == 1 else chunks)]
        stays = chunks if bit == 1 else stays
        waits = []
        if bit < 3 or bit == last:
            stop = spans if bit == last else at + 1
            begun = [*chunks[-1:], *([found[bit - 1]] if bit == last else [])]
            mixed, *waits = mix_local(at, stop, shared, mixed, begun, bit < last)
            at = stop
        if bit == 3:
            waits.append(rest)
        if bit < last:
            merged = {}
            order = list(reversed(range(CUTS)))
            for offset in order:
                ending = offset == order[-1]
                tokens_of = [*merged.values(), *(waits if ending else ())]
                merged[offset], *after = merge(
                    bit, offset, ending, chunks[offset], found[bit][offset], prefixes[bit], tokens_of
                )
            chunks = [merged[offset] for offset in range(CUTS)]
            newest = merged[order[-1]]
            prefixes += after
            found[bit] = both(f"found{bit}", found[bit], chunks[-1:])
            if bit > 1:
                across[bit] = trade(found[bit], 2)
            else:
                rest = trade(both("rest", stays, (newest,)), 2)

    quarters = [((core, side), [(0, 0, None)]) for core, side in sides]
    shared = (mixed, queries, sums, level_weight)
    mixed, token = add_levels(quarters, first_level, [0], shared, [zero], [other])
    state = both("state", found[last], (token,))
    beside = trade(state, 2)
    early = list(range(2, last))
    pieces = [(found[1], two), (rest, two)]
    for bit in early:
        pieces += [(found[bit], two), (across[bit], two)]
    near = pack("near", pieces, (state,))
    far = trade(near, 1)
    middle = [1, *early]
    ahead = [prefixes[bit] for bit in middle]

    def states_of(side, index, first):
        return [(first + slot, index, (2 * slot + side) * two) for slot in range(len(middle))]

    shared = (mixed, queries, sums, level_weight, gain)
    every = (first_level, [last, *middle], shared, [prefixes[last], *ahead])
    quarters = {(core, side): [(0, 0, 0), *states_of(side, 1, 1)] for core, side in sides}
    state_far = trade(pack("shared", [(state, two)], (near,)), 1)
    (block,) = finish([((0, 0), quarters[0, 0])], *every, [state, near], None, True, None)
    out, block = finish(
        [((1, 0), quarters[1, 0])], *every, [state_far, far, block], None, True, (2, (0, 0))
    )
    beside = pack("beside", [(beside, two)], (block,))
    (out,) = finish(
        [((0, 1), quarters[0, 1])], *every, [beside, near, block], out, False, (2, (1, 0))
    )
    beside_far = trade(beside, 1)
    return finish([((1, 1), quarters[1, 1])], *every, [beside_far, far], out, False, None)[0]


def solution(mesh):
    placed = (
        P(("wide", "narrow"), None),
        P(("wide", "narrow"), None),
        P(("wide", "narrow"), None),
        P(None, ("wide", "narrow")),
        P(None, None, ("wide", "narrow")),
        P(),
    )
    return jax.shard_map(
        per_device,
        mesh=mesh,
        in_specs=placed,
        out_specs=P(("wide", "narrow"), None),
        check_vma=False,
    )
```

```python
import functools

import jax
import jax.numpy as jnp
from jax import lax
from jax.experimental import pallas as pl
from jax.experimental.pallas import tpu as pltpu
from jax.sharding import PartitionSpec as P

SPAN = 256
SPLIT_BITS = 2
CUTS = 2
EPS = 1e-05
AXES = ("narrow", "wide")
NT = (((1,), (1,)), ((), ()))
COSTS = {"finish00": 20000000000, "finish10": 1000, "finish01": 20000000000, "local2": 1000, "reach": 1000}


def cost(name):
    flops = COSTS.get(name, 2000000000)
    return pl.CostEstimate(flops=flops, transcendentals=0, bytes_accessed=1_000_000)


PARAMS = pltpu.CompilerParams(vmem_limit_bytes=32 * 1024 * 1024)
HELD = pl.BlockSpec(memory_space=pltpu.VMEM)


def place():
    return lax.axis_index("wide") * lax.axis_size("narrow") + lax.axis_index("narrow")


def bit_of(value, bit):
    return jnp.bitwise_and(jnp.right_shift(value, bit), 1)


def spread_lanes(column, width):
    return jnp.broadcast_to(column, (column.shape[0], width))


ANYWHERE = pl.BlockSpec(memory_space=pl.ANY)


def hold(array):
    return pltpu.with_memory_space_constraint(array, pltpu.VMEM)


def call(kernel, name, inputs, outputs, scratch=(), in_specs=None, aliases=None):
    specs = in_specs or [HELD] * len(inputs)
    inputs = [hold(array) if spec is HELD else array for array, spec in zip(inputs, specs)]
    return pl.pallas_call(
        kernel,
        in_specs=specs,
        out_specs=[HELD] * len(outputs),
        out_shape=[pltpu.VMEM(shape, dtype) for shape, dtype in outputs],
        scratch_shapes=list(scratch),
        input_output_aliases=aliases or {},
        compiler_params=PARAMS,
        cost_estimate=cost(name),
        name=name,
    )(*inputs)


def running_sums(rows):
    high = rows.astype(jnp.bfloat16)
    rest = rows - high.astype(jnp.float32)
    middle = rest.astype(jnp.bfloat16)
    low = (rest - middle.astype(jnp.float32)).astype(jnp.bfloat16)
    width = rows.shape[1]
    source = lax.broadcasted_iota(jnp.int32, (width, width), 0)
    target = lax.broadcasted_iota(jnp.int32, (width, width), 1)
    upto = jnp.where(source <= target, 1.0, 0.0).astype(jnp.bfloat16)
    sums = jnp.dot(
        jnp.concatenate([high, middle, low], axis=0), upto, preferred_element_type=jnp.float32
    )
    count = rows.shape[0]
    return sums[:count] + (sums[count : 2 * count] + sums[2 * count :])


def state_kernel(*refs):
    q_hbm, k_hbm, v_hbm, decay_hbm, weight_hbm, gain_hbm = refs[:6]
    message_ref, local_ref, sums_ref, totals_ref = refs[6:10]
    q_ref, k_ref, v_ref, weight_ref, gain_ref, decay_ref, held, arrived = refs[10:]
    heads, tokens = decay_ref.shape
    head_width = v_ref.shape[1] // heads
    spans = tokens // SPAN
    rows_of = [slice(span * SPAN, (span + 1) * SPAN) for span in range(spans)]
    loads = [(decay_hbm, decay_ref), (k_hbm, k_ref)]
    loads += [(v_hbm.at[rows], v_ref.at[rows]) for rows in rows_of]
    loads += [(q_hbm, q_ref), (weight_hbm, weight_ref), (gain_hbm, gain_ref)]
    copies = [
        pltpu.make_async_copy(source, target, arrived.at[at])
        for at, (source, target) in enumerate(loads)
    ]
    for copy in copies:
        copy.start()
    copies[0].wait()
    within = running_sums(jnp.concatenate([decay_ref[:, rows] for rows in rows_of], axis=0))
    run = jnp.zeros((heads, 128), jnp.float32)
    fades, wholes = [], []
    for span, rows in enumerate(rows_of):
        here = within[span * heads : (span + 1) * heads]
        last = here[:, SPAN - 1 :]
        total = spread_lanes(last, 128)
        sums_ref[0, :, rows] = here
        sums_ref[1, :, rows] = here + spread_lanes(run[:, :1], SPAN)
        totals_ref[span] = total
        run = run + total
        fades.append(jnp.exp(spread_lanes(last, SPAN) - here))
        wholes.append(jnp.exp(total))
    copies[1].wait()
    across = [k_ref[rows].astype(jnp.float32).T for rows in rows_of]
    local_bits = spans.bit_length() - 1
    for span, rows in enumerate(rows_of):
        copies[2 + span].wait()
        for head in range(heads):
            columns = slice(head * head_width, (head + 1) * head_width)
            faded = (across[span] * fades[span][head : head + 1]).astype(jnp.bfloat16)
            state = jnp.dot(faded, v_ref[rows, columns], preferred_element_type=jnp.float32)
            at = 0
            for bit in range(local_bits + 1):
                if span >> bit & 1 == 0 or bit == local_bits:
                    group = state
                    if span % 2**bit > 0:
                        group = held[bit - 1, head] * wholes[span][head : head + 1] + state
                    if (span + 1) % 2**bit > 0:
                        held[bit - 1, head] = group
                    elif bit < local_bits:
                        local_ref[at + (span >> (bit + 1)), :, columns] = group.astype(
                            jnp.bfloat16
                        )
                    else:
                        message_ref[columns] = group.T
                at += spans >> (bit + 1)
    message_ref[heads * head_width :] = run
    for copy in copies[2 + spans :]:
        copy.wait()


def make_states(queries, keys, values, log_decay, level_weight, gain):
    tokens, key_width = keys.shape
    heads = log_decay.shape[0]
    width = values.shape[1]
    spans = tokens // SPAN
    inputs = [queries, keys, values, log_decay, level_weight, gain]
    kept = [queries, keys, values, level_weight, gain]
    return call(
        state_kernel,
        "states",
        [pltpu.with_memory_space_constraint(array, pltpu.HBM) for array in inputs],
        [
            ((width + heads, key_width), jnp.float32),
            ((spans - 1, key_width, width), jnp.bfloat16),
            ((2, heads, tokens), jnp.float32),
            ((spans, heads, 128), jnp.float32),
            *[(array.shape, array.dtype) for array in kept],
        ],
        [
            pltpu.VMEM(log_decay.shape, jnp.float32),
            pltpu.VMEM((spans.bit_length() - 1, heads, key_width, width // heads), jnp.float32),
            pltpu.SemaphoreType.DMA((spans + 5,)),
        ],
        [pl.BlockSpec(memory_space=pltpu.HBM)] * len(inputs),
    )


def local_kernel(first, last, has_token, *refs):
    q_ref, k_ref, v_ref, sums_ref, totals_ref, weight_ref, local_ref, near_ref = refs[:8]
    if has_token:
        mixed_ref, done_ref = refs[-2:]
        done_ref[...] = jnp.zeros_like(done_ref)
    else:
        mixed_ref = refs[-1]
    heads = weight_ref.shape[1]
    head_width = v_ref.shape[1] // heads
    spans = totals_ref.shape[0]
    local_bits = spans.bit_length() - 1
    half = SPAN // 2
    source = lax.broadcasted_iota(jnp.int32, (half, half), 0)
    target = lax.broadcasted_iota(jnp.int32, (half, half), 1)
    causal = source <= target
    empty = jnp.zeros((half, half), jnp.bfloat16)
    upper = jnp.where(bit_of(place(), 0) == 1, 1.0, 0.0)
    near = near_ref[: heads * head_width].astype(jnp.bfloat16)

    for span in range(first, last):
        tokens = slice(span * SPAN, (span + 1) * SPAN)
        queries = q_ref[tokens]
        scores = lax.dot_general(
            k_ref[tokens], queries, NT, preferred_element_type=jnp.float32
        )
        within = sums_ref[0, :, tokens]
        within_down = within.T
        weight = weight_ref[0, :, tokens]
        values_across = v_ref[tokens].T

        def mix(head, low, high):
            rows = slice(low * half, (low + 1) * half)
            columns = slice(high * half, (high + 1) * half)
            gap = within[head : head + 1, columns] - within_down[rows, head : head + 1]
            if low == high:
                gap = jnp.where(causal, gap, -1e30)
            mixing = scores[rows, columns] * jnp.exp(gap) * weight[head : head + 1, columns]
            return mixing.astype(jnp.bfloat16)

        levels = []
        offset = 0
        for bit in range(local_bits):
            if span >> bit & 1:
                since = within
                for back in range(1, span % 2**bit + 1):
                    since = since + spread_lanes(totals_ref[span - back][:, :1], SPAN)
                scale = jnp.exp(since) * weight_ref[1 + bit, :, tokens]
                levels.append((local_ref[offset + (span >> (bit + 1))].T, scale))
            offset += spans >> (bit + 1)
        reach = jnp.exp(sums_ref[1, :, tokens]) * weight_ref[1 + local_bits, :, tokens] * upper
        levels.append((near, reach))
        for head in range(heads):
            rows = slice(head * head_width, (head + 1) * head_width)
            mixing = jnp.concatenate(
                [
                    jnp.concatenate([mix(head, 0, 0), mix(head, 0, 1)], axis=1),
                    jnp.concatenate([empty, mix(head, 1, 1)], axis=1),
                ],
                axis=0,
            )
            mixed = jnp.dot(values_across[rows], mixing, preferred_element_type=jnp.float32)
            for level, scale in levels:
                found = lax.dot_general(
                    level[rows], queries, NT, preferred_element_type=jnp.float32
                )
                mixed = mixed + found * scale[head : head + 1]
            mixed_ref[rows, tokens] = mixed


def mix_local(first, last, shared, mixed, tokens, has_token):
    values = shared[2]
    rest = [] if mixed is None else [mixed]
    return call(
        functools.partial(local_kernel, first, last, has_token),
        f"local{first}",
        [*shared, *rest, *tokens],
        [(values.shape[::-1], jnp.float32), ((8, 128), jnp.float32)][: 1 + has_token],
        aliases={8: 0} if rest else None,
    )


def join(upper, mine, mine_total, other, other_total):
    fade = jnp.exp(jnp.where(upper, mine_total, other_total))
    return jnp.where(upper, other * fade + mine, mine * fade + other)


def first_head(far, heads):
    here = place()
    first = 0
    for bit, flip in enumerate(far):
        first = first + jnp.bitwise_xor(bit_of(here, bit), flip) * (heads >> (bit + 1))
    return first


def chip_kernel(mine_ref, other_ref, *refs):
    *message_refs, next_ref, whole_ref = refs
    heads = next_ref.shape[0]
    width = mine_ref.shape[0] - heads
    per = width // heads
    held = whole_ref.shape[0] // per
    here = place()
    upper = bit_of(here, 0) == 1
    first = first_head((0,), heads)
    for slot in range(held):
        part = pl.ds(pl.multiple_of((first + slot) * per, 8), per)
        total = pl.ds(width + first + slot, 1)
        whole_ref[slot * per : (slot + 1) * per] = join(
            upper, mine_ref[part], mine_ref[total], other_ref[part], other_ref[total]
        )
    other_total = other_ref[width:]
    total = mine_ref[width:] + other_total
    next_ref[...] = jnp.where(upper, other_total, 0.0)
    half = held * per // 2
    side = bit_of(here, 1)
    cuts = len(message_refs) // 2
    size = half // cuts
    for at, ref in enumerate(message_refs):
        start = (side if at < cuts else 1 - side) * half + at % cuts * size
        ref[:size] = whole_ref[pl.ds(pl.multiple_of(start, 8), size)]
        ref[size:] = total


def make_chip(mine, other, heads, cuts):
    rows, lanes = mine.shape
    half = (rows - heads) // 2
    *messages, prefix = call(
        chip_kernel,
        "chip",
        [mine, other],
        [
            *[((half // 2 // cuts + heads, lanes), jnp.float32)] * (2 * cuts),
            ((heads, lanes), jnp.float32),
        ],
        [pltpu.VMEM((half, lanes), jnp.float32)],
    )
    return messages[:cuts], messages[cuts:], prefix


def merge_kernel(bit, offset, has_prefix, *refs):
    mine_ref, other_ref, prefix_ref = refs[:3]
    merged_ref = refs[-2] if has_prefix else refs[-1]
    heads = prefix_ref.shape[0]
    rows = mine_ref.shape[0] - heads
    per = mine_ref.shape[1]
    upper = bit_of(place(), bit) == 1
    first = first_head((0,) * SPLIT_BITS, heads) + offset
    for slot in range(rows // per):
        part = slice(slot * per, (slot + 1) * per)
        total = pl.ds(rows + first + slot, 1)
        merged_ref[part] = join(
            upper, mine_ref[part], mine_ref[total], other_ref[part], other_ref[total]
        )
    other_total = other_ref[rows:]
    merged_ref[rows:] = mine_ref[rows:] + other_total
    if has_prefix:
        refs[-1][...] = prefix_ref[...] + jnp.where(upper, other_total, 0.0)


def merge(bit, offset, has_prefix, mine, other, prefix, tokens=()):
    return call(
        functools.partial(merge_kernel, bit, offset, has_prefix),
        f"merge{bit}{offset}",
        [mine, other, prefix, *tokens],
        [(mine.shape, jnp.float32), (prefix.shape, jnp.float32)][: 1 + has_prefix],
    )


def pack_kernel(takes, *refs):
    out_ref = refs[-1]
    at = 0
    for ref, rows in zip(refs, takes):
        out_ref[at : at + rows] = ref[:rows]
        at += rows


def pack(name, pieces, tokens=()):
    takes = [rows for _, rows in pieces]
    lanes = pieces[0][0].shape[1]
    return call(
        functools.partial(pack_kernel, takes),
        name,
        [*[array for array, _ in pieces], *tokens],
        [((sum(takes), lanes), jnp.float32)],
    )[0]


def level_scale(bit, first_level, prefix_ref, sums_ref, weight_ref, tokens):
    active = jnp.where(bit_of(place(), bit) == 1, 1.0, 0.0)
    reach = jnp.exp(sums_ref[1, :, tokens] + spread_lanes(prefix_ref[:, :1], SPAN))
    return reach * weight_ref[first_level + bit, :, tokens] * active


def gather_work(quarters, part_refs, heads, per):
    work = []
    for far, pieces in quarters:
        first = first_head(far, heads)
        for slot in range(heads // 4):
            states = []
            for level, index, start in pieces:
                if start is None:
                    rows = pl.ds(pl.multiple_of((first + slot) * per, 128), per)
                else:
                    rows = slice(start + slot * per, start + (slot + 1) * per)
                states.append((level, part_refs[index][rows].astype(jnp.bfloat16)))
            work.append((first + slot, states))
    return work


def add_found(mixed, queries, head, states, scale_ref):
    for level, state in states:
        found = lax.dot_general(state, queries, NT, preferred_element_type=jnp.float32)
        mixed = mixed + found * scale_ref[level, pl.ds(head, 1)]
    return mixed


def finish_kernel(quarters, first_level, bits, stays, carried, *refs):
    mixed_ref, q_ref, sums_ref, weight_ref, gain_ref = refs[:5]
    prefix_refs = refs[5 : 5 + len(bits)]
    part_refs = refs[5 + len(bits) :]
    out_refs, (own_ref, scale_ref, sent) = refs[-3 - FINISH_OUTS[stays, carried] : -3], refs[-3:]
    if stays:
        own_ref = out_refs[-1]
    heads = weight_ref.shape[1]
    head_width = mixed_ref.shape[0] // heads
    size = heads // 4 * head_width
    copies = []

    def send(block, far, rows):
        columns = pl.ds(pl.multiple_of(first_head(far, heads) * head_width, 128), size)
        copy = pltpu.make_async_copy(
            block.at[rows], out_refs[0].at[rows, columns], sent.at[len(copies)]
        )
        copy.start()
        copies.append(copy)

    if carried is not None:
        index, far = carried
        for start in range(0, q_ref.shape[0], SPAN):
            send(part_refs[index], far, slice(start, start + SPAN))
    work = gather_work(quarters, part_refs, heads, head_width)
    gains = []
    for head, _ in work:
        row = jnp.broadcast_to(gain_ref[pl.ds(head, 1)], (8, head_width))
        gains.append(row.T[:, :1])
    for span in range(q_ref.shape[0] // SPAN):
        tokens = slice(span * SPAN, (span + 1) * SPAN)
        queries = q_ref[tokens]
        for level, (bit, prefix_ref) in enumerate(zip(bits, prefix_refs)):
            scale_ref[level] = level_scale(
                bit, first_level, prefix_ref, sums_ref, weight_ref, tokens
            )
        for at, (head, states) in enumerate(work):
            rows = pl.ds(pl.multiple_of(head * head_width, 128), head_width)
            mixed = add_found(mixed_ref[rows, tokens], queries, head, states, scale_ref)
            square = jnp.mean(mixed * mixed, axis=0, keepdims=True)
            normed = mixed * lax.rsqrt(square + EPS) * gains[at]
            columns = slice(at * head_width, (at + 1) * head_width)
            own_ref[tokens, columns] = normed.astype(jnp.bfloat16).T
        if not stays:
            for start in range(tokens.start, tokens.stop, SPAN // 2):
                send(own_ref, quarters[0][0], slice(start, start + SPAN // 2))
    for copy in copies:
        copy.wait()


FINISH_OUTS = {}


def finish(quarters, first_level, bits, shared, prefixes, parts, begun, stays, carried):
    mixed, queries, sums, level_weight, gain = shared
    width, tokens = mixed.shape
    heads = level_weight.shape[1]
    inputs = [*shared, *prefixes, *parts]
    specs = [HELD] * len(inputs)
    inputs = [hold(array) for array in inputs]
    hbm = pl.BlockSpec(memory_space=pltpu.HBM)
    aliases = {}
    if begun is not None:
        aliases = {len(inputs): 0}
        specs.append(hbm)
        inputs.append(begun)
    name = "finish" + "".join(f"{core}{side}" for (core, side), _ in quarters)
    block = (tokens, width // 4)
    out_specs, shapes = [], []
    if carried is not None or not stays:
        out_specs.append(hbm)
        shapes.append(jax.ShapeDtypeStruct((tokens, width), jnp.bfloat16))
    if stays:
        out_specs.append(HELD)
        shapes.append(pltpu.VMEM(block, jnp.bfloat16))
    FINISH_OUTS[stays, carried] = len(shapes)
    return pl.pallas_call(
        functools.partial(finish_kernel, quarters, first_level, bits, stays, carried),
        in_specs=specs,
        out_specs=out_specs,
        out_shape=shapes,
        scratch_shapes=[
            pltpu.VMEM((8, 128) if stays else block, jnp.bfloat16),
            pltpu.VMEM((len(bits), heads, SPAN), jnp.float32),
            pltpu.SemaphoreType.DMA((3 * tokens // SPAN,)),
        ],
        input_output_aliases=aliases,
        compiler_params=PARAMS,
        cost_estimate=cost(name),
        name=name,
    )(*inputs)


def trade(value, mask):
    wide, narrow = lax.axis_size("wide"), lax.axis_size("narrow")

    def ranked(index):
        return index % narrow * wide + index // narrow

    pairs = [(ranked(source), ranked(source ^ mask)) for source in range(wide * narrow)]
    return lax.ppermute(value, AXES, pairs)


def per_device(queries, keys, values, log_decay, level_weight, norm_gain):
    heads = log_decay.shape[0]
    tokens, width = values.shape
    per = width // heads
    spans = tokens // SPAN
    group_bits = heads.bit_length() - 1
    bits = (lax.axis_size("wide") * lax.axis_size("narrow")).bit_length() - 1
    first_level = level_weight.shape[0] - bits
    gain = norm_gain.reshape(heads, per)
    message, local, sums, totals, queries, keys, values, level_weight, gain = make_states(
        queries, keys, values, log_decay, level_weight, gain
    )
    shared = (queries, keys, values, sums, totals, level_weight, local)
    last = bits - 1
    two = 2 * per
    size = two // CUTS
    sides = [(core, side) for core in (0, 1) for side in (0, 1)]
    other = trade(message, 1)
    shared = (*shared, other)
    chunks, give, prefix = make_chip(message, other, heads, CUTS)
    prefixes = [None, prefix]
    found, across = {}, {}
    mixed, at = None, 0

    def both(name, messages, tokens=()):
        return pack(name, [(state, size) for state in messages], tokens)

    for bit in range(1, bits):
        found[bit] = [trade(chunk, 2**bit) for chunk in (give if bit == 1 else chunks)]
        stays = chunks if bit == 1 else stays
        waits = []
        if at < spans:
            stop = spans if bit == last else at + 1
            begun = [*chunks[-1:], *([found[bit - 1]] if bit == last else [])]
            mixed, *waits = mix_local(at, stop, shared, mixed, begun, True)
            at = stop
        if bit == 3:
            waits.append(rest)
        if bit < last:
            merged = {}
            order = list(reversed(range(CUTS)))
            for offset in order:
                ending = offset == order[-1]
                tokens_of = [*merged.values(), *(waits if ending else ())]
                merged[offset], *after = merge(
                    bit, offset, ending, chunks[offset], found[bit][offset], prefixes[bit], tokens_of
                )
            chunks = [merged[offset] for offset in range(CUTS)]
            newest = merged[order[-1]]
            prefixes += after
            found[bit] = both(f"found{bit}", found[bit], (newest,))
            if bit > 1:
                across[bit] = trade(found[bit], 2)
            else:
                rest = trade(both("rest", stays, (newest,)), 2)

    state = both("state", found[last], waits)
    beside = trade(state, 2)
    early = list(range(2, last))
    pieces = [(found[1], two), (rest, two)]
    for bit in early:
        pieces += [(found[bit], two), (across[bit], two)]
    near = pack("near", pieces, (state,))
    far = trade(near, 1)
    middle = [1, *early]
    ahead = [prefixes[bit] for bit in middle]

    def states_of(side, index, first):
        return [(first + slot, index, (2 * slot + side) * two) for slot in range(len(middle))]

    shared = (mixed, queries, sums, level_weight, gain)
    every = (first_level, [last, *middle], shared, [prefixes[last], *ahead])
    quarters = {(core, side): [(0, 0, 0), *states_of(side, 1, 1)] for core, side in sides}
    state_far = trade(pack("shared", [(state, two)], (near,)), 1)
    (block,) = finish([((0, 0), quarters[0, 0])], *every, [state, near], None, True, None)
    out, block = finish(
        [((1, 0), quarters[1, 0])], *every, [state_far, far, block], None, True, (2, (0, 0))
    )
    beside = pack("beside", [(beside, two)], (block,))
    (out,) = finish(
        [((0, 1), quarters[0, 1])], *every, [beside, near, block], out, False, (2, (1, 0))
    )
    beside_far = trade(beside, 1)
    return finish([((1, 1), quarters[1, 1])], *every, [beside_far, far], out, False, None)[0]


def solution(mesh):
    placed = (
        P(("wide", "narrow"), None),
        P(("wide", "narrow"), None),
        P(("wide", "narrow"), None),
        P(None, ("wide", "narrow")),
        P(None, None, ("wide", "narrow")),
        P(),
    )
    return jax.shard_map(
        per_device,
        mesh=mesh,
        in_specs=placed,
        out_specs=P(("wide", "narrow"), None),
        check_vma=False,
    )
```

```python
import functools

import jax
import jax.numpy as jnp
from jax import lax
from jax.experimental import pallas as pl
from jax.experimental.pallas import tpu as pltpu
from jax.sharding import PartitionSpec as P

SPAN = 256
SPLIT_BITS = 2
CUTS = 2
EPS = 1e-05
AXES = ("narrow", "wide")
NT = (((1,), (1,)), ((), ()))
COSTS = {"finish00": 20000000000, "finish10": 1000, "finish01": 20000000000, "local2": 1000, "reach": 1000}


def cost(name):
    flops = COSTS.get(name, 2000000000)
    return pl.CostEstimate(flops=flops, transcendentals=0, bytes_accessed=1_000_000)


PARAMS = pltpu.CompilerParams(vmem_limit_bytes=32 * 1024 * 1024)
HELD = pl.BlockSpec(memory_space=pltpu.VMEM)


def place():
    return lax.axis_index("wide") * lax.axis_size("narrow") + lax.axis_index("narrow")


def bit_of(value, bit):
    return jnp.bitwise_and(jnp.right_shift(value, bit), 1)


def spread_lanes(column, width):
    return jnp.broadcast_to(column, (column.shape[0], width))


ANYWHERE = pl.BlockSpec(memory_space=pl.ANY)


def hold(array):
    return pltpu.with_memory_space_constraint(array, pltpu.VMEM)


def call(kernel, name, inputs, outputs, scratch=(), in_specs=None, aliases=None):
    specs = in_specs or [HELD] * len(inputs)
    inputs = [hold(array) if spec is HELD else array for array, spec in zip(inputs, specs)]
    return pl.pallas_call(
        kernel,
        in_specs=specs,
        out_specs=[HELD] * len(outputs),
        out_shape=[pltpu.VMEM(shape, dtype) for shape, dtype in outputs],
        scratch_shapes=list(scratch),
        input_output_aliases=aliases or {},
        compiler_params=PARAMS,
        cost_estimate=cost(name),
        name=name,
    )(*inputs)


def running_sums(rows):
    high = rows.astype(jnp.bfloat16)
    rest = rows - high.astype(jnp.float32)
    middle = rest.astype(jnp.bfloat16)
    low = (rest - middle.astype(jnp.float32)).astype(jnp.bfloat16)
    width = rows.shape[1]
    source = lax.broadcasted_iota(jnp.int32, (width, width), 0)
    target = lax.broadcasted_iota(jnp.int32, (width, width), 1)
    upto = jnp.where(source <= target, 1.0, 0.0).astype(jnp.bfloat16)
    sums = jnp.dot(
        jnp.concatenate([high, middle, low], axis=0), upto, preferred_element_type=jnp.float32
    )
    count = rows.shape[0]
    return sums[:count] + (sums[count : 2 * count] + sums[2 * count :])


def state_kernel(*refs):
    q_hbm, k_hbm, v_hbm, decay_hbm, weight_hbm, gain_hbm = refs[:6]
    message_ref, local_ref, sums_ref, totals_ref = refs[6:10]
    q_ref, k_ref, v_ref, weight_ref, gain_ref, decay_ref, held, arrived = refs[10:]
    heads, tokens = decay_ref.shape
    head_width = v_ref.shape[1] // heads
    spans = tokens // SPAN
    rows_of = [slice(span * SPAN, (span + 1) * SPAN) for span in range(spans)]
    loads = [(decay_hbm, decay_ref), (k_hbm, k_ref)]
    loads += [(v_hbm.at[rows], v_ref.at[rows]) for rows in rows_of]
    loads += [(q_hbm, q_ref), (weight_hbm, weight_ref), (gain_hbm, gain_ref)]
    copies = [
        pltpu.make_async_copy(source, target, arrived.at[at])
        for at, (source, target) in enumerate(loads)
    ]
    for copy in copies:
        copy.start()
    copies[0].wait()
    within = running_sums(jnp.concatenate([decay_ref[:, rows] for rows in rows_of], axis=0))
    run = jnp.zeros((heads, 128), jnp.float32)
    fades, wholes = [], []
    for span, rows in enumerate(rows_of):
        here = within[span * heads : (span + 1) * heads]
        last = here[:, SPAN - 1 :]
        total = spread_lanes(last, 128)
        sums_ref[0, :, rows] = here
        sums_ref[1, :, rows] = here + spread_lanes(run[:, :1], SPAN)
        totals_ref[span] = total
        run = run + total
        fades.append(jnp.exp(spread_lanes(last, SPAN) - here))
        wholes.append(jnp.exp(total))
    copies[1].wait()
    across = [k_ref[rows].astype(jnp.float32).T for rows in rows_of]
    local_bits = spans.bit_length() - 1
    for span, rows in enumerate(rows_of):
        copies[2 + span].wait()
        for head in range(heads):
            columns = slice(head * head_width, (head + 1) * head_width)
            faded = (across[span] * fades[span][head : head + 1]).astype(jnp.bfloat16)
            state = jnp.dot(faded, v_ref[rows, columns], preferred_element_type=jnp.float32)
            at = 0
            for bit in range(local_bits + 1):
                if span >> bit & 1 == 0 or bit == local_bits:
                    group = state
                    if span % 2**bit > 0:
                        group = held[bit - 1, head] * wholes[span][head : head + 1] + state
                    if (span + 1) % 2**bit > 0:
                        held[bit - 1, head] = group
                    elif bit < local_bits:
                        local_ref[at + (span >> (bit + 1)), :, columns] = group.astype(
                            jnp.bfloat16
                        )
                    else:
                        message_ref[columns] = group.T
                at += spans >> (bit + 1)
    message_ref[heads * head_width :] = run
    for copy in copies[2 + spans :]:
        copy.wait()


def make_states(queries, keys, values, log_decay, level_weight, gain):
    tokens, key_width = keys.shape
    heads = log_decay.shape[0]
    width = values.shape[1]
    spans = tokens // SPAN
    inputs = [queries, keys, values, log_decay, level_weight, gain]
    kept = [queries, keys, values, level_weight, gain]
    return call(
        state_kernel,
        "states",
        [pltpu.with_memory_space_constraint(array, pltpu.HBM) for array in inputs],
        [
            ((width + heads, key_width), jnp.float32),
            ((spans - 1, key_width, width), jnp.bfloat16),
            ((2, heads, tokens), jnp.float32),
            ((spans, heads, 128), jnp.float32),
            *[(array.shape, array.dtype) for array in kept],
        ],
        [
            pltpu.VMEM(log_decay.shape, jnp.float32),
            pltpu.VMEM((spans.bit_length() - 1, heads, key_width, width // heads), jnp.float32),
            pltpu.SemaphoreType.DMA((spans + 5,)),
        ],
        [pl.BlockSpec(memory_space=pltpu.HBM)] * len(inputs),
    )


def local_kernel(first, last, has_token, *refs):
    q_ref, k_ref, v_ref, sums_ref, totals_ref, weight_ref, local_ref, near_ref = refs[:8]
    if has_token:
        mixed_ref, done_ref = refs[-2:]
        done_ref[...] = jnp.zeros_like(done_ref)
    else:
        mixed_ref = refs[-1]
    heads = weight_ref.shape[1]
    head_width = v_ref.shape[1] // heads
    spans = totals_ref.shape[0]
    local_bits = spans.bit_length() - 1
    half = SPAN // 2
    source = lax.broadcasted_iota(jnp.int32, (half, half), 0)
    target = lax.broadcasted_iota(jnp.int32, (half, half), 1)
    causal = source <= target
    empty = jnp.zeros((half, half), jnp.bfloat16)
    upper = jnp.where(bit_of(place(), 0) == 1, 1.0, 0.0)
    near = near_ref[: heads * head_width].astype(jnp.bfloat16)

    for span in range(first, last):
        tokens = slice(span * SPAN, (span + 1) * SPAN)
        queries = q_ref[tokens]
        scores = lax.dot_general(
            k_ref[tokens], queries, NT, preferred_element_type=jnp.float32
        )
        within = sums_ref[0, :, tokens]
        within_down = within.T
        weight = weight_ref[0, :, tokens]
        values_across = v_ref[tokens].T

        def mix(head, low, high):
            rows = slice(low * half, (low + 1) * half)
            columns = slice(high * half, (high + 1) * half)
            gap = within[head : head + 1, columns] - within_down[rows, head : head + 1]
            if low == high:
                gap = jnp.where(causal, gap, -1e30)
            mixing = scores[rows, columns] * jnp.exp(gap) * weight[head : head + 1, columns]
            return mixing.astype(jnp.bfloat16)

        levels = []
        offset = 0
        for bit in range(local_bits):
            if span >> bit & 1:
                since = within
                for back in range(1, span % 2**bit + 1):
                    since = since + spread_lanes(totals_ref[span - back][:, :1], SPAN)
                scale = jnp.exp(since) * weight_ref[1 + bit, :, tokens]
                levels.append((local_ref[offset + (span >> (bit + 1))].T, scale))
            offset += spans >> (bit + 1)
        reach = jnp.exp(sums_ref[1, :, tokens]) * weight_ref[1 + local_bits, :, tokens] * upper
        levels.append((near, reach))
        for head in range(heads):
            rows = slice(head * head_width, (head + 1) * head_width)
            mixing = jnp.concatenate(
                [
                    jnp.concatenate([mix(head, 0, 0), mix(head, 0, 1)], axis=1),
                    jnp.concatenate([empty, mix(head, 1, 1)], axis=1),
                ],
                axis=0,
            )
            mixed = jnp.dot(values_across[rows], mixing, preferred_element_type=jnp.float32)
            for level, scale in levels:
                found = lax.dot_general(
                    level[rows], queries, NT, preferred_element_type=jnp.float32
                )
                mixed = mixed + found * scale[head : head + 1]
            mixed_ref[rows, tokens] = mixed


def mix_local(first, last, shared, mixed, tokens, has_token):
    values = shared[2]
    rest = [] if mixed is None else [mixed]
    return call(
        functools.partial(local_kernel, first, last, has_token),
        f"local{first}",
        [*shared, *rest, *tokens],
        [(values.shape[::-1], jnp.float32), ((8, 128), jnp.float32)][: 1 + has_token],
        aliases={8: 0} if rest else None,
    )


def join(upper, mine, mine_total, other, other_total):
    fade = jnp.exp(jnp.where(upper, mine_total, other_total))
    return jnp.where(upper, other * fade + mine, mine * fade + other)


def first_head(far, heads):
    here = place()
    first = 0
    for bit, flip in enumerate(far):
        first = first + jnp.bitwise_xor(bit_of(here, bit), flip) * (heads >> (bit + 1))
    return first


def chip_kernel(mine_ref, other_ref, *refs):
    *message_refs, next_ref, whole_ref = refs
    heads = next_ref.shape[0]
    width = mine_ref.shape[0] - heads
    per = width // heads
    held = whole_ref.shape[0] // per
    here = place()
    upper = bit_of(here, 0) == 1
    first = first_head((0,), heads)
    for slot in range(held):
        part = pl.ds(pl.multiple_of((first + slot) * per, 8), per)
        total = pl.ds(width + first + slot, 1)
        whole_ref[slot * per : (slot + 1) * per] = join(
            upper, mine_ref[part], mine_ref[total], other_ref[part], other_ref[total]
        )
    other_total = other_ref[width:]
    total = mine_ref[width:] + other_total
    next_ref[...] = jnp.where(upper, other_total, 0.0)
    half = held * per // 2
    side = bit_of(here, 1)
    cuts = len(message_refs) // 2
    size = half // cuts
    for at, ref in enumerate(message_refs):
        start = (side if at < cuts else 1 - side) * half + at % cuts * size
        ref[:size] = whole_ref[pl.ds(pl.multiple_of(start, 8), size)]
        ref[size:] = total


def make_chip(mine, other, heads, cuts):
    rows, lanes = mine.shape
    half = (rows - heads) // 2
    *messages, prefix = call(
        chip_kernel,
        "chip",
        [mine, other],
        [
            *[((half // 2 // cuts + heads, lanes), jnp.float32)] * (2 * cuts),
            ((heads, lanes), jnp.float32),
        ],
        [pltpu.VMEM((half, lanes), jnp.float32)],
    )
    return messages[:cuts], messages[cuts:], prefix


def merge_kernel(bit, offset, has_prefix, *refs):
    mine_ref, other_ref, prefix_ref = refs[:3]
    merged_ref = refs[-2] if has_prefix else refs[-1]
    heads = prefix_ref.shape[0]
    rows = mine_ref.shape[0] - heads
    per = mine_ref.shape[1]
    upper = bit_of(place(), bit) == 1
    first = first_head((0,) * SPLIT_BITS, heads) + offset
    for slot in range(rows // per):
        part = slice(slot * per, (slot + 1) * per)
        total = pl.ds(rows + first + slot, 1)
        merged_ref[part] = join(
            upper, mine_ref[part], mine_ref[total], other_ref[part], other_ref[total]
        )
    other_total = other_ref[rows:]
    merged_ref[rows:] = mine_ref[rows:] + other_total
    if has_prefix:
        refs[-1][...] = prefix_ref[...] + jnp.where(upper, other_total, 0.0)


def merge(bit, offset, has_prefix, mine, other, prefix, tokens=()):
    return call(
        functools.partial(merge_kernel, bit, offset, has_prefix),
        f"merge{bit}{offset}",
        [mine, other, prefix, *tokens],
        [(mine.shape, jnp.float32), (prefix.shape, jnp.float32)][: 1 + has_prefix],
    )


def pack_kernel(takes, *refs):
    out_ref = refs[-1]
    at = 0
    for ref, rows in zip(refs, takes):
        out_ref[at : at + rows] = ref[:rows]
        at += rows


def pack(name, pieces, tokens=()):
    takes = [rows for _, rows in pieces]
    lanes = pieces[0][0].shape[1]
    return call(
        functools.partial(pack_kernel, takes),
        name,
        [*[array for array, _ in pieces], *tokens],
        [((sum(takes), lanes), jnp.float32)],
    )[0]


def level_scale(bit, first_level, prefix_ref, sums_ref, weight_ref, tokens):
    active = jnp.where(bit_of(place(), bit) == 1, 1.0, 0.0)
    reach = jnp.exp(sums_ref[1, :, tokens] + spread_lanes(prefix_ref[:, :1], SPAN))
    return reach * weight_ref[first_level + bit, :, tokens] * active


def gather_work(quarters, part_refs, heads, per):
    work = []
    for far, pieces in quarters:
        first = first_head(far, heads)
        for slot in range(heads // 4):
            states = []
            for level, index, start in pieces:
                if start is None:
                    rows = pl.ds(pl.multiple_of((first + slot) * per, 128), per)
                else:
                    rows = slice(start + slot * per, start + (slot + 1) * per)
                states.append((level, part_refs[index][rows].astype(jnp.bfloat16)))
            work.append((first + slot, states))
    return work


def add_found(mixed, queries, head, states, scale_ref):
    for level, state in states:
        found = lax.dot_general(state, queries, NT, preferred_element_type=jnp.float32)
        mixed = mixed + found * scale_ref[level, pl.ds(head, 1)]
    return mixed


def finish_kernel(quarters, first_level, bits, stays, carried, *refs):
    mixed_ref, q_ref, sums_ref, weight_ref, gain_ref = refs[:5]
    prefix_refs = refs[5 : 5 + len(bits)]
    part_refs = refs[5 + len(bits) :]
    out_refs, (own_ref, scale_ref, sent) = refs[-3 - FINISH_OUTS[stays, carried] : -3], refs[-3:]
    if stays:
        own_ref = out_refs[-1]
    heads = weight_ref.shape[1]
    head_width = mixed_ref.shape[0] // heads
    size = heads // 4 * head_width
    copies = []

    def send(block, far, rows):
        columns = pl.ds(pl.multiple_of(first_head(far, heads) * head_width, 128), size)
        copy = pltpu.make_async_copy(
            block.at[rows], out_refs[0].at[rows, columns], sent.at[len(copies)]
        )
        copy.start()
        copies.append(copy)

    if carried is not None:
        index, far = carried
        for start in range(0, q_ref.shape[0], SPAN):
            send(part_refs[index], far, slice(start, start + SPAN))
    work = gather_work(quarters, part_refs, heads, head_width)
    gains = []
    for head, _ in work:
        row = jnp.broadcast_to(gain_ref[pl.ds(head, 1)], (8, head_width))
        gains.append(row.T[:, :1])
    for span in range(q_ref.shape[0] // SPAN):
        tokens = slice(span * SPAN, (span + 1) * SPAN)
        queries = q_ref[tokens]
        for level, (bit, prefix_ref) in enumerate(zip(bits, prefix_refs)):
            scale_ref[level] = level_scale(
                bit, first_level, prefix_ref, sums_ref, weight_ref, tokens
            )
        for at, (head, states) in enumerate(work):
            rows = pl.ds(pl.multiple_of(head * head_width, 128), head_width)
            mixed = add_found(mixed_ref[rows, tokens], queries, head, states, scale_ref)
            square = jnp.mean(mixed * mixed, axis=0, keepdims=True)
            normed = mixed * lax.rsqrt(square + EPS) * gains[at]
            columns = slice(at * head_width, (at + 1) * head_width)
            own_ref[tokens, columns] = normed.astype(jnp.bfloat16).T
        if not stays:
            for start in range(tokens.start, tokens.stop, SPAN // 2):
                send(own_ref, quarters[0][0], slice(start, start + SPAN // 2))
    for copy in copies:
        copy.wait()


FINISH_OUTS = {}


def finish(quarters, first_level, bits, shared, prefixes, parts, begun, stays, carried):
    mixed, queries, sums, level_weight, gain = shared
    width, tokens = mixed.shape
    heads = level_weight.shape[1]
    inputs = [*shared, *prefixes, *parts]
    specs = [HELD] * len(inputs)
    inputs = [hold(array) for array in inputs]
    hbm = pl.BlockSpec(memory_space=pltpu.HBM)
    aliases = {}
    if begun is not None:
        aliases = {len(inputs): 0}
        specs.append(hbm)
        inputs.append(begun)
    name = "finish" + "".join(f"{core}{side}" for (core, side), _ in quarters)
    block = (tokens, width // 4)
    out_specs, shapes = [], []
    if carried is not None or not stays:
        out_specs.append(hbm)
        shapes.append(jax.ShapeDtypeStruct((tokens, width), jnp.bfloat16))
    if stays:
        out_specs.append(HELD)
        shapes.append(pltpu.VMEM(block, jnp.bfloat16))
    FINISH_OUTS[stays, carried] = len(shapes)
    return pl.pallas_call(
        functools.partial(finish_kernel, quarters, first_level, bits, stays, carried),
        in_specs=specs,
        out_specs=out_specs,
        out_shape=shapes,
        scratch_shapes=[
            pltpu.VMEM((8, 128) if stays else block, jnp.bfloat16),
            pltpu.VMEM((len(bits), heads, SPAN), jnp.float32),
            pltpu.SemaphoreType.DMA((3 * tokens // SPAN,)),
        ],
        input_output_aliases=aliases,
        compiler_params=PARAMS,
        cost_estimate=cost(name),
        name=name,
    )(*inputs)


def trade(value, mask, sends=lambda source: True):
    wide, narrow = lax.axis_size("wide"), lax.axis_size("narrow")

    def ranked(index):
        return index % narrow * wide + index // narrow

    pairs = [
        (ranked(source), ranked(source ^ mask))
        for source in range(wide * narrow)
        if sends(source)
    ]
    return lax.ppermute(value, AXES, pairs)


def per_device(queries, keys, values, log_decay, level_weight, norm_gain):
    heads = log_decay.shape[0]
    tokens, width = values.shape
    per = width // heads
    spans = tokens // SPAN
    group_bits = heads.bit_length() - 1
    bits = (lax.axis_size("wide") * lax.axis_size("narrow")).bit_length() - 1
    first_level = level_weight.shape[0] - bits
    gain = norm_gain.reshape(heads, per)
    message, local, sums, totals, queries, keys, values, level_weight, gain = make_states(
        queries, keys, values, log_decay, level_weight, gain
    )
    shared = (queries, keys, values, sums, totals, level_weight, local)
    last = bits - 1
    two = 2 * per
    size = two // CUTS
    sides = [(core, side) for core in (0, 1) for side in (0, 1)]
    other = trade(message, 1)
    shared = (*shared, other)
    chunks, give, prefix = make_chip(message, other, heads, CUTS)
    prefixes = [None, prefix]
    found, across = {}, {}
    mixed, at = None, 0

    def both(name, messages, tokens=()):
        return pack(name, [(state, size) for state in messages], tokens)

    for bit in range(1, bits):
        lower = lambda source: bit < last or source >> last & 1 == 0
        sent = give if bit == 1 else chunks
        found[bit] = [trade(chunk, 2**bit, lower) for chunk in sent]
        stays = chunks if bit == 1 else stays
        waits = []
        if at < spans:
            stop = spans if bit == last else at + 1
            begun = [*chunks[-1:], *([found[bit - 1]] if bit == last else [])]
            mixed, *waits = mix_local(at, stop, shared, mixed, begun, True)
            at = stop
        if bit == 3:
            waits.append(rest)
        if bit < last:
            merged = {}
            order = list(reversed(range(CUTS)))
            for offset in order:
                ending = offset == order[-1]
                tokens_of = [*merged.values(), *(waits if ending else ())]
                merged[offset], *after = merge(
                    bit, offset, ending, chunks[offset], found[bit][offset], prefixes[bit], tokens_of
                )
            chunks = [merged[offset] for offset in range(CUTS)]
            newest = merged[order[-1]]
            prefixes += after
            found[bit] = both(f"found{bit}", found[bit], (newest,))
            if bit > 1:
                across[bit] = trade(found[bit], 2)
            else:
                rest = trade(both("rest", stays, (newest,)), 2)

    state = both("state", found[last], waits)
    beside = trade(state, 2)
    early = list(range(2, last))
    pieces = [(found[1], two), (rest, two)]
    for bit in early:
        pieces += [(found[bit], two), (across[bit], two)]
    near = pack("near", pieces, (state,))
    far = trade(near, 1)
    middle = [1, *early]
    ahead = [prefixes[bit] for bit in middle]

    def states_of(side, index, first):
        return [(first + slot, index, (2 * slot + side) * two) for slot in range(len(middle))]

    shared = (mixed, queries, sums, level_weight, gain)
    every = (first_level, [last, *middle], shared, [prefixes[last], *ahead])
    quarters = {(core, side): [(0, 0, 0), *states_of(side, 1, 1)] for core, side in sides}
    state_far = trade(pack("shared", [(state, two)], (near,)), 1)
    (block,) = finish([((0, 0), quarters[0, 0])], *every, [state, near], None, True, None)
    (block_far,) = finish(
        [((1, 0), quarters[1, 0])], *every, [state_far, far, block], None, True, None
    )
    beside = pack("beside", [(beside, two)], (block_far,))
    (out,) = finish(
        [((0, 1), quarters[0, 1])], *every, [beside, near, block], None, False, (2, (0, 0))
    )
    beside_far = trade(beside, 1)
    return finish(
        [((1, 1), quarters[1, 1])], *every, [beside_far, far, block_far], out, False, (2, (1, 0))
    )[0]


def solution(mesh):
    placed = (
        P(("wide", "narrow"), None),
        P(("wide", "narrow"), None),
        P(("wide", "narrow"), None),
        P(None, ("wide", "narrow")),
        P(None, None, ("wide", "narrow")),
        P(),
    )
    return jax.shard_map(
        per_device,
        mesh=mesh,
        in_specs=placed,
        out_specs=P(("wide", "narrow"), None),
        check_vma=False,
    )
```

```python
import functools

import jax
import jax.numpy as jnp
from jax import lax
from jax.experimental import pallas as pl
from jax.experimental.pallas import tpu as pltpu
from jax.sharding import PartitionSpec as P

SPAN = 256
SPLIT_BITS = 2
CUTS = 2
EPS = 1e-05
AXES = ("narrow", "wide")
NT = (((1,), (1,)), ((), ()))
COSTS = {"finish00": 20000000000, "finish10": 1000, "finish01": 20000000000, "local2": 1000, "reach": 1000}


def cost(name):
    flops = COSTS.get(name, 2000000000)
    return pl.CostEstimate(flops=flops, transcendentals=0, bytes_accessed=1_000_000)


PARAMS = pltpu.CompilerParams(vmem_limit_bytes=32 * 1024 * 1024)
HELD = pl.BlockSpec(memory_space=pltpu.VMEM)


def place():
    return lax.axis_index("wide") * lax.axis_size("narrow") + lax.axis_index("narrow")


def bit_of(value, bit):
    return jnp.bitwise_and(jnp.right_shift(value, bit), 1)


def spread_lanes(column, width):
    return jnp.broadcast_to(column, (column.shape[0], width))


ANYWHERE = pl.BlockSpec(memory_space=pl.ANY)


def hold(array):
    return pltpu.with_memory_space_constraint(array, pltpu.VMEM)


def call(kernel, name, inputs, outputs, scratch=(), in_specs=None, aliases=None):
    specs = in_specs or [HELD] * len(inputs)
    inputs = [hold(array) if spec is HELD else array for array, spec in zip(inputs, specs)]
    return pl.pallas_call(
        kernel,
        in_specs=specs,
        out_specs=[HELD] * len(outputs),
        out_shape=[pltpu.VMEM(shape, dtype) for shape, dtype in outputs],
        scratch_shapes=list(scratch),
        input_output_aliases=aliases or {},
        compiler_params=PARAMS,
        cost_estimate=cost(name),
        name=name,
    )(*inputs)


def running_sums(rows):
    high = rows.astype(jnp.bfloat16)
    rest = rows - high.astype(jnp.float32)
    middle = rest.astype(jnp.bfloat16)
    low = (rest - middle.astype(jnp.float32)).astype(jnp.bfloat16)
    width = rows.shape[1]
    source = lax.broadcasted_iota(jnp.int32, (width, width), 0)
    target = lax.broadcasted_iota(jnp.int32, (width, width), 1)
    upto = jnp.where(source <= target, 1.0, 0.0).astype(jnp.bfloat16)
    sums = jnp.dot(
        jnp.concatenate([high, middle, low], axis=0), upto, preferred_element_type=jnp.float32
    )
    count = rows.shape[0]
    return sums[:count] + (sums[count : 2 * count] + sums[2 * count :])


def state_kernel(*refs):
    q_hbm, k_hbm, v_hbm, decay_hbm, weight_hbm, gain_hbm = refs[:6]
    message_ref, local_ref, sums_ref, totals_ref = refs[6:10]
    q_ref, k_ref, v_ref, weight_ref, gain_ref, decay_ref, held, arrived = refs[10:]
    heads, tokens = decay_ref.shape
    head_width = v_ref.shape[1] // heads
    spans = tokens // SPAN
    rows_of = [slice(span * SPAN, (span + 1) * SPAN) for span in range(spans)]
    loads = [(decay_hbm, decay_ref), (k_hbm, k_ref)]
    loads += [(v_hbm.at[rows], v_ref.at[rows]) for rows in rows_of]
    loads += [(q_hbm, q_ref), (weight_hbm, weight_ref), (gain_hbm, gain_ref)]
    copies = [
        pltpu.make_async_copy(source, target, arrived.at[at])
        for at, (source, target) in enumerate(loads)
    ]
    for copy in copies:
        copy.start()
    copies[0].wait()
    within = running_sums(jnp.concatenate([decay_ref[:, rows] for rows in rows_of], axis=0))
    run = jnp.zeros((heads, 128), jnp.float32)
    fades, wholes = [], []
    for span, rows in enumerate(rows_of):
        here = within[span * heads : (span + 1) * heads]
        last = here[:, SPAN - 1 :]
        total = spread_lanes(last, 128)
        sums_ref[0, :, rows] = here
        sums_ref[1, :, rows] = here + spread_lanes(run[:, :1], SPAN)
        totals_ref[span] = total
        run = run + total
        fades.append(jnp.exp(spread_lanes(last, SPAN) - here))
        wholes.append(jnp.exp(total))
    copies[1].wait()
    across = [k_ref[rows].astype(jnp.float32).T for rows in rows_of]
    local_bits = spans.bit_length() - 1
    for span, rows in enumerate(rows_of):
        copies[2 + span].wait()
        for head in range(heads):
            columns = slice(head * head_width, (head + 1) * head_width)
            faded = (across[span] * fades[span][head : head + 1]).astype(jnp.bfloat16)
            state = jnp.dot(faded, v_ref[rows, columns], preferred_element_type=jnp.float32)
            at = 0
            for bit in range(local_bits + 1):
                if span >> bit & 1 == 0 or bit == local_bits:
                    group = state
                    if span % 2**bit > 0:
                        group = held[bit - 1, head] * wholes[span][head : head + 1] + state
                    if (span + 1) % 2**bit > 0:
                        held[bit - 1, head] = group
                    elif bit < local_bits:
                        local_ref[at + (span >> (bit + 1)), :, columns] = group.astype(
                            jnp.bfloat16
                        )
                    else:
                        message_ref[columns] = group.T
                at += spans >> (bit + 1)
    message_ref[heads * head_width :] = run
    for copy in copies[2 + spans :]:
        copy.wait()


def make_states(queries, keys, values, log_decay, level_weight, gain):
    tokens, key_width = keys.shape
    heads = log_decay.shape[0]
    width = values.shape[1]
    spans = tokens // SPAN
    inputs = [queries, keys, values, log_decay, level_weight, gain]
    kept = [queries, keys, values, level_weight, gain]
    return call(
        state_kernel,
        "states",
        [pltpu.with_memory_space_constraint(array, pltpu.HBM) for array in inputs],
        [
            ((width + heads, key_width), jnp.float32),
            ((spans - 1, key_width, width), jnp.bfloat16),
            ((2, heads, tokens), jnp.float32),
            ((spans, heads, 128), jnp.float32),
            *[(array.shape, array.dtype) for array in kept],
        ],
        [
            pltpu.VMEM(log_decay.shape, jnp.float32),
            pltpu.VMEM((spans.bit_length() - 1, heads, key_width, width // heads), jnp.float32),
            pltpu.SemaphoreType.DMA((spans + 5,)),
        ],
        [pl.BlockSpec(memory_space=pltpu.HBM)] * len(inputs),
    )


def local_kernel(first, last, has_token, *refs):
    q_ref, k_ref, v_ref, sums_ref, totals_ref, weight_ref, local_ref, near_ref = refs[:8]
    if has_token:
        mixed_ref, done_ref = refs[-2:]
        done_ref[...] = jnp.zeros_like(done_ref)
    else:
        mixed_ref = refs[-1]
    heads = weight_ref.shape[1]
    head_width = v_ref.shape[1] // heads
    spans = totals_ref.shape[0]
    local_bits = spans.bit_length() - 1
    half = SPAN // 2
    source = lax.broadcasted_iota(jnp.int32, (half, half), 0)
    target = lax.broadcasted_iota(jnp.int32, (half, half), 1)
    causal = source <= target
    empty = jnp.zeros((half, half), jnp.bfloat16)
    upper = jnp.where(bit_of(place(), 0) == 1, 1.0, 0.0)
    near = near_ref[: heads * head_width].astype(jnp.bfloat16)

    for span in range(first, last):
        tokens = slice(span * SPAN, (span + 1) * SPAN)
        queries = q_ref[tokens]
        scores = lax.dot_general(
            k_ref[tokens], queries, NT, preferred_element_type=jnp.float32
        )
        within = sums_ref[0, :, tokens]
        within_down = within.T
        weight = weight_ref[0, :, tokens]
        values_across = v_ref[tokens].T

        def mix(head, low, high):
            rows = slice(low * half, (low + 1) * half)
            columns = slice(high * half, (high + 1) * half)
            gap = within[head : head + 1, columns] - within_down[rows, head : head + 1]
            if low == high:
                gap = jnp.where(causal, gap, -1e30)
            mixing = scores[rows, columns] * jnp.exp(gap) * weight[head : head + 1, columns]
            return mixing.astype(jnp.bfloat16)

        levels = []
        offset = 0
        for bit in range(local_bits):
            if span >> bit & 1:
                since = within
                for back in range(1, span % 2**bit + 1):
                    since = since + spread_lanes(totals_ref[span - back][:, :1], SPAN)
                scale = jnp.exp(since) * weight_ref[1 + bit, :, tokens]
                levels.append((local_ref[offset + (span >> (bit + 1))].T, scale))
            offset += spans >> (bit + 1)
        reach = jnp.exp(sums_ref[1, :, tokens]) * weight_ref[1 + local_bits, :, tokens] * upper
        levels.append((near, reach))
        for head in range(heads):
            rows = slice(head * head_width, (head + 1) * head_width)
            mixing = jnp.concatenate(
                [
                    jnp.concatenate([mix(head, 0, 0), mix(head, 0, 1)], axis=1),
                    jnp.concatenate([empty, mix(head, 1, 1)], axis=1),
                ],
                axis=0,
            )
            mixed = jnp.dot(values_across[rows], mixing, preferred_element_type=jnp.float32)
            for level, scale in levels:
                found = lax.dot_general(
                    level[rows], queries, NT, preferred_element_type=jnp.float32
                )
                mixed = mixed + found * scale[head : head + 1]
            mixed_ref[rows, tokens] = mixed


def mix_local(first, last, shared, mixed, tokens, has_token):
    values = shared[2]
    rest = [] if mixed is None else [mixed]
    return call(
        functools.partial(local_kernel, first, last, has_token),
        f"local{first}",
        [*shared, *rest, *tokens],
        [(values.shape[::-1], jnp.float32), ((8, 128), jnp.float32)][: 1 + has_token],
        aliases={8: 0} if rest else None,
    )


def join(upper, mine, mine_total, other, other_total):
    fade = jnp.exp(jnp.where(upper, mine_total, other_total))
    return jnp.where(upper, other * fade + mine, mine * fade + other)


def first_head(far, heads):
    here = place()
    first = 0
    for bit, flip in enumerate(far):
        first = first + jnp.bitwise_xor(bit_of(here, bit), flip) * (heads >> (bit + 1))
    return first


def chip_kernel(mine_ref, other_ref, *refs):
    *message_refs, next_ref, whole_ref = refs
    heads = next_ref.shape[0]
    width = mine_ref.shape[0] - heads
    per = width // heads
    held = whole_ref.shape[0] // per
    here = place()
    upper = bit_of(here, 0) == 1
    first = first_head((0,), heads)
    for slot in range(held):
        part = pl.ds(pl.multiple_of((first + slot) * per, 8), per)
        total = pl.ds(width + first + slot, 1)
        whole_ref[slot * per : (slot + 1) * per] = join(
            upper, mine_ref[part], mine_ref[total], other_ref[part], other_ref[total]
        )
    other_total = other_ref[width:]
    total = mine_ref[width:] + other_total
    next_ref[...] = jnp.where(upper, other_total, 0.0)
    half = held * per // 2
    side = bit_of(here, 1)
    cuts = len(message_refs) // 2
    size = half // cuts
    for at, ref in enumerate(message_refs):
        start = (side if at < cuts else 1 - side) * half + at % cuts * size
        ref[:size] = whole_ref[pl.ds(pl.multiple_of(start, 8), size)]
        ref[size:] = total


def make_chip(mine, other, heads, cuts):
    rows, lanes = mine.shape
    half = (rows - heads) // 2
    *messages, prefix = call(
        chip_kernel,
        "chip",
        [mine, other],
        [
            *[((half // 2 // cuts + heads, lanes), jnp.float32)] * (2 * cuts),
            ((heads, lanes), jnp.float32),
        ],
        [pltpu.VMEM((half, lanes), jnp.float32)],
    )
    return messages[:cuts], messages[cuts:], prefix


def merge_kernel(bit, offset, has_prefix, *refs):
    mine_ref, other_ref, prefix_ref = refs[:3]
    merged_ref = refs[-2] if has_prefix else refs[-1]
    heads = prefix_ref.shape[0]
    rows = mine_ref.shape[0] - heads
    per = mine_ref.shape[1]
    upper = bit_of(place(), bit) == 1
    first = first_head((0,) * SPLIT_BITS, heads) + offset
    for slot in range(rows // per):
        part = slice(slot * per, (slot + 1) * per)
        total = pl.ds(rows + first + slot, 1)
        merged_ref[part] = join(
            upper, mine_ref[part], mine_ref[total], other_ref[part], other_ref[total]
        )
    other_total = other_ref[rows:]
    merged_ref[rows:] = mine_ref[rows:] + other_total
    if has_prefix:
        refs[-1][...] = prefix_ref[...] + jnp.where(upper, other_total, 0.0)


def merge(bit, offset, has_prefix, mine, other, prefix, tokens=()):
    return call(
        functools.partial(merge_kernel, bit, offset, has_prefix),
        f"merge{bit}{offset}",
        [mine, other, prefix, *tokens],
        [(mine.shape, jnp.float32), (prefix.shape, jnp.float32)][: 1 + has_prefix],
    )


def pack_kernel(takes, *refs):
    out_ref = refs[-1]
    at = 0
    for ref, rows in zip(refs, takes):
        out_ref[at : at + rows] = ref[:rows]
        at += rows


def pack(name, pieces, tokens=()):
    takes = [rows for _, rows in pieces]
    lanes = pieces[0][0].shape[1]
    return call(
        functools.partial(pack_kernel, takes),
        name,
        [*[array for array, _ in pieces], *tokens],
        [((sum(takes), lanes), jnp.float32)],
    )[0]


def level_scale(bit, first_level, prefix_ref, sums_ref, weight_ref, tokens):
    active = jnp.where(bit_of(place(), bit) == 1, 1.0, 0.0)
    reach = jnp.exp(sums_ref[1, :, tokens] + spread_lanes(prefix_ref[:, :1], SPAN))
    return reach * weight_ref[first_level + bit, :, tokens] * active


def gather_work(quarters, part_refs, heads, per):
    work = []
    for far, pieces in quarters:
        first = first_head(far, heads)
        for slot in range(heads // 4):
            states = []
            for level, index, start in pieces:
                if start is None:
                    rows = pl.ds(pl.multiple_of((first + slot) * per, 128), per)
                else:
                    rows = slice(start + slot * per, start + (slot + 1) * per)
                states.append((level, part_refs[index][rows].astype(jnp.bfloat16)))
            work.append((first + slot, states))
    return work


def add_found(mixed, queries, head, states, scale_ref):
    for level, state in states:
        found = lax.dot_general(state, queries, NT, preferred_element_type=jnp.float32)
        mixed = mixed + found * scale_ref[level, pl.ds(head, 1)]
    return mixed


def finish_kernel(quarters, first_level, bits, stays, carried, *refs):
    mixed_ref, q_ref, sums_ref, weight_ref, gain_ref = refs[:5]
    prefix_refs = refs[5 : 5 + len(bits)]
    part_refs = refs[5 + len(bits) :]
    out_refs, (own_ref, scale_ref, sent) = refs[-3 - FINISH_OUTS[stays, carried] : -3], refs[-3:]
    if stays:
        own_ref = out_refs[-1]
    heads = weight_ref.shape[1]
    head_width = mixed_ref.shape[0] // heads
    size = heads // 4 * head_width
    copies = []

    def send(block, far, rows):
        columns = pl.ds(pl.multiple_of(first_head(far, heads) * head_width, 128), size)
        copy = pltpu.make_async_copy(
            block.at[rows], out_refs[0].at[rows, columns], sent.at[len(copies)]
        )
        copy.start()
        copies.append(copy)

    if carried is not None:
        index, far = carried
        for start in range(0, q_ref.shape[0], SPAN):
            send(part_refs[index], far, slice(start, start + SPAN))
    work = gather_work(quarters, part_refs, heads, head_width)
    gains = []
    for head, _ in work:
        row = jnp.broadcast_to(gain_ref[pl.ds(head, 1)], (8, head_width))
        gains.append(row.T[:, :1])
    for span in range(q_ref.shape[0] // SPAN):
        tokens = slice(span * SPAN, (span + 1) * SPAN)
        queries = q_ref[tokens]
        for level, (bit, prefix_ref) in enumerate(zip(bits, prefix_refs)):
            scale_ref[level] = level_scale(
                bit, first_level, prefix_ref, sums_ref, weight_ref, tokens
            )
        for at, (head, states) in enumerate(work):
            rows = pl.ds(pl.multiple_of(head * head_width, 128), head_width)
            mixed = add_found(mixed_ref[rows, tokens], queries, head, states, scale_ref)
            square = jnp.mean(mixed * mixed, axis=0, keepdims=True)
            normed = mixed * lax.rsqrt(square + EPS) * gains[at]
            columns = slice(at * head_width, (at + 1) * head_width)
            own_ref[tokens, columns] = normed.astype(jnp.bfloat16).T
        if not stays:
            for start in range(tokens.start, tokens.stop, SPAN // 2):
                send(own_ref, quarters[0][0], slice(start, start + SPAN // 2))
    for copy in copies:
        copy.wait()


FINISH_OUTS = {}


def finish(quarters, first_level, bits, shared, prefixes, parts, begun, stays, carried):
    mixed, queries, sums, level_weight, gain = shared
    width, tokens = mixed.shape
    heads = level_weight.shape[1]
    inputs = [*shared, *prefixes, *parts]
    specs = [HELD] * len(inputs)
    inputs = [hold(array) for array in inputs]
    hbm = pl.BlockSpec(memory_space=pltpu.HBM)
    aliases = {}
    if begun is not None:
        aliases = {len(inputs): 0}
        specs.append(hbm)
        inputs.append(begun)
    name = "finish" + "".join(f"{core}{side}" for (core, side), _ in quarters)
    block = (tokens, width // 4)
    out_specs, shapes = [], []
    if carried is not None or not stays:
        out_specs.append(hbm)
        shapes.append(jax.ShapeDtypeStruct((tokens, width), jnp.bfloat16))
    if stays:
        out_specs.append(HELD)
        shapes.append(pltpu.VMEM(block, jnp.bfloat16))
    FINISH_OUTS[stays, carried] = len(shapes)
    return pl.pallas_call(
        functools.partial(finish_kernel, quarters, first_level, bits, stays, carried),
        in_specs=specs,
        out_specs=out_specs,
        out_shape=shapes,
        scratch_shapes=[
            pltpu.VMEM((8, 128) if stays else block, jnp.bfloat16),
            pltpu.VMEM((len(bits), heads, SPAN), jnp.float32),
            pltpu.SemaphoreType.DMA((3 * tokens // SPAN,)),
        ],
        input_output_aliases=aliases,
        compiler_params=PARAMS,
        cost_estimate=cost(name),
        name=name,
    )(*inputs)


def trade(value, mask):
    wide, narrow = lax.axis_size("wide"), lax.axis_size("narrow")

    def ranked(index):
        return index % narrow * wide + index // narrow

    pairs = [(ranked(source), ranked(source ^ mask)) for source in range(wide * narrow)]
    return lax.ppermute(value, AXES, pairs)


def per_device(queries, keys, values, log_decay, level_weight, norm_gain):
    heads = log_decay.shape[0]
    tokens, width = values.shape
    per = width // heads
    spans = tokens // SPAN
    group_bits = heads.bit_length() - 1
    bits = (lax.axis_size("wide") * lax.axis_size("narrow")).bit_length() - 1
    first_level = level_weight.shape[0] - bits
    gain = norm_gain.reshape(heads, per)
    message, local, sums, totals, queries, keys, values, level_weight, gain = make_states(
        queries, keys, values, log_decay, level_weight, gain
    )
    shared = (queries, keys, values, sums, totals, level_weight, local)
    last = bits - 1
    two = 2 * per
    size = two // CUTS
    sides = [(core, side) for core in (0, 1) for side in (0, 1)]
    other = trade(message, 1)
    shared = (*shared, other)
    chunks, give, prefix = make_chip(message, other, heads, CUTS)
    prefixes = [None, prefix]
    found, across = {}, {}
    mixed, at = None, 0

    def both(name, messages, tokens=()):
        return pack(name, [(state, size) for state in messages], tokens)

    for bit in range(1, bits):
        found[bit] = [trade(chunk, 2**bit) for chunk in (give if bit == 1 else chunks)]
        stays = chunks if bit == 1 else stays
        waits = []
        if bit < 3 or bit == last:
            stop = spans if bit == last else at + 1
            begun = [*chunks[-1:], *([found[bit - 1]] if bit == last else [])]
            mixed, *waits = mix_local(at, stop, shared, mixed, begun, True)
            at = stop
        if bit == 3:
            waits.append(rest)
        if bit < last:
            merged = {}
            order = list(reversed(range(CUTS)))
            for offset in order:
                ending = offset == order[-1]
                tokens_of = [*merged.values(), *(waits if ending else ())]
                merged[offset], *after = merge(
                    bit, offset, ending, chunks[offset], found[bit][offset], prefixes[bit], tokens_of
                )
            chunks = [merged[offset] for offset in range(CUTS)]
            newest = merged[order[-1]]
            prefixes += after
            found[bit] = both(f"found{bit}", found[bit], (newest,))
            if bit > 1:
                across[bit] = trade(found[bit], 2)
            else:
                rest = trade(both("rest", stays, (newest,)), 2)

    state = both("state", found[last], waits)
    beside = trade(state, 2)
    early = list(range(2, last))
    pieces = [(found[1], two), (rest, two)]
    for bit in early:
        pieces += [(found[bit], two), (across[bit], two)]
    near = pack("near", pieces, (state,))
    far = trade(near, 1)
    middle = [1, *early]
    ahead = [prefixes[bit] for bit in middle]

    def states_of(side, index, first):
        return [(first + slot, index, (2 * slot + side) * two) for slot in range(len(middle))]

    shared = (mixed, queries, sums, level_weight, gain)
    every = (first_level, [last, *middle], shared, [prefixes[last], *ahead])
    quarters = {(core, side): [(0, 0, 0), *states_of(side, 1, 1)] for core, side in sides}
    state_far = trade(pack("shared", [(state, two)], (near,)), 1)
    (block,) = finish([((0, 0), quarters[0, 0])], *every, [state, near], None, True, None)
    (block_far,) = finish(
        [((1, 0), quarters[1, 0])], *every, [state_far, far, block], None, True, None
    )
    beside = pack("beside", [(beside, two)], (block_far,))
    (out,) = finish(
        [((0, 1), quarters[0, 1])], *every, [beside, near, block], None, False, (2, (0, 0))
    )
    beside_far = trade(beside, 1)
    return finish(
        [((1, 1), quarters[1, 1])], *every, [beside_far, far, block_far], out, False, (2, (1, 0))
    )[0]


def solution(mesh):
    placed = (
        P(("wide", "narrow"), None),
        P(("wide", "narrow"), None),
        P(("wide", "narrow"), None),
        P(None, ("wide", "narrow")),
        P(None, None, ("wide", "narrow")),
        P(),
    )
    return jax.shard_map(
        per_device,
        mesh=mesh,
        in_specs=placed,
        out_specs=P(("wide", "narrow"), None),
        check_vma=False,
    )
```

```python
import functools

import jax
import jax.numpy as jnp
from jax import lax
from jax.experimental import pallas as pl
from jax.experimental.pallas import tpu as pltpu
from jax.sharding import PartitionSpec as P

SPAN = 256
SPLIT_BITS = 2
CUTS = 2
EPS = 1e-05
AXES = ("narrow", "wide")
NT = (((1,), (1,)), ((), ()))
COSTS = {"local0": 1000, "finish00": 20000000000, "finish10": 1000, "finish01": 20000000000, "local2": 1000, "reach": 1000}


def cost(name):
    flops = COSTS.get(name, 2000000000)
    return pl.CostEstimate(flops=flops, transcendentals=0, bytes_accessed=1_000_000)


PARAMS = pltpu.CompilerParams(vmem_limit_bytes=32 * 1024 * 1024)
HELD = pl.BlockSpec(memory_space=pltpu.VMEM)


def place():
    return lax.axis_index("wide") * lax.axis_size("narrow") + lax.axis_index("narrow")


def bit_of(value, bit):
    return jnp.bitwise_and(jnp.right_shift(value, bit), 1)


def spread_lanes(column, width):
    return jnp.broadcast_to(column, (column.shape[0], width))


ANYWHERE = pl.BlockSpec(memory_space=pl.ANY)


def hold(array):
    return pltpu.with_memory_space_constraint(array, pltpu.VMEM)


def call(kernel, name, inputs, outputs, scratch=(), in_specs=None, aliases=None):
    specs = in_specs or [HELD] * len(inputs)
    inputs = [hold(array) if spec is HELD else array for array, spec in zip(inputs, specs)]
    return pl.pallas_call(
        kernel,
        in_specs=specs,
        out_specs=[HELD] * len(outputs),
        out_shape=[pltpu.VMEM(shape, dtype) for shape, dtype in outputs],
        scratch_shapes=list(scratch),
        input_output_aliases=aliases or {},
        compiler_params=PARAMS,
        cost_estimate=cost(name),
        name=name,
    )(*inputs)


def running_sums(rows):
    high = rows.astype(jnp.bfloat16)
    rest = rows - high.astype(jnp.float32)
    middle = rest.astype(jnp.bfloat16)
    low = (rest - middle.astype(jnp.float32)).astype(jnp.bfloat16)
    width = rows.shape[1]
    source = lax.broadcasted_iota(jnp.int32, (width, width), 0)
    target = lax.broadcasted_iota(jnp.int32, (width, width), 1)
    upto = jnp.where(source <= target, 1.0, 0.0).astype(jnp.bfloat16)
    sums = jnp.dot(
        jnp.concatenate([high, middle, low], axis=0), upto, preferred_element_type=jnp.float32
    )
    count = rows.shape[0]
    return sums[:count] + (sums[count : 2 * count] + sums[2 * count :])


def state_kernel(*refs):
    k_hbm, v_hbm, decay_hbm = refs[:3]
    keep_ref, send_ref, local_ref, sums_ref, totals_ref = refs[3:8]
    k_ref, v_ref, decay_ref, held, message_ref, arrived = refs[8:]
    heads, tokens = decay_ref.shape
    head_width = v_ref.shape[1] // heads
    spans = tokens // SPAN
    rows_of = [slice(span * SPAN, (span + 1) * SPAN) for span in range(spans)]
    loads = [(decay_hbm, decay_ref), (k_hbm, k_ref)]
    loads += [(v_hbm.at[rows], v_ref.at[rows]) for rows in rows_of]
    copies = [
        pltpu.make_async_copy(source, target, arrived.at[at])
        for at, (source, target) in enumerate(loads)
    ]
    for copy in copies:
        copy.start()
    copies[0].wait()
    within = running_sums(jnp.concatenate([decay_ref[:, rows] for rows in rows_of], axis=0))
    run = jnp.zeros((heads, 128), jnp.float32)
    fades, wholes = [], []
    for span, rows in enumerate(rows_of):
        here = within[span * heads : (span + 1) * heads]
        last = here[:, SPAN - 1 :]
        total = spread_lanes(last, 128)
        sums_ref[0, :, rows] = here
        sums_ref[1, :, rows] = here + spread_lanes(run[:, :1], SPAN)
        totals_ref[span] = total
        run = run + total
        fades.append(jnp.exp(spread_lanes(last, SPAN) - here))
        wholes.append(jnp.exp(total))
    copies[1].wait()
    across = [k_ref[rows].astype(jnp.float32).T for rows in rows_of]
    local_bits = spans.bit_length() - 1
    for span, rows in enumerate(rows_of):
        copies[2 + span].wait()
        for head in range(heads):
            columns = slice(head * head_width, (head + 1) * head_width)
            faded = (across[span] * fades[span][head : head + 1]).astype(jnp.bfloat16)
            state = jnp.dot(faded, v_ref[rows, columns], preferred_element_type=jnp.float32)
            at = 0
            for bit in range(local_bits + 1):
                if span >> bit & 1 == 0 or bit == local_bits:
                    group = state
                    if span % 2**bit > 0:
                        group = held[bit - 1, head] * wholes[span][head : head + 1] + state
                    if (span + 1) % 2**bit > 0:
                        held[bit - 1, head] = group
                    elif bit < local_bits:
                        local_ref[at + (span >> (bit + 1)), :, columns] = group.astype(
                            jnp.bfloat16
                        )
                    else:
                        message_ref[columns] = group.T
                at += spans >> (bit + 1)
    half = message_ref.shape[0] // 2
    core = bit_of(place(), 0)
    keep_ref[:half] = message_ref[pl.ds(pl.multiple_of(core * half, 8), half)]
    send_ref[:half] = message_ref[pl.ds(pl.multiple_of((1 - core) * half, 8), half)]
    keep_ref[half:] = run
    send_ref[half:] = run


def make_states(keys, values, log_decay):
    tokens, key_width = keys.shape
    heads = log_decay.shape[0]
    width = values.shape[1]
    spans = tokens // SPAN
    inputs = [keys, values, log_decay]
    kept = [keys, values]
    return call(
        state_kernel,
        "states",
        [pltpu.with_memory_space_constraint(array, pltpu.HBM) for array in inputs],
        [
            ((width // 2 + heads, key_width), jnp.float32),
            ((width // 2 + heads, key_width), jnp.float32),
            ((spans - 1, key_width, width), jnp.bfloat16),
            ((2, heads, tokens), jnp.float32),
            ((spans, heads, 128), jnp.float32),
            *[(array.shape, array.dtype) for array in kept],
        ],
        [
            pltpu.VMEM(log_decay.shape, jnp.float32),
            pltpu.VMEM((spans.bit_length() - 1, heads, key_width, width // heads), jnp.float32),
            pltpu.VMEM((width, key_width), jnp.float32),
            pltpu.SemaphoreType.DMA((spans + 2,)),
        ],
        [pl.BlockSpec(memory_space=pltpu.HBM)] * len(inputs),
    )


def load_kernel(count, *refs):
    copies = [
        pltpu.make_async_copy(source, target, refs[-1].at[at])
        for at, (source, target) in enumerate(zip(refs[:count], refs[-1 - count : -1]))
    ]
    for copy in copies:
        copy.start()
    for copy in copies:
        copy.wait()


def load(arrays, token):
    count = len(arrays)
    hbm = pl.BlockSpec(memory_space=pltpu.HBM)
    return call(
        functools.partial(load_kernel, count),
        "load",
        [*[pltpu.with_memory_space_constraint(array, pltpu.HBM) for array in arrays], token],
        [(array.shape, array.dtype) for array in arrays],
        [pltpu.SemaphoreType.DMA((count,))],
        [*[hbm] * count, HELD],
    )


def local_kernel(first, last, has_token, *refs):
    q_ref, k_ref, v_ref, sums_ref, totals_ref, weight_ref, local_ref, near_ref, rest_ref = refs[:9]
    if has_token:
        mixed_ref, done_ref = refs[-2:]
        done_ref[...] = jnp.zeros_like(done_ref)
    else:
        mixed_ref = refs[-1]
    heads = weight_ref.shape[1]
    head_width = v_ref.shape[1] // heads
    spans = totals_ref.shape[0]
    local_bits = spans.bit_length() - 1
    half = SPAN // 2
    source = lax.broadcasted_iota(jnp.int32, (half, half), 0)
    target = lax.broadcasted_iota(jnp.int32, (half, half), 1)
    causal = source <= target
    empty = jnp.zeros((half, half), jnp.bfloat16)
    upper = jnp.where(bit_of(place(), 0) == 1, 1.0, 0.0)
    size = heads // 2 * head_width
    near, rest = near_ref[:size], rest_ref[:size]
    first_core = bit_of(place(), 0) == 0
    near = jnp.concatenate(
        [jnp.where(first_core, near, rest), jnp.where(first_core, rest, near)], axis=0
    ).astype(jnp.bfloat16)

    for span in range(first, last):
        tokens = slice(span * SPAN, (span + 1) * SPAN)
        queries = q_ref[tokens]
        scores = lax.dot_general(
            k_ref[tokens], queries, NT, preferred_element_type=jnp.float32
        )
        within = sums_ref[0, :, tokens]
        within_down = within.T
        weight = weight_ref[0, :, tokens]
        values_across = v_ref[tokens].T

        def mix(head, low, high):
            rows = slice(low * half, (low + 1) * half)
            columns = slice(high * half, (high + 1) * half)
            gap = within[head : head + 1, columns] - within_down[rows, head : head + 1]
            if low == high:
                gap = jnp.where(causal, gap, -1e30)
            mixing = scores[rows, columns] * jnp.exp(gap) * weight[head : head + 1, columns]
            return mixing.astype(jnp.bfloat16)

        levels = []
        offset = 0
        for bit in range(local_bits):
            if span >> bit & 1:
                since = within
                for back in range(1, span % 2**bit + 1):
                    since = since + spread_lanes(totals_ref[span - back][:, :1], SPAN)
                scale = jnp.exp(since) * weight_ref[1 + bit, :, tokens]
                levels.append((local_ref[offset + (span >> (bit + 1))].T, scale))
            offset += spans >> (bit + 1)
        reach = jnp.exp(sums_ref[1, :, tokens]) * weight_ref[1 + local_bits, :, tokens] * upper
        levels.append((near, reach))
        for head in range(heads):
            rows = slice(head * head_width, (head + 1) * head_width)
            mixing = jnp.concatenate(
                [
                    jnp.concatenate([mix(head, 0, 0), mix(head, 0, 1)], axis=1),
                    jnp.concatenate([empty, mix(head, 1, 1)], axis=1),
                ],
                axis=0,
            )
            mixed = jnp.dot(values_across[rows], mixing, preferred_element_type=jnp.float32)
            for level, scale in levels:
                found = lax.dot_general(
                    level[rows], queries, NT, preferred_element_type=jnp.float32
                )
                mixed = mixed + found * scale[head : head + 1]
            mixed_ref[rows, tokens] = mixed


def mix_local(first, last, shared, mixed, tokens, has_token):
    values = shared[2]
    rest = [] if mixed is None else [mixed]
    return call(
        functools.partial(local_kernel, first, last, has_token),
        f"local{first}",
        [*shared, *rest, *tokens],
        [(values.shape[::-1], jnp.float32), ((8, 128), jnp.float32)][: 1 + has_token],
        aliases={9: 0} if rest else None,
    )


def join(upper, mine, mine_total, other, other_total):
    fade = jnp.exp(jnp.where(upper, mine_total, other_total))
    return jnp.where(upper, other * fade + mine, mine * fade + other)


def first_head(far, heads):
    here = place()
    first = 0
    for bit, flip in enumerate(far):
        first = first + jnp.bitwise_xor(bit_of(here, bit), flip) * (heads >> (bit + 1))
    return first


def chip_kernel(mine_ref, other_ref, *refs):
    *message_refs, next_ref, whole_ref = refs
    heads = next_ref.shape[0]
    width = whole_ref.shape[0]
    held = heads // 2
    per = width // held
    here = place()
    upper = bit_of(here, 0) == 1
    first = first_head((0,), heads)
    for slot in range(held):
        part = slice(slot * per, (slot + 1) * per)
        total = pl.ds(width + first + slot, 1)
        whole_ref[part] = join(
            upper, mine_ref[part], mine_ref[total], other_ref[part], other_ref[total]
        )
    other_total = other_ref[width:]
    total = mine_ref[width:] + other_total
    next_ref[...] = jnp.where(upper, other_total, 0.0)
    half = width // 2
    side = bit_of(here, 1)
    cuts = len(message_refs) // 2
    size = half // cuts
    for at, ref in enumerate(message_refs):
        start = (side if at < cuts else 1 - side) * half + at % cuts * size
        ref[:size] = whole_ref[pl.ds(pl.multiple_of(start, 8), size)]
        ref[size:] = total


def make_chip(mine, other, heads, cuts):
    rows, lanes = mine.shape
    half = rows - heads
    *messages, prefix = call(
        chip_kernel,
        "chip",
        [mine, other],
        [
            *[((half // 2 // cuts + heads, lanes), jnp.float32)] * (2 * cuts),
            ((heads, lanes), jnp.float32),
        ],
        [pltpu.VMEM((half, lanes), jnp.float32)],
    )
    return messages[:cuts], messages[cuts:], prefix


def merge_kernel(bit, offset, has_prefix, *refs):
    mine_ref, other_ref, prefix_ref = refs[:3]
    merged_ref = refs[-2] if has_prefix else refs[-1]
    heads = prefix_ref.shape[0]
    rows = mine_ref.shape[0] - heads
    per = mine_ref.shape[1]
    upper = bit_of(place(), bit) == 1
    first = first_head((0,) * SPLIT_BITS, heads) + offset
    for slot in range(rows // per):
        part = slice(slot * per, (slot + 1) * per)
        total = pl.ds(rows + first + slot, 1)
        merged_ref[part] = join(
            upper, mine_ref[part], mine_ref[total], other_ref[part], other_ref[total]
        )
    other_total = other_ref[rows:]
    merged_ref[rows:] = mine_ref[rows:] + other_total
    if has_prefix:
        refs[-1][...] = prefix_ref[...] + jnp.where(upper, other_total, 0.0)


def merge(bit, offset, has_prefix, mine, other, prefix, tokens=()):
    return call(
        functools.partial(merge_kernel, bit, offset, has_prefix),
        f"merge{bit}{offset}",
        [mine, other, prefix, *tokens],
        [(mine.shape, jnp.float32), (prefix.shape, jnp.float32)][: 1 + has_prefix],
    )


def pack_kernel(takes, *refs):
    out_ref = refs[-1]
    at = 0
    for ref, rows in zip(refs, takes):
        out_ref[at : at + rows] = ref[:rows]
        at += rows


def pack(name, pieces, tokens=()):
    takes = [rows for _, rows in pieces]
    lanes = pieces[0][0].shape[1]
    return call(
        functools.partial(pack_kernel, takes),
        name,
        [*[array for array, _ in pieces], *tokens],
        [((sum(takes), lanes), jnp.float32)],
    )[0]


def level_scale(bit, first_level, prefix_ref, sums_ref, weight_ref, tokens):
    active = jnp.where(bit_of(place(), bit) == 1, 1.0, 0.0)
    reach = jnp.exp(sums_ref[1, :, tokens] + spread_lanes(prefix_ref[:, :1], SPAN))
    return reach * weight_ref[first_level + bit, :, tokens] * active


def gather_work(quarters, part_refs, heads, per):
    work = []
    for far, pieces in quarters:
        first = first_head(far, heads)
        for slot in range(heads // 4):
            states = []
            for level, index, start in pieces:
                if start is None:
                    rows = pl.ds(pl.multiple_of((first + slot) * per, 128), per)
                else:
                    rows = slice(start + slot * per, start + (slot + 1) * per)
                states.append((level, part_refs[index][rows].astype(jnp.bfloat16)))
            work.append((first + slot, states))
    return work


def add_found(mixed, queries, head, states, scale_ref):
    for level, state in states:
        found = lax.dot_general(state, queries, NT, preferred_element_type=jnp.float32)
        mixed = mixed + found * scale_ref[level, pl.ds(head, 1)]
    return mixed


def finish_kernel(quarters, first_level, bits, stays, carried, *refs):
    mixed_ref, q_ref, sums_ref, weight_ref, gain_ref = refs[:5]
    prefix_refs = refs[5 : 5 + len(bits)]
    part_refs = refs[5 + len(bits) :]
    out_refs, (own_ref, scale_ref, sent) = refs[-3 - FINISH_OUTS[stays, carried] : -3], refs[-3:]
    if stays:
        own_ref = out_refs[-1]
    heads = weight_ref.shape[1]
    head_width = mixed_ref.shape[0] // heads
    size = heads // 4 * head_width
    copies = []

    def send(block, far, rows):
        columns = pl.ds(pl.multiple_of(first_head(far, heads) * head_width, 128), size)
        copy = pltpu.make_async_copy(
            block.at[rows], out_refs[0].at[rows, columns], sent.at[len(copies)]
        )
        copy.start()
        copies.append(copy)

    if carried is not None:
        index, far = carried
        for start in range(0, q_ref.shape[0], SPAN):
            send(part_refs[index], far, slice(start, start + SPAN))
    work = gather_work(quarters, part_refs, heads, head_width)
    gains = []
    for head, _ in work:
        row = jnp.broadcast_to(gain_ref[pl.ds(head, 1)], (8, head_width))
        gains.append(row.T[:, :1])
    for span in range(q_ref.shape[0] // SPAN):
        tokens = slice(span * SPAN, (span + 1) * SPAN)
        queries = q_ref[tokens]
        for level, (bit, prefix_ref) in enumerate(zip(bits, prefix_refs)):
            scale_ref[level] = level_scale(
                bit, first_level, prefix_ref, sums_ref, weight_ref, tokens
            )
        for at, (head, states) in enumerate(work):
            rows = pl.ds(pl.multiple_of(head * head_width, 128), head_width)
            mixed = add_found(mixed_ref[rows, tokens], queries, head, states, scale_ref)
            square = jnp.mean(mixed * mixed, axis=0, keepdims=True)
            normed = mixed * lax.rsqrt(square + EPS) * gains[at]
            columns = slice(at * head_width, (at + 1) * head_width)
            own_ref[tokens, columns] = normed.astype(jnp.bfloat16).T
        if not stays:
            for start in range(tokens.start, tokens.stop, SPAN // 2):
                send(own_ref, quarters[0][0], slice(start, start + SPAN // 2))
    for copy in copies:
        copy.wait()


FINISH_OUTS = {}


def finish(quarters, first_level, bits, shared, prefixes, parts, begun, stays, carried):
    mixed, queries, sums, level_weight, gain = shared
    width, tokens = mixed.shape
    heads = level_weight.shape[1]
    inputs = [*shared, *prefixes, *parts]
    specs = [HELD] * len(inputs)
    inputs = [hold(array) for array in inputs]
    hbm = pl.BlockSpec(memory_space=pltpu.HBM)
    aliases = {}
    if begun is not None:
        aliases = {len(inputs): 0}
        specs.append(hbm)
        inputs.append(begun)
    name = "finish" + "".join(f"{core}{side}" for (core, side), _ in quarters)
    block = (tokens, width // 4)
    out_specs, shapes = [], []
    if carried is not None or not stays:
        out_specs.append(hbm)
        shapes.append(jax.ShapeDtypeStruct((tokens, width), jnp.bfloat16))
    if stays:
        out_specs.append(HELD)
        shapes.append(pltpu.VMEM(block, jnp.bfloat16))
    FINISH_OUTS[stays, carried] = len(shapes)
    return pl.pallas_call(
        functools.partial(finish_kernel, quarters, first_level, bits, stays, carried),
        in_specs=specs,
        out_specs=out_specs,
        out_shape=shapes,
        scratch_shapes=[
            pltpu.VMEM((8, 128) if stays else block, jnp.bfloat16),
            pltpu.VMEM((len(bits), heads, SPAN), jnp.float32),
            pltpu.SemaphoreType.DMA((3 * tokens // SPAN,)),
        ],
        input_output_aliases=aliases,
        compiler_params=PARAMS,
        cost_estimate=cost(name),
        name=name,
    )(*inputs)


def trade(value, mask):
    wide, narrow = lax.axis_size("wide"), lax.axis_size("narrow")

    def ranked(index):
        return index % narrow * wide + index // narrow

    pairs = [(ranked(source), ranked(source ^ mask)) for source in range(wide * narrow)]
    return lax.ppermute(value, AXES, pairs)


def per_device(queries, keys, values, log_decay, level_weight, norm_gain):
    heads = log_decay.shape[0]
    tokens, width = values.shape
    per = width // heads
    spans = tokens // SPAN
    group_bits = heads.bit_length() - 1
    bits = (lax.axis_size("wide") * lax.axis_size("narrow")).bit_length() - 1
    first_level = level_weight.shape[0] - bits
    gain = norm_gain.reshape(heads, per)
    keep, send, local, sums, totals, keys, values = make_states(keys, values, log_decay)
    last = bits - 1
    two = 2 * per
    size = two // CUTS
    sides = [(core, side) for core in (0, 1) for side in (0, 1)]
    other, other_rest = trade(send, 1), trade(keep, 1)
    chunks, give, prefix = make_chip(keep, other, heads, CUTS)
    queries, level_weight, gain = load([queries, level_weight, gain], chunks[0])
    shared = (queries, keys, values, sums, totals, level_weight, local, other, other_rest)
    prefixes = [None, prefix]
    found, across = {}, {}
    mixed, at = None, 0

    def both(name, messages, tokens=()):
        return pack(name, [(state, size) for state in messages], tokens)

    for bit in range(1, bits):
        found[bit] = [trade(chunk, 2**bit) for chunk in (give if bit == 1 else chunks)]
        stays = chunks if bit == 1 else stays
        waits = []
        if bit < 3 or bit == last:
            stop = spans if bit == last else at + 1
            begun = [*chunks[-1:], *([found[bit - 1]] if bit == last else [])]
            mixed, *waits = mix_local(at, stop, shared, mixed, begun, True)
            at = stop
        if bit == 3:
            waits.append(rest)
        if bit < last:
            merged = {}
            order = list(reversed(range(CUTS)))
            for offset in order:
                ending = offset == order[-1]
                tokens_of = [*merged.values(), *(waits if ending else ())]
                merged[offset], *after = merge(
                    bit, offset, ending, chunks[offset], found[bit][offset], prefixes[bit], tokens_of
                )
            chunks = [merged[offset] for offset in range(CUTS)]
            newest = merged[order[-1]]
            prefixes += after
            found[bit] = both(f"found{bit}", found[bit], (newest,))
            if bit > 1:
                across[bit] = trade(found[bit], 2)
            else:
                rest = trade(both("rest", stays, (newest,)), 2)

    state = both("state", found[last], waits)
    beside = trade(state, 2)
    early = list(range(2, last))
    pieces = [(found[1], two), (rest, two)]
    for bit in early:
        pieces += [(found[bit], two), (across[bit], two)]
    near = pack("near", pieces, (state,))
    far = trade(near, 1)
    middle = [1, *early]
    ahead = [prefixes[bit] for bit in middle]

    def states_of(side, index, first):
        return [(first + slot, index, (2 * slot + side) * two) for slot in range(len(middle))]

    shared = (mixed, queries, sums, level_weight, gain)
    every = (first_level, [last, *middle], shared, [prefixes[last], *ahead])
    quarters = {(core, side): [(0, 0, 0), *states_of(side, 1, 1)] for core, side in sides}
    state_far = trade(pack("shared", [(state, two)], (near,)), 1)
    (block,) = finish([((0, 0), quarters[0, 0])], *every, [state, near], None, True, None)
    (block_far,) = finish(
        [((1, 0), quarters[1, 0])], *every, [state_far, far, block], None, True, None
    )
    beside = pack("beside", [(beside, two)], (block_far,))
    (out,) = finish(
        [((0, 1), quarters[0, 1])], *every, [beside, near, block], None, False, (2, (0, 0))
    )
    beside_far = trade(beside, 1)
    return finish(
        [((1, 1), quarters[1, 1])], *every, [beside_far, far, block_far], out, False, (2, (1, 0))
    )[0]


def solution(mesh):
    placed = (
        P(("wide", "narrow"), None),
        P(("wide", "narrow"), None),
        P(("wide", "narrow"), None),
        P(None, ("wide", "narrow")),
        P(None, None, ("wide", "narrow")),
        P(),
    )
    return jax.shard_map(
        per_device,
        mesh=mesh,
        in_specs=placed,
        out_specs=P(("wide", "narrow"), None),
        check_vma=False,
    )
```

```python
import functools

import jax
import jax.numpy as jnp
from jax import lax
from jax.experimental import pallas as pl
from jax.experimental.pallas import tpu as pltpu
from jax.sharding import PartitionSpec as P

SPAN = 256
SPLIT_BITS = 2
CUTS = 2
EPS = 1e-05
AXES = ("narrow", "wide")
NT = (((1,), (1,)), ((), ()))
COSTS = {"local0": 1000, "finish00": 20000000000, "finish10": 1000, "finish01": 20000000000, "local2": 1000, "reach": 1000}


def cost(name):
    flops = COSTS.get(name, 2000000000)
    return pl.CostEstimate(flops=flops, transcendentals=0, bytes_accessed=1_000_000)


PARAMS = pltpu.CompilerParams(vmem_limit_bytes=32 * 1024 * 1024)
HELD = pl.BlockSpec(memory_space=pltpu.VMEM)


def place():
    return lax.axis_index("wide") * lax.axis_size("narrow") + lax.axis_index("narrow")


def bit_of(value, bit):
    return jnp.bitwise_and(jnp.right_shift(value, bit), 1)


def spread_lanes(column, width):
    return jnp.broadcast_to(column, (column.shape[0], width))


ANYWHERE = pl.BlockSpec(memory_space=pl.ANY)


def hold(array):
    return pltpu.with_memory_space_constraint(array, pltpu.VMEM)


def call(kernel, name, inputs, outputs, scratch=(), in_specs=None, aliases=None):
    specs = in_specs or [HELD] * len(inputs)
    inputs = [hold(array) if spec is HELD else array for array, spec in zip(inputs, specs)]
    return pl.pallas_call(
        kernel,
        in_specs=specs,
        out_specs=[HELD] * len(outputs),
        out_shape=[pltpu.VMEM(shape, dtype) for shape, dtype in outputs],
        scratch_shapes=list(scratch),
        input_output_aliases=aliases or {},
        compiler_params=PARAMS,
        cost_estimate=cost(name),
        name=name,
    )(*inputs)


def running_sums(rows):
    high = rows.astype(jnp.bfloat16)
    rest = rows - high.astype(jnp.float32)
    middle = rest.astype(jnp.bfloat16)
    low = (rest - middle.astype(jnp.float32)).astype(jnp.bfloat16)
    width = rows.shape[1]
    source = lax.broadcasted_iota(jnp.int32, (width, width), 0)
    target = lax.broadcasted_iota(jnp.int32, (width, width), 1)
    upto = jnp.where(source <= target, 1.0, 0.0).astype(jnp.bfloat16)
    sums = jnp.dot(
        jnp.concatenate([high, middle, low], axis=0), upto, preferred_element_type=jnp.float32
    )
    count = rows.shape[0]
    return sums[:count] + (sums[count : 2 * count] + sums[2 * count :])


def state_kernel(*refs):
    k_hbm, v_hbm, decay_hbm = refs[:3]
    keep_ref, send_ref, local_ref, sums_ref, totals_ref = refs[3:8]
    k_ref, v_ref, decay_ref, held, message_ref, arrived = refs[8:]
    heads, tokens = decay_ref.shape
    head_width = v_ref.shape[1] // heads
    spans = tokens // SPAN
    rows_of = [slice(span * SPAN, (span + 1) * SPAN) for span in range(spans)]
    loads = [(decay_hbm, decay_ref), (k_hbm, k_ref)]
    loads += [(v_hbm.at[rows], v_ref.at[rows]) for rows in rows_of]
    copies = [
        pltpu.make_async_copy(source, target, arrived.at[at])
        for at, (source, target) in enumerate(loads)
    ]
    for copy in copies:
        copy.start()
    copies[0].wait()
    copies[1].wait()
    within = running_sums(jnp.concatenate([decay_ref[:, rows] for rows in rows_of], axis=0))
    run = jnp.zeros((heads, 128), jnp.float32)
    fades, wholes = [], []
    for span, rows in enumerate(rows_of):
        here = within[span * heads : (span + 1) * heads]
        last = here[:, SPAN - 1 :]
        total = spread_lanes(last, 128)
        sums_ref[0, :, rows] = here
        sums_ref[1, :, rows] = here + spread_lanes(run[:, :1], SPAN)
        totals_ref[span] = total
        run = run + total
        fades.append(jnp.exp(spread_lanes(last, SPAN) - here))
        wholes.append(jnp.exp(total))
    across = [k_ref[rows].astype(jnp.float32).T for rows in rows_of]
    local_bits = spans.bit_length() - 1
    for span, rows in enumerate(rows_of):
        copies[2 + span].wait()
        for head in range(heads):
            columns = slice(head * head_width, (head + 1) * head_width)
            faded = (across[span] * fades[span][head : head + 1]).astype(jnp.bfloat16)
            state = jnp.dot(faded, v_ref[rows, columns], preferred_element_type=jnp.float32)
            at = 0
            for bit in range(local_bits + 1):
                if span >> bit & 1 == 0 or bit == local_bits:
                    group = state
                    if span % 2**bit > 0:
                        group = held[bit - 1, head] * wholes[span][head : head + 1] + state
                    if (span + 1) % 2**bit > 0:
                        held[bit - 1, head] = group
                    elif bit < local_bits:
                        local_ref[at + (span >> (bit + 1)), :, columns] = group.astype(
                            jnp.bfloat16
                        )
                    else:
                        message_ref[columns] = group.T
                at += spans >> (bit + 1)
    half = message_ref.shape[0] // 2
    core = bit_of(place(), 0)
    keep_ref[:half] = message_ref[pl.ds(pl.multiple_of(core * half, 8), half)]
    send_ref[:half] = message_ref[pl.ds(pl.multiple_of((1 - core) * half, 8), half)]
    keep_ref[half:] = run
    send_ref[half:] = run


def make_states(keys, values, log_decay):
    tokens, key_width = keys.shape
    heads = log_decay.shape[0]
    width = values.shape[1]
    spans = tokens // SPAN
    inputs = [keys, values, log_decay]
    kept = [keys, values]
    return call(
        state_kernel,
        "states",
        [pltpu.with_memory_space_constraint(array, pltpu.HBM) for array in inputs],
        [
            ((width // 2 + heads, key_width), jnp.float32),
            ((width // 2 + heads, key_width), jnp.float32),
            ((spans - 1, key_width, width), jnp.bfloat16),
            ((2, heads, tokens), jnp.float32),
            ((spans, heads, 128), jnp.float32),
            *[(array.shape, array.dtype) for array in kept],
        ],
        [
            pltpu.VMEM(log_decay.shape, jnp.float32),
            pltpu.VMEM((spans.bit_length() - 1, heads, key_width, width // heads), jnp.float32),
            pltpu.VMEM((width, key_width), jnp.float32),
            pltpu.SemaphoreType.DMA((spans + 2,)),
        ],
        [pl.BlockSpec(memory_space=pltpu.HBM)] * len(inputs),
    )


def load_kernel(count, *refs):
    copies = [
        pltpu.make_async_copy(source, target, refs[-1].at[at])
        for at, (source, target) in enumerate(zip(refs[:count], refs[-1 - count : -1]))
    ]
    for copy in copies:
        copy.start()
    for copy in copies:
        copy.wait()


def load(arrays, token):
    count = len(arrays)
    hbm = pl.BlockSpec(memory_space=pltpu.HBM)
    return call(
        functools.partial(load_kernel, count),
        "load",
        [*[pltpu.with_memory_space_constraint(array, pltpu.HBM) for array in arrays], token],
        [(array.shape, array.dtype) for array in arrays],
        [pltpu.SemaphoreType.DMA((count,))],
        [*[hbm] * count, HELD],
    )


def local_kernel(first, last, has_token, *refs):
    q_ref, k_ref, v_ref, sums_ref, totals_ref, weight_ref, local_ref, near_ref, rest_ref = refs[:9]
    if has_token:
        mixed_ref, done_ref = refs[-2:]
        done_ref[...] = jnp.zeros_like(done_ref)
    else:
        mixed_ref = refs[-1]
    heads = weight_ref.shape[1]
    head_width = v_ref.shape[1] // heads
    spans = totals_ref.shape[0]
    local_bits = spans.bit_length() - 1
    half = SPAN // 2
    source = lax.broadcasted_iota(jnp.int32, (half, half), 0)
    target = lax.broadcasted_iota(jnp.int32, (half, half), 1)
    causal = source <= target
    empty = jnp.zeros((half, half), jnp.bfloat16)
    upper = jnp.where(bit_of(place(), 0) == 1, 1.0, 0.0)
    size = heads // 2 * head_width
    near, rest = near_ref[:size], rest_ref[:size]
    first_core = bit_of(place(), 0) == 0
    near = jnp.concatenate(
        [jnp.where(first_core, near, rest), jnp.where(first_core, rest, near)], axis=0
    ).astype(jnp.bfloat16)

    for span in range(first, last):
        tokens = slice(span * SPAN, (span + 1) * SPAN)
        queries = q_ref[tokens]
        scores = lax.dot_general(
            k_ref[tokens], queries, NT, preferred_element_type=jnp.float32
        )
        within = sums_ref[0, :, tokens]
        within_down = within.T
        weight = weight_ref[0, :, tokens]
        values_across = v_ref[tokens].T

        def mix(head, low, high):
            rows = slice(low * half, (low + 1) * half)
            columns = slice(high * half, (high + 1) * half)
            gap = within[head : head + 1, columns] - within_down[rows, head : head + 1]
            if low == high:
                gap = jnp.where(causal, gap, -1e30)
            mixing = scores[rows, columns] * jnp.exp(gap) * weight[head : head + 1, columns]
            return mixing.astype(jnp.bfloat16)

        levels = []
        offset = 0
        for bit in range(local_bits):
            if span >> bit & 1:
                since = within
                for back in range(1, span % 2**bit + 1):
                    since = since + spread_lanes(totals_ref[span - back][:, :1], SPAN)
                scale = jnp.exp(since) * weight_ref[1 + bit, :, tokens]
                levels.append((local_ref[offset + (span >> (bit + 1))].T, scale))
            offset += spans >> (bit + 1)
        reach = jnp.exp(sums_ref[1, :, tokens]) * weight_ref[1 + local_bits, :, tokens] * upper
        levels.append((near, reach))
        for head in range(heads):
            rows = slice(head * head_width, (head + 1) * head_width)
            mixing = jnp.concatenate(
                [
                    jnp.concatenate([mix(head, 0, 0), mix(head, 0, 1)], axis=1),
                    jnp.concatenate([empty, mix(head, 1, 1)], axis=1),
                ],
                axis=0,
            )
            mixed = jnp.dot(values_across[rows], mixing, preferred_element_type=jnp.float32)
            for level, scale in levels:
                found = lax.dot_general(
                    level[rows], queries, NT, preferred_element_type=jnp.float32
                )
                mixed = mixed + found * scale[head : head + 1]
            mixed_ref[rows, tokens] = mixed


def mix_local(first, last, shared, mixed, tokens, has_token):
    values = shared[2]
    rest = [] if mixed is None else [mixed]
    return call(
        functools.partial(local_kernel, first, last, has_token),
        f"local{first}",
        [*shared, *rest, *tokens],
        [(values.shape[::-1], jnp.float32), ((8, 128), jnp.float32)][: 1 + has_token],
        aliases={9: 0} if rest else None,
    )


def join(upper, mine, mine_total, other, other_total):
    fade = jnp.exp(jnp.where(upper, mine_total, other_total))
    return jnp.where(upper, other * fade + mine, mine * fade + other)


def first_head(far, heads):
    here = place()
    first = 0
    for bit, flip in enumerate(far):
        first = first + jnp.bitwise_xor(bit_of(here, bit), flip) * (heads >> (bit + 1))
    return first


def chip_kernel(mine_ref, other_ref, *refs):
    *message_refs, next_ref, whole_ref = refs
    heads = next_ref.shape[0]
    width = whole_ref.shape[0]
    held = heads // 2
    per = width // held
    here = place()
    upper = bit_of(here, 0) == 1
    first = first_head((0,), heads)
    for slot in range(held):
        part = slice(slot * per, (slot + 1) * per)
        total = pl.ds(width + first + slot, 1)
        whole_ref[part] = join(
            upper, mine_ref[part], mine_ref[total], other_ref[part], other_ref[total]
        )
    other_total = other_ref[width:]
    total = mine_ref[width:] + other_total
    next_ref[...] = jnp.where(upper, other_total, 0.0)
    half = width // 2
    side = bit_of(here, 1)
    cuts = len(message_refs) // 2
    size = half // cuts
    for at, ref in enumerate(message_refs):
        start = (side if at < cuts else 1 - side) * half + at % cuts * size
        ref[:size] = whole_ref[pl.ds(pl.multiple_of(start, 8), size)]
        ref[size:] = total


def make_chip(mine, other, heads, cuts):
    rows, lanes = mine.shape
    half = rows - heads
    *messages, prefix = call(
        chip_kernel,
        "chip",
        [mine, other],
        [
            *[((half // 2 // cuts + heads, lanes), jnp.float32)] * (2 * cuts),
            ((heads, lanes), jnp.float32),
        ],
        [pltpu.VMEM((half, lanes), jnp.float32)],
    )
    return messages[:cuts], messages[cuts:], prefix


def merge_kernel(bit, offset, has_prefix, *refs):
    mine_ref, other_ref, prefix_ref = refs[:3]
    merged_ref = refs[-2] if has_prefix else refs[-1]
    heads = prefix_ref.shape[0]
    rows = mine_ref.shape[0] - heads
    per = mine_ref.shape[1]
    upper = bit_of(place(), bit) == 1
    first = first_head((0,) * SPLIT_BITS, heads) + offset
    for slot in range(rows // per):
        part = slice(slot * per, (slot + 1) * per)
        total = pl.ds(rows + first + slot, 1)
        merged_ref[part] = join(
            upper, mine_ref[part], mine_ref[total], other_ref[part], other_ref[total]
        )
    other_total = other_ref[rows:]
    merged_ref[rows:] = mine_ref[rows:] + other_total
    if has_prefix:
        refs[-1][...] = prefix_ref[...] + jnp.where(upper, other_total, 0.0)


def merge(bit, offset, has_prefix, mine, other, prefix, tokens=()):
    return call(
        functools.partial(merge_kernel, bit, offset, has_prefix),
        f"merge{bit}{offset}",
        [mine, other, prefix, *tokens],
        [(mine.shape, jnp.float32), (prefix.shape, jnp.float32)][: 1 + has_prefix],
    )


def pack_kernel(takes, *refs):
    out_ref = refs[-1]
    at = 0
    for ref, rows in zip(refs, takes):
        out_ref[at : at + rows] = ref[:rows]
        at += rows


def pack(name, pieces, tokens=()):
    takes = [rows for _, rows in pieces]
    lanes = pieces[0][0].shape[1]
    return call(
        functools.partial(pack_kernel, takes),
        name,
        [*[array for array, _ in pieces], *tokens],
        [((sum(takes), lanes), jnp.float32)],
    )[0]


def level_scale(bit, first_level, prefix_ref, sums_ref, weight_ref, tokens):
    active = jnp.where(bit_of(place(), bit) == 1, 1.0, 0.0)
    reach = jnp.exp(sums_ref[1, :, tokens] + spread_lanes(prefix_ref[:, :1], SPAN))
    return reach * weight_ref[first_level + bit, :, tokens] * active


def gather_work(quarters, part_refs, heads, per):
    work = []
    for far, pieces in quarters:
        first = first_head(far, heads)
        for slot in range(heads // 4):
            states = []
            for level, index, start in pieces:
                if start is None:
                    rows = pl.ds(pl.multiple_of((first + slot) * per, 128), per)
                else:
                    rows = slice(start + slot * per, start + (slot + 1) * per)
                states.append((level, part_refs[index][rows].astype(jnp.bfloat16)))
            work.append((first + slot, states))
    return work


def add_found(mixed, queries, head, states, scale_ref):
    for level, state in states:
        found = lax.dot_general(state, queries, NT, preferred_element_type=jnp.float32)
        mixed = mixed + found * scale_ref[level, pl.ds(head, 1)]
    return mixed


def finish_kernel(quarters, first_level, bits, stays, carried, *refs):
    mixed_ref, q_ref, sums_ref, weight_ref, gain_ref = refs[:5]
    prefix_refs = refs[5 : 5 + len(bits)]
    part_refs = refs[5 + len(bits) :]
    out_refs, (own_ref, scale_ref, sent) = refs[-3 - FINISH_OUTS[stays, carried] : -3], refs[-3:]
    if stays:
        own_ref = out_refs[-1]
    heads = weight_ref.shape[1]
    head_width = mixed_ref.shape[0] // heads
    size = heads // 4 * head_width
    copies = []

    def send(block, far, rows):
        columns = pl.ds(pl.multiple_of(first_head(far, heads) * head_width, 128), size)
        copy = pltpu.make_async_copy(
            block.at[rows], out_refs[0].at[rows, columns], sent.at[len(copies)]
        )
        copy.start()
        copies.append(copy)

    if carried is not None:
        index, far = carried
        for start in range(0, q_ref.shape[0], SPAN):
            send(part_refs[index], far, slice(start, start + SPAN))
    work = gather_work(quarters, part_refs, heads, head_width)
    gains = []
    for head, _ in work:
        row = jnp.broadcast_to(gain_ref[pl.ds(head, 1)], (8, head_width))
        gains.append(row.T[:, :1])
    for span in range(q_ref.shape[0] // SPAN):
        tokens = slice(span * SPAN, (span + 1) * SPAN)
        queries = q_ref[tokens]
        for level, (bit, prefix_ref) in enumerate(zip(bits, prefix_refs)):
            scale_ref[level] = level_scale(
                bit, first_level, prefix_ref, sums_ref, weight_ref, tokens
            )
        for at, (head, states) in enumerate(work):
            rows = pl.ds(pl.multiple_of(head * head_width, 128), head_width)
            mixed = add_found(mixed_ref[rows, tokens], queries, head, states, scale_ref)
            square = jnp.mean(mixed * mixed, axis=0, keepdims=True)
            normed = mixed * lax.rsqrt(square + EPS) * gains[at]
            columns = slice(at * head_width, (at + 1) * head_width)
            own_ref[tokens, columns] = normed.astype(jnp.bfloat16).T
        if not stays:
            for start in range(tokens.start, tokens.stop, SPAN // 2):
                send(own_ref, quarters[0][0], slice(start, start + SPAN // 2))
    for copy in copies:
        copy.wait()


FINISH_OUTS = {}


def finish(quarters, first_level, bits, shared, prefixes, parts, begun, stays, carried):
    mixed, queries, sums, level_weight, gain = shared
    width, tokens = mixed.shape
    heads = level_weight.shape[1]
    inputs = [*shared, *prefixes, *parts]
    specs = [HELD] * len(inputs)
    inputs = [hold(array) for array in inputs]
    hbm = pl.BlockSpec(memory_space=pltpu.HBM)
    aliases = {}
    if begun is not None:
        aliases = {len(inputs): 0}
        specs.append(hbm)
        inputs.append(begun)
    name = "finish" + "".join(f"{core}{side}" for (core, side), _ in quarters)
    block = (tokens, width // 4)
    out_specs, shapes = [], []
    if carried is not None or not stays:
        out_specs.append(hbm)
        shapes.append(jax.ShapeDtypeStruct((tokens, width), jnp.bfloat16))
    if stays:
        out_specs.append(HELD)
        shapes.append(pltpu.VMEM(block, jnp.bfloat16))
    FINISH_OUTS[stays, carried] = len(shapes)
    return pl.pallas_call(
        functools.partial(finish_kernel, quarters, first_level, bits, stays, carried),
        in_specs=specs,
        out_specs=out_specs,
        out_shape=shapes,
        scratch_shapes=[
            pltpu.VMEM((8, 128) if stays else block, jnp.bfloat16),
            pltpu.VMEM((len(bits), heads, SPAN), jnp.float32),
            pltpu.SemaphoreType.DMA((3 * tokens // SPAN,)),
        ],
        input_output_aliases=aliases,
        compiler_params=PARAMS,
        cost_estimate=cost(name),
        name=name,
    )(*inputs)


def trade(value, mask):
    wide, narrow = lax.axis_size("wide"), lax.axis_size("narrow")

    def ranked(index):
        return index % narrow * wide + index // narrow

    pairs = [(ranked(source), ranked(source ^ mask)) for source in range(wide * narrow)]
    return lax.ppermute(value, AXES, pairs)


def per_device(queries, keys, values, log_decay, level_weight, norm_gain):
    heads = log_decay.shape[0]
    tokens, width = values.shape
    per = width // heads
    spans = tokens // SPAN
    group_bits = heads.bit_length() - 1
    bits = (lax.axis_size("wide") * lax.axis_size("narrow")).bit_length() - 1
    first_level = level_weight.shape[0] - bits
    gain = norm_gain.reshape(heads, per)
    keep, send, local, sums, totals, keys, values = make_states(keys, values, log_decay)
    last = bits - 1
    two = 2 * per
    size = two // CUTS
    sides = [(core, side) for core in (0, 1) for side in (0, 1)]
    other, other_rest = trade(send, 1), trade(keep, 1)
    chunks, give, prefix = make_chip(keep, other, heads, CUTS)
    queries, level_weight, gain = load([queries, level_weight, gain], chunks[0])
    shared = (queries, keys, values, sums, totals, level_weight, local, other, other_rest)
    prefixes = [None, prefix]
    found, across = {}, {}
    mixed, at = None, 0

    def both(name, messages, tokens=()):
        return pack(name, [(state, size) for state in messages], tokens)

    for bit in range(1, bits):
        sent = give if bit == 1 else chunks
        if bit == last:
            sent = [both("top", chunks)]
        found[bit] = [trade(chunk, 2**bit) for chunk in sent]
        stays = chunks if bit == 1 else stays
        waits = []
        if bit < 3 or bit == last:
            stop = spans if bit == last else at + 1
            begun = [*chunks[-1:], *([found[bit - 1]] if bit == last else [])]
            mixed, *waits = mix_local(at, stop, shared, mixed, begun, True)
            at = stop
        if bit == 3:
            waits.append(rest)
        if bit < last:
            merged = {}
            order = list(reversed(range(CUTS)))
            for offset in order:
                ending = offset == order[-1]
                tokens_of = [*merged.values(), *(waits if ending else ())]
                merged[offset], *after = merge(
                    bit, offset, ending, chunks[offset], found[bit][offset], prefixes[bit], tokens_of
                )
            chunks = [merged[offset] for offset in range(CUTS)]
            newest = merged[order[-1]]
            prefixes += after
            found[bit] = both(f"found{bit}", found[bit], (newest,))
            if bit > 1:
                across[bit] = trade(found[bit], 2)
            else:
                rest = trade(both("rest", stays, (newest,)), 2)

    state = pack("state", [(found[last][0], two)], waits)
    beside = trade(state, 2)
    early = list(range(2, last))
    pieces = [(found[1], two), (rest, two)]
    for bit in early:
        pieces += [(found[bit], two), (across[bit], two)]
    near = pack("near", pieces, (state,))
    far = trade(near, 1)
    middle = [1, *early]
    ahead = [prefixes[bit] for bit in middle]

    def states_of(side, index, first):
        return [(first + slot, index, (2 * slot + side) * two) for slot in range(len(middle))]

    shared = (mixed, queries, sums, level_weight, gain)
    every = (first_level, [last, *middle], shared, [prefixes[last], *ahead])
    quarters = {(core, side): [(0, 0, 0), *states_of(side, 1, 1)] for core, side in sides}
    state_far = trade(pack("shared", [(state, two)], (near,)), 1)
    (block,) = finish([((0, 0), quarters[0, 0])], *every, [state, near], None, True, None)
    (block_far,) = finish(
        [((1, 0), quarters[1, 0])], *every, [state_far, far, block], None, True, None
    )
    beside = pack("beside", [(beside, two)], (block_far,))
    (out,) = finish(
        [((0, 1), quarters[0, 1])], *every, [beside, near, block], None, False, (2, (0, 0))
    )
    beside_far = trade(beside, 1)
    return finish(
        [((1, 1), quarters[1, 1])], *every, [beside_far, far, block_far], out, False, (2, (1, 0))
    )[0]


def solution(mesh):
    placed = (
        P(("wide", "narrow"), None),
        P(("wide", "narrow"), None),
        P(("wide", "narrow"), None),
        P(None, ("wide", "narrow")),
        P(None, None, ("wide", "narrow")),
        P(),
    )
    return jax.shard_map(
        per_device,
        mesh=mesh,
        in_specs=placed,
        out_specs=P(("wide", "narrow"), None),
        check_vma=False,
    )
```

```python
import functools

import jax
import jax.numpy as jnp
from jax import lax
from jax.experimental import pallas as pl
from jax.experimental.pallas import tpu as pltpu
from jax.sharding import PartitionSpec as P

SPAN = 256
SPLIT_BITS = 2
CUTS = 2
LOADS = 4
EPS = 1e-05
AXES = ("narrow", "wide")
NT = (((1,), (1,)), ((), ()))
COSTS = {"local0": 1000, "finish00": 20000000000, "finish10": 1000, "finish01": 20000000000, "local2": 1000, "reach": 1000}


def cost(name):
    flops = COSTS.get(name, 2000000000)
    return pl.CostEstimate(flops=flops, transcendentals=0, bytes_accessed=1_000_000)


PARAMS = pltpu.CompilerParams(vmem_limit_bytes=32 * 1024 * 1024)
HELD = pl.BlockSpec(memory_space=pltpu.VMEM)


def place():
    return lax.axis_index("wide") * lax.axis_size("narrow") + lax.axis_index("narrow")


def bit_of(value, bit):
    return jnp.bitwise_and(jnp.right_shift(value, bit), 1)


def spread_lanes(column, width):
    return jnp.broadcast_to(column, (column.shape[0], width))


ANYWHERE = pl.BlockSpec(memory_space=pl.ANY)


def hold(array):
    return pltpu.with_memory_space_constraint(array, pltpu.VMEM)


def call(kernel, name, inputs, outputs, scratch=(), in_specs=None, aliases=None):
    specs = in_specs or [HELD] * len(inputs)
    inputs = [hold(array) if spec is HELD else array for array, spec in zip(inputs, specs)]
    return pl.pallas_call(
        kernel,
        in_specs=specs,
        out_specs=[HELD] * len(outputs),
        out_shape=[pltpu.VMEM(shape, dtype) for shape, dtype in outputs],
        scratch_shapes=list(scratch),
        input_output_aliases=aliases or {},
        compiler_params=PARAMS,
        cost_estimate=cost(name),
        name=name,
    )(*inputs)


def running_sums(rows):
    high = rows.astype(jnp.bfloat16)
    rest = rows - high.astype(jnp.float32)
    middle = rest.astype(jnp.bfloat16)
    low = (rest - middle.astype(jnp.float32)).astype(jnp.bfloat16)
    width = rows.shape[1]
    source = lax.broadcasted_iota(jnp.int32, (width, width), 0)
    target = lax.broadcasted_iota(jnp.int32, (width, width), 1)
    upto = jnp.where(source <= target, 1.0, 0.0).astype(jnp.bfloat16)
    sums = jnp.dot(
        jnp.concatenate([high, middle, low], axis=0), upto, preferred_element_type=jnp.float32
    )
    count = rows.shape[0]
    return sums[:count] + (sums[count : 2 * count] + sums[2 * count :])


def state_kernel(*refs):
    k_hbm, v_hbm, decay_hbm = refs[:3]
    keep_ref, send_ref, local_ref, sums_ref, totals_ref = refs[3:8]
    k_ref, v_ref, decay_ref, held, message_ref, arrived = refs[8:]
    heads, tokens = decay_ref.shape
    head_width = v_ref.shape[1] // heads
    spans = tokens // SPAN
    rows_of = [slice(span * SPAN, (span + 1) * SPAN) for span in range(spans)]
    loads = [(decay_hbm, decay_ref), (k_hbm, k_ref)]
    step = SPAN // LOADS
    pieces = [slice(start, start + step) for start in range(0, tokens, step)]
    loads += [(v_hbm.at[rows], v_ref.at[rows]) for rows in pieces]
    copies = [
        pltpu.make_async_copy(source, target, arrived.at[at])
        for at, (source, target) in enumerate(loads)
    ]
    for copy in copies:
        copy.start()
    copies[0].wait()
    copies[1].wait()
    within = running_sums(jnp.concatenate([decay_ref[:, rows] for rows in rows_of], axis=0))
    run = jnp.zeros((heads, 128), jnp.float32)
    fades, wholes = [], []
    for span, rows in enumerate(rows_of):
        here = within[span * heads : (span + 1) * heads]
        last = here[:, SPAN - 1 :]
        total = spread_lanes(last, 128)
        sums_ref[0, :, rows] = here
        sums_ref[1, :, rows] = here + spread_lanes(run[:, :1], SPAN)
        totals_ref[span] = total
        run = run + total
        fades.append(jnp.exp(spread_lanes(last, SPAN) - here))
        wholes.append(jnp.exp(total))
    across = [k_ref[rows].astype(jnp.float32).T for rows in rows_of]
    local_bits = spans.bit_length() - 1
    for span, rows in enumerate(rows_of):
        for copy in copies[2 + span * LOADS : 2 + (span + 1) * LOADS]:
            copy.wait()
        for head in range(heads):
            columns = slice(head * head_width, (head + 1) * head_width)
            faded = (across[span] * fades[span][head : head + 1]).astype(jnp.bfloat16)
            state = jnp.dot(faded, v_ref[rows, columns], preferred_element_type=jnp.float32)
            at = 0
            for bit in range(local_bits + 1):
                if span >> bit & 1 == 0 or bit == local_bits:
                    group = state
                    if span % 2**bit > 0:
                        group = held[bit - 1, head] * wholes[span][head : head + 1] + state
                    if (span + 1) % 2**bit > 0:
                        held[bit - 1, head] = group
                    elif bit < local_bits:
                        local_ref[at + (span >> (bit + 1)), :, columns] = group.astype(
                            jnp.bfloat16
                        )
                    else:
                        message_ref[columns] = group.T
                at += spans >> (bit + 1)
    half = message_ref.shape[0] // 2
    core = bit_of(place(), 0)
    keep_ref[:half] = message_ref[pl.ds(pl.multiple_of(core * half, 8), half)]
    send_ref[:half] = message_ref[pl.ds(pl.multiple_of((1 - core) * half, 8), half)]
    keep_ref[half:] = run
    send_ref[half:] = run


def make_states(keys, values, log_decay):
    tokens, key_width = keys.shape
    heads = log_decay.shape[0]
    width = values.shape[1]
    spans = tokens // SPAN
    inputs = [keys, values, log_decay]
    kept = [keys, values]
    return call(
        state_kernel,
        "states",
        [pltpu.with_memory_space_constraint(array, pltpu.HBM) for array in inputs],
        [
            ((width // 2 + heads, key_width), jnp.float32),
            ((width // 2 + heads, key_width), jnp.float32),
            ((spans - 1, key_width, width), jnp.bfloat16),
            ((2, heads, tokens), jnp.float32),
            ((spans, heads, 128), jnp.float32),
            *[(array.shape, array.dtype) for array in kept],
        ],
        [
            pltpu.VMEM(log_decay.shape, jnp.float32),
            pltpu.VMEM((spans.bit_length() - 1, heads, key_width, width // heads), jnp.float32),
            pltpu.VMEM((width, key_width), jnp.float32),
            pltpu.SemaphoreType.DMA((LOADS * spans + 2,)),
        ],
        [pl.BlockSpec(memory_space=pltpu.HBM)] * len(inputs),
    )


def load_kernel(count, *refs):
    copies = [
        pltpu.make_async_copy(source, target, refs[-1].at[at])
        for at, (source, target) in enumerate(zip(refs[:count], refs[-1 - count : -1]))
    ]
    for copy in copies:
        copy.start()
    for copy in copies:
        copy.wait()


def load(arrays, token):
    count = len(arrays)
    hbm = pl.BlockSpec(memory_space=pltpu.HBM)
    return call(
        functools.partial(load_kernel, count),
        "load",
        [*[pltpu.with_memory_space_constraint(array, pltpu.HBM) for array in arrays], token],
        [(array.shape, array.dtype) for array in arrays],
        [pltpu.SemaphoreType.DMA((count,))],
        [*[hbm] * count, HELD],
    )


def local_kernel(first, last, has_token, *refs):
    q_ref, k_ref, v_ref, sums_ref, totals_ref, weight_ref, local_ref, near_ref, rest_ref = refs[:9]
    if has_token:
        mixed_ref, done_ref = refs[-2:]
        done_ref[...] = jnp.zeros_like(done_ref)
    else:
        mixed_ref = refs[-1]
    heads = weight_ref.shape[1]
    head_width = v_ref.shape[1] // heads
    spans = totals_ref.shape[0]
    local_bits = spans.bit_length() - 1
    half = SPAN // 2
    source = lax.broadcasted_iota(jnp.int32, (half, half), 0)
    target = lax.broadcasted_iota(jnp.int32, (half, half), 1)
    causal = source <= target
    empty = jnp.zeros((half, half), jnp.bfloat16)
    upper = jnp.where(bit_of(place(), 0) == 1, 1.0, 0.0)
    size = heads // 2 * head_width
    near, rest = near_ref[:size], rest_ref[:size]
    first_core = bit_of(place(), 0) == 0
    near = jnp.concatenate(
        [jnp.where(first_core, near, rest), jnp.where(first_core, rest, near)], axis=0
    ).astype(jnp.bfloat16)

    for span in range(first, last):
        tokens = slice(span * SPAN, (span + 1) * SPAN)
        queries = q_ref[tokens]
        scores = lax.dot_general(
            k_ref[tokens], queries, NT, preferred_element_type=jnp.float32
        )
        within = sums_ref[0, :, tokens]
        within_down = within.T
        weight = weight_ref[0, :, tokens]
        values_across = v_ref[tokens].T

        def mix(head, low, high):
            rows = slice(low * half, (low + 1) * half)
            columns = slice(high * half, (high + 1) * half)
            gap = within[head : head + 1, columns] - within_down[rows, head : head + 1]
            if low == high:
                gap = jnp.where(causal, gap, -1e30)
            mixing = scores[rows, columns] * jnp.exp(gap) * weight[head : head + 1, columns]
            return mixing.astype(jnp.bfloat16)

        levels = []
        offset = 0
        for bit in range(local_bits):
            if span >> bit & 1:
                since = within
                for back in range(1, span % 2**bit + 1):
                    since = since + spread_lanes(totals_ref[span - back][:, :1], SPAN)
                scale = jnp.exp(since) * weight_ref[1 + bit, :, tokens]
                levels.append((local_ref[offset + (span >> (bit + 1))].T, scale))
            offset += spans >> (bit + 1)
        reach = jnp.exp(sums_ref[1, :, tokens]) * weight_ref[1 + local_bits, :, tokens] * upper
        levels.append((near, reach))
        for head in range(heads):
            rows = slice(head * head_width, (head + 1) * head_width)
            mixing = jnp.concatenate(
                [
                    jnp.concatenate([mix(head, 0, 0), mix(head, 0, 1)], axis=1),
                    jnp.concatenate([empty, mix(head, 1, 1)], axis=1),
                ],
                axis=0,
            )
            mixed = jnp.dot(values_across[rows], mixing, preferred_element_type=jnp.float32)
            for level, scale in levels:
                found = lax.dot_general(
                    level[rows], queries, NT, preferred_element_type=jnp.float32
                )
                mixed = mixed + found * scale[head : head + 1]
            mixed_ref[rows, tokens] = mixed


def mix_local(first, last, shared, mixed, tokens, has_token):
    values = shared[2]
    rest = [] if mixed is None else [mixed]
    return call(
        functools.partial(local_kernel, first, last, has_token),
        f"local{first}",
        [*shared, *rest, *tokens],
        [(values.shape[::-1], jnp.float32), ((8, 128), jnp.float32)][: 1 + has_token],
        aliases={9: 0} if rest else None,
    )


def join(upper, mine, mine_total, other, other_total):
    fade = jnp.exp(jnp.where(upper, mine_total, other_total))
    return jnp.where(upper, other * fade + mine, mine * fade + other)


def first_head(far, heads):
    here = place()
    first = 0
    for bit, flip in enumerate(far):
        first = first + jnp.bitwise_xor(bit_of(here, bit), flip) * (heads >> (bit + 1))
    return first


def chip_kernel(mine_ref, other_ref, *refs):
    *message_refs, next_ref, whole_ref = refs
    heads = next_ref.shape[0]
    width = whole_ref.shape[0]
    held = heads // 2
    per = width // held
    here = place()
    upper = bit_of(here, 0) == 1
    first = first_head((0,), heads)
    for slot in range(held):
        part = slice(slot * per, (slot + 1) * per)
        total = pl.ds(width + first + slot, 1)
        whole_ref[part] = join(
            upper, mine_ref[part], mine_ref[total], other_ref[part], other_ref[total]
        )
    other_total = other_ref[width:]
    total = mine_ref[width:] + other_total
    next_ref[...] = jnp.where(upper, other_total, 0.0)
    half = width // 2
    side = bit_of(here, 1)
    cuts = len(message_refs) // 2
    size = half // cuts
    for at, ref in enumerate(message_refs):
        start = (side if at < cuts else 1 - side) * half + at % cuts * size
        ref[:size] = whole_ref[pl.ds(pl.multiple_of(start, 8), size)]
        ref[size:] = total


def make_chip(mine, other, heads, cuts):
    rows, lanes = mine.shape
    half = rows - heads
    *messages, prefix = call(
        chip_kernel,
        "chip",
        [mine, other],
        [
            *[((half // 2 // cuts + heads, lanes), jnp.float32)] * (2 * cuts),
            ((heads, lanes), jnp.float32),
        ],
        [pltpu.VMEM((half, lanes), jnp.float32)],
    )
    return messages[:cuts], messages[cuts:], prefix


def merge_kernel(bit, offset, has_prefix, *refs):
    mine_ref, other_ref, prefix_ref = refs[:3]
    merged_ref = refs[-2] if has_prefix else refs[-1]
    heads = prefix_ref.shape[0]
    rows = mine_ref.shape[0] - heads
    per = mine_ref.shape[1]
    upper = bit_of(place(), bit) == 1
    first = first_head((0,) * SPLIT_BITS, heads) + offset
    for slot in range(rows // per):
        part = slice(slot * per, (slot + 1) * per)
        total = pl.ds(rows + first + slot, 1)
        merged_ref[part] = join(
            upper, mine_ref[part], mine_ref[total], other_ref[part], other_ref[total]
        )
    other_total = other_ref[rows:]
    merged_ref[rows:] = mine_ref[rows:] + other_total
    if has_prefix:
        refs[-1][...] = prefix_ref[...] + jnp.where(upper, other_total, 0.0)


def merge(bit, offset, has_prefix, mine, other, prefix, tokens=()):
    return call(
        functools.partial(merge_kernel, bit, offset, has_prefix),
        f"merge{bit}{offset}",
        [mine, other, prefix, *tokens],
        [(mine.shape, jnp.float32), (prefix.shape, jnp.float32)][: 1 + has_prefix],
    )


def pack_kernel(takes, *refs):
    out_ref = refs[-1]
    at = 0
    for ref, rows in zip(refs, takes):
        out_ref[at : at + rows] = ref[:rows]
        at += rows


def pack(name, pieces, tokens=()):
    takes = [rows for _, rows in pieces]
    lanes = pieces[0][0].shape[1]
    return call(
        functools.partial(pack_kernel, takes),
        name,
        [*[array for array, _ in pieces], *tokens],
        [((sum(takes), lanes), jnp.float32)],
    )[0]


def level_scale(bit, first_level, prefix_ref, sums_ref, weight_ref, tokens):
    active = jnp.where(bit_of(place(), bit) == 1, 1.0, 0.0)
    reach = jnp.exp(sums_ref[1, :, tokens] + spread_lanes(prefix_ref[:, :1], SPAN))
    return reach * weight_ref[first_level + bit, :, tokens] * active


def gather_work(quarters, part_refs, heads, per):
    work = []
    for far, pieces in quarters:
        first = first_head(far, heads)
        for slot in range(heads // 4):
            states = []
            for level, index, start in pieces:
                if start is None:
                    rows = pl.ds(pl.multiple_of((first + slot) * per, 128), per)
                else:
                    rows = slice(start + slot * per, start + (slot + 1) * per)
                states.append((level, part_refs[index][rows].astype(jnp.bfloat16)))
            work.append((first + slot, states))
    return work


def add_found(mixed, queries, head, states, scale_ref):
    for level, state in states:
        found = lax.dot_general(state, queries, NT, preferred_element_type=jnp.float32)
        mixed = mixed + found * scale_ref[level, pl.ds(head, 1)]
    return mixed


def finish_kernel(quarters, first_level, bits, stays, carried, *refs):
    mixed_ref, q_ref, sums_ref, weight_ref, gain_ref = refs[:5]
    prefix_refs = refs[5 : 5 + len(bits)]
    part_refs = refs[5 + len(bits) :]
    out_ref, own_ref, scale_ref, sent = refs[-4:]
    if stays:
        own_ref = out_ref
    heads = weight_ref.shape[1]
    head_width = mixed_ref.shape[0] // heads
    size = heads // 4 * head_width
    copies = []
    far = quarters[0][0]
    base = 0
    if not stays:
        side = jnp.bitwise_xor(bit_of(place(), 1), far[1])
        base = side * size
        left = pl.ds(pl.multiple_of((1 - side) * size, 128), size)
        own_ref[:, left] = part_refs[carried][...]
        half = pl.ds(pl.multiple_of(first_head(far[:1], heads) * head_width, 128), 2 * size)

    work = gather_work(quarters, part_refs, heads, head_width)
    gains = []
    for head, _ in work:
        row = jnp.broadcast_to(gain_ref[pl.ds(head, 1)], (8, head_width))
        gains.append(row.T[:, :1])
    for span in range(q_ref.shape[0] // SPAN):
        tokens = slice(span * SPAN, (span + 1) * SPAN)
        queries = q_ref[tokens]
        for level, (bit, prefix_ref) in enumerate(zip(bits, prefix_refs)):
            scale_ref[level] = level_scale(
                bit, first_level, prefix_ref, sums_ref, weight_ref, tokens
            )
        for at, (head, states) in enumerate(work):
            rows = pl.ds(pl.multiple_of(head * head_width, 128), head_width)
            mixed = add_found(mixed_ref[rows, tokens], queries, head, states, scale_ref)
            square = jnp.mean(mixed * mixed, axis=0, keepdims=True)
            normed = mixed * lax.rsqrt(square + EPS) * gains[at]
            columns = pl.ds(pl.multiple_of(base + at * head_width, 128), head_width)
            own_ref[tokens, columns] = normed.astype(jnp.bfloat16).T
        if not stays:
            copy = pltpu.make_async_copy(
                own_ref.at[tokens], out_ref.at[tokens, half], sent.at[span]
            )
            copy.start()
            copies.append(copy)
    for copy in copies:
        copy.wait()


def finish(quarters, first_level, bits, shared, prefixes, parts, begun, stays, carried):
    mixed, queries, sums, level_weight, gain = shared
    width, tokens = mixed.shape
    heads = level_weight.shape[1]
    inputs = [*shared, *prefixes, *parts]
    specs = [HELD] * len(inputs)
    inputs = [hold(array) for array in inputs]
    hbm = pl.BlockSpec(memory_space=pltpu.HBM)
    aliases = {}
    if begun is not None:
        aliases = {len(inputs): 0}
        specs.append(hbm)
        inputs.append(begun)
    name = "finish" + "".join(f"{core}{side}" for (core, side), _ in quarters)
    block = (tokens, width // 4)
    if stays:
        out_spec, shape = HELD, pltpu.VMEM(block, jnp.bfloat16)
    else:
        out_spec, shape = hbm, jax.ShapeDtypeStruct((tokens, width), jnp.bfloat16)
    return pl.pallas_call(
        functools.partial(finish_kernel, quarters, first_level, bits, stays, carried),
        in_specs=specs,
        out_specs=out_spec,
        out_shape=shape,
        scratch_shapes=[
            pltpu.VMEM((8, 128) if stays else (tokens, width // 2), jnp.bfloat16),
            pltpu.VMEM((len(bits), heads, SPAN), jnp.float32),
            pltpu.SemaphoreType.DMA((tokens // SPAN,)),
        ],
        input_output_aliases=aliases,
        compiler_params=PARAMS,
        cost_estimate=cost(name),
        name=name,
    )(*inputs)


def trade(value, mask):
    wide, narrow = lax.axis_size("wide"), lax.axis_size("narrow")

    def ranked(index):
        return index % narrow * wide + index // narrow

    pairs = [(ranked(source), ranked(source ^ mask)) for source in range(wide * narrow)]
    return lax.ppermute(value, AXES, pairs)


def per_device(queries, keys, values, log_decay, level_weight, norm_gain):
    heads = log_decay.shape[0]
    tokens, width = values.shape
    per = width // heads
    spans = tokens // SPAN
    group_bits = heads.bit_length() - 1
    bits = (lax.axis_size("wide") * lax.axis_size("narrow")).bit_length() - 1
    first_level = level_weight.shape[0] - bits
    gain = norm_gain.reshape(heads, per)
    keep, send, local, sums, totals, keys, values = make_states(keys, values, log_decay)
    last = bits - 1
    two = 2 * per
    size = two // CUTS
    sides = [(core, side) for core in (0, 1) for side in (0, 1)]
    other, other_rest = trade(send, 1), trade(keep, 1)
    chunks, give, prefix = make_chip(keep, other, heads, CUTS)
    queries, level_weight, gain = load([queries, level_weight, gain], chunks[0])
    shared = (queries, keys, values, sums, totals, level_weight, local, other, other_rest)
    prefixes = [None, prefix]
    found, across = {}, {}
    mixed, at = None, 0

    def both(name, messages, tokens=()):
        return pack(name, [(state, size) for state in messages], tokens)

    for bit in range(1, bits):
        found[bit] = [trade(chunk, 2**bit) for chunk in (give if bit == 1 else chunks)]
        stays = chunks if bit == 1 else stays
        waits = []
        if bit < 3 or bit == last:
            stop = spans if bit == last else at + 1
            begun = [*chunks[-1:], *([found[bit - 1]] if bit == last else [])]
            mixed, *waits = mix_local(at, stop, shared, mixed, begun, True)
            at = stop
        if bit == 3:
            waits.append(rest)
        if bit < last:
            merged = {}
            order = list(reversed(range(CUTS)))
            for offset in order:
                ending = offset == order[-1]
                tokens_of = [*merged.values(), *(waits if ending else ())]
                merged[offset], *after = merge(
                    bit, offset, ending, chunks[offset], found[bit][offset], prefixes[bit], tokens_of
                )
            chunks = [merged[offset] for offset in range(CUTS)]
            newest = merged[order[-1]]
            prefixes += after
            found[bit] = both(f"found{bit}", found[bit], (newest,))
            if bit > 1:
                across[bit] = trade(found[bit], 2)
            else:
                rest = trade(both("rest", stays, (newest,)), 2)

    state = both("state", found[last], waits)
    beside = trade(state, 2)
    early = list(range(2, last))
    pieces = [(found[1], two), (rest, two)]
    for bit in early:
        pieces += [(found[bit], two), (across[bit], two)]
    near = pack("near", pieces, (state,))
    far = trade(near, 1)
    middle = [1, *early]
    ahead = [prefixes[bit] for bit in middle]

    def states_of(side, index, first):
        return [(first + slot, index, (2 * slot + side) * two) for slot in range(len(middle))]

    shared = (mixed, queries, sums, level_weight, gain)
    every = (first_level, [last, *middle], shared, [prefixes[last], *ahead])
    quarters = {(core, side): [(0, 0, 0), *states_of(side, 1, 1)] for core, side in sides}
    state_far = trade(pack("shared", [(state, two)], (near,)), 1)
    block = finish([((0, 0), quarters[0, 0])], *every, [state, near], None, True, None)
    block_far = finish(
        [((1, 0), quarters[1, 0])], *every, [state_far, far, block], None, True, None
    )
    beside = pack("beside", [(beside, two)], (block_far,))
    out = finish([((0, 1), quarters[0, 1])], *every, [beside, near, block], None, False, 2)
    beside_far = trade(beside, 1)
    return finish(
        [((1, 1), quarters[1, 1])], *every, [beside_far, far, block_far], out, False, 2
    )


def solution(mesh):
    placed = (
        P(("wide", "narrow"), None),
        P(("wide", "narrow"), None),
        P(("wide", "narrow"), None),
        P(None, ("wide", "narrow")),
        P(None, None, ("wide", "narrow")),
        P(),
    )
    return jax.shard_map(
        per_device,
        mesh=mesh,
        in_specs=placed,
        out_specs=P(("wide", "narrow"), None),
        check_vma=False,
    )
```

```python
import functools

import jax
import jax.numpy as jnp
from jax import lax
from jax.experimental import pallas as pl
from jax.experimental.pallas import tpu as pltpu
from jax.sharding import PartitionSpec as P

SPAN = 256
SPLIT_BITS = 2
CUTS = 2
EPS = 1e-05
AXES = ("narrow", "wide")
NT = (((1,), (1,)), ((), ()))
COSTS = {"local0": 1000, "finish00": 20000000000, "finish10": 1000, "finish01": 20000000000, "local2": 1000, "reach": 1000}


def cost(name):
    flops = COSTS.get(name, 2000000000)
    return pl.CostEstimate(flops=flops, transcendentals=0, bytes_accessed=1_000_000)


PARAMS = pltpu.CompilerParams(vmem_limit_bytes=32 * 1024 * 1024)
HELD = pl.BlockSpec(memory_space=pltpu.VMEM)


def place():
    return lax.axis_index("wide") * lax.axis_size("narrow") + lax.axis_index("narrow")


def bit_of(value, bit):
    return jnp.bitwise_and(jnp.right_shift(value, bit), 1)


def spread_lanes(column, width):
    return jnp.broadcast_to(column, (column.shape[0], width))


ANYWHERE = pl.BlockSpec(memory_space=pl.ANY)


def hold(array):
    return pltpu.with_memory_space_constraint(array, pltpu.VMEM)


def call(kernel, name, inputs, outputs, scratch=(), in_specs=None, aliases=None):
    specs = in_specs or [HELD] * len(inputs)
    inputs = [hold(array) if spec is HELD else array for array, spec in zip(inputs, specs)]
    return pl.pallas_call(
        kernel,
        in_specs=specs,
        out_specs=[HELD] * len(outputs),
        out_shape=[pltpu.VMEM(shape, dtype) for shape, dtype in outputs],
        scratch_shapes=list(scratch),
        input_output_aliases=aliases or {},
        compiler_params=PARAMS,
        cost_estimate=cost(name),
        name=name,
    )(*inputs)


def running_sums(rows):
    high = rows.astype(jnp.bfloat16)
    rest = rows - high.astype(jnp.float32)
    middle = rest.astype(jnp.bfloat16)
    low = (rest - middle.astype(jnp.float32)).astype(jnp.bfloat16)
    width = rows.shape[1]
    source = lax.broadcasted_iota(jnp.int32, (width, width), 0)
    target = lax.broadcasted_iota(jnp.int32, (width, width), 1)
    upto = jnp.where(source <= target, 1.0, 0.0).astype(jnp.bfloat16)
    sums = jnp.dot(
        jnp.concatenate([high, middle, low], axis=0), upto, preferred_element_type=jnp.float32
    )
    count = rows.shape[0]
    return sums[:count] + (sums[count : 2 * count] + sums[2 * count :])


def state_kernel(*refs):
    k_hbm, v_hbm, decay_hbm = refs[:3]
    keep_ref, send_ref, local_ref, sums_ref, totals_ref = refs[3:8]
    k_ref, v_ref, decay_ref, held, message_ref, arrived = refs[8:]
    heads, tokens = decay_ref.shape
    head_width = v_ref.shape[1] // heads
    spans = tokens // SPAN
    rows_of = [slice(span * SPAN, (span + 1) * SPAN) for span in range(spans)]
    loads = [(decay_hbm, decay_ref), (k_hbm, k_ref)]
    loads += [(v_hbm.at[rows], v_ref.at[rows]) for rows in rows_of]
    copies = [
        pltpu.make_async_copy(source, target, arrived.at[at])
        for at, (source, target) in enumerate(loads)
    ]
    for copy in copies:
        copy.start()
    copies[0].wait()
    within = running_sums(jnp.concatenate([decay_ref[:, rows] for rows in rows_of], axis=0))
    run = jnp.zeros((heads, 128), jnp.float32)
    fades, wholes = [], []
    for span, rows in enumerate(rows_of):
        here = within[span * heads : (span + 1) * heads]
        last = here[:, SPAN - 1 :]
        total = spread_lanes(last, 128)
        sums_ref[0, :, rows] = here
        sums_ref[1, :, rows] = here + spread_lanes(run[:, :1], SPAN)
        totals_ref[span] = total
        run = run + total
        fades.append(jnp.exp(spread_lanes(last, SPAN) - here))
        wholes.append(jnp.exp(total))
    copies[1].wait()
    across = [k_ref[rows].astype(jnp.float32).T for rows in rows_of]
    local_bits = spans.bit_length() - 1
    for span, rows in enumerate(rows_of):
        copies[2 + span].wait()
        for head in range(heads):
            columns = slice(head * head_width, (head + 1) * head_width)
            faded = (across[span] * fades[span][head : head + 1]).astype(jnp.bfloat16)
            state = jnp.dot(faded, v_ref[rows, columns], preferred_element_type=jnp.float32)
            at = 0
            for bit in range(local_bits + 1):
                if span >> bit & 1 == 0 or bit == local_bits:
                    group = state
                    if span % 2**bit > 0:
                        group = held[bit - 1, head] * wholes[span][head : head + 1] + state
                    if (span + 1) % 2**bit > 0:
                        held[bit - 1, head] = group
                    elif bit < local_bits:
                        local_ref[at + (span >> (bit + 1)), :, columns] = group.astype(
                            jnp.bfloat16
                        )
                    else:
                        message_ref[columns] = group.T
                at += spans >> (bit + 1)
    half = message_ref.shape[0] // 2
    core = bit_of(place(), 0)
    keep_ref[:half] = message_ref[pl.ds(pl.multiple_of(core * half, 8), half)]
    send_ref[:half] = message_ref[pl.ds(pl.multiple_of((1 - core) * half, 8), half)]
    keep_ref[half:] = run
    send_ref[half:] = run


def make_states(keys, values, log_decay):
    tokens, key_width = keys.shape
    heads = log_decay.shape[0]
    width = values.shape[1]
    spans = tokens // SPAN
    inputs = [keys, values, log_decay]
    kept = [keys, values]
    return call(
        state_kernel,
        "states",
        [pltpu.with_memory_space_constraint(array, pltpu.HBM) for array in inputs],
        [
            ((width // 2 + heads, key_width), jnp.float32),
            ((width // 2 + heads, key_width), jnp.float32),
            ((spans - 1, key_width, width), jnp.bfloat16),
            ((2, heads, tokens), jnp.float32),
            ((spans, heads, 128), jnp.float32),
            *[(array.shape, array.dtype) for array in kept],
        ],
        [
            pltpu.VMEM(log_decay.shape, jnp.float32),
            pltpu.VMEM((spans.bit_length() - 1, heads, key_width, width // heads), jnp.float32),
            pltpu.VMEM((width, key_width), jnp.float32),
            pltpu.SemaphoreType.DMA((spans + 2,)),
        ],
        [pl.BlockSpec(memory_space=pltpu.HBM)] * len(inputs),
    )


def load_kernel(count, *refs):
    copies = [
        pltpu.make_async_copy(source, target, refs[-1].at[at])
        for at, (source, target) in enumerate(zip(refs[:count], refs[-1 - count : -1]))
    ]
    for copy in copies:
        copy.start()
    for copy in copies:
        copy.wait()


def load(arrays, token):
    count = len(arrays)
    hbm = pl.BlockSpec(memory_space=pltpu.HBM)
    return call(
        functools.partial(load_kernel, count),
        "load",
        [*[pltpu.with_memory_space_constraint(array, pltpu.HBM) for array in arrays], token],
        [(array.shape, array.dtype) for array in arrays],
        [pltpu.SemaphoreType.DMA((count,))],
        [*[hbm] * count, HELD],
    )


def local_kernel(first, last, has_token, *refs):
    q_ref, k_ref, v_ref, sums_ref, totals_ref, weight_ref, local_ref, near_ref, rest_ref = refs[:9]
    if has_token:
        mixed_ref, done_ref = refs[-2:]
        done_ref[...] = jnp.zeros_like(done_ref)
    else:
        mixed_ref = refs[-1]
    heads = weight_ref.shape[1]
    head_width = v_ref.shape[1] // heads
    spans = totals_ref.shape[0]
    local_bits = spans.bit_length() - 1
    half = SPAN // 2
    source = lax.broadcasted_iota(jnp.int32, (half, half), 0)
    target = lax.broadcasted_iota(jnp.int32, (half, half), 1)
    causal = source <= target
    empty = jnp.zeros((half, half), jnp.bfloat16)
    upper = jnp.where(bit_of(place(), 0) == 1, 1.0, 0.0)
    size = heads // 2 * head_width
    near, rest = near_ref[:size], rest_ref[:size]
    first_core = bit_of(place(), 0) == 0
    near = jnp.concatenate(
        [jnp.where(first_core, near, rest), jnp.where(first_core, rest, near)], axis=0
    ).astype(jnp.bfloat16)

    for span in range(first, last):
        tokens = slice(span * SPAN, (span + 1) * SPAN)
        queries = q_ref[tokens]
        scores = lax.dot_general(
            k_ref[tokens], queries, NT, preferred_element_type=jnp.float32
        )
        within = sums_ref[0, :, tokens]
        within_down = within.T
        weight = weight_ref[0, :, tokens]
        values_across = v_ref[tokens].T

        def mix(head, low, high):
            rows = slice(low * half, (low + 1) * half)
            columns = slice(high * half, (high + 1) * half)
            gap = within[head : head + 1, columns] - within_down[rows, head : head + 1]
            if low == high:
                gap = jnp.where(causal, gap, -1e30)
            mixing = scores[rows, columns] * jnp.exp(gap) * weight[head : head + 1, columns]
            return mixing.astype(jnp.bfloat16)

        levels = []
        offset = 0
        for bit in range(local_bits):
            if span >> bit & 1:
                since = within
                for back in range(1, span % 2**bit + 1):
                    since = since + spread_lanes(totals_ref[span - back][:, :1], SPAN)
                scale = jnp.exp(since) * weight_ref[1 + bit, :, tokens]
                levels.append((local_ref[offset + (span >> (bit + 1))].T, scale))
            offset += spans >> (bit + 1)
        reach = jnp.exp(sums_ref[1, :, tokens]) * weight_ref[1 + local_bits, :, tokens] * upper
        levels.append((near, reach))
        for head in range(heads):
            rows = slice(head * head_width, (head + 1) * head_width)
            mixing = jnp.concatenate(
                [
                    jnp.concatenate([mix(head, 0, 0), mix(head, 0, 1)], axis=1),
                    jnp.concatenate([empty, mix(head, 1, 1)], axis=1),
                ],
                axis=0,
            )
            mixed = jnp.dot(values_across[rows], mixing, preferred_element_type=jnp.float32)
            for level, scale in levels:
                found = lax.dot_general(
                    level[rows], queries, NT, preferred_element_type=jnp.float32
                )
                mixed = mixed + found * scale[head : head + 1]
            mixed_ref[rows, tokens] = mixed


def mix_local(first, last, shared, mixed, tokens, has_token):
    values = shared[2]
    rest = [] if mixed is None else [mixed]
    return call(
        functools.partial(local_kernel, first, last, has_token),
        f"local{first}",
        [*shared, *rest, *tokens],
        [(values.shape[::-1], jnp.float32), ((8, 128), jnp.float32)][: 1 + has_token],
        aliases={9: 0} if rest else None,
    )


def join(upper, mine, mine_total, other, other_total):
    fade = jnp.exp(jnp.where(upper, mine_total, other_total))
    return jnp.where(upper, other * fade + mine, mine * fade + other)


def first_head(far, heads):
    here = place()
    first = 0
    for bit, flip in enumerate(far):
        first = first + jnp.bitwise_xor(bit_of(here, bit), flip) * (heads >> (bit + 1))
    return first


def chip_kernel(mine_ref, other_ref, *refs):
    *message_refs, next_ref, whole_ref = refs
    heads = next_ref.shape[0]
    width = whole_ref.shape[0]
    held = heads // 2
    per = width // held
    here = place()
    upper = bit_of(here, 0) == 1
    first = first_head((0,), heads)
    for slot in range(held):
        part = slice(slot * per, (slot + 1) * per)
        total = pl.ds(width + first + slot, 1)
        whole_ref[part] = join(
            upper, mine_ref[part], mine_ref[total], other_ref[part], other_ref[total]
        )
    other_total = other_ref[width:]
    total = mine_ref[width:] + other_total
    next_ref[...] = jnp.where(upper, other_total, 0.0)
    half = width // 2
    side = bit_of(here, 1)
    cuts = len(message_refs) // 2
    size = half // cuts
    for at, ref in enumerate(message_refs):
        start = (side if at < cuts else 1 - side) * half + at % cuts * size
        ref[:size] = whole_ref[pl.ds(pl.multiple_of(start, 8), size)]
        ref[size:] = total


def make_chip(mine, other, heads, cuts):
    rows, lanes = mine.shape
    half = rows - heads
    *messages, prefix = call(
        chip_kernel,
        "chip",
        [mine, other],
        [
            *[((half // 2 // cuts + heads, lanes), jnp.float32)] * (2 * cuts),
            ((heads, lanes), jnp.float32),
        ],
        [pltpu.VMEM((half, lanes), jnp.float32)],
    )
    return messages[:cuts], messages[cuts:], prefix


def merge_kernel(bit, offset, has_prefix, *refs):
    mine_ref, other_ref, prefix_ref = refs[:3]
    merged_ref = refs[-2] if has_prefix else refs[-1]
    heads = prefix_ref.shape[0]
    rows = mine_ref.shape[0] - heads
    per = mine_ref.shape[1]
    upper = bit_of(place(), bit) == 1
    first = first_head((0,) * SPLIT_BITS, heads) + offset
    for slot in range(rows // per):
        part = slice(slot * per, (slot + 1) * per)
        total = pl.ds(rows + first + slot, 1)
        merged_ref[part] = join(
            upper, mine_ref[part], mine_ref[total], other_ref[part], other_ref[total]
        )
    other_total = other_ref[rows:]
    merged_ref[rows:] = mine_ref[rows:] + other_total
    if has_prefix:
        refs[-1][...] = prefix_ref[...] + jnp.where(upper, other_total, 0.0)


def merge(bit, offset, has_prefix, mine, other, prefix, tokens=()):
    return call(
        functools.partial(merge_kernel, bit, offset, has_prefix),
        f"merge{bit}{offset}",
        [mine, other, prefix, *tokens],
        [(mine.shape, jnp.float32), (prefix.shape, jnp.float32)][: 1 + has_prefix],
    )


def pack_kernel(takes, *refs):
    out_ref = refs[-1]
    at = 0
    for ref, rows in zip(refs, takes):
        out_ref[at : at + rows] = ref[:rows]
        at += rows


def pack(name, pieces, tokens=()):
    takes = [rows for _, rows in pieces]
    lanes = pieces[0][0].shape[1]
    return call(
        functools.partial(pack_kernel, takes),
        name,
        [*[array for array, _ in pieces], *tokens],
        [((sum(takes), lanes), jnp.float32)],
    )[0]


def level_scale(bit, first_level, prefix_ref, sums_ref, weight_ref, tokens):
    active = jnp.where(bit_of(place(), bit) == 1, 1.0, 0.0)
    reach = jnp.exp(sums_ref[1, :, tokens] + spread_lanes(prefix_ref[:, :1], SPAN))
    return reach * weight_ref[first_level + bit, :, tokens] * active


def gather_work(quarters, part_refs, heads, per):
    work = []
    for far, pieces in quarters:
        first = first_head(far, heads)
        for slot in range(heads // 4):
            states = []
            for level, index, start in pieces:
                if start is None:
                    rows = pl.ds(pl.multiple_of((first + slot) * per, 128), per)
                else:
                    rows = slice(start + slot * per, start + (slot + 1) * per)
                states.append((level, part_refs[index][rows].astype(jnp.bfloat16)))
            work.append((first + slot, states))
    return work


def add_found(mixed, queries, head, states, scale_ref):
    for level, state in states:
        found = lax.dot_general(state, queries, NT, preferred_element_type=jnp.float32)
        mixed = mixed + found * scale_ref[level, pl.ds(head, 1)]
    return mixed


def finish_kernel(quarters, first_level, bits, stays, carried, *refs):
    mixed_ref, q_ref, sums_ref, weight_ref, gain_ref = refs[:5]
    prefix_refs = refs[5 : 5 + len(bits)]
    part_refs = refs[5 + len(bits) :]
    out_refs, (own_ref, scale_ref, sent) = refs[-3 - FINISH_OUTS[stays, carried] : -3], refs[-3:]
    if stays:
        own_ref = out_refs[-1]
    heads = weight_ref.shape[1]
    head_width = mixed_ref.shape[0] // heads
    size = heads // 4 * head_width
    copies = []

    def send(block, far, rows):
        columns = pl.ds(pl.multiple_of(first_head(far, heads) * head_width, 128), size)
        copy = pltpu.make_async_copy(
            block.at[rows], out_refs[0].at[rows, columns], sent.at[len(copies)]
        )
        copy.start()
        copies.append(copy)

    if carried is not None:
        index, far = carried
        for start in range(0, q_ref.shape[0], SPAN):
            send(part_refs[index], far, slice(start, start + SPAN))
    work = gather_work(quarters, part_refs, heads, head_width)
    gains = []
    for head, _ in work:
        row = jnp.broadcast_to(gain_ref[pl.ds(head, 1)], (8, head_width))
        gains.append(row.T[:, :1])
    for span in range(q_ref.shape[0] // SPAN):
        tokens = slice(span * SPAN, (span + 1) * SPAN)
        queries = q_ref[tokens]
        for level, (bit, prefix_ref) in enumerate(zip(bits, prefix_refs)):
            scale_ref[level] = level_scale(
                bit, first_level, prefix_ref, sums_ref, weight_ref, tokens
            )
        for at, (head, states) in enumerate(work):
            rows = pl.ds(pl.multiple_of(head * head_width, 128), head_width)
            mixed = add_found(mixed_ref[rows, tokens], queries, head, states, scale_ref)
            square = jnp.mean(mixed * mixed, axis=0, keepdims=True)
            normed = mixed * lax.rsqrt(square + EPS) * gains[at]
            columns = slice(at * head_width, (at + 1) * head_width)
            own_ref[tokens, columns] = normed.astype(jnp.bfloat16).T
        if not stays:
            for start in range(tokens.start, tokens.stop, SPAN // 2):
                send(own_ref, quarters[0][0], slice(start, start + SPAN // 2))
    for copy in copies:
        copy.wait()


FINISH_OUTS = {}


def finish(quarters, first_level, bits, shared, prefixes, parts, begun, stays, carried):
    mixed, queries, sums, level_weight, gain = shared
    width, tokens = mixed.shape
    heads = level_weight.shape[1]
    inputs = [*shared, *prefixes, *parts]
    specs = [HELD] * len(inputs)
    inputs = [hold(array) for array in inputs]
    hbm = pl.BlockSpec(memory_space=pltpu.HBM)
    aliases = {}
    if begun is not None:
        aliases = {len(inputs): 0}
        specs.append(hbm)
        inputs.append(begun)
    name = "finish" + "".join(f"{core}{side}" for (core, side), _ in quarters)
    block = (tokens, width // 4)
    out_specs, shapes = [], []
    if carried is not None or not stays:
        out_specs.append(hbm)
        shapes.append(jax.ShapeDtypeStruct((tokens, width), jnp.bfloat16))
    if stays:
        out_specs.append(HELD)
        shapes.append(pltpu.VMEM(block, jnp.bfloat16))
    FINISH_OUTS[stays, carried] = len(shapes)
    return pl.pallas_call(
        functools.partial(finish_kernel, quarters, first_level, bits, stays, carried),
        in_specs=specs,
        out_specs=out_specs,
        out_shape=shapes,
        scratch_shapes=[
            pltpu.VMEM((8, 128) if stays else block, jnp.bfloat16),
            pltpu.VMEM((len(bits), heads, SPAN), jnp.float32),
            pltpu.SemaphoreType.DMA((3 * tokens // SPAN,)),
        ],
        input_output_aliases=aliases,
        compiler_params=PARAMS,
        cost_estimate=cost(name),
        name=name,
    )(*inputs)


def trade(value, mask):
    wide, narrow = lax.axis_size("wide"), lax.axis_size("narrow")

    def ranked(index):
        return index % narrow * wide + index // narrow

    pairs = [(ranked(source), ranked(source ^ mask)) for source in range(wide * narrow)]
    return lax.ppermute(value, AXES, pairs)


def per_device(queries, keys, values, log_decay, level_weight, norm_gain):
    heads = log_decay.shape[0]
    tokens, width = values.shape
    per = width // heads
    spans = tokens // SPAN
    group_bits = heads.bit_length() - 1
    bits = (lax.axis_size("wide") * lax.axis_size("narrow")).bit_length() - 1
    first_level = level_weight.shape[0] - bits
    gain = norm_gain.reshape(heads, per)
    keep, send, local, sums, totals, keys, values = make_states(keys, values, log_decay)
    last = bits - 1
    two = 2 * per
    size = two // CUTS
    sides = [(core, side) for core in (0, 1) for side in (0, 1)]
    other, other_rest = trade(send, 1), trade(keep, 1)
    chunks, give, prefix = make_chip(keep, other, heads, CUTS)
    queries, level_weight, gain = load([queries, level_weight, gain], chunks[0])
    shared = (queries, keys, values, sums, totals, level_weight, local, other, other_rest)
    prefixes = [None, prefix]
    found, across = {}, {}
    mixed, at = None, 0

    def both(name, messages, tokens=()):
        return pack(name, [(state, size) for state in messages], tokens)

    for bit in range(1, bits):
        found[bit] = [trade(chunk, 2**bit) for chunk in (give if bit == 1 else chunks)]
        stays = chunks if bit == 1 else stays
        waits = []
        if bit < 3 or bit == last:
            stop = spans if bit == last else at + 1
            begun = [*chunks[-1:], *([found[bit - 1]] if bit == last else [])]
            mixed, *waits = mix_local(at, stop, shared, mixed, begun, True)
            at = stop
        if bit == 3:
            waits.append(rest)
        if bit < last:
            merged = {}
            order = list(reversed(range(CUTS)))
            for offset in order:
                ending = offset == order[-1]
                tokens_of = [*merged.values(), *(waits if ending else ())]
                merged[offset], *after = merge(
                    bit, offset, ending, chunks[offset], found[bit][offset], prefixes[bit], tokens_of
                )
            chunks = [merged[offset] for offset in range(CUTS)]
            newest = merged[order[-1]]
            prefixes += after
            found[bit] = both(f"found{bit}", found[bit], (newest,))
            if bit > 1:
                across[bit] = trade(found[bit], 2)
            else:
                rest = trade(both("rest", stays, (newest,)), 2)

    state = both("state", found[last], waits)
    beside = trade(state, 2)
    early = list(range(1, last))
    ours = pack("ours", [(found[bit], two) for bit in early], ())
    theirs = pack("theirs", [(rest if bit == 1 else across[bit], two) for bit in early], (state,))
    joined = pack("joined", [(ours, len(early) * two), (state, two)])
    joined_far = trade(joined, 1)
    theirs_far = trade(theirs, 1)
    ahead = [prefixes[bit] for bit in early]
    shared = (mixed, queries, sums, level_weight, gain)
    every = (first_level, [*early, last], shared, [*ahead, prefixes[last]])
    levels = [(slot, 0, slot * two) for slot in range(len(early))]
    whole = [*levels, (len(early), 0, len(early) * two)]
    parted = [*levels, (len(early), 1, 0)]
    (block,) = finish([((0, 0), whole)], *every, [joined], None, True, None)
    (block_far,) = finish([((1, 0), whole)], *every, [joined_far, block], None, True, None)
    beside = pack("beside", [(beside, two)], (block_far,))
    (out,) = finish(
        [((0, 1), parted)], *every, [theirs, beside, block], None, False, (2, (0, 0))
    )
    beside_far = trade(beside, 1)
    return finish(
        [((1, 1), parted)], *every, [theirs_far, beside_far, block_far], out, False, (2, (1, 0))
    )[0]


def solution(mesh):
    placed = (
        P(("wide", "narrow"), None),
        P(("wide", "narrow"), None),
        P(("wide", "narrow"), None),
        P(None, ("wide", "narrow")),
        P(None, None, ("wide", "narrow")),
        P(),
    )
    return jax.shard_map(
        per_device,
        mesh=mesh,
        in_specs=placed,
        out_specs=P(("wide", "narrow"), None),
        check_vma=False,
    )
```

```python
import functools

import jax
import jax.numpy as jnp
from jax import lax
from jax.experimental import pallas as pl
from jax.experimental.pallas import tpu as pltpu
from jax.sharding import PartitionSpec as P

SPAN = 256
SPLIT_BITS = 2
CUTS = 2
EPS = 1e-05
AXES = ("narrow", "wide")
NT = (((1,), (1,)), ((), ()))
COSTS = {"local0": 1000, "finish00": 20000000000, "finish10": 1000, "finish01": 20000000000, "local2": 1000, "reach": 1000}


def cost(name):
    flops = COSTS.get(name, 2000000000)
    return pl.CostEstimate(flops=flops, transcendentals=0, bytes_accessed=1_000_000)


PARAMS = pltpu.CompilerParams(vmem_limit_bytes=32 * 1024 * 1024)
HELD = pl.BlockSpec(memory_space=pltpu.VMEM)


def place():
    return lax.axis_index("wide") * lax.axis_size("narrow") + lax.axis_index("narrow")


def bit_of(value, bit):
    return jnp.bitwise_and(jnp.right_shift(value, bit), 1)


def spread_lanes(column, width):
    return jnp.broadcast_to(column, (column.shape[0], width))


ANYWHERE = pl.BlockSpec(memory_space=pl.ANY)


def hold(array):
    return pltpu.with_memory_space_constraint(array, pltpu.VMEM)


def call(kernel, name, inputs, outputs, scratch=(), in_specs=None, aliases=None):
    specs = in_specs or [HELD] * len(inputs)
    inputs = [hold(array) if spec is HELD else array for array, spec in zip(inputs, specs)]
    return pl.pallas_call(
        kernel,
        in_specs=specs,
        out_specs=[HELD] * len(outputs),
        out_shape=[pltpu.VMEM(shape, dtype) for shape, dtype in outputs],
        scratch_shapes=list(scratch),
        input_output_aliases=aliases or {},
        compiler_params=PARAMS,
        cost_estimate=cost(name),
        name=name,
    )(*inputs)


def running_sums(rows):
    high = rows.astype(jnp.bfloat16)
    rest = rows - high.astype(jnp.float32)
    middle = rest.astype(jnp.bfloat16)
    low = (rest - middle.astype(jnp.float32)).astype(jnp.bfloat16)
    width = rows.shape[1]
    source = lax.broadcasted_iota(jnp.int32, (width, width), 0)
    target = lax.broadcasted_iota(jnp.int32, (width, width), 1)
    upto = jnp.where(source <= target, 1.0, 0.0).astype(jnp.bfloat16)
    sums = jnp.dot(
        jnp.concatenate([high, middle, low], axis=0), upto, preferred_element_type=jnp.float32
    )
    count = rows.shape[0]
    return sums[:count] + (sums[count : 2 * count] + sums[2 * count :])


def state_kernel(*refs):
    k_hbm, v_hbm, decay_hbm = refs[:3]
    keep_ref, send_ref, local_ref, sums_ref, totals_ref = refs[3:8]
    k_ref, v_ref, decay_ref, held, message_ref, arrived = refs[8:]
    heads, tokens = decay_ref.shape
    head_width = v_ref.shape[1] // heads
    spans = tokens // SPAN
    rows_of = [slice(span * SPAN, (span + 1) * SPAN) for span in range(spans)]
    loads = [(decay_hbm, decay_ref), (k_hbm, k_ref)]
    loads += [(v_hbm.at[rows], v_ref.at[rows]) for rows in rows_of]
    copies = [
        pltpu.make_async_copy(source, target, arrived.at[at])
        for at, (source, target) in enumerate(loads)
    ]
    for copy in copies:
        copy.start()
    copies[0].wait()
    within = running_sums(jnp.concatenate([decay_ref[:, rows] for rows in rows_of], axis=0))
    run = jnp.zeros((heads, 128), jnp.float32)
    fades, wholes = [], []
    for span, rows in enumerate(rows_of):
        here = within[span * heads : (span + 1) * heads]
        last = here[:, SPAN - 1 :]
        total = spread_lanes(last, 128)
        sums_ref[0, :, rows] = here
        sums_ref[1, :, rows] = here + spread_lanes(run[:, :1], SPAN)
        totals_ref[span] = total
        run = run + total
        fades.append(jnp.exp(spread_lanes(last, SPAN) - here))
        wholes.append(jnp.exp(total))
    copies[1].wait()
    across = [k_ref[rows].astype(jnp.float32).T for rows in rows_of]
    local_bits = spans.bit_length() - 1
    for span, rows in enumerate(rows_of):
        copies[2 + span].wait()
        for head in range(heads):
            columns = slice(head * head_width, (head + 1) * head_width)
            faded = (across[span] * fades[span][head : head + 1]).astype(jnp.bfloat16)
            state = jnp.dot(faded, v_ref[rows, columns], preferred_element_type=jnp.float32)
            at = 0
            for bit in range(local_bits + 1):
                if span >> bit & 1 == 0 or bit == local_bits:
                    group = state
                    if span % 2**bit > 0:
                        group = held[bit - 1, head] * wholes[span][head : head + 1] + state
                    if (span + 1) % 2**bit > 0:
                        held[bit - 1, head] = group
                    elif bit < local_bits:
                        local_ref[at + (span >> (bit + 1)), :, columns] = group.astype(
                            jnp.bfloat16
                        )
                    else:
                        message_ref[columns] = group.T
                at += spans >> (bit + 1)
    half = message_ref.shape[0] // 2
    core = bit_of(place(), 0)
    keep_ref[:half] = message_ref[pl.ds(pl.multiple_of(core * half, 8), half)]
    send_ref[:half] = message_ref[pl.ds(pl.multiple_of((1 - core) * half, 8), half)]
    keep_ref[half:] = run
    send_ref[half:] = run


def make_states(keys, values, log_decay):
    tokens, key_width = keys.shape
    heads = log_decay.shape[0]
    width = values.shape[1]
    spans = tokens // SPAN
    inputs = [keys, values, log_decay]
    kept = [keys, values]
    return call(
        state_kernel,
        "states",
        [pltpu.with_memory_space_constraint(array, pltpu.HBM) for array in inputs],
        [
            ((width // 2 + heads, key_width), jnp.float32),
            ((width // 2 + heads, key_width), jnp.float32),
            ((spans - 1, key_width, width), jnp.bfloat16),
            ((2, heads, tokens), jnp.float32),
            ((spans, heads, 128), jnp.float32),
            *[(array.shape, array.dtype) for array in kept],
        ],
        [
            pltpu.VMEM(log_decay.shape, jnp.float32),
            pltpu.VMEM((spans.bit_length() - 1, heads, key_width, width // heads), jnp.float32),
            pltpu.VMEM((width, key_width), jnp.float32),
            pltpu.SemaphoreType.DMA((spans + 2,)),
        ],
        [pl.BlockSpec(memory_space=pltpu.HBM)] * len(inputs),
    )


def load_kernel(count, *refs):
    copies = [
        pltpu.make_async_copy(source, target, refs[-1].at[at])
        for at, (source, target) in enumerate(zip(refs[:count], refs[-1 - count : -1]))
    ]
    for copy in copies:
        copy.start()
    for copy in copies:
        copy.wait()


def load(arrays, token):
    count = len(arrays)
    hbm = pl.BlockSpec(memory_space=pltpu.HBM)
    return call(
        functools.partial(load_kernel, count),
        "load",
        [*[pltpu.with_memory_space_constraint(array, pltpu.HBM) for array in arrays], token],
        [(array.shape, array.dtype) for array in arrays],
        [pltpu.SemaphoreType.DMA((count,))],
        [*[hbm] * count, HELD],
    )


def local_kernel(first, last, has_token, *refs):
    q_ref, k_ref, v_ref, sums_ref, totals_ref, weight_ref, local_ref, near_ref, rest_ref = refs[:9]
    if has_token:
        mixed_ref, done_ref = refs[-2:]
        done_ref[...] = jnp.zeros_like(done_ref)
    else:
        mixed_ref = refs[-1]
    heads = weight_ref.shape[1]
    head_width = v_ref.shape[1] // heads
    spans = totals_ref.shape[0]
    local_bits = spans.bit_length() - 1
    half = SPAN // 2
    source = lax.broadcasted_iota(jnp.int32, (half, half), 0)
    target = lax.broadcasted_iota(jnp.int32, (half, half), 1)
    causal = source <= target
    empty = jnp.zeros((half, half), jnp.bfloat16)
    upper = jnp.where(bit_of(place(), 0) == 1, 1.0, 0.0)
    size = heads // 2 * head_width
    near, rest = near_ref[:size], rest_ref[:size]
    first_core = bit_of(place(), 0) == 0
    near = jnp.concatenate(
        [jnp.where(first_core, near, rest), jnp.where(first_core, rest, near)], axis=0
    ).astype(jnp.bfloat16)

    for span in range(first, last):
        tokens = slice(span * SPAN, (span + 1) * SPAN)
        queries = q_ref[tokens]
        scores = lax.dot_general(
            k_ref[tokens], queries, NT, preferred_element_type=jnp.float32
        )
        within = sums_ref[0, :, tokens]
        within_down = within.T
        weight = weight_ref[0, :, tokens]
        values_across = v_ref[tokens].T

        def mix(head, low, high):
            rows = slice(low * half, (low + 1) * half)
            columns = slice(high * half, (high + 1) * half)
            gap = within[head : head + 1, columns] - within_down[rows, head : head + 1]
            if low == high:
                gap = jnp.where(causal, gap, -1e30)
            mixing = scores[rows, columns] * jnp.exp(gap) * weight[head : head + 1, columns]
            return mixing.astype(jnp.bfloat16)

        levels = []
        offset = 0
        for bit in range(local_bits):
            if span >> bit & 1:
                since = within
                for back in range(1, span % 2**bit + 1):
                    since = since + spread_lanes(totals_ref[span - back][:, :1], SPAN)
                scale = jnp.exp(since) * weight_ref[1 + bit, :, tokens]
                levels.append((local_ref[offset + (span >> (bit + 1))].T, scale))
            offset += spans >> (bit + 1)
        reach = jnp.exp(sums_ref[1, :, tokens]) * weight_ref[1 + local_bits, :, tokens] * upper
        levels.append((near, reach))
        for head in range(heads):
            rows = slice(head * head_width, (head + 1) * head_width)
            mixing = jnp.concatenate(
                [
                    jnp.concatenate([mix(head, 0, 0), mix(head, 0, 1)], axis=1),
                    jnp.concatenate([empty, mix(head, 1, 1)], axis=1),
                ],
                axis=0,
            )
            mixed = jnp.dot(values_across[rows], mixing, preferred_element_type=jnp.float32)
            for level, scale in levels:
                found = lax.dot_general(
                    level[rows], queries, NT, preferred_element_type=jnp.float32
                )
                mixed = mixed + found * scale[head : head + 1]
            mixed_ref[rows, tokens] = mixed


def mix_local(first, last, shared, mixed, tokens, has_token):
    values = shared[2]
    rest = [] if mixed is None else [mixed]
    return call(
        functools.partial(local_kernel, first, last, has_token),
        f"local{first}",
        [*shared, *rest, *tokens],
        [(values.shape[::-1], jnp.float32), ((8, 128), jnp.float32)][: 1 + has_token],
        aliases={9: 0} if rest else None,
    )


def join(upper, mine, mine_total, other, other_total):
    fade = jnp.exp(jnp.where(upper, mine_total, other_total))
    return jnp.where(upper, other * fade + mine, mine * fade + other)


def first_head(far, heads):
    here = place()
    first = 0
    for bit, flip in enumerate(far):
        first = first + jnp.bitwise_xor(bit_of(here, bit), flip) * (heads >> (bit + 1))
    return first


def chip_kernel(mine_ref, other_ref, *refs):
    *message_refs, next_ref, whole_ref = refs
    heads = next_ref.shape[0]
    width = whole_ref.shape[0]
    held = heads // 2
    per = width // held
    here = place()
    upper = bit_of(here, 0) == 1
    first = first_head((0,), heads)
    for slot in range(held):
        part = slice(slot * per, (slot + 1) * per)
        total = pl.ds(width + first + slot, 1)
        whole_ref[part] = join(
            upper, mine_ref[part], mine_ref[total], other_ref[part], other_ref[total]
        )
    other_total = other_ref[width:]
    total = mine_ref[width:] + other_total
    next_ref[...] = jnp.where(upper, other_total, 0.0)
    half = width // 2
    side = bit_of(here, 1)
    cuts = len(message_refs) // 2
    size = half // cuts
    for at, ref in enumerate(message_refs):
        start = (side if at < cuts else 1 - side) * half + at % cuts * size
        ref[:size] = whole_ref[pl.ds(pl.multiple_of(start, 8), size)]
        ref[size:] = total


def make_chip(mine, other, heads, cuts):
    rows, lanes = mine.shape
    half = rows - heads
    *messages, prefix = call(
        chip_kernel,
        "chip",
        [mine, other],
        [
            *[((half // 2 // cuts + heads, lanes), jnp.float32)] * (2 * cuts),
            ((heads, lanes), jnp.float32),
        ],
        [pltpu.VMEM((half, lanes), jnp.float32)],
    )
    return messages[:cuts], messages[cuts:], prefix


def merge_kernel(bit, offset, has_prefix, *refs):
    mine_ref, other_ref, prefix_ref = refs[:3]
    merged_ref = refs[-2] if has_prefix else refs[-1]
    heads = prefix_ref.shape[0]
    rows = mine_ref.shape[0] - heads
    per = mine_ref.shape[1]
    upper = bit_of(place(), bit) == 1
    first = first_head((0,) * SPLIT_BITS, heads) + offset
    for slot in range(rows // per):
        part = slice(slot * per, (slot + 1) * per)
        total = pl.ds(rows + first + slot, 1)
        merged_ref[part] = join(
            upper, mine_ref[part], mine_ref[total], other_ref[part], other_ref[total]
        )
    other_total = other_ref[rows:]
    merged_ref[rows:] = mine_ref[rows:] + other_total
    if has_prefix:
        refs[-1][...] = prefix_ref[...] + jnp.where(upper, other_total, 0.0)


def merge(bit, offset, has_prefix, mine, other, prefix, tokens=()):
    return call(
        functools.partial(merge_kernel, bit, offset, has_prefix),
        f"merge{bit}{offset}",
        [mine, other, prefix, *tokens],
        [(mine.shape, jnp.float32), (prefix.shape, jnp.float32)][: 1 + has_prefix],
    )


def pack_kernel(takes, *refs):
    out_ref = refs[-1]
    at = 0
    for ref, rows in zip(refs, takes):
        out_ref[at : at + rows] = ref[:rows]
        at += rows


def pack(name, pieces, tokens=()):
    takes = [rows for _, rows in pieces]
    lanes = pieces[0][0].shape[1]
    return call(
        functools.partial(pack_kernel, takes),
        name,
        [*[array for array, _ in pieces], *tokens],
        [((sum(takes), lanes), jnp.float32)],
    )[0]


def level_scale(bit, first_level, prefix_ref, sums_ref, weight_ref, tokens):
    active = jnp.where(bit_of(place(), bit) == 1, 1.0, 0.0)
    reach = jnp.exp(sums_ref[1, :, tokens] + spread_lanes(prefix_ref[:, :1], SPAN))
    return reach * weight_ref[first_level + bit, :, tokens] * active


def gather_work(quarters, part_refs, heads, per):
    work = []
    for far, pieces in quarters:
        first = first_head(far, heads)
        for slot in range(heads // 4):
            states = []
            for level, index, start in pieces:
                if start is None:
                    rows = pl.ds(pl.multiple_of((first + slot) * per, 128), per)
                else:
                    rows = slice(start + slot * per, start + (slot + 1) * per)
                states.append((level, part_refs[index][rows].astype(jnp.bfloat16)))
            work.append((first + slot, states))
    return work


def add_found(mixed, queries, head, states, scale_ref):
    for level, state in states:
        found = lax.dot_general(state, queries, NT, preferred_element_type=jnp.float32)
        mixed = mixed + found * scale_ref[level, pl.ds(head, 1)]
    return mixed


def finish_kernel(quarters, first_level, bits, stays, carried, *refs):
    mixed_ref, q_ref, sums_ref, weight_ref, gain_ref = refs[:5]
    prefix_refs = refs[5 : 5 + len(bits)]
    part_refs = refs[5 + len(bits) :]
    out_refs, (own_ref, scale_ref, sent) = refs[-3 - FINISH_OUTS[stays, carried] : -3], refs[-3:]
    if stays:
        own_ref = out_refs[-1]
    heads = weight_ref.shape[1]
    head_width = mixed_ref.shape[0] // heads
    size = heads // 4 * head_width
    copies = []

    def send(block, far, rows):
        columns = pl.ds(pl.multiple_of(first_head(far, heads) * head_width, 128), size)
        copy = pltpu.make_async_copy(
            block.at[rows], out_refs[0].at[rows, columns], sent.at[len(copies)]
        )
        copy.start()
        copies.append(copy)

    if carried is not None:
        index, far = carried
        for start in range(0, q_ref.shape[0], SPAN):
            send(part_refs[index], far, slice(start, start + SPAN))
    work = gather_work(quarters, part_refs, heads, head_width)
    gains = []
    for head, _ in work:
        row = jnp.broadcast_to(gain_ref[pl.ds(head, 1)], (8, head_width))
        gains.append(row.T[:, :1])
    for span in range(q_ref.shape[0] // SPAN):
        tokens = slice(span * SPAN, (span + 1) * SPAN)
        queries = q_ref[tokens]
        for level, (bit, prefix_ref) in enumerate(zip(bits, prefix_refs)):
            scale_ref[level] = level_scale(
                bit, first_level, prefix_ref, sums_ref, weight_ref, tokens
            )
        for at, (head, states) in enumerate(work):
            rows = pl.ds(pl.multiple_of(head * head_width, 128), head_width)
            mixed = add_found(mixed_ref[rows, tokens], queries, head, states, scale_ref)
            square = jnp.mean(mixed * mixed, axis=0, keepdims=True)
            normed = mixed * lax.rsqrt(square + EPS) * gains[at]
            columns = slice(at * head_width, (at + 1) * head_width)
            own_ref[tokens, columns] = normed.astype(jnp.bfloat16).T
        if not stays:
            for start in range(tokens.start, tokens.stop, SPAN // 2):
                send(own_ref, quarters[0][0], slice(start, start + SPAN // 2))
    for copy in copies:
        copy.wait()


FINISH_OUTS = {}


def finish(quarters, first_level, bits, shared, prefixes, parts, begun, stays, carried):
    mixed, queries, sums, level_weight, gain = shared
    width, tokens = mixed.shape
    heads = level_weight.shape[1]
    inputs = [*shared, *prefixes, *parts]
    specs = [HELD] * len(inputs)
    inputs = [hold(array) for array in inputs]
    hbm = pl.BlockSpec(memory_space=pltpu.HBM)
    aliases = {}
    if begun is not None:
        aliases = {len(inputs): 0}
        specs.append(hbm)
        inputs.append(begun)
    name = "finish" + "".join(f"{core}{side}" for (core, side), _ in quarters)
    block = (tokens, width // 4)
    out_specs, shapes = [], []
    if carried is not None or not stays:
        out_specs.append(hbm)
        shapes.append(jax.ShapeDtypeStruct((tokens, width), jnp.bfloat16))
    if stays:
        out_specs.append(HELD)
        shapes.append(pltpu.VMEM(block, jnp.bfloat16))
    FINISH_OUTS[stays, carried] = len(shapes)
    return pl.pallas_call(
        functools.partial(finish_kernel, quarters, first_level, bits, stays, carried),
        in_specs=specs,
        out_specs=out_specs,
        out_shape=shapes,
        scratch_shapes=[
            pltpu.VMEM((8, 128) if stays else block, jnp.bfloat16),
            pltpu.VMEM((len(bits), heads, SPAN), jnp.float32),
            pltpu.SemaphoreType.DMA((3 * tokens // SPAN,)),
        ],
        input_output_aliases=aliases,
        compiler_params=PARAMS,
        cost_estimate=cost(name),
        name=name,
    )(*inputs)


def trade(value, mask):
    wide, narrow = lax.axis_size("wide"), lax.axis_size("narrow")

    def ranked(index):
        return index % narrow * wide + index // narrow

    pairs = [(ranked(source), ranked(source ^ mask)) for source in range(wide * narrow)]
    return lax.ppermute(value, AXES, pairs)


def per_device(queries, keys, values, log_decay, level_weight, norm_gain):
    heads = log_decay.shape[0]
    tokens, width = values.shape
    per = width // heads
    spans = tokens // SPAN
    group_bits = heads.bit_length() - 1
    bits = (lax.axis_size("wide") * lax.axis_size("narrow")).bit_length() - 1
    first_level = level_weight.shape[0] - bits
    gain = norm_gain.reshape(heads, per)
    keep, send, local, sums, totals, keys, values = make_states(keys, values, log_decay)
    last = bits - 1
    two = 2 * per
    size = two // CUTS
    sides = [(core, side) for core in (0, 1) for side in (0, 1)]
    other, other_rest = trade(send, 1), trade(keep, 1)
    chunks, give, prefix = make_chip(keep, other, heads, CUTS)
    queries, level_weight, gain = load([queries, level_weight, gain], chunks[0])
    shared = (queries, keys, values, sums, totals, level_weight, local, other, other_rest)
    prefixes = [None, prefix]
    found, across = {}, {}
    mixed, at = None, 0

    def both(name, messages, tokens=()):
        return pack(name, [(state, size) for state in messages], tokens)

    for bit in range(1, bits):
        found[bit] = [trade(chunk, 2**bit) for chunk in (give if bit == 1 else chunks)]
        stays = chunks if bit == 1 else stays
        waits = []
        if bit < 3 or bit == last:
            stop = spans if bit == last else at + 1
            begun = [*chunks[-1:], *([found[bit - 1]] if bit == last else [])]
            mixed, *waits = mix_local(at, stop, shared, mixed, begun, True)
            at = stop
        if bit == 3:
            waits.append(rest)
        if bit < last:
            merged = {}
            order = list(reversed(range(CUTS)))
            for offset in order:
                ending = offset == order[-1]
                tokens_of = [*merged.values(), *(waits if ending else ())]
                merged[offset], *after = merge(
                    bit, offset, ending, chunks[offset], found[bit][offset], prefixes[bit], tokens_of
                )
            chunks = [merged[offset] for offset in range(CUTS)]
            newest = merged[order[-1]]
            prefixes += after
            found[bit] = both(f"found{bit}", found[bit], (newest,))
            if bit > 1:
                across[bit] = trade(found[bit], 2)
            else:
                rest = trade(both("rest", stays, (newest,)), 2)

    state = both("state", found[last], waits)
    beside = trade(state, 2)
    early = list(range(1, last))
    ours = pack("ours", [(found[bit], two) for bit in early], ())
    theirs = pack("theirs", [(rest if bit == 1 else across[bit], two) for bit in early], (state,))
    joined = pack("joined", [(ours, len(early) * two), (state, two)])
    joined_far = trade(joined, 1)
    theirs_far = trade(theirs, 1)
    ahead = [prefixes[bit] for bit in early]
    shared = (mixed, queries, sums, level_weight, gain)
    every = (first_level, [*early, last], shared, [*ahead, prefixes[last]])
    levels = [(slot, 0, slot * two) for slot in range(len(early))]
    whole = [*levels, (len(early), 0, len(early) * two)]
    parted = [*levels, (len(early), 1, 0)]
    (block,) = finish([((0, 0), whole)], *every, [joined], None, True, None)
    out, block_far = finish(
        [((1, 0), whole)], *every, [joined_far, block], None, True, (1, (0, 0))
    )
    beside = pack("beside", [(beside, two)], (block_far,))
    (out,) = finish(
        [((0, 1), parted)], *every, [theirs, beside, block_far], out, False, (2, (1, 0))
    )
    beside_far = trade(beside, 1)
    return finish(
        [((1, 1), parted)], *every, [theirs_far, beside_far], out, False, None
    )[0]


def solution(mesh):
    placed = (
        P(("wide", "narrow"), None),
        P(("wide", "narrow"), None),
        P(("wide", "narrow"), None),
        P(None, ("wide", "narrow")),
        P(None, None, ("wide", "narrow")),
        P(),
    )
    return jax.shard_map(
        per_device,
        mesh=mesh,
        in_specs=placed,
        out_specs=P(("wide", "narrow"), None),
        check_vma=False,
    )
```

```python
import functools

import jax
import jax.numpy as jnp
from jax import lax
from jax.experimental import pallas as pl
from jax.experimental.pallas import tpu as pltpu
from jax.sharding import PartitionSpec as P

SPAN = 256
SPLIT_BITS = 2
CUTS = 2
EPS = 1e-05
AXES = ("narrow", "wide")
NT = (((1,), (1,)), ((), ()))
COSTS = {"local0": 1000, "finish00": 20000000000, "finish10": 1000, "finish01": 20000000000, "local2": 1000, "reach": 1000}


def cost(name):
    flops = COSTS.get(name, 2000000000)
    return pl.CostEstimate(flops=flops, transcendentals=0, bytes_accessed=1_000_000)


PARAMS = pltpu.CompilerParams(vmem_limit_bytes=32 * 1024 * 1024)
HELD = pl.BlockSpec(memory_space=pltpu.VMEM)


def place():
    return lax.axis_index("wide") * lax.axis_size("narrow") + lax.axis_index("narrow")


def bit_of(value, bit):
    return jnp.bitwise_and(jnp.right_shift(value, bit), 1)


def spread_lanes(column, width):
    return jnp.broadcast_to(column, (column.shape[0], width))


ANYWHERE = pl.BlockSpec(memory_space=pl.ANY)


def hold(array):
    return pltpu.with_memory_space_constraint(array, pltpu.VMEM)


def call(kernel, name, inputs, outputs, scratch=(), in_specs=None, aliases=None):
    specs = in_specs or [HELD] * len(inputs)
    inputs = [hold(array) if spec is HELD else array for array, spec in zip(inputs, specs)]
    return pl.pallas_call(
        kernel,
        in_specs=specs,
        out_specs=[HELD] * len(outputs),
        out_shape=[pltpu.VMEM(shape, dtype) for shape, dtype in outputs],
        scratch_shapes=list(scratch),
        input_output_aliases=aliases or {},
        compiler_params=PARAMS,
        cost_estimate=cost(name),
        name=name,
    )(*inputs)


def running_sums(rows):
    high = rows.astype(jnp.bfloat16)
    rest = rows - high.astype(jnp.float32)
    middle = rest.astype(jnp.bfloat16)
    low = (rest - middle.astype(jnp.float32)).astype(jnp.bfloat16)
    width = rows.shape[1]
    source = lax.broadcasted_iota(jnp.int32, (width, width), 0)
    target = lax.broadcasted_iota(jnp.int32, (width, width), 1)
    upto = jnp.where(source <= target, 1.0, 0.0).astype(jnp.bfloat16)
    sums = jnp.dot(
        jnp.concatenate([high, middle, low], axis=0), upto, preferred_element_type=jnp.float32
    )
    count = rows.shape[0]
    return sums[:count] + (sums[count : 2 * count] + sums[2 * count :])


def state_kernel(*refs):
    k_hbm, v_hbm, decay_hbm = refs[:3]
    keep_ref, send_ref, local_ref, sums_ref, totals_ref = refs[3:8]
    k_ref, v_ref, decay_ref, held, message_ref, arrived = refs[8:]
    heads, tokens = decay_ref.shape
    head_width = v_ref.shape[1] // heads
    spans = tokens // SPAN
    rows_of = [slice(span * SPAN, (span + 1) * SPAN) for span in range(spans)]
    loads = [(decay_hbm, decay_ref), (k_hbm, k_ref)]
    loads += [(v_hbm.at[rows], v_ref.at[rows]) for rows in rows_of]
    copies = [
        pltpu.make_async_copy(source, target, arrived.at[at])
        for at, (source, target) in enumerate(loads)
    ]
    for copy in copies:
        copy.start()
    copies[0].wait()
    within = running_sums(jnp.concatenate([decay_ref[:, rows] for rows in rows_of], axis=0))
    run = jnp.zeros((heads, 128), jnp.float32)
    fades, wholes = [], []
    for span, rows in enumerate(rows_of):
        here = within[span * heads : (span + 1) * heads]
        last = here[:, SPAN - 1 :]
        total = spread_lanes(last, 128)
        sums_ref[0, :, rows] = here
        sums_ref[1, :, rows] = here + spread_lanes(run[:, :1], SPAN)
        totals_ref[span] = total
        run = run + total
        fades.append(jnp.exp(spread_lanes(last, SPAN) - here))
        wholes.append(jnp.exp(total))
    copies[1].wait()
    across = [k_ref[rows].astype(jnp.float32).T for rows in rows_of]
    local_bits = spans.bit_length() - 1
    for span, rows in enumerate(rows_of):
        copies[2 + span].wait()
        for head in range(heads):
            columns = slice(head * head_width, (head + 1) * head_width)
            faded = (across[span] * fades[span][head : head + 1]).astype(jnp.bfloat16)
            state = jnp.dot(faded, v_ref[rows, columns], preferred_element_type=jnp.float32)
            at = 0
            for bit in range(local_bits + 1):
                if span >> bit & 1 == 0 or bit == local_bits:
                    group = state
                    if span % 2**bit > 0:
                        group = held[bit - 1, head] * wholes[span][head : head + 1] + state
                    if (span + 1) % 2**bit > 0:
                        held[bit - 1, head] = group
                    elif bit < local_bits:
                        local_ref[at + (span >> (bit + 1)), :, columns] = group.astype(
                            jnp.bfloat16
                        )
                    else:
                        message_ref[columns] = group.T
                at += spans >> (bit + 1)
    half = message_ref.shape[0] // 2
    core = bit_of(place(), 0)
    keep_ref[:half] = message_ref[pl.ds(pl.multiple_of(core * half, 8), half)]
    send_ref[:half] = message_ref[pl.ds(pl.multiple_of((1 - core) * half, 8), half)]
    keep_ref[half:] = run
    send_ref[half:] = run


def make_states(keys, values, log_decay):
    tokens, key_width = keys.shape
    heads = log_decay.shape[0]
    width = values.shape[1]
    spans = tokens // SPAN
    inputs = [keys, values, log_decay]
    kept = [keys, values]
    return call(
        state_kernel,
        "states",
        [pltpu.with_memory_space_constraint(array, pltpu.HBM) for array in inputs],
        [
            ((width // 2 + heads, key_width), jnp.float32),
            ((width // 2 + heads, key_width), jnp.float32),
            ((spans - 1, key_width, width), jnp.bfloat16),
            ((2, heads, tokens), jnp.float32),
            ((spans, heads, 128), jnp.float32),
            *[(array.shape, array.dtype) for array in kept],
        ],
        [
            pltpu.VMEM(log_decay.shape, jnp.float32),
            pltpu.VMEM((spans.bit_length() - 1, heads, key_width, width // heads), jnp.float32),
            pltpu.VMEM((width, key_width), jnp.float32),
            pltpu.SemaphoreType.DMA((spans + 2,)),
        ],
        [pl.BlockSpec(memory_space=pltpu.HBM)] * len(inputs),
    )


def load_kernel(count, *refs):
    copies = [
        pltpu.make_async_copy(source, target, refs[-1].at[at])
        for at, (source, target) in enumerate(zip(refs[:count], refs[-1 - count : -1]))
    ]
    for copy in copies:
        copy.start()
    for copy in copies:
        copy.wait()


def load(arrays, token):
    count = len(arrays)
    hbm = pl.BlockSpec(memory_space=pltpu.HBM)
    return call(
        functools.partial(load_kernel, count),
        "load",
        [*[pltpu.with_memory_space_constraint(array, pltpu.HBM) for array in arrays], token],
        [(array.shape, array.dtype) for array in arrays],
        [pltpu.SemaphoreType.DMA((count,))],
        [*[hbm] * count, HELD],
    )


def local_kernel(first, last, has_token, *refs):
    q_ref, k_ref, v_ref, sums_ref, totals_ref, weight_ref, local_ref, near_ref, rest_ref = refs[:9]
    if has_token:
        mixed_ref, done_ref = refs[-2:]
        done_ref[...] = jnp.zeros_like(done_ref)
    else:
        mixed_ref = refs[-1]
    heads = weight_ref.shape[1]
    head_width = v_ref.shape[1] // heads
    spans = totals_ref.shape[0]
    local_bits = spans.bit_length() - 1
    half = SPAN // 2
    source = lax.broadcasted_iota(jnp.int32, (half, half), 0)
    target = lax.broadcasted_iota(jnp.int32, (half, half), 1)
    causal = source <= target
    empty = jnp.zeros((half, half), jnp.bfloat16)
    upper = jnp.where(bit_of(place(), 0) == 1, 1.0, 0.0)
    size = heads // 2 * head_width
    near, rest = near_ref[:size], rest_ref[:size]
    first_core = bit_of(place(), 0) == 0
    near = jnp.concatenate(
        [jnp.where(first_core, near, rest), jnp.where(first_core, rest, near)], axis=0
    ).astype(jnp.bfloat16)

    for span in range(first, last):
        tokens = slice(span * SPAN, (span + 1) * SPAN)
        queries = q_ref[tokens]
        scores = lax.dot_general(
            k_ref[tokens], queries, NT, preferred_element_type=jnp.float32
        )
        within = sums_ref[0, :, tokens]
        within_down = within.T
        weight = weight_ref[0, :, tokens]
        values_across = v_ref[tokens].T

        def mix(head, low, high):
            rows = slice(low * half, (low + 1) * half)
            columns = slice(high * half, (high + 1) * half)
            gap = within[head : head + 1, columns] - within_down[rows, head : head + 1]
            if low == high:
                gap = jnp.where(causal, gap, -1e30)
            mixing = scores[rows, columns] * jnp.exp(gap) * weight[head : head + 1, columns]
            return mixing.astype(jnp.bfloat16)

        levels = []
        offset = 0
        for bit in range(local_bits):
            if span >> bit & 1:
                since = within
                for back in range(1, span % 2**bit + 1):
                    since = since + spread_lanes(totals_ref[span - back][:, :1], SPAN)
                scale = jnp.exp(since) * weight_ref[1 + bit, :, tokens]
                levels.append((local_ref[offset + (span >> (bit + 1))].T, scale))
            offset += spans >> (bit + 1)
        reach = jnp.exp(sums_ref[1, :, tokens]) * weight_ref[1 + local_bits, :, tokens] * upper
        levels.append((near, reach))
        for head in range(heads):
            rows = slice(head * head_width, (head + 1) * head_width)
            mixing = jnp.concatenate(
                [
                    jnp.concatenate([mix(head, 0, 0), mix(head, 0, 1)], axis=1),
                    jnp.concatenate([empty, mix(head, 1, 1)], axis=1),
                ],
                axis=0,
            )
            mixed = jnp.dot(values_across[rows], mixing, preferred_element_type=jnp.float32)
            for level, scale in levels:
                found = lax.dot_general(
                    level[rows], queries, NT, preferred_element_type=jnp.float32
                )
                mixed = mixed + found * scale[head : head + 1]
            mixed_ref[rows, tokens] = mixed


def mix_local(first, last, shared, mixed, tokens, has_token):
    values = shared[2]
    rest = [] if mixed is None else [mixed]
    return call(
        functools.partial(local_kernel, first, last, has_token),
        f"local{first}",
        [*shared, *rest, *tokens],
        [(values.shape[::-1], jnp.float32), ((8, 128), jnp.float32)][: 1 + has_token],
        aliases={9: 0} if rest else None,
    )


def join(upper, mine, mine_total, other, other_total):
    fade = jnp.exp(jnp.where(upper, mine_total, other_total))
    return jnp.where(upper, other * fade + mine, mine * fade + other)


def first_head(far, heads):
    here = place()
    first = 0
    for bit, flip in enumerate(far):
        first = first + jnp.bitwise_xor(bit_of(here, bit), flip) * (heads >> (bit + 1))
    return first


def chip_kernel(mine_ref, other_ref, *refs):
    *message_refs, next_ref, whole_ref = refs
    heads = next_ref.shape[0]
    width = whole_ref.shape[0]
    held = heads // 2
    per = width // held
    here = place()
    upper = bit_of(here, 0) == 1
    first = first_head((0,), heads)
    for slot in range(held):
        part = slice(slot * per, (slot + 1) * per)
        total = pl.ds(width + first + slot, 1)
        whole_ref[part] = join(
            upper, mine_ref[part], mine_ref[total], other_ref[part], other_ref[total]
        )
    other_total = other_ref[width:]
    total = mine_ref[width:] + other_total
    next_ref[...] = jnp.where(upper, other_total, 0.0)
    half = width // 2
    side = bit_of(here, 1)
    cuts = len(message_refs) // 2
    size = half // cuts
    for at, ref in enumerate(message_refs):
        start = (side if at < cuts else 1 - side) * half + at % cuts * size
        ref[:size] = whole_ref[pl.ds(pl.multiple_of(start, 8), size)]
        ref[size:] = total


def make_chip(mine, other, heads, cuts):
    rows, lanes = mine.shape
    half = rows - heads
    *messages, prefix = call(
        chip_kernel,
        "chip",
        [mine, other],
        [
            *[((half // 2 // cuts + heads, lanes), jnp.float32)] * (2 * cuts),
            ((heads, lanes), jnp.float32),
        ],
        [pltpu.VMEM((half, lanes), jnp.float32)],
    )
    return messages[:cuts], messages[cuts:], prefix


def merge_kernel(bit, offset, has_prefix, *refs):
    mine_ref, other_ref, prefix_ref = refs[:3]
    merged_ref = refs[-2] if has_prefix else refs[-1]
    heads = prefix_ref.shape[0]
    rows = mine_ref.shape[0] - heads
    per = mine_ref.shape[1]
    upper = bit_of(place(), bit) == 1
    first = first_head((0,) * SPLIT_BITS, heads) + offset
    for slot in range(rows // per):
        part = slice(slot * per, (slot + 1) * per)
        total = pl.ds(rows + first + slot, 1)
        merged_ref[part] = join(
            upper, mine_ref[part], mine_ref[total], other_ref[part], other_ref[total]
        )
    other_total = other_ref[rows:]
    merged_ref[rows:] = mine_ref[rows:] + other_total
    if has_prefix:
        refs[-1][...] = prefix_ref[...] + jnp.where(upper, other_total, 0.0)


def merge(bit, offset, has_prefix, mine, other, prefix, tokens=()):
    return call(
        functools.partial(merge_kernel, bit, offset, has_prefix),
        f"merge{bit}{offset}",
        [mine, other, prefix, *tokens],
        [(mine.shape, jnp.float32), (prefix.shape, jnp.float32)][: 1 + has_prefix],
    )


def pack_kernel(takes, *refs):
    out_ref = refs[-1]
    at = 0
    for ref, rows in zip(refs, takes):
        out_ref[at : at + rows] = ref[:rows]
        at += rows


def pack(name, pieces, tokens=()):
    takes = [rows for _, rows in pieces]
    lanes = pieces[0][0].shape[1]
    return call(
        functools.partial(pack_kernel, takes),
        name,
        [*[array for array, _ in pieces], *tokens],
        [((sum(takes), lanes), jnp.float32)],
    )[0]


def level_scale(bit, first_level, prefix_ref, sums_ref, weight_ref, tokens):
    active = jnp.where(bit_of(place(), bit) == 1, 1.0, 0.0)
    reach = jnp.exp(sums_ref[1, :, tokens] + spread_lanes(prefix_ref[:, :1], SPAN))
    return reach * weight_ref[first_level + bit, :, tokens] * active


def gather_work(quarters, part_refs, heads, per):
    work = []
    for far, pieces in quarters:
        first = first_head(far, heads)
        for slot in range(heads // 4):
            states = []
            for level, index, start in pieces:
                if start is None:
                    rows = pl.ds(pl.multiple_of((first + slot) * per, 128), per)
                else:
                    rows = slice(start + slot * per, start + (slot + 1) * per)
                states.append((level, part_refs[index][rows].astype(jnp.bfloat16)))
            work.append((first + slot, states))
    return work


def add_found(mixed, queries, head, states, scale_ref):
    for level, state in states:
        found = lax.dot_general(state, queries, NT, preferred_element_type=jnp.float32)
        mixed = mixed + found * scale_ref[level, pl.ds(head, 1)]
    return mixed


def finish_kernel(quarters, first_level, bits, stays, carried, *refs):
    mixed_ref, q_ref, sums_ref, weight_ref, gain_ref = refs[:5]
    prefix_refs = refs[5 : 5 + len(bits)]
    part_refs = refs[5 + len(bits) :]
    out_refs, (own_ref, scale_ref, sent) = refs[-3 - FINISH_OUTS[stays, carried] : -3], refs[-3:]
    if stays:
        own_ref = out_refs[-1]
    heads = weight_ref.shape[1]
    head_width = mixed_ref.shape[0] // heads
    size = heads // 4 * head_width
    copies = []

    def send(block, far, rows):
        columns = pl.ds(pl.multiple_of(first_head(far, heads) * head_width, 128), size)
        copy = pltpu.make_async_copy(
            block.at[rows], out_refs[0].at[rows, columns], sent.at[len(copies)]
        )
        copy.start()
        copies.append(copy)

    if carried is not None:
        index, far = carried
        for start in range(0, q_ref.shape[0], SPAN):
            send(part_refs[index], far, slice(start, start + SPAN))
    work = gather_work(quarters, part_refs, heads, head_width)
    gains = []
    for head, _ in work:
        row = jnp.broadcast_to(gain_ref[pl.ds(head, 1)], (8, head_width))
        gains.append(row.T[:, :1])
    for span in range(q_ref.shape[0] // SPAN):
        tokens = slice(span * SPAN, (span + 1) * SPAN)
        queries = q_ref[tokens]
        for level, (bit, prefix_ref) in enumerate(zip(bits, prefix_refs)):
            scale_ref[level] = level_scale(
                bit, first_level, prefix_ref, sums_ref, weight_ref, tokens
            )
        for at, (head, states) in enumerate(work):
            rows = pl.ds(pl.multiple_of(head * head_width, 128), head_width)
            mixed = add_found(mixed_ref[rows, tokens], queries, head, states, scale_ref)
            square = jnp.mean(mixed * mixed, axis=0, keepdims=True)
            normed = mixed * lax.rsqrt(square + EPS) * gains[at]
            columns = slice(at * head_width, (at + 1) * head_width)
            own_ref[tokens, columns] = normed.astype(jnp.bfloat16).T
        if not stays:
            for start in range(tokens.start, tokens.stop, SPAN // 2):
                send(own_ref, quarters[0][0], slice(start, start + SPAN // 2))
    for copy in copies:
        copy.wait()


FINISH_OUTS = {}


def finish(quarters, first_level, bits, shared, prefixes, parts, begun, stays, carried):
    mixed, queries, sums, level_weight, gain = shared
    width, tokens = mixed.shape
    heads = level_weight.shape[1]
    inputs = [*shared, *prefixes, *parts]
    specs = [HELD] * len(inputs)
    inputs = [hold(array) for array in inputs]
    hbm = pl.BlockSpec(memory_space=pltpu.HBM)
    aliases = {}
    if begun is not None:
        aliases = {len(inputs): 0}
        specs.append(hbm)
        inputs.append(begun)
    name = "finish" + "".join(f"{core}{side}" for (core, side), _ in quarters)
    block = (tokens, width // 4)
    out_specs, shapes = [], []
    if carried is not None or not stays:
        out_specs.append(hbm)
        shapes.append(jax.ShapeDtypeStruct((tokens, width), jnp.bfloat16))
    if stays:
        out_specs.append(HELD)
        shapes.append(pltpu.VMEM(block, jnp.bfloat16))
    FINISH_OUTS[stays, carried] = len(shapes)
    return pl.pallas_call(
        functools.partial(finish_kernel, quarters, first_level, bits, stays, carried),
        in_specs=specs,
        out_specs=out_specs,
        out_shape=shapes,
        scratch_shapes=[
            pltpu.VMEM((8, 128) if stays else block, jnp.bfloat16),
            pltpu.VMEM((len(bits), heads, SPAN), jnp.float32),
            pltpu.SemaphoreType.DMA((3 * tokens // SPAN,)),
        ],
        input_output_aliases=aliases,
        compiler_params=PARAMS,
        cost_estimate=cost(name),
        name=name,
    )(*inputs)


def trade(value, mask):
    wide, narrow = lax.axis_size("wide"), lax.axis_size("narrow")

    def ranked(index):
        return index % narrow * wide + index // narrow

    pairs = [(ranked(source), ranked(source ^ mask)) for source in range(wide * narrow)]
    return lax.ppermute(value, AXES, pairs)


def per_device(queries, keys, values, log_decay, level_weight, norm_gain):
    heads = log_decay.shape[0]
    tokens, width = values.shape
    per = width // heads
    spans = tokens // SPAN
    group_bits = heads.bit_length() - 1
    bits = (lax.axis_size("wide") * lax.axis_size("narrow")).bit_length() - 1
    first_level = level_weight.shape[0] - bits
    gain = norm_gain.reshape(heads, per)
    keep, send, local, sums, totals, keys, values = make_states(keys, values, log_decay)
    last = bits - 1
    two = 2 * per
    size = two // CUTS
    sides = [(core, side) for core in (0, 1) for side in (0, 1)]
    other, other_rest = trade(send, 1), trade(keep, 1)
    chunks, give, prefix = make_chip(keep, other, heads, CUTS)
    queries, level_weight, gain = load([queries, level_weight, gain], chunks[0])
    shared = (queries, keys, values, sums, totals, level_weight, local, other, other_rest)
    prefixes = [None, prefix]
    found, across = {}, {}
    mixed, at = None, 0

    def both(name, messages, tokens=()):
        return pack(name, [(state, size) for state in messages], tokens)

    for bit in range(1, bits):
        found[bit] = [trade(chunk, 2**bit) for chunk in (give if bit == 1 else chunks)]
        stays = chunks if bit == 1 else stays
        waits = []
        if bit < 3 or bit == last:
            stop = spans if bit == last else at + 1
            begun = [*chunks[-1:], *([found[bit - 1]] if bit == last else [])]
            mixed, *waits = mix_local(at, stop, shared, mixed, begun, True)
            at = stop
        if bit == 3:
            waits.append(rest)
        if bit < last:
            merged = {}
            order = list(reversed(range(CUTS)))
            for offset in order:
                ending = offset == order[-1]
                tokens_of = [*merged.values(), *(waits if ending else ())]
                merged[offset], *after = merge(
                    bit, offset, ending, chunks[offset], found[bit][offset], prefixes[bit], tokens_of
                )
            chunks = [merged[offset] for offset in range(CUTS)]
            newest = merged[order[-1]]
            prefixes += after
            if bit == 1:
                found[bit] = both("found1", found[bit], (newest,))
                rest = trade(both("rest", stays, (newest,)), 2)
            if bit == last - 1:
                for level in range(2, last):
                    found[level] = both(f"found{level}", found[level], (newest,))
                    across[level] = trade(found[level], 2)

    state = both("state", found[last], waits)
    beside = trade(state, 2)
    early = list(range(1, last))
    ours = pack("ours", [(found[bit], two) for bit in early], ())
    theirs = pack("theirs", [(rest if bit == 1 else across[bit], two) for bit in early], (state,))
    joined = pack("joined", [(ours, len(early) * two), (state, two)])
    joined_far = trade(joined, 1)
    theirs_far = trade(theirs, 1)
    ahead = [prefixes[bit] for bit in early]
    shared = (mixed, queries, sums, level_weight, gain)
    every = (first_level, [*early, last], shared, [*ahead, prefixes[last]])
    levels = [(slot, 0, slot * two) for slot in range(len(early))]
    whole = [*levels, (len(early), 0, len(early) * two)]
    parted = [*levels, (len(early), 1, 0)]
    (block,) = finish([((0, 0), whole)], *every, [joined], None, True, None)
    out, block_far = finish(
        [((1, 0), whole)], *every, [joined_far, block], None, True, (1, (0, 0))
    )
    beside = pack("beside", [(beside, two)], (block_far,))
    (out,) = finish(
        [((0, 1), parted)], *every, [theirs, beside, block_far], out, False, (2, (1, 0))
    )
    beside_far = trade(beside, 1)
    return finish(
        [((1, 1), parted)], *every, [theirs_far, beside_far], out, False, None
    )[0]


def solution(mesh):
    placed = (
        P(("wide", "narrow"), None),
        P(("wide", "narrow"), None),
        P(("wide", "narrow"), None),
        P(None, ("wide", "narrow")),
        P(None, None, ("wide", "narrow")),
        P(),
    )
    return jax.shard_map(
        per_device,
        mesh=mesh,
        in_specs=placed,
        out_specs=P(("wide", "narrow"), None),
        check_vma=False,
    )
```

```python
import functools

import jax
import jax.numpy as jnp
from jax import lax
from jax.experimental import pallas as pl
from jax.experimental.pallas import tpu as pltpu
from jax.sharding import PartitionSpec as P

SPAN = 256
SPLIT_BITS = 2
CUTS = 2
EPS = 1e-05
AXES = ("narrow", "wide")
NT = (((1,), (1,)), ((), ()))
COSTS = {"local0": 1000, "finish00": 20000000000, "finish10": 1000, "finish01": 20000000000, "local2": 1000, "reach": 1000}


def cost(name):
    flops = COSTS.get(name, 2000000000)
    return pl.CostEstimate(flops=flops, transcendentals=0, bytes_accessed=1_000_000)


PARAMS = pltpu.CompilerParams(vmem_limit_bytes=32 * 1024 * 1024)
HELD = pl.BlockSpec(memory_space=pltpu.VMEM)


def place():
    return lax.axis_index("wide") * lax.axis_size("narrow") + lax.axis_index("narrow")


def bit_of(value, bit):
    return jnp.bitwise_and(jnp.right_shift(value, bit), 1)


def spread_lanes(column, width):
    return jnp.broadcast_to(column, (column.shape[0], width))


ANYWHERE = pl.BlockSpec(memory_space=pl.ANY)


def hold(array):
    return pltpu.with_memory_space_constraint(array, pltpu.VMEM)


def call(kernel, name, inputs, outputs, scratch=(), in_specs=None, aliases=None):
    specs = in_specs or [HELD] * len(inputs)
    inputs = [hold(array) if spec is HELD else array for array, spec in zip(inputs, specs)]
    return pl.pallas_call(
        kernel,
        in_specs=specs,
        out_specs=[HELD] * len(outputs),
        out_shape=[pltpu.VMEM(shape, dtype) for shape, dtype in outputs],
        scratch_shapes=list(scratch),
        input_output_aliases=aliases or {},
        compiler_params=PARAMS,
        cost_estimate=cost(name),
        name=name,
    )(*inputs)


def running_sums(rows):
    high = rows.astype(jnp.bfloat16)
    rest = rows - high.astype(jnp.float32)
    middle = rest.astype(jnp.bfloat16)
    low = (rest - middle.astype(jnp.float32)).astype(jnp.bfloat16)
    width = rows.shape[1]
    source = lax.broadcasted_iota(jnp.int32, (width, width), 0)
    target = lax.broadcasted_iota(jnp.int32, (width, width), 1)
    upto = jnp.where(source <= target, 1.0, 0.0).astype(jnp.bfloat16)
    sums = jnp.dot(
        jnp.concatenate([high, middle, low], axis=0), upto, preferred_element_type=jnp.float32
    )
    count = rows.shape[0]
    return sums[:count] + (sums[count : 2 * count] + sums[2 * count :])


def state_kernel(*refs):
    k_hbm, v_hbm, decay_hbm = refs[:3]
    keep_ref, send_ref, local_ref, sums_ref, totals_ref = refs[3:8]
    k_ref, v_ref, decay_ref, held, message_ref, arrived = refs[8:]
    heads, tokens = decay_ref.shape
    head_width = v_ref.shape[1] // heads
    spans = tokens // SPAN
    rows_of = [slice(span * SPAN, (span + 1) * SPAN) for span in range(spans)]
    loads = [(decay_hbm, decay_ref), (k_hbm, k_ref)]
    loads += [(v_hbm.at[rows], v_ref.at[rows]) for rows in rows_of]
    copies = [
        pltpu.make_async_copy(source, target, arrived.at[at])
        for at, (source, target) in enumerate(loads)
    ]
    for copy in copies:
        copy.start()
    copies[0].wait()
    within = running_sums(jnp.concatenate([decay_ref[:, rows] for rows in rows_of], axis=0))
    run = jnp.zeros((heads, 128), jnp.float32)
    fades, wholes = [], []
    for span, rows in enumerate(rows_of):
        here = within[span * heads : (span + 1) * heads]
        last = here[:, SPAN - 1 :]
        total = spread_lanes(last, 128)
        sums_ref[0, :, rows] = here
        sums_ref[1, :, rows] = here + spread_lanes(run[:, :1], SPAN)
        totals_ref[span] = total
        run = run + total
        fades.append(jnp.exp(spread_lanes(last, SPAN) - here))
        wholes.append(jnp.exp(total))
    copies[1].wait()
    across = [k_ref[rows].astype(jnp.float32).T for rows in rows_of]
    local_bits = spans.bit_length() - 1
    for span, rows in enumerate(rows_of):
        copies[2 + span].wait()
        for head in range(heads):
            columns = slice(head * head_width, (head + 1) * head_width)
            faded = (across[span] * fades[span][head : head + 1]).astype(jnp.bfloat16)
            state = jnp.dot(faded, v_ref[rows, columns], preferred_element_type=jnp.float32)
            at = 0
            for bit in range(local_bits + 1):
                if span >> bit & 1 == 0 or bit == local_bits:
                    group = state
                    if span % 2**bit > 0:
                        group = held[bit - 1, head] * wholes[span][head : head + 1] + state
                    if (span + 1) % 2**bit > 0:
                        held[bit - 1, head] = group
                    elif bit < local_bits:
                        local_ref[at + (span >> (bit + 1)), :, columns] = group.astype(
                            jnp.bfloat16
                        )
                    else:
                        message_ref[columns] = group.T
                at += spans >> (bit + 1)
    half = message_ref.shape[0] // 2
    core = bit_of(place(), 0)
    keep_ref[:half] = message_ref[pl.ds(pl.multiple_of(core * half, 8), half)]
    send_ref[:half] = message_ref[pl.ds(pl.multiple_of((1 - core) * half, 8), half)]
    keep_ref[half:] = run
    send_ref[half:] = run


def make_states(keys, values, log_decay):
    tokens, key_width = keys.shape
    heads = log_decay.shape[0]
    width = values.shape[1]
    spans = tokens // SPAN
    inputs = [keys, values, log_decay]
    kept = [keys, values]
    return call(
        state_kernel,
        "states",
        [pltpu.with_memory_space_constraint(array, pltpu.HBM) for array in inputs],
        [
            ((width // 2 + heads, key_width), jnp.float32),
            ((width // 2 + heads, key_width), jnp.float32),
            ((spans - 1, key_width, width), jnp.bfloat16),
            ((2, heads, tokens), jnp.float32),
            ((spans, heads, 128), jnp.float32),
            *[(array.shape, array.dtype) for array in kept],
        ],
        [
            pltpu.VMEM(log_decay.shape, jnp.float32),
            pltpu.VMEM((spans.bit_length() - 1, heads, key_width, width // heads), jnp.float32),
            pltpu.VMEM((width, key_width), jnp.float32),
            pltpu.SemaphoreType.DMA((spans + 2,)),
        ],
        [pl.BlockSpec(memory_space=pltpu.HBM)] * len(inputs),
    )


def load_kernel(count, *refs):
    copies = [
        pltpu.make_async_copy(source, target, refs[-1].at[at])
        for at, (source, target) in enumerate(zip(refs[:count], refs[-1 - count : -1]))
    ]
    for copy in copies:
        copy.start()
    for copy in copies:
        copy.wait()


def load(arrays, token):
    count = len(arrays)
    hbm = pl.BlockSpec(memory_space=pltpu.HBM)
    return call(
        functools.partial(load_kernel, count),
        "load",
        [*[pltpu.with_memory_space_constraint(array, pltpu.HBM) for array in arrays], token],
        [(array.shape, array.dtype) for array in arrays],
        [pltpu.SemaphoreType.DMA((count,))],
        [*[hbm] * count, HELD],
    )


def local_kernel(first, last, has_token, *refs):
    q_ref, k_ref, v_ref, sums_ref, totals_ref, weight_ref, local_ref, near_ref, rest_ref = refs[:9]
    if has_token:
        mixed_ref, done_ref = refs[-2:]
        done_ref[...] = jnp.zeros_like(done_ref)
    else:
        mixed_ref = refs[-1]
    heads = weight_ref.shape[1]
    head_width = v_ref.shape[1] // heads
    spans = totals_ref.shape[0]
    local_bits = spans.bit_length() - 1
    half = SPAN // 2
    source = lax.broadcasted_iota(jnp.int32, (half, half), 0)
    target = lax.broadcasted_iota(jnp.int32, (half, half), 1)
    causal = source <= target
    empty = jnp.zeros((half, half), jnp.bfloat16)
    upper = jnp.where(bit_of(place(), 0) == 1, 1.0, 0.0)
    size = heads // 2 * head_width
    near, rest = near_ref[:size], rest_ref[:size]
    first_core = bit_of(place(), 0) == 0
    near = jnp.concatenate(
        [jnp.where(first_core, near, rest), jnp.where(first_core, rest, near)], axis=0
    ).astype(jnp.bfloat16)

    for span in range(first, last):
        tokens = slice(span * SPAN, (span + 1) * SPAN)
        queries = q_ref[tokens]
        scores = lax.dot_general(
            k_ref[tokens], queries, NT, preferred_element_type=jnp.float32
        )
        within = sums_ref[0, :, tokens]
        within_down = within.T
        weight = weight_ref[0, :, tokens]
        values_across = v_ref[tokens].T

        def mix(head, low, high):
            rows = slice(low * half, (low + 1) * half)
            columns = slice(high * half, (high + 1) * half)
            gap = within[head : head + 1, columns] - within_down[rows, head : head + 1]
            if low == high:
                gap = jnp.where(causal, gap, -1e30)
            mixing = scores[rows, columns] * jnp.exp(gap) * weight[head : head + 1, columns]
            return mixing.astype(jnp.bfloat16)

        levels = []
        offset = 0
        for bit in range(local_bits):
            if span >> bit & 1:
                since = within
                for back in range(1, span % 2**bit + 1):
                    since = since + spread_lanes(totals_ref[span - back][:, :1], SPAN)
                scale = jnp.exp(since) * weight_ref[1 + bit, :, tokens]
                levels.append((local_ref[offset + (span >> (bit + 1))].T, scale))
            offset += spans >> (bit + 1)
        reach = jnp.exp(sums_ref[1, :, tokens]) * weight_ref[1 + local_bits, :, tokens] * upper
        levels.append((near, reach))
        for head in range(heads):
            rows = slice(head * head_width, (head + 1) * head_width)
            mixing = jnp.concatenate(
                [
                    jnp.concatenate([mix(head, 0, 0), mix(head, 0, 1)], axis=1),
                    jnp.concatenate([empty, mix(head, 1, 1)], axis=1),
                ],
                axis=0,
            )
            mixed = jnp.dot(values_across[rows], mixing, preferred_element_type=jnp.float32)
            for level, scale in levels:
                found = lax.dot_general(
                    level[rows], queries, NT, preferred_element_type=jnp.float32
                )
                mixed = mixed + found * scale[head : head + 1]
            mixed_ref[rows, tokens] = mixed


def mix_local(first, last, shared, mixed, tokens, has_token):
    values = shared[2]
    rest = [] if mixed is None else [mixed]
    return call(
        functools.partial(local_kernel, first, last, has_token),
        f"local{first}",
        [*shared, *rest, *tokens],
        [(values.shape[::-1], jnp.float32), ((8, 128), jnp.float32)][: 1 + has_token],
        aliases={9: 0} if rest else None,
    )


def join(upper, mine, mine_total, other, other_total):
    fade = jnp.exp(jnp.where(upper, mine_total, other_total))
    return jnp.where(upper, other * fade + mine, mine * fade + other)


def first_head(far, heads):
    here = place()
    first = 0
    for bit, flip in enumerate(far):
        first = first + jnp.bitwise_xor(bit_of(here, bit), flip) * (heads >> (bit + 1))
    return first


def chip_kernel(mine_ref, other_ref, *refs):
    *message_refs, next_ref, whole_ref = refs
    heads = next_ref.shape[0]
    width = whole_ref.shape[0]
    held = heads // 2
    per = width // held
    here = place()
    upper = bit_of(here, 0) == 1
    first = first_head((0,), heads)
    for slot in range(held):
        part = slice(slot * per, (slot + 1) * per)
        total = pl.ds(width + first + slot, 1)
        whole_ref[part] = join(
            upper, mine_ref[part], mine_ref[total], other_ref[part], other_ref[total]
        )
    other_total = other_ref[width:]
    total = mine_ref[width:] + other_total
    next_ref[...] = jnp.where(upper, other_total, 0.0)
    half = width // 2
    side = bit_of(here, 1)
    cuts = len(message_refs) // 2
    size = half // cuts
    for at, ref in enumerate(message_refs):
        start = (side if at < cuts else 1 - side) * half + at % cuts * size
        ref[:size] = whole_ref[pl.ds(pl.multiple_of(start, 8), size)]
        ref[size:] = total


def make_chip(mine, other, heads, cuts):
    rows, lanes = mine.shape
    half = rows - heads
    *messages, prefix = call(
        chip_kernel,
        "chip",
        [mine, other],
        [
            *[((half // 2 // cuts + heads, lanes), jnp.float32)] * (2 * cuts),
            ((heads, lanes), jnp.float32),
        ],
        [pltpu.VMEM((half, lanes), jnp.float32)],
    )
    return messages[:cuts], messages[cuts:], prefix


def merge_kernel(bit, offset, has_prefix, *refs):
    mine_ref, other_ref, prefix_ref = refs[:3]
    merged_ref = refs[-2] if has_prefix else refs[-1]
    heads = prefix_ref.shape[0]
    rows = mine_ref.shape[0] - heads
    per = mine_ref.shape[1]
    upper = bit_of(place(), bit) == 1
    first = first_head((0,) * SPLIT_BITS, heads) + offset
    for slot in range(rows // per):
        part = slice(slot * per, (slot + 1) * per)
        total = pl.ds(rows + first + slot, 1)
        merged_ref[part] = join(
            upper, mine_ref[part], mine_ref[total], other_ref[part], other_ref[total]
        )
    other_total = other_ref[rows:]
    merged_ref[rows:] = mine_ref[rows:] + other_total
    if has_prefix:
        refs[-1][...] = prefix_ref[...] + jnp.where(upper, other_total, 0.0)


def merge(bit, offset, has_prefix, mine, other, prefix, tokens=()):
    return call(
        functools.partial(merge_kernel, bit, offset, has_prefix),
        f"merge{bit}{offset}",
        [mine, other, prefix, *tokens],
        [(mine.shape, jnp.float32), (prefix.shape, jnp.float32)][: 1 + has_prefix],
    )


def pack_kernel(takes, *refs):
    out_ref = refs[-1]
    at = 0
    for ref, rows in zip(refs, takes):
        out_ref[at : at + rows] = ref[:rows]
        at += rows


def pack(name, pieces, tokens=()):
    takes = [rows for _, rows in pieces]
    lanes = pieces[0][0].shape[1]
    return call(
        functools.partial(pack_kernel, takes),
        name,
        [*[array for array, _ in pieces], *tokens],
        [((sum(takes), lanes), jnp.float32)],
    )[0]


def level_scale(bit, first_level, prefix_ref, sums_ref, weight_ref, tokens):
    active = jnp.where(bit_of(place(), bit) == 1, 1.0, 0.0)
    reach = jnp.exp(sums_ref[1, :, tokens] + spread_lanes(prefix_ref[:, :1], SPAN))
    return reach * weight_ref[first_level + bit, :, tokens] * active


def gather_work(quarter, part_refs, heads, per):
    far, pieces = quarter
    rows = heads // 4 * per
    states = [
        (level, part_refs[index][start : start + rows].astype(jnp.bfloat16))
        for level, index, start in pieces
    ]
    return first_head(far, heads), states


def finish_kernel(quarters, first_level, bits, stays, carried, *refs):
    mixed_ref, q_ref, sums_ref, weight_ref, gain_ref = refs[:5]
    prefix_refs = refs[5 : 5 + len(bits)]
    part_refs = refs[5 + len(bits) :]
    out_refs, (own_ref, scale_ref, sent) = refs[-3 - FINISH_OUTS[stays, carried] : -3], refs[-3:]
    if stays:
        own_ref = out_refs[-1]
    heads = weight_ref.shape[1]
    head_width = mixed_ref.shape[0] // heads
    size = heads // 4 * head_width
    copies = []

    def send(block, far, rows):
        columns = pl.ds(pl.multiple_of(first_head(far, heads) * head_width, 128), size)
        copy = pltpu.make_async_copy(
            block.at[rows], out_refs[0].at[rows, columns], sent.at[len(copies)]
        )
        copy.start()
        copies.append(copy)

    if carried is not None:
        index, far = carried
        for start in range(0, q_ref.shape[0], SPAN):
            send(part_refs[index], far, slice(start, start + SPAN))
    first, states = gather_work(quarters[0], part_refs, heads, head_width)
    gains = []
    for slot in range(heads // 4):
        row = jnp.broadcast_to(gain_ref[pl.ds(first + slot, 1)], (8, head_width))
        gains.append(row.T[:, :1])
    for span in range(q_ref.shape[0] // SPAN):
        tokens = slice(span * SPAN, (span + 1) * SPAN)
        queries = q_ref[tokens]
        for level, (bit, prefix_ref) in enumerate(zip(bits, prefix_refs)):
            scale_ref[level] = level_scale(
                bit, first_level, prefix_ref, sums_ref, weight_ref, tokens
            )
        founds = [
            (level, lax.dot_general(state, queries, NT, preferred_element_type=jnp.float32))
            for level, state in states
        ]
        for at in range(heads // 4):
            rows = pl.ds(pl.multiple_of((first + at) * head_width, 128), head_width)
            mixed = mixed_ref[rows, tokens]
            for level, found in founds:
                part = found[at * head_width : (at + 1) * head_width]
                mixed = mixed + part * scale_ref[level, pl.ds(first + at, 1)]
            square = jnp.mean(mixed * mixed, axis=0, keepdims=True)
            normed = mixed * lax.rsqrt(square + EPS) * gains[at]
            columns = slice(at * head_width, (at + 1) * head_width)
            own_ref[tokens, columns] = normed.astype(jnp.bfloat16).T
        if not stays:
            for start in range(tokens.start, tokens.stop, SPAN // 2):
                send(own_ref, quarters[0][0], slice(start, start + SPAN // 2))
    for copy in copies:
        copy.wait()


FINISH_OUTS = {}


def finish(quarters, first_level, bits, shared, prefixes, parts, begun, stays, carried):
    mixed, queries, sums, level_weight, gain = shared
    width, tokens = mixed.shape
    heads = level_weight.shape[1]
    inputs = [*shared, *prefixes, *parts]
    specs = [HELD] * len(inputs)
    inputs = [hold(array) for array in inputs]
    hbm = pl.BlockSpec(memory_space=pltpu.HBM)
    aliases = {}
    if begun is not None:
        aliases = {len(inputs): 0}
        specs.append(hbm)
        inputs.append(begun)
    name = "finish" + "".join(f"{core}{side}" for (core, side), _ in quarters)
    block = (tokens, width // 4)
    out_specs, shapes = [], []
    if carried is not None or not stays:
        out_specs.append(hbm)
        shapes.append(jax.ShapeDtypeStruct((tokens, width), jnp.bfloat16))
    if stays:
        out_specs.append(HELD)
        shapes.append(pltpu.VMEM(block, jnp.bfloat16))
    FINISH_OUTS[stays, carried] = len(shapes)
    return pl.pallas_call(
        functools.partial(finish_kernel, quarters, first_level, bits, stays, carried),
        in_specs=specs,
        out_specs=out_specs,
        out_shape=shapes,
        scratch_shapes=[
            pltpu.VMEM((8, 128) if stays else block, jnp.bfloat16),
            pltpu.VMEM((len(bits), heads, SPAN), jnp.float32),
            pltpu.SemaphoreType.DMA((3 * tokens // SPAN,)),
        ],
        input_output_aliases=aliases,
        compiler_params=PARAMS,
        cost_estimate=cost(name),
        name=name,
    )(*inputs)


def trade(value, mask):
    wide, narrow = lax.axis_size("wide"), lax.axis_size("narrow")

    def ranked(index):
        return index % narrow * wide + index // narrow

    pairs = [(ranked(source), ranked(source ^ mask)) for source in range(wide * narrow)]
    return lax.ppermute(value, AXES, pairs)


def per_device(queries, keys, values, log_decay, level_weight, norm_gain):
    heads = log_decay.shape[0]
    tokens, width = values.shape
    per = width // heads
    spans = tokens // SPAN
    group_bits = heads.bit_length() - 1
    bits = (lax.axis_size("wide") * lax.axis_size("narrow")).bit_length() - 1
    first_level = level_weight.shape[0] - bits
    gain = norm_gain.reshape(heads, per)
    keep, send, local, sums, totals, keys, values = make_states(keys, values, log_decay)
    last = bits - 1
    two = 2 * per
    size = two // CUTS
    sides = [(core, side) for core in (0, 1) for side in (0, 1)]
    other, other_rest = trade(send, 1), trade(keep, 1)
    chunks, give, prefix = make_chip(keep, other, heads, CUTS)
    queries, level_weight, gain = load([queries, level_weight, gain], chunks[0])
    shared = (queries, keys, values, sums, totals, level_weight, local, other, other_rest)
    prefixes = [None, prefix]
    found, across = {}, {}
    mixed, at = None, 0

    def both(name, messages, tokens=()):
        return pack(name, [(state, size) for state in messages], tokens)

    for bit in range(1, bits):
        found[bit] = [trade(chunk, 2**bit) for chunk in (give if bit == 1 else chunks)]
        stays = chunks if bit == 1 else stays
        waits = []
        if bit < 3 or bit == last:
            stop = spans if bit == last else at + 1
            begun = [*chunks[-1:], *([found[bit - 1]] if bit == last else [])]
            mixed, *waits = mix_local(at, stop, shared, mixed, begun, True)
            at = stop
        if bit == 3:
            waits.append(rest)
        if bit < last:
            merged = {}
            order = list(reversed(range(CUTS)))
            for offset in order:
                ending = offset == order[-1]
                tokens_of = [*merged.values(), *(waits if ending else ())]
                merged[offset], *after = merge(
                    bit, offset, ending, chunks[offset], found[bit][offset], prefixes[bit], tokens_of
                )
            chunks = [merged[offset] for offset in range(CUTS)]
            newest = merged[order[-1]]
            prefixes += after
            found[bit] = both(f"found{bit}", found[bit], (newest,))
            if bit > 1:
                across[bit] = trade(found[bit], 2)
            else:
                rest = trade(both("rest", stays, (newest,)), 2)

    state = both("state", found[last], waits)
    beside = trade(state, 2)
    early = list(range(1, last))
    ours = pack("ours", [(found[bit], two) for bit in early], ())
    theirs = pack("theirs", [(rest if bit == 1 else across[bit], two) for bit in early], (state,))
    joined = pack("joined", [(ours, len(early) * two), (state, two)])
    joined_far = trade(joined, 1)
    theirs_far = trade(theirs, 1)
    ahead = [prefixes[bit] for bit in early]
    shared = (mixed, queries, sums, level_weight, gain)
    every = (first_level, [*early, last], shared, [*ahead, prefixes[last]])
    levels = [(slot, 0, slot * two) for slot in range(len(early))]
    whole = [*levels, (len(early), 0, len(early) * two)]
    parted = [*levels, (len(early), 1, 0)]
    (block,) = finish([((0, 0), whole)], *every, [joined], None, True, None)
    out, block_far = finish(
        [((1, 0), whole)], *every, [joined_far, block], None, True, (1, (0, 0))
    )
    beside = pack("beside", [(beside, two)], (block_far,))
    (out,) = finish(
        [((0, 1), parted)], *every, [theirs, beside, block_far], out, False, (2, (1, 0))
    )
    beside_far = trade(beside, 1)
    return finish(
        [((1, 1), parted)], *every, [theirs_far, beside_far], out, False, None
    )[0]


def solution(mesh):
    placed = (
        P(("wide", "narrow"), None),
        P(("wide", "narrow"), None),
        P(("wide", "narrow"), None),
        P(None, ("wide", "narrow")),
        P(None, None, ("wide", "narrow")),
        P(),
    )
    return jax.shard_map(
        per_device,
        mesh=mesh,
        in_specs=placed,
        out_specs=P(("wide", "narrow"), None),
        check_vma=False,
    )
```

```python
import functools

import jax
import jax.numpy as jnp
from jax import lax
from jax.experimental import pallas as pl
from jax.experimental.pallas import tpu as pltpu
from jax.sharding import PartitionSpec as P

SPAN = 256
SPLIT_BITS = 2
CUTS = 2
EPS = 1e-05
AXES = ("narrow", "wide")
NT = (((1,), (1,)), ((), ()))
COSTS = {"local0": 1000, "finish00": 20000000000, "finish10": 1000, "finish01": 20000000000, "local2": 1000, "reach": 1000}


def cost(name):
    flops = COSTS.get(name, 2000000000)
    return pl.CostEstimate(flops=flops, transcendentals=0, bytes_accessed=1_000_000)


PARAMS = pltpu.CompilerParams(vmem_limit_bytes=32 * 1024 * 1024)
HELD = pl.BlockSpec(memory_space=pltpu.VMEM)


def place():
    return lax.axis_index("wide") * lax.axis_size("narrow") + lax.axis_index("narrow")


def bit_of(value, bit):
    return jnp.bitwise_and(jnp.right_shift(value, bit), 1)


def spread_lanes(column, width):
    return jnp.broadcast_to(column, (column.shape[0], width))


ANYWHERE = pl.BlockSpec(memory_space=pl.ANY)


def hold(array):
    return pltpu.with_memory_space_constraint(array, pltpu.VMEM)


def call(kernel, name, inputs, outputs, scratch=(), in_specs=None, aliases=None):
    specs = in_specs or [HELD] * len(inputs)
    inputs = [hold(array) if spec is HELD else array for array, spec in zip(inputs, specs)]
    return pl.pallas_call(
        kernel,
        in_specs=specs,
        out_specs=[HELD] * len(outputs),
        out_shape=[pltpu.VMEM(shape, dtype) for shape, dtype in outputs],
        scratch_shapes=list(scratch),
        input_output_aliases=aliases or {},
        compiler_params=PARAMS,
        cost_estimate=cost(name),
        name=name,
    )(*inputs)


def running_sums(rows):
    high = rows.astype(jnp.bfloat16)
    rest = rows - high.astype(jnp.float32)
    middle = rest.astype(jnp.bfloat16)
    low = (rest - middle.astype(jnp.float32)).astype(jnp.bfloat16)
    width = rows.shape[1]
    source = lax.broadcasted_iota(jnp.int32, (width, width), 0)
    target = lax.broadcasted_iota(jnp.int32, (width, width), 1)
    upto = jnp.where(source <= target, 1.0, 0.0).astype(jnp.bfloat16)
    sums = jnp.dot(
        jnp.concatenate([high, middle, low], axis=0), upto, preferred_element_type=jnp.float32
    )
    count = rows.shape[0]
    return sums[:count] + (sums[count : 2 * count] + sums[2 * count :])


def state_kernel(*refs):
    k_hbm, v_hbm, decay_hbm = refs[:3]
    keep_ref, send_ref, local_ref, sums_ref, totals_ref = refs[3:8]
    k_ref, v_ref, decay_ref, held, message_ref, arrived = refs[8:]
    heads, tokens = decay_ref.shape
    head_width = v_ref.shape[1] // heads
    spans = tokens // SPAN
    rows_of = [slice(span * SPAN, (span + 1) * SPAN) for span in range(spans)]
    loads = [(decay_hbm, decay_ref), (k_hbm, k_ref)]
    loads += [(v_hbm.at[rows], v_ref.at[rows]) for rows in rows_of]
    copies = [
        pltpu.make_async_copy(source, target, arrived.at[at])
        for at, (source, target) in enumerate(loads)
    ]
    for copy in copies:
        copy.start()
    copies[0].wait()
    within = running_sums(jnp.concatenate([decay_ref[:, rows] for rows in rows_of], axis=0))
    run = jnp.zeros((heads, 128), jnp.float32)
    fades, wholes = [], []
    for span, rows in enumerate(rows_of):
        here = within[span * heads : (span + 1) * heads]
        last = here[:, SPAN - 1 :]
        total = spread_lanes(last, 128)
        sums_ref[0, :, rows] = here
        sums_ref[1, :, rows] = here + spread_lanes(run[:, :1], SPAN)
        totals_ref[span] = total
        run = run + total
        fades.append(jnp.exp(spread_lanes(last, SPAN) - here))
        wholes.append(jnp.exp(total))
    copies[1].wait()
    across = [k_ref[rows].astype(jnp.float32).T for rows in rows_of]
    local_bits = spans.bit_length() - 1
    for span, rows in enumerate(rows_of):
        copies[2 + span].wait()
        for head in range(heads):
            columns = slice(head * head_width, (head + 1) * head_width)
            faded = (across[span] * fades[span][head : head + 1]).astype(jnp.bfloat16)
            state = jnp.dot(faded, v_ref[rows, columns], preferred_element_type=jnp.float32)
            at = 0
            for bit in range(local_bits + 1):
                if span >> bit & 1 == 0 or bit == local_bits:
                    group = state
                    if span % 2**bit > 0:
                        group = held[bit - 1, head] * wholes[span][head : head + 1] + state
                    if (span + 1) % 2**bit > 0:
                        held[bit - 1, head] = group
                    elif bit < local_bits:
                        local_ref[at + (span >> (bit + 1)), :, columns] = group.astype(
                            jnp.bfloat16
                        )
                    else:
                        message_ref[columns] = group.T
                at += spans >> (bit + 1)
    half = message_ref.shape[0] // 2
    core = bit_of(place(), 0)
    keep_ref[:half] = message_ref[pl.ds(pl.multiple_of(core * half, 8), half)]
    send_ref[:half] = message_ref[pl.ds(pl.multiple_of((1 - core) * half, 8), half)]
    keep_ref[half:] = run
    send_ref[half:] = run


def make_states(keys, values, log_decay):
    tokens, key_width = keys.shape
    heads = log_decay.shape[0]
    width = values.shape[1]
    spans = tokens // SPAN
    inputs = [keys, values, log_decay]
    kept = [keys, values]
    return call(
        state_kernel,
        "states",
        [pltpu.with_memory_space_constraint(array, pltpu.HBM) for array in inputs],
        [
            ((width // 2 + heads, key_width), jnp.float32),
            ((width // 2 + heads, key_width), jnp.float32),
            ((spans - 1, key_width, width), jnp.bfloat16),
            ((2, heads, tokens), jnp.float32),
            ((spans, heads, 128), jnp.float32),
            *[(array.shape, array.dtype) for array in kept],
        ],
        [
            pltpu.VMEM(log_decay.shape, jnp.float32),
            pltpu.VMEM((spans.bit_length() - 1, heads, key_width, width // heads), jnp.float32),
            pltpu.VMEM((width, key_width), jnp.float32),
            pltpu.SemaphoreType.DMA((spans + 2,)),
        ],
        [pl.BlockSpec(memory_space=pltpu.HBM)] * len(inputs),
    )


def load_kernel(count, *refs):
    copies = [
        pltpu.make_async_copy(source, target, refs[-1].at[at])
        for at, (source, target) in enumerate(zip(refs[:count], refs[-1 - count : -1]))
    ]
    for copy in copies:
        copy.start()
    for copy in copies:
        copy.wait()


def load(arrays, token):
    count = len(arrays)
    hbm = pl.BlockSpec(memory_space=pltpu.HBM)
    return call(
        functools.partial(load_kernel, count),
        "load",
        [*[pltpu.with_memory_space_constraint(array, pltpu.HBM) for array in arrays], token],
        [(array.shape, array.dtype) for array in arrays],
        [pltpu.SemaphoreType.DMA((count,))],
        [*[hbm] * count, HELD],
    )


def local_kernel(first, last, has_token, *refs):
    q_ref, k_ref, v_ref, sums_ref, totals_ref, weight_ref, local_ref, near_ref, rest_ref = refs[:9]
    if has_token:
        mixed_ref, done_ref = refs[-2:]
        done_ref[...] = jnp.zeros_like(done_ref)
    else:
        mixed_ref = refs[-1]
    heads = weight_ref.shape[1]
    head_width = v_ref.shape[1] // heads
    spans = totals_ref.shape[0]
    local_bits = spans.bit_length() - 1
    half = SPAN // 2
    source = lax.broadcasted_iota(jnp.int32, (half, half), 0)
    target = lax.broadcasted_iota(jnp.int32, (half, half), 1)
    causal = source <= target
    empty = jnp.zeros((half, half), jnp.bfloat16)
    upper = jnp.where(bit_of(place(), 0) == 1, 1.0, 0.0)
    size = heads // 2 * head_width
    near, rest = near_ref[:size], rest_ref[:size]
    first_core = bit_of(place(), 0) == 0
    near = jnp.concatenate(
        [jnp.where(first_core, near, rest), jnp.where(first_core, rest, near)], axis=0
    ).astype(jnp.bfloat16)

    for span in range(first, last):
        tokens = slice(span * SPAN, (span + 1) * SPAN)
        queries = q_ref[tokens]
        scores = lax.dot_general(
            k_ref[tokens], queries, NT, preferred_element_type=jnp.float32
        )
        within = sums_ref[0, :, tokens]
        within_down = within.T
        weight = weight_ref[0, :, tokens]
        values_across = v_ref[tokens].T

        def mix(head, low, high):
            rows = slice(low * half, (low + 1) * half)
            columns = slice(high * half, (high + 1) * half)
            gap = within[head : head + 1, columns] - within_down[rows, head : head + 1]
            if low == high:
                gap = jnp.where(causal, gap, -1e30)
            mixing = scores[rows, columns] * jnp.exp(gap) * weight[head : head + 1, columns]
            return mixing.astype(jnp.bfloat16)

        levels = []
        offset = 0
        for bit in range(local_bits):
            if span >> bit & 1:
                since = within
                for back in range(1, span % 2**bit + 1):
                    since = since + spread_lanes(totals_ref[span - back][:, :1], SPAN)
                scale = jnp.exp(since) * weight_ref[1 + bit, :, tokens]
                levels.append((local_ref[offset + (span >> (bit + 1))].T, scale))
            offset += spans >> (bit + 1)
        reach = jnp.exp(sums_ref[1, :, tokens]) * weight_ref[1 + local_bits, :, tokens] * upper
        levels.append((near, reach))
        for head in range(heads):
            rows = slice(head * head_width, (head + 1) * head_width)
            mixing = jnp.concatenate(
                [
                    jnp.concatenate([mix(head, 0, 0), mix(head, 0, 1)], axis=1),
                    jnp.concatenate([empty, mix(head, 1, 1)], axis=1),
                ],
                axis=0,
            )
            mixed = jnp.dot(values_across[rows], mixing, preferred_element_type=jnp.float32)
            for level, scale in levels:
                found = lax.dot_general(
                    level[rows], queries, NT, preferred_element_type=jnp.float32
                )
                mixed = mixed + found * scale[head : head + 1]
            mixed_ref[rows, tokens] = mixed


def mix_local(first, last, shared, mixed, tokens, has_token):
    values = shared[2]
    rest = [] if mixed is None else [mixed]
    return call(
        functools.partial(local_kernel, first, last, has_token),
        f"local{first}",
        [*shared, *rest, *tokens],
        [(values.shape[::-1], jnp.float32), ((8, 128), jnp.float32)][: 1 + has_token],
        aliases={9: 0} if rest else None,
    )


def join(upper, mine, mine_total, other, other_total):
    fade = jnp.exp(jnp.where(upper, mine_total, other_total))
    return jnp.where(upper, other * fade + mine, mine * fade + other)


def first_head(far, heads):
    here = place()
    first = 0
    for bit, flip in enumerate(far):
        first = first + jnp.bitwise_xor(bit_of(here, bit), flip) * (heads >> (bit + 1))
    return first


def chip_kernel(mine_ref, other_ref, token_ref, *refs):
    *message_refs, next_ref, whole_ref = refs
    heads = next_ref.shape[0]
    width = whole_ref.shape[0]
    held = heads // 2
    per = width // held
    here = place()
    upper = bit_of(here, 0) == 1
    first = first_head((0,), heads)
    for slot in range(held):
        part = slice(slot * per, (slot + 1) * per)
        total = pl.ds(width + first + slot, 1)
        whole_ref[part] = join(
            upper, mine_ref[part], mine_ref[total], other_ref[part], other_ref[total]
        )
    other_total = other_ref[width:]
    total = mine_ref[width:] + other_total
    next_ref[...] = jnp.where(upper, other_total, 0.0)
    half = width // 2
    side = bit_of(here, 1)
    cuts = len(message_refs) // 2
    size = half // cuts
    for at, ref in enumerate(message_refs):
        start = (side if at < cuts else 1 - side) * half + at % cuts * size
        ref[:size] = whole_ref[pl.ds(pl.multiple_of(start, 8), size)]
        ref[size:] = total


def make_chip(mine, other, token, heads, cuts):
    rows, lanes = mine.shape
    half = rows - heads
    *messages, prefix = call(
        chip_kernel,
        "chip",
        [mine, other, token],
        [
            *[((half // 2 // cuts + heads, lanes), jnp.float32)] * (2 * cuts),
            ((heads, lanes), jnp.float32),
        ],
        [pltpu.VMEM((half, lanes), jnp.float32)],
    )
    return messages[:cuts], messages[cuts:], prefix


def merge_kernel(bit, offset, has_prefix, *refs):
    mine_ref, other_ref, prefix_ref = refs[:3]
    merged_ref = refs[-2] if has_prefix else refs[-1]
    heads = prefix_ref.shape[0]
    rows = mine_ref.shape[0] - heads
    per = mine_ref.shape[1]
    upper = bit_of(place(), bit) == 1
    first = first_head((0,) * SPLIT_BITS, heads) + offset
    for slot in range(rows // per):
        part = slice(slot * per, (slot + 1) * per)
        total = pl.ds(rows + first + slot, 1)
        merged_ref[part] = join(
            upper, mine_ref[part], mine_ref[total], other_ref[part], other_ref[total]
        )
    other_total = other_ref[rows:]
    merged_ref[rows:] = mine_ref[rows:] + other_total
    if has_prefix:
        refs[-1][...] = prefix_ref[...] + jnp.where(upper, other_total, 0.0)


def merge(bit, offset, has_prefix, mine, other, prefix, tokens=()):
    return call(
        functools.partial(merge_kernel, bit, offset, has_prefix),
        f"merge{bit}{offset}",
        [mine, other, prefix, *tokens],
        [(mine.shape, jnp.float32), (prefix.shape, jnp.float32)][: 1 + has_prefix],
    )


def pack_kernel(takes, *refs):
    out_ref = refs[-1]
    at = 0
    for ref, rows in zip(refs, takes):
        out_ref[at : at + rows] = ref[:rows]
        at += rows


def pack(name, pieces, tokens=()):
    takes = [rows for _, rows in pieces]
    lanes = pieces[0][0].shape[1]
    return call(
        functools.partial(pack_kernel, takes),
        name,
        [*[array for array, _ in pieces], *tokens],
        [((sum(takes), lanes), jnp.float32)],
    )[0]


def level_scale(bit, first_level, prefix_ref, sums_ref, weight_ref, tokens):
    active = jnp.where(bit_of(place(), bit) == 1, 1.0, 0.0)
    reach = jnp.exp(sums_ref[1, :, tokens] + spread_lanes(prefix_ref[:, :1], SPAN))
    return reach * weight_ref[first_level + bit, :, tokens] * active


def gather_work(quarters, part_refs, heads, per):
    work = []
    for far, pieces in quarters:
        first = first_head(far, heads)
        for slot in range(heads // 4):
            states = []
            for level, index, start in pieces:
                if start is None:
                    rows = pl.ds(pl.multiple_of((first + slot) * per, 128), per)
                else:
                    rows = slice(start + slot * per, start + (slot + 1) * per)
                states.append((level, part_refs[index][rows].astype(jnp.bfloat16)))
            work.append((first + slot, states))
    return work


def add_found(mixed, queries, head, states, scale_ref):
    for level, state in states:
        found = lax.dot_general(state, queries, NT, preferred_element_type=jnp.float32)
        mixed = mixed + found * scale_ref[level, pl.ds(head, 1)]
    return mixed


def finish_kernel(quarters, first_level, bits, stays, carried, *refs):
    mixed_ref, q_ref, sums_ref, weight_ref, gain_ref = refs[:5]
    prefix_refs = refs[5 : 5 + len(bits)]
    part_refs = refs[5 + len(bits) :]
    out_refs, (own_ref, scale_ref, sent) = refs[-3 - FINISH_OUTS[stays, carried] : -3], refs[-3:]
    if stays:
        own_ref = out_refs[-1]
    heads = weight_ref.shape[1]
    head_width = mixed_ref.shape[0] // heads
    size = heads // 4 * head_width
    copies = []

    def send(block, far, rows):
        columns = pl.ds(pl.multiple_of(first_head(far, heads) * head_width, 128), size)
        copy = pltpu.make_async_copy(
            block.at[rows], out_refs[0].at[rows, columns], sent.at[len(copies)]
        )
        copy.start()
        copies.append(copy)

    if carried is not None:
        index, far = carried
        for start in range(0, q_ref.shape[0], SPAN):
            send(part_refs[index], far, slice(start, start + SPAN))
    work = gather_work(quarters, part_refs, heads, head_width)
    gains = []
    for head, _ in work:
        row = jnp.broadcast_to(gain_ref[pl.ds(head, 1)], (8, head_width))
        gains.append(row.T[:, :1])
    for span in range(q_ref.shape[0] // SPAN):
        tokens = slice(span * SPAN, (span + 1) * SPAN)
        queries = q_ref[tokens]
        for level, (bit, prefix_ref) in enumerate(zip(bits, prefix_refs)):
            scale_ref[level] = level_scale(
                bit, first_level, prefix_ref, sums_ref, weight_ref, tokens
            )
        for at, (head, states) in enumerate(work):
            rows = pl.ds(pl.multiple_of(head * head_width, 128), head_width)
            mixed = add_found(mixed_ref[rows, tokens], queries, head, states, scale_ref)
            square = jnp.mean(mixed * mixed, axis=0, keepdims=True)
            normed = mixed * lax.rsqrt(square + EPS) * gains[at]
            columns = slice(at * head_width, (at + 1) * head_width)
            own_ref[tokens, columns] = normed.astype(jnp.bfloat16).T
        if not stays:
            for start in range(tokens.start, tokens.stop, SPAN // 2):
                send(own_ref, quarters[0][0], slice(start, start + SPAN // 2))
    for copy in copies:
        copy.wait()


FINISH_OUTS = {}


def finish(quarters, first_level, bits, shared, prefixes, parts, begun, stays, carried):
    mixed, queries, sums, level_weight, gain = shared
    width, tokens = mixed.shape
    heads = level_weight.shape[1]
    inputs = [*shared, *prefixes, *parts]
    specs = [HELD] * len(inputs)
    inputs = [hold(array) for array in inputs]
    hbm = pl.BlockSpec(memory_space=pltpu.HBM)
    aliases = {}
    if begun is not None:
        aliases = {len(inputs): 0}
        specs.append(hbm)
        inputs.append(begun)
    name = "finish" + "".join(f"{core}{side}" for (core, side), _ in quarters)
    block = (tokens, width // 4)
    out_specs, shapes = [], []
    if carried is not None or not stays:
        out_specs.append(hbm)
        shapes.append(jax.ShapeDtypeStruct((tokens, width), jnp.bfloat16))
    if stays:
        out_specs.append(HELD)
        shapes.append(pltpu.VMEM(block, jnp.bfloat16))
    FINISH_OUTS[stays, carried] = len(shapes)
    return pl.pallas_call(
        functools.partial(finish_kernel, quarters, first_level, bits, stays, carried),
        in_specs=specs,
        out_specs=out_specs,
        out_shape=shapes,
        scratch_shapes=[
            pltpu.VMEM((8, 128) if stays else block, jnp.bfloat16),
            pltpu.VMEM((len(bits), heads, SPAN), jnp.float32),
            pltpu.SemaphoreType.DMA((3 * tokens // SPAN,)),
        ],
        input_output_aliases=aliases,
        compiler_params=PARAMS,
        cost_estimate=cost(name),
        name=name,
    )(*inputs)


def trade(value, mask):
    wide, narrow = lax.axis_size("wide"), lax.axis_size("narrow")

    def ranked(index):
        return index % narrow * wide + index // narrow

    pairs = [(ranked(source), ranked(source ^ mask)) for source in range(wide * narrow)]
    return lax.ppermute(value, AXES, pairs)


def per_device(queries, keys, values, log_decay, level_weight, norm_gain):
    heads = log_decay.shape[0]
    tokens, width = values.shape
    per = width // heads
    spans = tokens // SPAN
    group_bits = heads.bit_length() - 1
    bits = (lax.axis_size("wide") * lax.axis_size("narrow")).bit_length() - 1
    first_level = level_weight.shape[0] - bits
    gain = norm_gain.reshape(heads, per)
    keep, send, local, sums, totals, keys, values = make_states(keys, values, log_decay)
    last = bits - 1
    two = 2 * per
    size = two // CUTS
    sides = [(core, side) for core in (0, 1) for side in (0, 1)]
    other, other_rest = trade(send, 1), trade(keep, 1)
    queries, level_weight, gain = load([queries, level_weight, gain], send)
    chunks, give, prefix = make_chip(keep, other, gain, heads, CUTS)
    shared = (queries, keys, values, sums, totals, level_weight, local, other, other_rest)
    prefixes = [None, prefix]
    found, across = {}, {}
    mixed, at = None, 0

    def both(name, messages, tokens=()):
        return pack(name, [(state, size) for state in messages], tokens)

    for bit in range(1, bits):
        found[bit] = [trade(chunk, 2**bit) for chunk in (give if bit == 1 else chunks)]
        stays = chunks if bit == 1 else stays
        waits = []
        if bit < 3 or bit == last:
            stop = spans if bit == last else at + 1
            begun = [*chunks[-1:], *([found[bit - 1]] if bit == last else [])]
            mixed, *waits = mix_local(at, stop, shared, mixed, begun, True)
            at = stop
        if bit == 3:
            waits.append(rest)
        if bit < last:
            merged = {}
            order = list(reversed(range(CUTS)))
            for offset in order:
                ending = offset == order[-1]
                tokens_of = [*merged.values(), *(waits if ending else ())]
                merged[offset], *after = merge(
                    bit, offset, ending, chunks[offset], found[bit][offset], prefixes[bit], tokens_of
                )
            chunks = [merged[offset] for offset in range(CUTS)]
            newest = merged[order[-1]]
            prefixes += after
            found[bit] = both(f"found{bit}", found[bit], (newest,))
            if bit > 1:
                across[bit] = trade(found[bit], 2)
            else:
                rest = trade(both("rest", stays, (newest,)), 2)

    state = both("state", found[last], waits)
    beside = trade(state, 2)
    early = list(range(1, last))
    ours = pack("ours", [(found[bit], two) for bit in early], ())
    theirs = pack("theirs", [(rest if bit == 1 else across[bit], two) for bit in early], (state,))
    joined = pack("joined", [(ours, len(early) * two), (state, two)])
    joined_far = trade(joined, 1)
    theirs_far = trade(theirs, 1)
    ahead = [prefixes[bit] for bit in early]
    shared = (mixed, queries, sums, level_weight, gain)
    every = (first_level, [*early, last], shared, [*ahead, prefixes[last]])
    levels = [(slot, 0, slot * two) for slot in range(len(early))]
    whole = [*levels, (len(early), 0, len(early) * two)]
    parted = [*levels, (len(early), 1, 0)]
    (block,) = finish([((0, 0), whole)], *every, [joined], None, True, None)
    out, block_far = finish(
        [((1, 0), whole)], *every, [joined_far, block], None, True, (1, (0, 0))
    )
    beside = pack("beside", [(beside, two)], (block_far,))
    (out,) = finish(
        [((0, 1), parted)], *every, [theirs, beside, block_far], out, False, (2, (1, 0))
    )
    beside_far = trade(beside, 1)
    return finish(
        [((1, 1), parted)], *every, [theirs_far, beside_far], out, False, None
    )[0]


def solution(mesh):
    placed = (
        P(("wide", "narrow"), None),
        P(("wide", "narrow"), None),
        P(("wide", "narrow"), None),
        P(None, ("wide", "narrow")),
        P(None, None, ("wide", "narrow")),
        P(),
    )
    return jax.shard_map(
        per_device,
        mesh=mesh,
        in_specs=placed,
        out_specs=P(("wide", "narrow"), None),
        check_vma=False,
    )
```
